32 devices in a mesh: fsdp: 4 (over x, core), ctx: 2 (over y), tp: 4 (over z).
Axes of the slice: x: 2, y: 2, z: 4, core: 2. Of those that a mesh axis runs over, the one named last changes fastest.
Arguments:
- layer_input: bfloat16 [6144, 2048], P(('fsdp', 'ctx'), 'tp'), may hold values from -6 to 6
- token_order: int32 [4, 1536], P('fsdp', 'ctx'), may hold values from 0 to 1535, each once within a row
- doc_lengths: int32 [4, 3], P('fsdp'), may hold values from 1 to 1024, 1536 in all within a row
- expert_routes: int32 [6144, 8], P(('fsdp', 'ctx')), may hold values from 0 to 31, all different within a row; in each aligned block of 768 rows (0 to 767, 768 to 1535, ...) at most 240 rows name the same one
- attn_gain: bfloat16 [2048], P(('fsdp', 'ctx')), may hold values from 0.5 to 1.5
- query_weight: bfloat16 [2048, 2048], P(('fsdp', 'ctx'), 'tp'), may hold values from -0.125 to 0.125
- key_weight: bfloat16 [2048, 2048], P(('fsdp', 'ctx'), 'tp'), may hold values from -0.125 to 0.125
- value_weight: bfloat16 [2048, 2048], P(('fsdp', 'ctx'), 'tp'), may hold values from -0.125 to 0.125
- query_gain: float32 [128], replicated, may hold values from 1 to 2
- key_gain: float32 [128], replicated, may hold values from 1 to 2
- out_weight: bfloat16 [2048, 2048], P('tp', ('fsdp', 'ctx')), may hold values from -0.5 to 0.5
- moe_gain: bfloat16 [2048], P(('fsdp', 'ctx')), may hold values from 0.5 to 1.5
- router_weight: bfloat16 [2048, 32], P(('fsdp', 'ctx')), may hold values from -0.0625 to 0.0625
- gate_weight: bfloat16 [32, 2048, 1024], P(('fsdp', 'ctx'), None, 'tp'), may hold values from -0.125 to 0.125
- up_weight: bfloat16 [32, 2048, 1024], P(('fsdp', 'ctx'), None, 'tp'), may hold values from -0.125 to 0.125
- down_weight: bfloat16 [32, 1024, 2048], P(('fsdp', 'ctx'), 'tp'), may hold values from -0.5 to 0.5
- out_grad: bfloat16 [6144, 2048], P(('fsdp', 'ctx'), 'tp'), may hold values from -6 to 6
Outputs:
- layer_output: bfloat16 [6144, 2048], P(('fsdp', 'ctx'), 'tp')
- grad_input: float32 [6144, 2048], P(('fsdp', 'ctx'), 'tp')
- grad_attn_gain: float32 [2048], P(('fsdp', 'ctx'))
- grad_query_weight: float32 [2048, 2048], P(('fsdp', 'ctx'), 'tp')
- grad_key_weight: float32 [2048, 2048], P(('fsdp', 'ctx'), 'tp')
- grad_value_weight: float32 [2048, 2048], P(('fsdp', 'ctx'), 'tp')
- grad_query_gain: float32 [128], replicated
- grad_key_gain: float32 [128], replicated
- grad_out_weight: float32 [2048, 2048], P('tp', ('fsdp', 'ctx'))
- grad_moe_gain: float32 [2048], P(('fsdp', 'ctx'))
- grad_router_weight: float32 [2048, 32], P(('fsdp', 'ctx'))
- grad_gate_weight: float32 [32, 2048, 1024], P(('fsdp', 'ctx'), None, 'tp')
- grad_up_weight: float32 [32, 2048, 1024], P(('fsdp', 'ctx'), None, 'tp')
- grad_down_weight: float32 [32, 1024, 2048], P(('fsdp', 'ctx'), 'tp')
The draws below stay inside these ranges and needn't reach their ends.
Inputs may be any that keep to these rules, and one draw needn't show every extreme that they name: `token_order`: each row is a permutation of 0 to 1535. `doc_lengths`: each row holds the lengths of its group's 3 documents and sums to 1536. `expert_routes`: each row names 8 different experts; within the rows of one device no expert is named more than 240 times.
All inputs are finite; a program needn't handle non-finite values.
Results may differ from the reference program's by a relative error of at most 0.028.
Values may be sent and summed in bfloat16 or wider, within the bound.
A program may use at most 512 MiB of HBM per device.

```python
import math
import jax
import jax.numpy as jnp
import numpy as np
from jax import lax

D = 2048
HEADS = 16
HEAD_DIM = 128
FF = 1024
EXPERTS = 32
TOP = 8
GROUP_TOK = 1536
MAXLEN = 1024
KEY_BLOCK = 512
DOCS = 3
TOK_DEV = 768
TOKENS = 6144
CAP = 240
N_FSDP = 4
N_CTX = 2


def shard_levels(rng, shape, cuts, low, top_value):
    def one(dim, parts):
        steps = jax.random.uniform(jax.random.fold_in(jax.random.fold_in(rng, 6), dim), (parts,), jnp.float32, low / len(cuts), top_value / len(cuts))
        return jnp.repeat(jnp.exp(steps), shape[dim] // parts).reshape((-1,) + (1,) * (len(shape) - dim - 1))

    level = one(*cuts[0])
    for cut in cuts[1:]:
        level = level * one(*cut)
    return level


def length_profile(count, total, most, slope):
    portions = [(1 << 20) // math.isqrt(standing ** slope) + 1 for standing in range(2, count + 1)]
    spare, counts = total - most - (count - 1), [1] * (count - 1)
    while spare > 0:
        candidates = [i for i in range(count - 1) if counts[i] < most]
        mass, left = sum([portions[i] for i in candidates]), spare
        for i in candidates:
            addition = min(most - counts[i], max(1, left * portions[i] // mass), spare)
            counts[i] = counts[i] + addition
            spare = spare - addition
    return np.array([most] + counts)


def uneven(key, number_of, total, bound, slope):
    if number_of == 2:
        one = jax.random.randint(key, (), max(1, total - bound), min(bound, total - 1) + 1)
        return jnp.stack([one, total - one])
    tallies = jnp.asarray(length_profile(number_of, total, bound, slope), jnp.int32)
    pairs = (number_of - 1) // 2
    giver, receiver = tallies[1:1 + 2 * pairs:2], tallies[2:2 + 2 * pairs:2]
    room = jnp.minimum(giver - 1, bound - receiver)
    shifted = jax.random.randint(jax.random.fold_in(key, 1), (pairs,), 0, 1 << 20) % (room + 1)
    tallies = tallies.at[1:1 + 2 * pairs:2].set(giver - shifted).at[2:2 + 2 * pairs:2].set(receiver + shifted)
    return tallies[jax.random.permutation(jax.random.fold_in(key, 2), number_of)]


def assign_block(stream_key, own, number, rows, amount, top, most, slope):
    order = jax.random.permutation(stream_key, amount)
    heavy_load, ordinary = shares(amount, rows * top, most, slope, True), shares(amount, rows * top, most, slope, False)
    places = jnp.arange(amount)

    def named(tallies, offset_by):
        used = int((tallies > 0).sum())
        fixed = max(1, used // 4)
        shifted = fixed + (places - fixed + offset_by * (used - fixed)) % max(1, amount - fixed)
        return jnp.zeros((amount,), jnp.int32).at[order[jnp.where(places < fixed, places, shifted)]].set(jnp.asarray(tallies, jnp.int32))

    tallies = jnp.where(number % 4 == 0, named(heavy_load, number // 4), named(ordinary, number - number // 4 - 1))
    mixed = jax.random.permutation(jax.random.fold_in(own, 3), amount)
    giver, receiver = mixed[0:amount // 2 * 2:2], mixed[1:amount // 2 * 2:2]
    margin = jnp.minimum(tallies[giver] - 1, most - tallies[receiver]) // 2
    margin = jnp.where((giver == order[0]) | (receiver == order[0]) | (tallies[receiver] == 0), 0, jnp.maximum(margin, 0))
    shifted = jax.random.randint(jax.random.fold_in(own, 4), (amount // 2,), 0, 1 << 20) % (margin + 1)
    tallies = tallies.at[giver].add(-shifted).at[receiver].add(shifted)
    labels = jnp.searchsorted(jnp.cumsum(tallies), jnp.arange(rows * top), side="right").astype(jnp.int32)
    listing = labels.reshape(top, rows).T
    listing = listing[jax.random.permutation(jax.random.fold_in(own, 1), rows)]
    offset_by = jax.random.randint(jax.random.fold_in(own, 2), (rows, 1), 0, top)
    return jnp.take_along_axis(listing, (jnp.arange(top)[None, :] + offset_by) % top, axis=1)


def shares(amount, total, most, slope, full):
    weights = [(1 << 20) // math.isqrt(rank ** slope) + 1 for rank in range(1, amount + 1)]
    largest = most if full else min(most, max(-(-total // amount), total * weights[0] // sum(weights)))
    least = 1 if total - largest >= amount - 1 else 0
    given, rest = [largest] + [least] * (amount - 1), total - largest - least * (amount - 1)
    while rest > 0:
        movable = [i for i in range(1, amount) if given[i] < largest] or [i for i in range(1, amount) if given[i] < most]
        pool, budget = sum([weights[i] for i in movable]), rest
        for i in movable:
            extra = min(most - given[i], max(1, budget * weights[i] // pool), rest)
            given[i] = given[i] + extra
            rest = rest - extra
    return np.array(given)


def noise(own_key, shape, scale, limit, cuts=(), held_as=jnp.bfloat16):
    entries = scale * jax.random.normal(own_key, shape, jnp.float32)
    if cuts:
        entries = entries * shard_levels(own_key, shape, cuts, -0.22, 0.18)
    return jnp.clip(entries, -limit, limit).astype(held_as)


def setup_inputs(seed: int = 0) -> dict:
    streams_of = jax.random.split(jax.random.key(seed), 18)
    layer_input = noise(streams_of[0], (TOKENS, D), 1.0, 6.0, ((0, 8), (1, 4)))
    token_order = jax.vmap(lambda own: jax.random.permutation(own, GROUP_TOK))(jax.random.split(streams_of[1], N_FSDP)).reshape((N_FSDP, GROUP_TOK)).astype(jnp.int32)
    doc_lengths = jax.vmap(lambda own: uneven(own, DOCS, GROUP_TOK, MAXLEN, 2))(jax.random.split(streams_of[2], N_FSDP)).reshape((N_FSDP, DOCS)).astype(jnp.int32)
    expert_routes_keys = jax.random.split(jax.random.fold_in(streams_of[3], 1), TOKENS // TOK_DEV)
    expert_routes_turns = jax.random.permutation(jax.random.fold_in(streams_of[3], 3), TOKENS // TOK_DEV)
    expert_routes = jax.vmap(lambda own, number: assign_block(jax.random.fold_in(streams_of[3], 2), own, number, TOK_DEV, EXPERTS, TOP, CAP, 2))(expert_routes_keys, expert_routes_turns).reshape((TOKENS, TOP))
    attn_gain = jnp.clip(1.0 + 0.1 * jax.random.normal(streams_of[4], (D,), jnp.float32), 0.5, 1.5).astype(jnp.bfloat16)
    query_weight = noise(streams_of[5], (D, HEADS * HEAD_DIM), D ** -0.5, 0.125, ((0, 8), (1, 4)))
    key_weight = noise(streams_of[6], (D, HEADS * HEAD_DIM), D ** -0.5, 0.125, ((0, 8), (1, 4)))
    value_weight = noise(streams_of[7], (D, HEADS * HEAD_DIM), D ** -0.5, 0.125, ((0, 8), (1, 4)))
    query_gain = jnp.clip(jax.random.uniform(streams_of[8], (HEAD_DIM,), jnp.float32, 1.0, 2.0), 1.0, 2.0)
    key_gain = jnp.clip(jax.random.uniform(streams_of[9], (HEAD_DIM,), jnp.float32, 1.0, 2.0), 1.0, 2.0)
    out_weight = noise(streams_of[10], (HEADS * HEAD_DIM, D), (HEADS * HEAD_DIM // 16) ** -0.5, 0.5, ((0, 4), (1, 8)))
    moe_gain = jnp.clip(1.0 + 0.1 * jax.random.normal(streams_of[11], (D,), jnp.float32), 0.5, 1.5).astype(jnp.bfloat16)
    router_weight = noise(streams_of[12], (D, EXPERTS), (4 * D) ** -0.5, 0.0625, ((0, 8),))
    gate_weight = noise(streams_of[13], (EXPERTS, D, FF), D ** -0.5, 0.125, ((0, 8), (2, 4)))
    up_weight = noise(streams_of[14], (EXPERTS, D, FF), D ** -0.5, 0.125, ((0, 8), (2, 4)))
    down_weight = noise(streams_of[15], (EXPERTS, FF, D), (FF // 8) ** -0.5, 0.5, ((0, 8), (1, 4)))
    out_grad = noise(streams_of[16], (TOKENS, D), 1.0, 6.0, ((0, 8), (1, 4)))
    return {"layer_input": layer_input, "token_order": token_order, "doc_lengths": doc_lengths, "expert_routes": expert_routes, "attn_gain": attn_gain, "query_weight": query_weight, "key_weight": key_weight, "value_weight": value_weight, "query_gain": query_gain, "key_gain": key_gain, "out_weight": out_weight, "moe_gain": moe_gain, "router_weight": router_weight, "gate_weight": gate_weight, "up_weight": up_weight, "down_weight": down_weight, "out_grad": out_grad}


epsilon = 1e-05
rope_base = 50000.0
masked_score = -1e+30
highest = lax.Precision.HIGHEST

@jax.custom_vjp
def low(v):
    return lax.optimization_barrier(v.astype(jnp.bfloat16)).astype(jnp.float32)

@jax.custom_vjp
def low_back(v):
    return v

def low_keep(v):
    return (low(v), None)

def low_pass(kept, grad):
    return (grad,)

def back_keep(v):
    return (v, None)

def back_low(kept, grad):
    return (low(grad),)
low.defvjp(low_keep, low_pass)
low_back.defvjp(back_keep, back_low)

def rms_norm(values, gain):
    inverse = lax.rsqrt(lax.optimization_barrier(jnp.mean(values * values, axis=-1, keepdims=True)) + epsilon)
    return values * inverse * gain

def doc_places(order_row, length_row):
    ends = jnp.cumsum(length_row, dtype=jnp.int32)
    passed = (order_row[:, None] >= ends[None, :]).astype(jnp.int32)
    segment = lax.optimization_barrier(jnp.sum(passed, axis=1, dtype=jnp.int32))
    start = lax.optimization_barrier(jnp.sum(passed * length_row[None, :], axis=1, dtype=jnp.int32))
    return (segment, order_row - start)

def rope_tables(position):
    half = HEAD_DIM // 2
    freqs = rope_base ** (-(jnp.arange(half, dtype=jnp.float32) * (2.0 / HEAD_DIM)))
    angles = position.astype(jnp.float32)[:, None] * freqs[None, :]
    return (jnp.cos(angles)[:, None, :], jnp.sin(angles)[:, None, :])

def rotate(values, cosine, sine):
    half = values.shape[-1] // 2
    first = values[..., :half]
    second = values[..., half:]
    return jnp.concatenate([first * cosine - second * sine, second * cosine + first * sine], axis=-1)

def attend(query_block, seg_block, key_group, value_group, seg_group):
    scores = jnp.einsum('qhd,khd->hqk', query_block, key_group, precision=highest) * HEAD_DIM ** (-0.5)
    scores = low_back(scores)
    allowed = (seg_block[:, None] == seg_group[None, :])[None]
    scores = jnp.where(allowed, scores, masked_score)
    probs = jax.nn.softmax(scores, axis=-1)
    return jnp.einsum('hqk,khd->qhd', low(probs), value_group, precision=highest)

def expert_block(normed_rows, route_rows, router_weight, gate_weight, up_weight, down_weight):
    logits = jnp.dot(normed_rows, router_weight, precision=highest)
    gates = jax.nn.softmax(jnp.take_along_axis(logits, route_rows, axis=1), axis=-1)
    flat_routes = route_rows.reshape(TOK_DEV * TOP)
    one_hot = (flat_routes[:, None] == jnp.arange(EXPERTS, dtype=jnp.int32)[None, :]).astype(jnp.int32)
    ranks = jnp.cumsum(one_hot, axis=0, dtype=jnp.int32) - one_hot
    place = flat_routes * CAP + lax.optimization_barrier(jnp.sum(ranks * one_hot, axis=1, dtype=jnp.int32))
    token_ids = jnp.arange(TOK_DEV * TOP, dtype=jnp.int32) // TOP
    source_token = jnp.zeros((EXPERTS * CAP,), jnp.int32).at[place].set(token_ids)
    filled = jnp.zeros((EXPERTS * CAP,), jnp.float32).at[place].set(1.0)
    expert_in = low_back(normed_rows[source_token] * filled[:, None]).reshape(EXPERTS, CAP, D)
    gate_act = low_back(jnp.einsum('ecd,edf->ecf', expert_in, gate_weight, precision=highest))
    up_act = low_back(jnp.einsum('ecd,edf->ecf', expert_in, up_weight, precision=highest))
    hidden = low(jax.nn.silu(gate_act) * up_act)
    expert_out = low(low_back(jnp.einsum('ecf,efd->ecd', hidden, down_weight, precision=highest)))
    picked = expert_out.reshape(EXPERTS * CAP, D)[place].reshape(TOK_DEV, TOP, D)
    return jnp.einsum('tk,tkd->td', gates, picked, precision=highest)

def reference(layer_input, token_order, doc_lengths, expert_routes, attn_gain, query_weight, key_weight, value_weight, query_gain, key_gain, out_weight, moe_gain, router_weight, gate_weight, up_weight, down_weight, out_grad):
    segment, position = jax.vmap(doc_places)(token_order, doc_lengths)
    segment = segment.reshape(TOKENS)
    cosine, sine = rope_tables(position.reshape(TOKENS))
    blocks = GROUP_TOK // KEY_BLOCK
    checked_attend = jax.checkpoint(attend)
    checked_expert = jax.checkpoint(expert_block)

    def layer(inputs, gain_one, query_w, key_w, value_w, query_g, key_g, out_w, gain_two, router_w, gate_w, up_w, down_w):
        normed = low(rms_norm(inputs, gain_one))
        query_pre = low_back(jnp.dot(normed, query_w, precision=highest)).reshape(TOKENS, HEADS, HEAD_DIM)
        key_pre = low_back(jnp.dot(normed, key_w, precision=highest)).reshape(TOKENS, HEADS, HEAD_DIM)
        query = low(rotate(rms_norm(query_pre, query_g), cosine, sine))
        key = low(rotate(rms_norm(key_pre, key_g), cosine, sine))
        value = low(low_back(jnp.dot(normed, value_w, precision=highest))).reshape(TOKENS, HEADS, HEAD_DIM)

        def group_attend(pieces):
            query_group, key_group, value_group, seg_group = pieces

            def one_block(items):
                return checked_attend(items[0], items[1], key_group, value_group, seg_group)
            return lax.map(one_block, (query_group.reshape(blocks, KEY_BLOCK, HEADS, HEAD_DIM), seg_group.reshape(blocks, KEY_BLOCK)))
        attended = lax.map(group_attend, (query.reshape(N_FSDP, GROUP_TOK, HEADS, HEAD_DIM), key.reshape(N_FSDP, GROUP_TOK, HEADS, HEAD_DIM), value.reshape(N_FSDP, GROUP_TOK, HEADS, HEAD_DIM), segment.reshape(N_FSDP, GROUP_TOK)))
        attn_rows = low(low_back(attended.reshape(TOKENS, HEADS * HEAD_DIM)))
        resid = inputs + low_back(jnp.dot(attn_rows, out_w, precision=highest))
        moe_in = low(rms_norm(resid, gain_two))

        def one_device(items):
            return checked_expert(items[0], items[1], router_w, gate_w, up_w, down_w)
        moe_out = lax.map(one_device, (moe_in.reshape(N_FSDP * N_CTX, TOK_DEV, D), expert_routes.reshape(N_FSDP * N_CTX, TOK_DEV, TOP)))
        return resid + moe_out.reshape(TOKENS, D)
    floats = [values.astype(jnp.float32) for values in (layer_input, attn_gain, query_weight, key_weight, value_weight, query_gain, key_gain, out_weight, moe_gain, router_weight, gate_weight, up_weight, down_weight)]
    result, pullback = jax.vjp(layer, *floats)
    grads = pullback(out_grad.astype(jnp.float32))
    return (result.astype(jnp.bfloat16), grads[0], grads[1], grads[2], grads[3], grads[4], grads[5], grads[6], grads[7], grads[8], grads[9], grads[10], grads[11], grads[12])
```

```python
import functools

import jax
import jax.numpy as jnp
from jax import lax
from jax.experimental import pallas as pl
from jax.experimental.pallas import tpu as pltpu
from jax.sharding import PartitionSpec as P

KEY_BLOCK = 512
CHUNK = 768
SLOTS = 256
EXTRA = 128
VMEM_BYTES = 60 * 1024 * 1024


epsilon = 1e-05
rope_base = 50000.0
masked_score = -1e30
highest = lax.Precision.HIGHEST
bf16 = jnp.bfloat16
f32 = jnp.float32
ROWS = ("fsdp", "ctx")
ALL = ("fsdp", "ctx", "tp")


def doc_places(order_row, length_row):
    ends = jnp.cumsum(length_row, dtype=jnp.int32)
    passed = (order_row[:, None] >= ends[None, :]).astype(jnp.int32)
    segment = jnp.sum(passed, axis=1, dtype=jnp.int32)
    start = jnp.sum(passed * length_row[None, :], axis=1, dtype=jnp.int32)
    return (segment, order_row - start)


def rope_tables(position, head_dim):
    half = head_dim // 2
    freqs = rope_base ** (-(jnp.arange(half, dtype=jnp.float32) * (2.0 / head_dim)))
    angles = position.astype(jnp.float32)[:, None] * freqs[None, :]
    return (jnp.cos(angles)[:, None, :], jnp.sin(angles)[:, None, :])


def rotate(values, cosine, sine):
    half = values.shape[-1] // 2
    first = values[..., :half]
    second = values[..., half:]
    return jnp.concatenate(
        [first * cosine - second * sine, second * cosine + first * sine], axis=-1
    )


def rotate_back(grads, cosine, sine):
    half = grads.shape[-1] // 2
    first = grads[..., :half]
    second = grads[..., half:]
    return jnp.concatenate(
        [first * cosine + second * sine, second * cosine - first * sine], axis=-1
    )


def norm_scale(values):
    return lax.rsqrt(jnp.mean(values * values, axis=-1, keepdims=True) + epsilon)


def norm_back(incoming, values, inverse, gain):
    scaled = incoming * gain
    value_grad = inverse * (
        scaled - values * inverse * inverse * jnp.mean(scaled * values, axis=-1, keepdims=True)
    )
    return (value_grad, incoming * values * inverse)


def matmul(left, right):
    return jnp.dot(left, right, preferred_element_type=f32)


def matmul_nt(left, right):
    return lax.dot_general(left, right, (((1,), (1,)), ((), ())), preferred_element_type=f32)


def slot_rows(rank_row):
    slots = lax.broadcasted_iota(jnp.int32, (SLOTS, rank_row.shape[1]), 0)
    return slots == rank_row


def slot_columns(rank_column):
    slots = lax.broadcasted_iota(jnp.int32, (rank_column.shape[0], SLOTS), 1)
    return jnp.where(slots == rank_column, 1.0, 0.0).astype(bf16)


def as_one_hot(mask):
    return jnp.where(mask, 1.0, 0.0).astype(bf16)


def select_grads(rank_ref, grad_ref, down_ref, rows_ref, product_ref):
    expert = pl.program_id(1)
    rows = matmul(as_one_hot(slot_rows(rank_ref[...])), grad_ref[...]).astype(bf16)
    rows_ref[...] = rows
    product_ref[...] = matmul_nt(rows, down_ref[expert])


def expert_pass(
    first_ref,
    rank_ref,
    column_ref,
    token_ref,
    product_ref,
    gate_ref,
    up_ref,
    rows_ref,
    hidden_ref,
    gate_grad_ref,
    up_grad_ref,
    route_ref,
    back_ref,
    held_ref,
):
    expert = pl.program_id(1)
    local = pl.num_programs(1)
    width = rows_ref.shape[1]
    mask = slot_rows(rank_ref[...])
    picked = matmul(as_one_hot(mask), token_ref[...])
    rows = picked[:, :width].astype(bf16)
    rows_ref[...] = rows
    lane = lax.broadcasted_iota(jnp.int32, (SLOTS, EXTRA), 1)
    mine = jnp.logical_and(lax.rem(lane, 32) == first_ref[0] + expert, lane < 96)
    gate = jnp.sum(jnp.where(mine, picked[:, width:], 0.0), axis=1, keepdims=True)
    gate_act = matmul(rows, gate_ref[expert])
    up_act = matmul(rows, up_ref[expert])
    sigmoid_g = 1.0 / (1.0 + jnp.exp(-gate_act))
    silu_g = gate_act * sigmoid_g
    hidden = silu_g * up_act
    hidden_ref[...] = (gate * hidden).astype(bf16)
    product = product_ref[...]
    route = jnp.sum(hidden.astype(bf16).astype(f32) * product, axis=1, keepdims=True)
    route_ref[...] = jnp.sum(jnp.where(mask, route, 0.0), axis=0, keepdims=True)
    hidden_grad = gate * product
    gate_grad = (
        hidden_grad * up_act * sigmoid_g * (1.0 + gate_act * (1.0 - sigmoid_g))
    ).astype(bf16)
    up_grad = (hidden_grad * silu_g).astype(bf16)
    gate_grad_ref[...] = gate_grad
    up_grad_ref[...] = up_grad
    back = matmul_nt(gate_grad, gate_ref[expert]) + matmul_nt(up_grad, up_ref[expert])
    held_ref[pl.ds(pl.multiple_of(expert * SLOTS, SLOTS), SLOTS), :] = back.astype(bf16)

    @pl.when(expert == local - 1)
    def _():
        columns = column_ref[...]
        places = jnp.concatenate(
            [slot_columns(columns[:, e : e + 1]) for e in range(columns.shape[1])], axis=1
        )
        back_ref[...] = matmul(places, held_ref[...]).astype(bf16)


def expert_sums(column_ref, hidden_ref, down_ref, out_ref):
    columns = column_ref[...]
    dense = [
        matmul(slot_columns(columns[:, e : e + 1]), hidden_ref[e]).astype(bf16)
        for e in range(columns.shape[1])
    ]
    out_ref[...] = matmul(jnp.concatenate(dense, axis=1), down_ref[...]).astype(bf16)


def params(dims):
    return pltpu.CompilerParams(
        dimension_semantics=("arbitrary",) * dims, vmem_limit_bytes=VMEM_BYTES
    )


def once(shape):
    return pl.BlockSpec(
        shape, lambda *ids: (0,) * len(shape), pipeline_mode=pl.Buffered(1)
    )


def run_select_grads(rank_rows, grad_all, down_weight):
    chunks, local = rank_rows.shape[:2]
    hidden, width = down_weight.shape[1:]
    slots = chunks * local * SLOTS
    return pl.pallas_call(
        select_grads,
        grid=(chunks, local),
        in_specs=[
            pl.BlockSpec((None, None, 1, CHUNK), lambda g, e: (g, e, 0, 0)),
            pl.BlockSpec((CHUNK, width), lambda g, e: (g, 0)),
            once(down_weight.shape),
        ],
        out_specs=[
            pl.BlockSpec((None, None, SLOTS, width), lambda g, e: (g, e, 0, 0)),
            pl.BlockSpec((None, None, SLOTS, hidden), lambda g, e: (g, e, 0, 0)),
        ],
        out_shape=[
            jax.ShapeDtypeStruct((chunks, local, SLOTS, width), bf16),
            jax.ShapeDtypeStruct((chunks, local, SLOTS, hidden), f32),
        ],
        compiler_params=params(2),
        cost_estimate=pl.CostEstimate(
            flops=2 * slots * width * (CHUNK + hidden),
            bytes_accessed=2 * (chunks * CHUNK + slots) * width,
            transcendentals=0,
        ),
        name="select_grads",
    )(rank_rows, grad_all, down_weight)


def run_expert_pass(first, rank_rows, rank_columns, token_all, product, gate_weight, up_weight):
    chunks, local = rank_rows.shape[:2]
    width, hidden = gate_weight.shape[1:]
    slots = chunks * local * SLOTS
    per_expert = lambda g, e: (g, e, 0, 0)
    narrow = pl.BlockSpec((None, None, SLOTS, hidden), per_expert)
    return pl.pallas_call(
        expert_pass,
        grid=(chunks, local),
        in_specs=[
            pl.BlockSpec(memory_space=pltpu.SMEM),
            pl.BlockSpec((None, None, 1, CHUNK), per_expert),
            pl.BlockSpec((None, CHUNK, local), lambda g, e: (g, 0, 0)),
            pl.BlockSpec((CHUNK, width + EXTRA), lambda g, e: (g, 0)),
            narrow,
            once(gate_weight.shape),
            once(up_weight.shape),
        ],
        out_specs=[
            pl.BlockSpec((None, None, SLOTS, width), per_expert),
            narrow,
            narrow,
            narrow,
            pl.BlockSpec((None, None, 1, CHUNK), per_expert),
            pl.BlockSpec((CHUNK, width), lambda g, e: (g, 0)),
        ],
        out_shape=[
            jax.ShapeDtypeStruct((chunks, local, SLOTS, width), bf16),
            jax.ShapeDtypeStruct((chunks, local, SLOTS, hidden), bf16),
            jax.ShapeDtypeStruct((chunks, local, SLOTS, hidden), bf16),
            jax.ShapeDtypeStruct((chunks, local, SLOTS, hidden), bf16),
            jax.ShapeDtypeStruct((chunks, local, 1, CHUNK), f32),
            jax.ShapeDtypeStruct((chunks * CHUNK, width), bf16),
        ],
        scratch_shapes=[pltpu.VMEM((local * SLOTS, width), bf16)],
        compiler_params=params(2),
        cost_estimate=pl.CostEstimate(
            flops=2 * slots * width * (2 * CHUNK + 4 * hidden),
            bytes_accessed=2 * (2 * chunks * CHUNK + slots) * width,
            transcendentals=slots * hidden,
        ),
        name="expert_pass",
    )(first, rank_rows, rank_columns, token_all, product, gate_weight, up_weight)


def run_expert_sums(rank_columns, hidden_rows, down_weight):
    chunks, local, unused, hidden = hidden_rows.shape
    width = down_weight.shape[2]
    flat = down_weight.reshape(local * hidden, width)
    return pl.pallas_call(
        expert_sums,
        grid=(chunks,),
        in_specs=[
            pl.BlockSpec((None, CHUNK, local), lambda g: (g, 0, 0)),
            pl.BlockSpec((None, local, SLOTS, hidden), lambda g: (g, 0, 0, 0)),
            once(flat.shape),
        ],
        out_specs=pl.BlockSpec((CHUNK, width), lambda g: (g, 0)),
        out_shape=jax.ShapeDtypeStruct((chunks * CHUNK, width), bf16),
        compiler_params=params(1),
        cost_estimate=pl.CostEstimate(
            flops=2 * chunks * CHUNK * local * hidden * (width + SLOTS),
            bytes_accessed=2 * chunks * CHUNK * width,
            transcendentals=0,
        ),
        name="expert_sums",
    )(rank_columns, hidden_rows, flat)


def attend(query_b, seg_b, key_blocks, value_blocks, seg_blocks, scale):
    tok_count, heads, head_dim = query_b.shape

    def forward_step(carry, pieces):
        run_max, run_sum, accum = carry
        key_blk, value_blk, seg_blk = pieces
        scores = (
            jnp.einsum("qhd,khd->hqk", query_b, key_blk, preferred_element_type=f32) * scale
        )
        allowed = (seg_b[:, None] == seg_blk[None, :])[None]
        scores = jnp.where(allowed, scores, masked_score)
        new_max = jnp.maximum(run_max, jnp.max(scores, axis=-1))
        probs = jnp.where(allowed, jnp.exp(scores - new_max[..., None]), 0.0)
        factor = jnp.exp(run_max - new_max)
        run_sum = run_sum * factor + jnp.sum(probs, axis=-1)
        accum = accum * factor[..., None] + jnp.einsum(
            "hqk,khd->hqd", probs.astype(bf16), value_blk, preferred_element_type=f32
        )
        return ((new_max, run_sum, accum), None)

    start_carry = (
        jnp.full((heads, tok_count), masked_score, f32),
        jnp.zeros((heads, tok_count), f32),
        jnp.zeros((heads, tok_count, head_dim), f32),
    )
    (run_max, run_sum, accum), unused = lax.scan(
        forward_step, start_carry, (key_blocks, value_blocks, seg_blocks)
    )
    log_total = run_max + jnp.log(run_sum)
    return (jnp.transpose(accum / run_sum[..., None], (1, 0, 2)), log_total)


def attend_back(
    query_b, seg_b, key_blocks, value_blocks, seg_blocks, scale, attn_grad, log_total, delta
):
    tok_count, heads, head_dim = query_b.shape

    def backward_step(query_accum, pieces):
        key_blk, value_blk, seg_blk = pieces
        scores = (
            jnp.einsum("qhd,khd->hqk", query_b, key_blk, preferred_element_type=f32) * scale
        )
        allowed = (seg_b[:, None] == seg_blk[None, :])[None]
        probs = jnp.where(allowed, jnp.exp(scores - log_total[..., None]), 0.0)
        prob_grad = jnp.einsum("qhd,khd->hqk", attn_grad, value_blk, preferred_element_type=f32)
        score_grad = (probs * (prob_grad - delta[..., None])).astype(bf16)
        query_accum = (
            query_accum
            + jnp.einsum("hqk,khd->qhd", score_grad, key_blk, preferred_element_type=f32) * scale
        )
        key_blk_grad = (
            jnp.einsum("hqk,qhd->khd", score_grad, query_b, preferred_element_type=f32) * scale
        )
        value_blk_grad = jnp.einsum(
            "hqk,qhd->khd", probs.astype(bf16), attn_grad, preferred_element_type=f32
        )
        return (query_accum, (key_blk_grad.astype(bf16), value_blk_grad.astype(bf16)))

    return lax.scan(
        backward_step,
        jnp.zeros((tok_count, heads, head_dim), f32),
        (key_blocks, value_blocks, seg_blocks),
    )


def split_three(values):
    high = values.astype(bf16)
    rest = values - high.astype(f32)
    middle = rest.astype(bf16)
    return (high, middle, (rest - middle.astype(f32)).astype(bf16))


def on_device(
    layer_input,
    token_order,
    doc_lengths,
    expert_routes,
    attn_gain,
    query_weight,
    key_weight,
    value_weight,
    query_gain,
    key_gain,
    out_weight,
    moe_gain,
    router_weight,
    gate_weight,
    up_weight,
    down_weight,
    out_grad,
):
    tp_index = lax.axis_index("tp")
    ctx_size = lax.axis_size("ctx")
    fc_size = lax.axis_size("fsdp") * ctx_size
    fc_index = lax.axis_index("fsdp") * ctx_size + lax.axis_index("ctx")
    tok_count, quarter = layer_input.shape
    share = tok_count // lax.axis_size("tp")
    head_dim = query_gain.shape[0]
    head_width = query_weight.shape[1]
    heads = head_width // head_dim
    scale = head_dim ** (-0.5)
    experts = router_weight.shape[1]
    top = expert_routes.shape[1]
    local_experts = gate_weight.shape[0]
    capacity = tok_count * top * 5 // (4 * experts)
    own_rows = lambda values: lax.dynamic_slice_in_dim(values, tp_index * share, share, 0)
    own_width = lambda values: lax.dynamic_slice_in_dim(values, tp_index * quarter, quarter, 1)

    packed = jnp.concatenate(
        [
            query_weight,
            key_weight,
            value_weight,
            router_weight,
            attn_gain[:, None],
            moe_gain[:, None],
            jnp.zeros((attn_gain.shape[0], EXTRA - experts - 2), bf16),
        ],
        axis=1,
    )
    full = lax.all_gather(packed, ROWS, axis=0, tiled=True)
    full_out = lax.all_gather(out_weight.T, ROWS, axis=0, tiled=True)
    side = 3 * head_width
    qkv_weight = full[:, :side]
    full_router = full[:, side : side + experts]
    attn_gain_f = full[:, side + experts].astype(f32)
    moe_gain_f = full[:, side + experts + 1].astype(f32)
    input_f = lax.all_gather(layer_input, "tp", axis=1, tiled=True).astype(f32)
    width = input_f.shape[1]

    expert_ids = jnp.arange(experts, dtype=jnp.int32)
    named = jnp.any(expert_routes[:, :, None] == expert_ids[None, None, :], axis=1)
    earlier = jnp.tri(tok_count, tok_count, -1, dtype=bf16)
    before = matmul(earlier, named.astype(bf16))
    first_slot = (lax.rem(fc_index, CHUNK // tok_count) * capacity).astype(f32)
    ranks = jnp.where(named, before + first_slot, -1.0).astype(bf16)
    grad_rows_b = lax.all_gather(out_grad, "tp", axis=1, tiled=True)
    grad_packed = jnp.concatenate(
        [grad_rows_b, ranks, jnp.zeros((tok_count, EXTRA - experts), bf16)], axis=1
    )
    grad_all = lax.all_gather(grad_packed, ROWS, axis=0, tiled=True)
    chunks = grad_all.shape[0] // CHUNK
    first_expert = fc_index * local_experts
    local_ranks = lax.dynamic_slice_in_dim(
        grad_all[:, width:], first_expert, local_experts, 1
    ).astype(jnp.int32)
    rank_columns = local_ranks.reshape(chunks, CHUNK, local_experts)
    rank_rows = jnp.transpose(rank_columns, (0, 2, 1))[:, :, None, :]

    segment, position = doc_places(token_order[0], doc_lengths[0])
    cosine, sine = rope_tables(position, head_dim)
    inverse_one = norm_scale(input_f)
    normed = (input_f * inverse_one * attn_gain_f).astype(bf16)
    qkv = matmul(normed, qkv_weight)
    query_pre = qkv[:, :head_width].reshape(tok_count, heads, head_dim)
    key_pre = qkv[:, head_width : 2 * head_width].reshape(tok_count, heads, head_dim)
    value_b = qkv[:, 2 * head_width :].astype(bf16)
    query_inv = norm_scale(query_pre)
    key_inv = norm_scale(key_pre)
    query_b = rotate(query_pre * query_inv * query_gain, cosine, sine).astype(bf16)
    key_b = rotate(key_pre * key_inv * key_gain, cosine, sine).astype(bf16)
    seg_b = segment.astype(bf16)
    group = lax.all_gather(
        jnp.concatenate(
            [
                key_b.reshape(tok_count, head_width),
                value_b,
                jnp.broadcast_to(seg_b[:, None], (tok_count, EXTRA)),
            ],
            axis=1,
        ),
        "ctx",
        axis=0,
        tiled=True,
    )
    blocks = group.shape[0] // KEY_BLOCK
    key_blocks = group[:, :head_width].reshape(blocks, KEY_BLOCK, heads, head_dim)
    value_blocks = group[:, head_width : 2 * head_width].reshape(
        blocks, KEY_BLOCK, heads, head_dim
    )
    seg_blocks = group[:, 2 * head_width].reshape(blocks, KEY_BLOCK)
    attn_heads, log_total = attend(query_b, seg_b, key_blocks, value_blocks, seg_blocks, scale)
    attn_b = attn_heads.reshape(tok_count, head_width).astype(bf16)
    attn_part = matmul_nt(attn_b, full_out).astype(bf16)
    attn_out = lax.psum_scatter(attn_part, "tp", scatter_dimension=0, tiled=True).astype(f32)
    resid = own_rows(input_f) + attn_out
    inverse_two = norm_scale(resid)
    moe_in = (resid * inverse_two * moe_gain_f).astype(bf16)
    logits = matmul(moe_in, full_router)
    own_named = own_rows(named)
    chosen = jnp.where(own_named, logits, -jnp.inf)
    gates = jax.nn.softmax(chosen, axis=-1)
    token_all = lax.all_gather(
        jnp.concatenate(
            [moe_in, *split_three(gates), jnp.zeros((share, EXTRA - 3 * experts), bf16)], axis=1
        ),
        ALL,
        axis=0,
        tiled=True,
    )

    grad_slots, product = run_select_grads(rank_rows, grad_all, down_weight)
    token_slots, hidden_rows, gate_act_grad, up_act_grad, route_part, back_part = run_expert_pass(
        first_expert.reshape(1), rank_rows, rank_columns, token_all, product, gate_weight, up_weight
    )
    back_sum = lax.psum_scatter(back_part, ROWS, scatter_dimension=0, tiled=True)
    route_sum = lax.psum(route_part, "tp")
    route_sum = jnp.transpose(route_sum[:, :, 0, :], (1, 0, 2)).reshape(
        local_experts, fc_size, tok_count
    )
    gate_grad = lax.all_to_all(
        jnp.transpose(route_sum, (1, 0, 2)), ROWS, split_axis=0, concat_axis=0, tiled=True
    ).reshape(experts, tok_count)
    out_part = run_expert_sums(rank_columns, hidden_rows, down_weight)
    grad_down = jnp.einsum(
        "gesf,gesd->efd", hidden_rows, grad_slots, preferred_element_type=f32
    )
    grad_gate = jnp.einsum(
        "gesd,gesf->edf", token_slots, gate_act_grad, preferred_element_type=f32
    )
    grad_up = jnp.einsum("gesd,gesf->edf", token_slots, up_act_grad, preferred_element_type=f32)

    own_tokens = lax.dynamic_slice_in_dim(token_all, fc_index * tok_count, tok_count, 0)
    parts = own_tokens[:, width : width + 3 * experts].astype(f32)
    all_gates = parts[:, :experts] + parts[:, experts : 2 * experts] + parts[:, 2 * experts :]
    gate_grad = gate_grad.T
    logit_grad = all_gates * (
        gate_grad - jnp.sum(all_gates * gate_grad, axis=-1, keepdims=True)
    )
    grad_router = lax.dot_general(
        own_tokens[:, :width].astype(f32),
        logit_grad,
        (((0,), (0,)), ((), ())),
        precision=highest,
    )
    own_logit_grad = own_rows(logit_grad)
    router_back = lax.dot_general(
        own_logit_grad, full_router.astype(f32), (((1,), (1,)), ((), ())), precision=highest
    )
    moe_in_grad = (
        lax.psum_scatter(back_sum, "tp", scatter_dimension=0, tiled=True).astype(f32) + router_back
    )
    resid_norm_grad, gain_terms = norm_back(moe_in_grad, resid, inverse_two, moe_gain_f)
    grad_moe_gain = jnp.sum(gain_terms, axis=0)
    resid_grad = own_rows(grad_rows_b).astype(f32) + resid_norm_grad
    resid_grad_b = lax.all_gather(resid_grad.astype(bf16), "tp", axis=0, tiled=True)

    out_sum = lax.psum_scatter(out_part, ROWS, scatter_dimension=0, tiled=True)
    out_sum = lax.psum_scatter(out_sum, "tp", scatter_dimension=0, tiled=True).astype(f32)
    layer_output = lax.all_to_all(
        (resid + out_sum).astype(bf16), "tp", split_axis=1, concat_axis=0, tiled=True
    )

    grad_out = lax.dot_general(
        resid_grad_b, attn_b, (((0,), (0,)), ((), ())), preferred_element_type=f32
    )
    attn_grad = matmul(resid_grad_b, full_out).astype(bf16).reshape(tok_count, heads, head_dim)
    delta = jnp.transpose(jnp.sum(attn_grad.astype(f32) * attn_heads, axis=-1))
    query_rot_grad, (key_stack, value_stack) = attend_back(
        query_b, seg_b, key_blocks, value_blocks, seg_blocks, scale, attn_grad, log_total, delta
    )
    group_rows = blocks * KEY_BLOCK
    group_grad = lax.psum_scatter(
        jnp.concatenate(
            [
                key_stack.reshape(group_rows, head_width),
                value_stack.reshape(group_rows, head_width),
            ],
            axis=1,
        ),
        "ctx",
        scatter_dimension=0,
        tiled=True,
    )
    key_rot_grad = group_grad[:, :head_width].astype(f32).reshape(tok_count, heads, head_dim)
    query_pre_grad, query_gain_terms = norm_back(
        rotate_back(query_rot_grad, cosine, sine), query_pre, query_inv, query_gain
    )
    key_pre_grad, key_gain_terms = norm_back(
        rotate_back(key_rot_grad, cosine, sine), key_pre, key_inv, key_gain
    )
    qkv_grad = jnp.concatenate(
        [
            query_pre_grad.reshape(tok_count, head_width).astype(bf16),
            key_pre_grad.reshape(tok_count, head_width).astype(bf16),
            group_grad[:, head_width:],
        ],
        axis=1,
    )
    normed_part = matmul_nt(qkv_grad, qkv_weight)
    normed_grad = lax.psum_scatter(
        normed_part.astype(bf16), "tp", scatter_dimension=1, tiled=True
    ).astype(f32)
    attn_terms = jnp.sum(normed_part * input_f * inverse_one, axis=0)
    along = jnp.sum(normed_part * input_f * attn_gain_f, axis=1)
    along = lax.psum(along, "tp")[:, None] / width
    input_quarter = layer_input.astype(f32)
    gain_quarter = lax.dynamic_slice_in_dim(attn_gain_f, tp_index * quarter, quarter, 0)
    grad_input = own_width(resid_grad_b).astype(f32) + inverse_one * (
        normed_grad * gain_quarter - input_quarter * inverse_one * inverse_one * along
    )
    grad_qkv = lax.dot_general(
        normed, qkv_grad, (((0,), (0,)), ((), ())), preferred_element_type=f32
    )
    owned_out = lax.psum_scatter(
        jnp.concatenate(
            [grad_out, grad_router, jnp.zeros((width, EXTRA - experts), f32)], axis=1
        ).astype(bf16),
        ROWS,
        scatter_dimension=0,
        tiled=True,
    ).astype(f32)
    owned_qkv = lax.psum_scatter(
        grad_qkv.astype(bf16), ROWS, scatter_dimension=0, tiled=True
    ).astype(f32)
    gains = lax.psum(
        jnp.concatenate(
            [
                attn_terms,
                grad_moe_gain,
                jnp.sum(query_gain_terms, axis=(0, 1)),
                jnp.sum(key_gain_terms, axis=(0, 1)),
            ]
        ),
        ALL,
    )
    owned_gain = attn_gain.shape[0]
    own_gain = lambda at: lax.dynamic_slice_in_dim(
        gains, at * width + fc_index * owned_gain, owned_gain, 0
    )
    return (
        layer_output,
        grad_input,
        own_gain(0),
        owned_qkv[:, :head_width],
        owned_qkv[:, head_width : 2 * head_width],
        owned_qkv[:, 2 * head_width :],
        gains[2 * width : 2 * width + head_dim],
        gains[2 * width + head_dim :],
        owned_out[:, :head_width].T,
        own_gain(1),
        owned_out[:, head_width : head_width + experts],
        grad_gate,
        grad_up,
        grad_down,
    )


def solution(mesh):
    in_specs = (
        P(("fsdp", "ctx"), "tp"),
        P("fsdp", "ctx"),
        P("fsdp", None),
        P(("fsdp", "ctx"), None),
        P(("fsdp", "ctx")),
        P(("fsdp", "ctx"), "tp"),
        P(("fsdp", "ctx"), "tp"),
        P(("fsdp", "ctx"), "tp"),
        P(),
        P(),
        P("tp", ("fsdp", "ctx")),
        P(("fsdp", "ctx")),
        P(("fsdp", "ctx"), None),
        P(("fsdp", "ctx"), None, "tp"),
        P(("fsdp", "ctx"), None, "tp"),
        P(("fsdp", "ctx"), "tp", None),
        P(("fsdp", "ctx"), "tp"),
    )
    out_specs = (
        P(("fsdp", "ctx"), "tp"),
        P(("fsdp", "ctx"), "tp"),
        P(("fsdp", "ctx")),
        P(("fsdp", "ctx"), "tp"),
        P(("fsdp", "ctx"), "tp"),
        P(("fsdp", "ctx"), "tp"),
        P(),
        P(),
        P("tp", ("fsdp", "ctx")),
        P(("fsdp", "ctx")),
        P(("fsdp", "ctx"), None),
        P(("fsdp", "ctx"), None, "tp"),
        P(("fsdp", "ctx"), None, "tp"),
        P(("fsdp", "ctx"), "tp", None),
    )
    return jax.shard_map(
        on_device, mesh=mesh, in_specs=in_specs, out_specs=out_specs, check_vma=False
    )
```

```python
import functools

import jax
import jax.numpy as jnp
from jax import lax
from jax.experimental import pallas as pl
from jax.experimental.pallas import tpu as pltpu
from jax.sharding import PartitionSpec as P

QUERY_BLOCK = 256
CHUNK = 768
SLOTS = 256
EXTRA = 128
VMEM_BYTES = 60 * 1024 * 1024


epsilon = 1e-05
rope_base = 50000.0
masked_score = -1e30
highest = lax.Precision.HIGHEST
bf16 = jnp.bfloat16
f32 = jnp.float32
ROWS = ("fsdp", "ctx")
ALL = ("fsdp", "ctx", "tp")
MESH = pl.DeviceIdType.MESH


def doc_places(order_row, length_row):
    ends = jnp.cumsum(length_row, dtype=jnp.int32)
    passed = (order_row[:, None] >= ends[None, :]).astype(jnp.int32)
    segment = jnp.sum(passed, axis=1, dtype=jnp.int32)
    start = jnp.sum(passed * length_row[None, :], axis=1, dtype=jnp.int32)
    return (segment, order_row - start)


def rope_tables(position, head_dim):
    half = head_dim // 2
    freqs = rope_base ** (-(jnp.arange(half, dtype=jnp.float32) * (2.0 / head_dim)))
    angles = position.astype(jnp.float32)[:, None] * freqs[None, :]
    cosine, sine = jnp.cos(angles), jnp.sin(angles)
    return jnp.concatenate([cosine, cosine], axis=1), jnp.concatenate([-sine, sine], axis=1)


def norm_scale(values):
    return lax.rsqrt(jnp.mean(values * values, axis=-1, keepdims=True) + epsilon)


def norm_back(incoming, values, inverse, gain):
    scaled = incoming * gain
    value_grad = inverse * (
        scaled - values * inverse * inverse * jnp.mean(scaled * values, axis=-1, keepdims=True)
    )
    return (value_grad, incoming * values * inverse)


def matmul(left, right):
    return jnp.dot(left, right, preferred_element_type=f32)


def matmul_nt(left, right):
    return lax.dot_general(left, right, (((1,), (1,)), ((), ())), preferred_element_type=f32)


def slot_rows(rank_row):
    slots = lax.broadcasted_iota(jnp.int32, (SLOTS, rank_row.shape[1]), 0)
    return slots == rank_row


def slot_columns(rank_column):
    slots = lax.broadcasted_iota(jnp.int32, (rank_column.shape[0], SLOTS), 1)
    return jnp.where(slots == rank_column, 1.0, 0.0).astype(bf16)


def as_one_hot(mask):
    return jnp.where(mask, 1.0, 0.0).astype(bf16)


def select_grads(ids_ref, rank_ref, grad_ref, down_ref, rows_ref, product_ref):
    expert = pl.program_id(1)
    rows = matmul(as_one_hot(slot_rows(rank_ref[...])), grad_ref[...]).astype(bf16)
    rows_ref[...] = rows
    product_ref[...] = matmul_nt(rows, down_ref[expert])


def expert_step(
    expert,
    named,
    rank_ref,
    tokens,
    product_ref,
    gate_ref,
    up_ref,
    await_weights,
    rows_ref,
    hidden_ref,
    gate_grad_ref,
    up_grad_ref,
    route_ref,
    held_ref,
):
    width = rows_ref.shape[1]
    mask = slot_rows(rank_ref[...])
    picked = matmul(as_one_hot(mask), tokens)
    rows = picked[:, :width].astype(bf16)
    rows_ref[...] = rows
    lane = lax.broadcasted_iota(jnp.int32, (SLOTS, EXTRA), 1)
    mine = jnp.logical_and(lax.rem(lane, 32) == named, lane < 96)
    gate = jnp.sum(jnp.where(mine, picked[:, width:], 0.0), axis=1, keepdims=True)
    await_weights()
    gate_act = matmul(rows, gate_ref[expert])
    up_act = matmul(rows, up_ref[expert])
    sigmoid_g = 1.0 / (1.0 + jnp.exp(-gate_act))
    silu_g = gate_act * sigmoid_g
    hidden = silu_g * up_act
    hidden_ref[...] = (gate * hidden).astype(bf16)
    product = product_ref[...]
    route = jnp.sum(hidden.astype(bf16).astype(f32) * product, axis=1, keepdims=True)
    route_ref[...] = jnp.sum(jnp.where(mask, route, 0.0), axis=0, keepdims=True)
    hidden_grad = gate * product
    gate_grad = (
        hidden_grad * up_act * sigmoid_g * (1.0 + gate_act * (1.0 - sigmoid_g))
    ).astype(bf16)
    up_grad = (hidden_grad * silu_g).astype(bf16)
    gate_grad_ref[...] = gate_grad
    up_grad_ref[...] = up_grad
    back = matmul_nt(gate_grad, gate_ref[expert]) + matmul_nt(up_grad, up_ref[expert])
    held_ref[pl.ds(pl.multiple_of(expert * SLOTS, SLOTS), SLOTS), :] = back.astype(bf16)


def chunk_places(column_ref):
    columns = column_ref[...]
    return jnp.concatenate(
        [slot_columns(columns[:, e : e + 1]) for e in range(columns.shape[1])], axis=1
    )


def expert_pass(
    ids_ref,
    first_ref,
    rank_ref,
    column_ref,
    near_ref,
    far_ref,
    product_ref,
    gate_in_ref,
    up_in_ref,
    *refs,
):
    (
        rows_ref,
        hidden_ref,
        gate_grad_ref,
        up_grad_ref,
        route_ref,
        near_back_ref,
        far_back_ref,
        token_ref,
        gate_ref,
        up_ref,
        held_ref,
        back_ref,
        token_sem,
        gate_sem,
        up_sem,
        back_sem,
    ) = refs[-16:]
    chunk, expert = pl.program_id(0), pl.program_id(1)
    local = gate_ref.shape[0]
    width = rows_ref.shape[1]
    tiles = back_sem.shape[1]
    tile = width // tiles
    loads = [
        pltpu.make_async_copy(source, token_ref.at[at], token_sem.at[at])
        for at, source in enumerate((near_ref, far_ref))
    ]

    def weight_load(source, held, sem, at):
        return pltpu.make_async_copy(source.at[at], held.at[at], sem.at[at])

    def back_store(to, at, step):
        columns = pl.ds(step * tile, tile)
        return pltpu.make_async_copy(
            back_ref.at[at, :, columns], to.at[:, columns], back_sem.at[at, step]
        )

    @pl.when(jnp.logical_and(chunk == 0, expert == 0))
    def _():
        loads[0].start()
        for at in range(local):
            weight_load(gate_in_ref, gate_ref, gate_sem, at).start()
            weight_load(up_in_ref, up_ref, up_sem, at).start()
        loads[1].start()
        loads[0].wait()

    @pl.when(jnp.logical_and(chunk == 1, expert == 0))
    def _():
        loads[1].wait()

    def await_weights():
        @pl.when(chunk == 0)
        def _():
            weight_load(gate_in_ref, gate_ref, gate_sem, expert).wait()
            weight_load(up_in_ref, up_ref, up_sem, expert).wait()

    expert_step(
        expert,
        first_ref[0] + expert,
        rank_ref,
        token_ref[chunk],
        product_ref,
        gate_ref,
        up_ref,
        await_weights,
        rows_ref,
        hidden_ref,
        gate_grad_ref,
        up_grad_ref,
        route_ref,
        held_ref,
    )

    @pl.when(expert == local - 1)
    def _():
        places = chunk_places(column_ref)
        for step in range(tiles):
            at = pl.ds(step * tile, tile)
            back_ref[chunk, :, at] = matmul(places, held_ref[:, at]).astype(bf16)

            @pl.when(chunk == 0)
            def _():
                back_store(near_back_ref, 0, step).start()

            @pl.when(chunk == 1)
            def _():
                back_store(far_back_ref, 1, step).start()

    @pl.when(jnp.logical_and(chunk == 1, expert == local - 1))
    def _():
        for step in range(tiles):
            back_store(near_back_ref, 0, step).wait()
            back_store(far_back_ref, 1, step).wait()


def exchange_pass(
    rank_ref,
    column_ref,
    product_ref,
    gate_in_ref,
    up_in_ref,
    down_in_ref,
    own_ref,
    sibling_ref,
    from_across_ref,
    from_other_ref,
    rows_ref,
    hidden_ref,
    gate_grad_ref,
    up_grad_ref,
    route_ref,
    sum_ref,
    out_ref,
    inbox_ref,
    landing_ref,
    token_ref,
    gate_ref,
    up_ref,
    down_ref,
    hidden_held_ref,
    held_ref,
    far_ref,
    beside_ref,
    chip_ref,
    corner_ref,
    token_sem,
    gate_sem,
    up_sem,
    pass_send,
    pass_recv,
    far_send,
    far_recv,
    link_send,
    link_recv,
    store_sem,
    down_sem,
    out_sem,
    landing_sem,
):
    step, expert = pl.program_id(0), pl.program_id(1)
    local = gate_ref.shape[0]
    rows, width = far_ref.shape
    half = rows // 2
    fsdp, ctx = lax.axis_index("fsdp"), lax.axis_index("ctx")
    beside_id = {"fsdp": fsdp + 1 - 2 * lax.rem(fsdp, 2)}
    across_id = {"fsdp": lax.rem(fsdp + 2, 4)}
    other_id = {"ctx": 1 - ctx}
    last = expert == local - 1
    low, high = pl.ds(0, half), pl.ds(half, half)
    sources = (
        inbox_ref.at[0],
        from_across_ref,
        inbox_ref.at[1],
        from_other_ref,
        inbox_ref.at[3],
        inbox_ref.at[2],
        sibling_ref,
        own_ref,
    )

    def token_load(at):
        slot = at % 2
        return pltpu.make_async_copy(sources[at], token_ref.at[slot], token_sem.at[slot])

    def weight_load(source, held, sem, at):
        return pltpu.make_async_copy(source.at[at], held.at[at], sem.at[at])

    def pass_copy(number):
        source, to, peer = (
            (from_across_ref, inbox_ref.at[0], beside_id),
            (from_other_ref, inbox_ref.at[1], beside_id),
            (from_other_ref.at[low], inbox_ref.at[2, low], across_id),
            (from_across_ref.at[high], inbox_ref.at[2, high], other_id),
            (inbox_ref.at[2], inbox_ref.at[3], beside_id),
        )[number]
        return pltpu.make_async_remote_copy(
            src_ref=source,
            dst_ref=to,
            send_sem=pass_send.at[number],
            recv_sem=pass_recv.at[number],
            device_id=peer,
            device_id_type=MESH,
        )

    def far_copy(turn):
        return pltpu.make_async_remote_copy(
            src_ref=far_ref,
            dst_ref=beside_ref.at[turn % 2],
            send_sem=far_send.at[turn],
            recv_sem=far_recv.at[turn],
            device_id=beside_id,
            device_id_type=MESH,
        )

    def link_copy(number):
        source, to, peer = (
            (chip_ref.at[0, high], landing_ref.at[0, high], across_id),
            (chip_ref.at[1, low], landing_ref.at[1, low], other_id),
            (chip_ref.at[2, low], corner_ref.at[0], other_id),
            (chip_ref.at[2, high], corner_ref.at[1], across_id),
            (chip_ref.at[1, high], landing_ref.at[1, high], other_id),
            (chip_ref.at[0, low], landing_ref.at[0, low], across_id),
        )[number]
        return pltpu.make_async_remote_copy(
            src_ref=source,
            dst_ref=to,
            send_sem=link_send.at[number],
            recv_sem=link_recv.at[number],
            device_id=peer,
            device_id_type=MESH,
        )

    @pl.when(jnp.logical_and(step == 0, expert == 0))
    def _():
        barrier = pltpu.get_barrier_semaphore()
        for peer in (beside_id, across_id, other_id):
            pl.semaphore_signal(barrier, inc=1, device_id=peer, device_id_type=MESH)
        pl.semaphore_wait(barrier, 3)
        for number in range(4):
            pass_copy(number).start()
        for at in range(local):
            weight_load(gate_in_ref, gate_ref, gate_sem, at).start()
            weight_load(up_in_ref, up_ref, up_sem, at).start()
        down_load = pltpu.make_async_copy(down_in_ref, down_ref, down_sem)
        down_load.start()
        pass_copy(0).wait_recv()
        token_load(0).start()

    @pl.when(jnp.logical_and(step == 3, expert == 0))
    def _():
        pass_copy(2).wait_recv()
        pass_copy(3).wait_recv()
        pass_copy(4).start()

    for at in range(8):

        @pl.when(jnp.logical_and(step == at, expert == 0))
        def _():
            token_load(at).wait()

        if at < 7:

            @pl.when(jnp.logical_and(step == at, last))
            def _():
                if at == 1:
                    pass_copy(1).wait_recv()
                if at == 3:
                    pass_copy(4).wait_recv()
                token_load(at + 1).start()

    def await_weights():
        @pl.when(step == 0)
        def _():
            weight_load(gate_in_ref, gate_ref, gate_sem, expert).wait()
            weight_load(up_in_ref, up_ref, up_sem, expert).wait()

    first = (fsdp * 2 + ctx) * local

    @pl.when(step < 8)
    def _():
        expert_step(
            expert,
            first + expert,
            rank_ref,
            token_ref[lax.rem(step, 2)],
            product_ref,
            gate_ref,
            up_ref,
            await_weights,
            rows_ref,
            hidden_ref,
            gate_grad_ref,
            up_grad_ref,
            route_ref,
            held_ref,
        )
        hidden_held_ref[step, expert] = hidden_ref[...]

    tile = 512

    def tiles():
        for at in range(0, width, tile):
            yield pl.ds(at, tile)

    def add_half(turn, part, landed):
        total = chip_ref[turn, part, :].astype(f32) + corner_ref[landed].astype(f32)
        chip_ref[turn, part, :] = total.astype(bf16)

    for turn in range(4):

        @pl.when(jnp.logical_and(step == 2 * turn, last))
        def _():
            if turn > 0:
                far_copy(turn - 1).wait_send()
            places = chunk_places(column_ref)
            for at in tiles():
                far_ref[:, at] = matmul(places, held_ref[:, at]).astype(bf16)
            far_copy(turn).start()

        @pl.when(jnp.logical_and(step == 2 * turn + 1, last))
        def _():
            far_copy(turn).wait_recv()
            if turn == 3:
                far_copy(3).wait_send()
            places = chunk_places(column_ref)
            for at in tiles():
                total = matmul(places, held_ref[:, at]) + beside_ref[turn % 2, :, at].astype(f32)
                if turn < 3:
                    chip_ref[turn, :, at] = total.astype(bf16)
                else:
                    far_ref[:, at] = total.astype(bf16)
            if turn < 2:
                link_copy(turn).start()
            if turn == 2:
                link_copy(2).start()
                link_copy(3).start()


    number = step - 8
    turn = number // 2
    chip = lax.rem(fsdp + 2 * (1 - lax.rem(turn, 2)), 4)
    core = chip + (1 - lax.rem(number, 2)) * (1 - 2 * lax.rem(fsdp, 2))
    line = lax.rem(ctx + lax.rem((turn + 1) // 2, 2), 2)
    places_at = (core * 2 + line) * rows
    slot = lax.rem(step, 2)
    columns_of = width // local
    hidden = gate_ref.shape[2]

    def out_store(at, which):
        columns = pl.ds(pl.multiple_of(which * columns_of, columns_of), columns_of)
        return pltpu.make_async_copy(
            token_ref.at[slot, :, columns],
            out_ref.at[pl.ds(pl.multiple_of(at, rows), rows), columns],
            out_sem.at[slot, which],
        )

    @pl.when(step >= 8)
    def _():
        @pl.when(jnp.logical_and(step == 8, expert == 0))
        def _():
            pltpu.make_async_copy(down_in_ref, down_ref, down_sem).wait()

        @pl.when(expert == 0)
        def _():
            columns = column_ref[...]
            for e in range(local):
                held_ref[pl.ds(0, rows), pl.ds(e * hidden, hidden)] = matmul(
                    slot_columns(columns[:, e : e + 1]), hidden_held_ref[number, e]
                ).astype(bf16)

        @pl.when(step >= 10)
        def _():
            out_store(places_at, expert).wait()

        at = pl.ds(pl.multiple_of(expert * columns_of, columns_of), columns_of)
        token_ref[slot, :, at] = matmul(
            held_ref[pl.ds(0, rows), pl.ds(0, local * hidden)], down_ref[:, at]
        ).astype(bf16)
        out_store(places_at, expert).start()

    @pl.when(jnp.logical_and(step == 9, expert == 1))
    def _():
        link_copy(3).wait_recv()
        add_half(1, high, 1)
        link_copy(4).start()
        link_copy(2).wait_recv()
        add_half(0, low, 0)
        link_copy(5).start()

    @pl.when(jnp.logical_and(step == 15, last))
    def _():
        landing = []
        for way, numbers in enumerate(((0, 5), (1, 4))):
            for number in numbers:
                link_copy(number).wait_recv()
            copy = pltpu.make_async_copy(
                landing_ref.at[way], beside_ref.at[way], landing_sem.at[way]
            )
            copy.start()
            landing.append(copy)
        for copy in landing:
            copy.wait()
        for part in (low, high):
            held_ref[part, :] = (
                far_ref[part, :].astype(f32)
                + beside_ref[0, part, :].astype(f32)
                + beside_ref[1, part, :].astype(f32)
            ).astype(bf16)
        store = pltpu.make_async_copy(held_ref.at[pl.ds(0, rows)], sum_ref, store_sem)
        store.start()
        for number in range(5):
            pass_copy(number).wait_send()
        for number in range(6):
            link_copy(number).wait_send()
        for other_slot in (0, 1):
            for which in range(local):
                columns = pl.ds(which * columns_of, columns_of)
                pltpu.make_async_copy(
                    token_ref.at[other_slot, :, columns],
                    out_ref.at[pl.ds(0, rows), columns],
                    out_sem.at[other_slot, which],
                ).wait()
        store.wait()


def expert_sums(ids_ref, column_ref, hidden_ref, down_ref, out_ref):
    columns = column_ref[...]
    dense = [
        matmul(slot_columns(columns[:, e : e + 1]), hidden_ref[e]).astype(bf16)
        for e in range(columns.shape[1])
    ]
    out_ref[...] = matmul(jnp.concatenate(dense, axis=1), down_ref[...]).astype(bf16)


def params(dims):
    return pltpu.CompilerParams(
        dimension_semantics=("arbitrary",) * dims, vmem_limit_bytes=VMEM_BYTES
    )


def once(shape):
    return pl.BlockSpec(
        shape, lambda *ids: (0,) * len(shape), pipeline_mode=pl.Buffered(1)
    )


def run_select_grads(ids, rank_rows, grad_all, down_weight):
    chunks, local = rank_rows.shape[:2]
    hidden, width = down_weight.shape[1:]
    slots = chunks * local * SLOTS
    place = lambda g, e, ids: (g, e, 0, 0)
    return pl.pallas_call(
        select_grads,
        grid_spec=pltpu.PrefetchScalarGridSpec(
            num_scalar_prefetch=1,
            grid=(chunks, local),
            in_specs=[
                pl.BlockSpec((None, None, 1, CHUNK), place),
                pl.BlockSpec((CHUNK, width), lambda g, e, ids: (ids[g], 0)),
                once(down_weight.shape),
            ],
            out_specs=[
                pl.BlockSpec((None, None, SLOTS, width), place),
                pl.BlockSpec((None, None, SLOTS, hidden), place),
            ],
        ),
        out_shape=[
            jax.ShapeDtypeStruct((chunks, local, SLOTS, width), bf16),
            jax.ShapeDtypeStruct((chunks, local, SLOTS, hidden), f32),
        ],
        compiler_params=params(2),
        cost_estimate=pl.CostEstimate(
            flops=2 * slots * width * (CHUNK + hidden),
            bytes_accessed=2 * (chunks * CHUNK + slots) * width,
            transcendentals=0,
        ),
        name="select_grads",
    )(ids, rank_rows, grad_all, down_weight)


def run_exchange_pass(rank_rows, rank_columns, product, weights, sources):
    gate_weight, up_weight, down_weight = weights
    chunks, local = rank_rows.shape[:2]
    width, hidden = gate_weight.shape[1:]
    slots = chunks * local * SLOTS
    flat_down = down_weight.reshape(local * hidden, width)

    def per_expert(g, e):
        return (jnp.minimum(g, chunks - 1), jnp.where(g < chunks, e, local - 1), 0, 0)

    narrow = pl.BlockSpec((None, None, SLOTS, hidden), per_expert)
    anywhere = pl.BlockSpec(memory_space=pl.ANY)
    half = (2, CHUNK // 2, width)
    narrow_shape = jax.ShapeDtypeStruct((chunks, local, SLOTS, hidden), bf16)
    outs = pl.pallas_call(
        exchange_pass,
        grid=(2 * chunks, local),
        in_specs=[
            pl.BlockSpec((None, None, 1, CHUNK), per_expert),
            pl.BlockSpec((None, CHUNK, local), lambda g, e: (lax.rem(g, chunks), 0, 0)),
            narrow,
            *[anywhere] * 7,
        ],
        out_specs=[
            pl.BlockSpec((None, None, SLOTS, width), per_expert),
            narrow,
            narrow,
            narrow,
            pl.BlockSpec((None, None, 1, CHUNK), per_expert),
            *[anywhere] * 4,
        ],
        out_shape=[
            jax.ShapeDtypeStruct((chunks, local, SLOTS, width), bf16),
            narrow_shape,
            narrow_shape,
            narrow_shape,
            jax.ShapeDtypeStruct((chunks, local, 1, CHUNK), f32),
            jax.ShapeDtypeStruct((CHUNK, width), bf16),
            jax.ShapeDtypeStruct((chunks * CHUNK, width), bf16),
            jax.ShapeDtypeStruct((4, *sources[0].shape), bf16),
            jax.ShapeDtypeStruct((2, CHUNK, width), bf16),
        ],
        scratch_shapes=[
            pltpu.VMEM((2, CHUNK, width + EXTRA), bf16),
            pltpu.VMEM(gate_weight.shape, bf16),
            pltpu.VMEM(up_weight.shape, bf16),
            pltpu.VMEM(flat_down.shape, bf16),
            pltpu.VMEM((chunks, local, SLOTS, hidden), bf16),
            pltpu.VMEM((local * SLOTS, width), bf16),
            pltpu.VMEM((CHUNK, width), bf16),
            pltpu.VMEM((2, CHUNK, width), bf16),
            pltpu.VMEM((3, CHUNK, width), bf16),
            pltpu.VMEM(half, bf16),
            pltpu.SemaphoreType.DMA((2,)),
            pltpu.SemaphoreType.DMA((local,)),
            pltpu.SemaphoreType.DMA((local,)),
            pltpu.SemaphoreType.DMA((5,)),
            pltpu.SemaphoreType.DMA((5,)),
            pltpu.SemaphoreType.DMA((4,)),
            pltpu.SemaphoreType.DMA((4,)),
            pltpu.SemaphoreType.DMA((6,)),
            pltpu.SemaphoreType.DMA((6,)),
            pltpu.SemaphoreType.DMA,
            pltpu.SemaphoreType.DMA,
            pltpu.SemaphoreType.DMA((2, local)),
            pltpu.SemaphoreType.DMA((2,)),
        ],
        compiler_params=pltpu.CompilerParams(
            dimension_semantics=("arbitrary",) * 2,
            collective_id=9,
            has_side_effects=True,
            vmem_limit_bytes=VMEM_BYTES,
        ),
        cost_estimate=pl.CostEstimate(
            flops=2 * slots * width * (2 * CHUNK + 4 * hidden),
            bytes_accessed=2 * (12 * CHUNK + slots) * width,
            transcendentals=slots * hidden,
        ),
        name="exchange_pass",
    )(rank_rows, rank_columns, product, gate_weight, up_weight, flat_down, *sources)
    return outs[:5], outs[5], outs[6]


def run_expert_pass(
    ids, first, rank_rows, rank_columns, near, far, product, gate_weight, up_weight, kept
):
    chunks, local = rank_rows.shape[:2]
    width, hidden = gate_weight.shape[1:]
    slots = 2 * local * SLOTS
    per_expert = lambda g, e, ids: (ids[g], e, 0, 0)
    narrow = pl.BlockSpec((None, None, SLOTS, hidden), per_expert)
    in_specs = [
        pl.BlockSpec(memory_space=pltpu.SMEM),
        pl.BlockSpec((None, None, 1, CHUNK), per_expert),
        pl.BlockSpec((None, CHUNK, local), lambda g, e, ids: (ids[g], 0, 0)),
        pl.BlockSpec(memory_space=pl.ANY),
        pl.BlockSpec(memory_space=pl.ANY),
        narrow,
        pl.BlockSpec(memory_space=pl.ANY),
        pl.BlockSpec(memory_space=pl.ANY),
    ]
    kept_shapes = [
        jax.ShapeDtypeStruct((chunks, local, SLOTS, width), bf16),
        jax.ShapeDtypeStruct((chunks, local, SLOTS, hidden), bf16),
        jax.ShapeDtypeStruct((chunks, local, SLOTS, hidden), bf16),
        jax.ShapeDtypeStruct((chunks, local, SLOTS, hidden), bf16),
        jax.ShapeDtypeStruct((chunks, local, 1, CHUNK), f32),
    ]
    outs = pl.pallas_call(
        expert_pass,
        grid_spec=pltpu.PrefetchScalarGridSpec(
            num_scalar_prefetch=1,
            grid=(2, local),
            in_specs=in_specs + [pl.BlockSpec(memory_space=pl.ANY)] * len(kept),
            out_specs=[
                pl.BlockSpec((None, None, SLOTS, width), per_expert),
                narrow,
                narrow,
                narrow,
                pl.BlockSpec((None, None, 1, CHUNK), per_expert),
                pl.BlockSpec(memory_space=pl.ANY),
                pl.BlockSpec(memory_space=pl.ANY),
            ],
            scratch_shapes=[
                pltpu.VMEM((2, CHUNK, width + EXTRA), bf16),
                pltpu.VMEM(gate_weight.shape, bf16),
                pltpu.VMEM(up_weight.shape, bf16),
                pltpu.VMEM((local * SLOTS, width), bf16),
                pltpu.VMEM((2, CHUNK, width), bf16),
                pltpu.SemaphoreType.DMA((2,)),
                pltpu.SemaphoreType.DMA((local,)),
                pltpu.SemaphoreType.DMA((local,)),
                pltpu.SemaphoreType.DMA((2, 4)),
            ],
        ),
        out_shape=kept_shapes + [jax.ShapeDtypeStruct((CHUNK, width), bf16)] * 2,
        input_output_aliases={9 + at: at for at in range(len(kept))},
        compiler_params=params(2),
        cost_estimate=pl.CostEstimate(
            flops=2 * slots * width * (2 * CHUNK + 4 * hidden),
            bytes_accessed=2 * (4 * CHUNK + slots) * width,
            transcendentals=slots * hidden,
        ),
        name="expert_pass",
    )(ids, first, rank_rows, rank_columns, near, far, product, gate_weight, up_weight, *kept)
    return outs[:5], outs[5], outs[6]


def run_expert_sums(ids, rank_columns, hidden_rows, down_weight):
    chunks, local, unused, hidden = hidden_rows.shape
    width = down_weight.shape[2]
    flat = down_weight.reshape(local * hidden, width)
    return pl.pallas_call(
        expert_sums,
        grid_spec=pltpu.PrefetchScalarGridSpec(
            num_scalar_prefetch=1,
            grid=(chunks,),
            in_specs=[
                pl.BlockSpec((None, CHUNK, local), lambda g, ids: (g, 0, 0)),
                pl.BlockSpec((None, local, SLOTS, hidden), lambda g, ids: (g, 0, 0, 0)),
                once(flat.shape),
            ],
            out_specs=pl.BlockSpec((CHUNK, width), lambda g, ids: (ids[g], 0)),
        ),
        out_shape=jax.ShapeDtypeStruct((chunks * CHUNK, width), bf16),
        compiler_params=params(1),
        cost_estimate=pl.CostEstimate(
            flops=2 * chunks * CHUNK * local * hidden * (width + SLOTS),
            bytes_accessed=2 * chunks * CHUNK * width,
            transcendentals=0,
        ),
        name="expert_sums",
    )(ids, rank_columns, hidden_rows, flat)


def line_barrier(size):
    place = lax.axis_index("tp")
    barrier = pltpu.get_barrier_semaphore()

    @pl.when(place > 0)
    def _():
        pl.semaphore_signal(barrier, inc=1, device_id={"tp": place - 1}, device_id_type=MESH)

    @pl.when(place < size - 1)
    def _():
        pl.semaphore_signal(barrier, inc=1, device_id={"tp": place + 1}, device_id_type=MESH)

    has_left = jnp.where(place > 0, 1, 0)
    has_right = jnp.where(place < size - 1, 1, 0)
    pl.semaphore_wait(barrier, has_left + has_right)


def line_gather(size, columns, in_ref, out_ref, own_sem, send_sem, recv_sem):
    place = lax.axis_index("tp")
    extent = in_ref.shape[1] if columns else in_ref.shape[0]

    def block(index):
        at = pl.ds(pl.multiple_of(index * extent, extent), extent)
        return out_ref.at[:, at] if columns else out_ref.at[at, :]

    line_barrier(size)
    own = pltpu.make_async_copy(in_ref, block(place), own_sem)
    own.start()

    def sending(way, step):
        source = place - step if way == 0 else place + step
        to = place + 1 if way == 0 else place - 1
        return pltpu.make_async_remote_copy(
            src_ref=in_ref if step == 0 else block(source),
            dst_ref=block(source),
            send_sem=send_sem.at[way, step],
            recv_sem=recv_sem.at[way, step],
            device_id={"tp": to},
            device_id_type=MESH,
        )

    def sends(way, step):
        if way == 0:
            return jnp.logical_and(place >= step, place < size - 1)
        return jnp.logical_and(place + step < size, place > 0)

    def receiving(way, step):
        source = place - 1 - step if way == 0 else place + 1 + step
        origin = place - 1 if way == 0 else place + 1
        return pltpu.make_async_remote_copy(
            src_ref=block(source),
            dst_ref=block(source),
            send_sem=send_sem.at[way, step],
            recv_sem=recv_sem.at[way, step],
            device_id={"tp": origin},
            device_id_type=MESH,
        )

    def receives(way, step):
        return place > step if way == 0 else place + 1 + step < size

    for step in range(size - 1):
        for way in (0, 1):

            @pl.when(sends(way, step))
            def _():
                sending(way, step).start()

        for way in (0, 1):

            @pl.when(receives(way, step))
            def _():
                receiving(way, step).wait_recv()

    for step in range(size - 1):
        for way in (0, 1):

            @pl.when(sends(way, step))
            def _():
                sending(way, step).wait_send()

    own.wait()


def line_scatter(
    size, columns, in_ref, out_ref, staged_ref, landed_ref, send_sem, recv_sem, stages=()
):
    place = lax.axis_index("tp")
    extent = out_ref.shape[1] if columns else out_ref.shape[0]

    def block(index):
        at = pl.ds(pl.multiple_of(index * extent, extent), extent)
        values = in_ref[:, at] if columns else in_ref[at, :]
        return values.astype(f32)

    if not stages:
        line_barrier(size)

    def copying(way, step, to):
        return pltpu.make_async_remote_copy(
            src_ref=staged_ref.at[way, step],
            dst_ref=landed_ref.at[way, step],
            send_sem=send_sem.at[way, step],
            recv_sem=recv_sem.at[way, step],
            device_id={"tp": to},
            device_id_type=MESH,
        )

    for step in range(size - 1):
        for way in (0, 1):
            rank = place if way == 0 else size - 1 - place
            target = size - 1 - step + place if way == 0 else place - (size - 1 - step)
            to = place + 1 if way == 0 else place - 1
            active = jnp.logical_and(rank <= step, rank < size - 1)

            @pl.when(active)
            def _():
                values = block(target)
                if step == 0:
                    staged_ref[way, step] = values.astype(bf16)
                else:

                    @pl.when(rank == 0)
                    def _():
                        staged_ref[way, step] = values.astype(bf16)

                    @pl.when(rank > 0)
                    def _():
                        landed = landed_ref[way, step - 1].astype(f32)
                        staged_ref[way, step] = (values + landed).astype(bf16)

                copying(way, step, to).start()

        if step < len(stages):
            stages[step]()

        for way in (0, 1):
            rank = place if way == 0 else size - 1 - place
            origin = place - 1 if way == 0 else place + 1

            @pl.when(jnp.logical_and(rank > 0, rank - 1 <= step))
            def _():
                copying(way, step, origin).wait_recv()

    for stage in stages[size - 1 :]:
        stage()
    out_ref[...] = block(place)
    for way in (0, 1):
        rank = place if way == 0 else size - 1 - place

        @pl.when(rank > 0)
        def _():
            out_ref[...] += landed_ref[way, size - 2].astype(f32)

    for step in range(size - 1):
        for way in (0, 1):
            rank = place if way == 0 else size - 1 - place
            to = place + 1 if way == 0 else place - 1

            @pl.when(jnp.logical_and(rank <= step, rank < size - 1))
            def _():
                copying(way, step, to).wait_send()


def closing_sums(
    sizes,
    narrow,
    in_ref,
    small_ref,
    out_ref,
    every_ref,
    line_ref,
    staged_ref,
    landed_ref,
    total_ref,
    small_tp_ref,
    small_ctx_ref,
    small_fsdp_ref,
    send_sem,
    recv_sem,
    small_send_sem,
    small_recv_sem,
):
    axes = ("tp", "ctx", "fsdp")
    barrier = pltpu.get_barrier_semaphore()
    for axis, size in zip(axes, sizes):
        place = lax.axis_index(axis)
        for offset in range(1, size):
            peer = lax.rem(place + offset, size)
            pl.semaphore_signal(barrier, inc=1, device_id={axis: peer}, device_id_type=MESH)
    pl.semaphore_wait(barrier, sum(sizes) - len(sizes))
    landings = (small_tp_ref, small_ctx_ref, small_fsdp_ref)

    def copying(axis, offset, peer):
        return pltpu.make_async_remote_copy(
            src_ref=small_ref if axis == 0 else total_ref.at[axis - 1],
            dst_ref=landings[axis].at[offset - 1],
            send_sem=small_send_sem.at[axis, offset - 1],
            recv_sem=small_recv_sem.at[axis, offset - 1],
            device_id={axes[axis]: peer},
            device_id_type=MESH,
        )

    def each(axis):
        size, place = sizes[axis], lax.axis_index(axes[axis])
        for offset in range(1, size):
            yield (
                offset,
                lax.rem(place + offset, size),
                lax.rem(place + size - offset, size),
            )

    def start(axis):
        for offset, to, origin in each(axis):
            copying(axis, offset, to).start()

    def finish(axis):
        total = small_ref[...] if axis == 0 else total_ref[axis - 1]
        for offset, to, origin in each(axis):
            copying(axis, offset, origin).wait_recv()
            total = total + landings[axis][offset - 1]
        for offset, to, origin in each(axis):
            copying(axis, offset, to).wait_send()
        return total

    def first():
        start(0)

    def second():
        total = finish(0)
        total_ref[0] = total
        line_ref[...] = total[:, narrow:]
        start(1)

    def third():
        total_ref[1] = finish(1)
        start(2)

    def last():
        every_ref[...] = finish(2)[:, :narrow]

    line_scatter(
        sizes[0],
        True,
        in_ref,
        out_ref,
        staged_ref,
        landed_ref,
        send_sem,
        recv_sem,
        stages=(first, second, third, last),
    )


def peer_barrier(axis, size):
    place = lax.axis_index(axis)
    barrier = pltpu.get_barrier_semaphore()
    for offset in range(1, size):
        peer = lax.rem(place + offset, size)
        pl.semaphore_signal(barrier, inc=1, device_id={axis: peer}, device_id_type=MESH)
    pl.semaphore_wait(barrier, size - 1)


def peer_gather(size, in_ref, out_ref, own_sem, send_sem, recv_sem):
    place = lax.axis_index("ctx")
    rows = in_ref.shape[0]

    def block(index):
        return out_ref.at[pl.ds(pl.multiple_of(index * rows, rows), rows), :]

    def copying(offset, source, peer):
        return pltpu.make_async_remote_copy(
            src_ref=in_ref,
            dst_ref=block(source),
            send_sem=send_sem.at[offset - 1],
            recv_sem=recv_sem.at[offset - 1],
            device_id={"ctx": peer},
            device_id_type=MESH,
        )

    peer_barrier("ctx", size)
    own = pltpu.make_async_copy(in_ref, block(place), own_sem)
    own.start()
    for offset in range(1, size):
        copying(offset, place, lax.rem(place + offset, size)).start()
    for offset in range(1, size):
        origin = lax.rem(place + size - offset, size)
        copying(offset, origin, origin).wait_recv()
    for offset in range(1, size):
        copying(offset, place, lax.rem(place + offset, size)).wait_send()
    own.wait()


def peer_scatter(size, in_ref, out_ref, landed_ref, send_sem, recv_sem):
    place = lax.axis_index("ctx")
    rows = out_ref.shape[0]

    def at(index):
        return pl.ds(pl.multiple_of(index * rows, rows), rows)

    def copying(offset, peer):
        return pltpu.make_async_remote_copy(
            src_ref=in_ref.at[at(peer), :],
            dst_ref=landed_ref.at[offset - 1],
            send_sem=send_sem.at[offset - 1],
            recv_sem=recv_sem.at[offset - 1],
            device_id={"ctx": peer},
            device_id_type=MESH,
        )

    peer_barrier("ctx", size)
    for offset in range(1, size):
        copying(offset, lax.rem(place + offset, size)).start()
    total = in_ref[at(place), :].astype(f32)
    for offset in range(1, size):
        origin = lax.rem(place + size - offset, size)
        copying(offset, origin).wait_recv()
        total = total + landed_ref[offset - 1].astype(f32)
    out_ref[...] = total.astype(bf16)
    for offset in range(1, size):
        copying(offset, lax.rem(place + offset, size)).wait_send()


def remote_params(number):
    return pltpu.CompilerParams(
        collective_id=number, has_side_effects=True, vmem_limit_bytes=VMEM_BYTES
    )


def gather_tp(values, columns, number):
    size = lax.axis_size("tp")
    rows, width = values.shape
    shape = (rows, size * width) if columns else (size * rows, width)
    return pl.pallas_call(
        functools.partial(line_gather, size, columns),
        in_specs=[pl.BlockSpec(memory_space=pl.ANY)],
        out_specs=pl.BlockSpec(memory_space=pl.ANY),
        out_shape=jax.ShapeDtypeStruct(shape, values.dtype),
        scratch_shapes=[
            pltpu.SemaphoreType.DMA,
            pltpu.SemaphoreType.DMA((2, size - 1)),
            pltpu.SemaphoreType.DMA((2, size - 1)),
        ],
        compiler_params=remote_params(number),
        cost_estimate=pl.CostEstimate(flops=0, bytes_accessed=150_000_000, transcendentals=0),
        name="gather_tp",
    )(values)


def scatter_tp(values, columns, number):
    size = lax.axis_size("tp")
    rows, width = values.shape
    shape = (rows, width // size) if columns else (rows // size, width)
    return pl.pallas_call(
        functools.partial(line_scatter, size, columns),
        in_specs=[pl.BlockSpec(memory_space=pltpu.VMEM)],
        out_specs=pl.BlockSpec(memory_space=pltpu.VMEM),
        out_shape=jax.ShapeDtypeStruct(shape, f32),
        scratch_shapes=[
            pltpu.VMEM((2, size - 1, *shape), bf16),
            pltpu.VMEM((2, size - 1, *shape), bf16),
            pltpu.SemaphoreType.DMA((2, size - 1)),
            pltpu.SemaphoreType.DMA((2, size - 1)),
        ],
        compiler_params=remote_params(number),
        cost_estimate=pl.CostEstimate(flops=0, bytes_accessed=150_000_000, transcendentals=0),
        name="scatter_tp",
    )(values)


def close_tp(values, gains, along, number):
    sizes = tuple(lax.axis_size(axis) for axis in ("tp", "ctx", "fsdp"))
    rows, width = values.shape
    shape = (rows, width // sizes[0])
    pad = lambda row: jnp.pad(row, (0, -row.shape[0] % 1024)).reshape(8, -1)
    gains_b, along_b = pad(gains), pad(along)
    narrow, wide = gains_b.shape[1], along_b.shape[1]
    small = jnp.concatenate([gains_b, along_b], axis=1)
    peers = max(sizes) - 1
    out, every, line = pl.pallas_call(
        functools.partial(closing_sums, sizes, narrow),
        in_specs=[pl.BlockSpec(memory_space=pltpu.VMEM)] * 2,
        out_specs=[pl.BlockSpec(memory_space=pltpu.VMEM)] * 3,
        out_shape=[
            jax.ShapeDtypeStruct(shape, f32),
            jax.ShapeDtypeStruct((8, narrow), f32),
            jax.ShapeDtypeStruct((8, wide), f32),
        ],
        scratch_shapes=[
            pltpu.VMEM((2, sizes[0] - 1, *shape), bf16),
            pltpu.VMEM((2, sizes[0] - 1, *shape), bf16),
            pltpu.VMEM((2, *small.shape), f32),
            *[pltpu.VMEM((size - 1, *small.shape), f32) for size in sizes],
            pltpu.SemaphoreType.DMA((2, sizes[0] - 1)),
            pltpu.SemaphoreType.DMA((2, sizes[0] - 1)),
            pltpu.SemaphoreType.DMA((3, peers)),
            pltpu.SemaphoreType.DMA((3, peers)),
        ],
        compiler_params=remote_params(number),
        cost_estimate=pl.CostEstimate(flops=0, bytes_accessed=150_000_000, transcendentals=0),
        name="close_tp",
    )(values, small)
    return out, every.reshape(-1)[: gains.shape[0]], line.reshape(-1)[: along.shape[0]]


def gather_ctx(values, number):
    size = lax.axis_size("ctx")
    rows, width = values.shape
    return pl.pallas_call(
        functools.partial(peer_gather, size),
        in_specs=[pl.BlockSpec(memory_space=pl.ANY)],
        out_specs=pl.BlockSpec(memory_space=pl.ANY),
        out_shape=jax.ShapeDtypeStruct((size * rows, width), values.dtype),
        scratch_shapes=[
            pltpu.SemaphoreType.DMA,
            pltpu.SemaphoreType.DMA((size - 1,)),
            pltpu.SemaphoreType.DMA((size - 1,)),
        ],
        compiler_params=remote_params(number),
        cost_estimate=pl.CostEstimate(flops=0, bytes_accessed=100_000_000, transcendentals=0),
        name="gather_ctx",
    )(values)


def scatter_ctx(values, number):
    size = lax.axis_size("ctx")
    rows, width = values.shape
    shape = (rows // size, width)
    return pl.pallas_call(
        functools.partial(peer_scatter, size),
        in_specs=[pl.BlockSpec(memory_space=pltpu.VMEM)],
        out_specs=pl.BlockSpec(memory_space=pltpu.VMEM),
        out_shape=jax.ShapeDtypeStruct(shape, values.dtype),
        scratch_shapes=[
            pltpu.VMEM((size - 1, *shape), bf16),
            pltpu.SemaphoreType.DMA((size - 1,)),
            pltpu.SemaphoreType.DMA((size - 1,)),
        ],
        compiler_params=remote_params(number),
        cost_estimate=pl.CostEstimate(flops=0, bytes_accessed=100_000_000, transcendentals=0),
        name="scatter_ctx",
    )(values)


def attend(scale, query_ref, key_ref, value_ref, seg_row_ref, seg_column_ref, out_ref, total_ref):
    scores = matmul_nt(key_ref[...], query_ref[...]) * scale
    scores = jnp.where(seg_column_ref[...] == seg_row_ref[...], scores, masked_score)
    most = jnp.max(scores, axis=0, keepdims=True)
    probs = jnp.exp(scores - most)
    total = jnp.sum(probs, axis=0, keepdims=True)
    mixed = matmul(value_ref[...].T, probs.astype(bf16)) / total
    out_ref[...] = mixed.T.astype(bf16)
    total_ref[...] = most + jnp.log(total)


def attend_back(
    scale,
    query_ref,
    key_ref,
    value_ref,
    seg_row_ref,
    seg_column_ref,
    out_ref,
    total_ref,
    grad_ref,
    query_grad_ref,
    key_grad_ref,
    value_grad_ref,
    key_sum_ref,
    value_sum_ref,
):
    step = pl.program_id(1)
    query, key, grad = query_ref[...], key_ref[...], grad_ref[...]
    scores = matmul_nt(key, query) * scale
    scores = jnp.where(seg_column_ref[...] == seg_row_ref[...], scores, masked_score)
    probs = jnp.exp(scores - total_ref[...])
    products = grad.astype(f32) * out_ref[...].astype(f32)
    delta = jnp.sum(products.T, axis=0, keepdims=True)
    score_grad = (probs * (matmul_nt(value_ref[...], grad) - delta)).astype(bf16)
    query_grad_ref[...] = (matmul(key.T, score_grad) * scale).T
    key_part = matmul(score_grad, query) * scale
    value_part = matmul(probs.astype(bf16), grad)

    @pl.when(step == 0)
    def _():
        key_sum_ref[...] = key_part
        value_sum_ref[...] = value_part

    @pl.when(step > 0)
    def _():
        key_sum_ref[...] += key_part
        value_sum_ref[...] += value_part

    @pl.when(step == pl.num_programs(1) - 1)
    def _():
        key_grad_ref[...] = key_sum_ref[...].astype(bf16)
        value_grad_ref[...] = value_sum_ref[...].astype(bf16)


def attention_specs(rows, keys, heads, head_dim):
    block = min(rows, QUERY_BLOCK)
    query = pl.BlockSpec((block, head_dim), lambda h, i: (i, h))
    return (
        (heads, rows // block),
        [
            query,
            pl.BlockSpec((keys, head_dim), lambda h, i: (0, h)),
            pl.BlockSpec((keys, head_dim), lambda h, i: (0, h + heads)),
            pl.BlockSpec((None, 1, block), lambda h, i: (i, 0, 0)),
            pl.BlockSpec((keys, 1), lambda h, i: (0, 0)),
        ],
        query,
        pl.BlockSpec((None, None, 1, block), lambda h, i: (h, i, 0, 0)),
        pl.BlockSpec((keys, head_dim), lambda h, i: (0, h)),
    )


def run_attend(query_b, group, seg_rows, seg_columns, heads, scale):
    rows, keys = query_b.shape[0], group.shape[0]
    head_dim = query_b.shape[1] // heads
    grid, specs, query, total, unused = attention_specs(rows, keys, heads, head_dim)
    work = heads * rows * keys
    return pl.pallas_call(
        functools.partial(attend, scale),
        grid=grid,
        in_specs=specs,
        out_specs=[query, total],
        out_shape=[
            jax.ShapeDtypeStruct(query_b.shape, bf16),
            jax.ShapeDtypeStruct((*grid, 1, rows // grid[1]), f32),
        ],
        compiler_params=params(2),
        cost_estimate=pl.CostEstimate(
            flops=4 * work * head_dim, bytes_accessed=8 * query_b.size, transcendentals=work
        ),
        name="attend",
    )(query_b, group, group, seg_rows, seg_columns)


def run_attend_back(query_b, group, seg_rows, seg_columns, out_b, total, grad_b, heads, scale):
    rows, keys = query_b.shape[0], group.shape[0]
    head_dim = query_b.shape[1] // heads
    grid, specs, query, total_spec, key = attention_specs(rows, keys, heads, head_dim)
    work = heads * rows * keys
    return pl.pallas_call(
        functools.partial(attend_back, scale),
        grid=grid,
        in_specs=[*specs, query, total_spec, query],
        out_specs=[query, key, key],
        out_shape=[
            jax.ShapeDtypeStruct(query_b.shape, f32),
            jax.ShapeDtypeStruct((keys, query_b.shape[1]), bf16),
            jax.ShapeDtypeStruct((keys, query_b.shape[1]), bf16),
        ],
        scratch_shapes=[pltpu.VMEM((keys, head_dim), f32)] * 2,
        compiler_params=params(2),
        cost_estimate=pl.CostEstimate(
            flops=10 * work * head_dim, bytes_accessed=16 * query_b.size, transcendentals=work
        ),
        name="attend_back",
    )(query_b, group, group, seg_rows, seg_columns, out_b, total, grad_b)


def beside(values):
    return lax.ppermute(values, "fsdp", [(0, 1), (1, 0), (2, 3), (3, 2)])


def across(values):
    return lax.ppermute(values, "fsdp", [(0, 2), (1, 3), (2, 0), (3, 1)])


def other(values):
    return lax.ppermute(values, "ctx", [(0, 1), (1, 0)])


def added(*values):
    total = values[0].astype(f32)
    for value in values[1:]:
        total = total + value.astype(f32)
    return total.astype(bf16)


def then(first, *values):
    return lax.optimization_barrier((first, *values))[1:]


def weight_grad(left, right):
    return jnp.einsum("gesa,gesb->eab", left, right, preferred_element_type=f32)


def by_chips():
    return lax.axis_size("fsdp") == 4 and lax.axis_size("ctx") == 2


def chunk_order(chunks):
    if not by_chips():
        return jnp.arange(chunks, dtype=jnp.int32)
    fsdp, ctx = lax.axis_index("fsdp"), lax.axis_index("ctx")
    sibling = fsdp + 1 - 2 * lax.rem(fsdp, 2)
    flip = lambda core: lax.rem(core + 2, 4)
    places = (
        (flip(sibling), ctx),
        (flip(fsdp), ctx),
        (sibling, 1 - ctx),
        (fsdp, 1 - ctx),
        (flip(sibling), 1 - ctx),
        (flip(fsdp), 1 - ctx),
        (sibling, ctx),
        (fsdp, ctx),
    )
    return jnp.stack([jnp.asarray(2 * f + c, jnp.int32) for f, c in places])


def expert_steps(ids, own_tokens, grad_all, rank_rows, rank_columns, first, weights):
    gate_weight, up_weight, down_weight = weights
    chunks = rank_rows.shape[0]

    def one_pass(at, near, far, product, kept):
        return run_expert_pass(
            jnp.array([at, at + 1], jnp.int32),
            first,
            rank_rows,
            rank_columns,
            near,
            far,
            product,
            gate_weight,
            up_weight,
            kept,
        )

    if not by_chips():
        token_all = lax.all_gather(own_tokens, ROWS, axis=0, tiled=True)
        blocks = token_all.reshape(chunks, CHUNK, -1)
        grad_slots, product = run_select_grads(ids, rank_rows, grad_all, down_weight)
        kept, backs = (), []
        for at in range(0, chunks, 2):
            kept, near, far = one_pass(at, blocks[at], blocks[at + 1], product, kept)
            backs += [near, far]
        back_sum = lax.psum_scatter(
            jnp.concatenate(backs), ROWS, scatter_dimension=0, tiled=True
        )
        out_part = run_expert_sums(ids, rank_columns, kept[1], down_weight)
        return kept, grad_slots, back_sum, out_part

    from_across, from_other = across(own_tokens), other(own_tokens)
    from_beside = beside(own_tokens)
    grad_slots, product = run_select_grads(ids, rank_rows, grad_all, down_weight)
    from_across, from_other = then(product, from_across, from_other)
    kept, back_sum, out_part = run_exchange_pass(
        rank_rows,
        rank_columns,
        product,
        weights,
        (own_tokens, from_beside, from_across, from_other),
    )
    return kept, grad_slots, back_sum, out_part


def rotated_sum(values):
    size = lax.axis_size("tp")
    total = values
    for offset in range(1, size):
        pairs = [(at, (at + offset) % size) for at in range(size)]
        total = total + lax.ppermute(values, "tp", pairs)
    return total


def scatter_line(values, beside_steps):
    size, place = lax.axis_size("tp"), lax.axis_index("tp")
    rows = values.shape[0] // size
    block = lambda at: lax.dynamic_slice_in_dim(
        values, jnp.clip(at, 0, size - 1) * rows, rows, 0
    )
    right, left, made = None, None, []
    for step in range(size - 1):
        to_right = block(size - 1 - step + place)
        to_left = block(place - (size - 1 - step))
        if step > 0:
            to_right, to_left = added(to_right, right), added(to_left, left)
        right = lax.ppermute(
            to_right, "tp", [(at, at + 1) for at in range(size - 1) if at <= step]
        )
        left = lax.ppermute(
            to_left, "tp", [(at, at - 1) for at in range(1, size) if size - 1 - at <= step]
        )
        if step < len(beside_steps):
            made.append(beside_steps[step]())
            right, left = then(made[-1], right, left)
    total = block(place).astype(f32) + right.astype(f32) + left.astype(f32)
    return total, made


def head_blocks(width, head_dim):
    for at in range(0, width, head_dim):
        yield slice(at, at + head_dim)


def project(
    input_ref,
    gain_ref,
    weight_ref,
    cosine_ref,
    sine_ref,
    head_gain_ref,
    segment_ref,
    normed_ref,
    inverse_ref,
    pre_ref,
    query_ref,
    group_ref,
):
    values = input_ref[...].astype(f32)
    inverse = norm_scale(values)
    normed = (values * inverse * gain_ref[...]).astype(bf16)
    normed_ref[...] = normed
    inverse_ref[...] = inverse
    qkv = matmul(normed, weight_ref[...])
    width = query_ref.shape[1]
    head_dim = cosine_ref.shape[1]
    pre_ref[...] = qkv[:, : 2 * width]
    cosine, sine = cosine_ref[...], sine_ref[...]
    for which in (0, 1):
        gain = head_gain_ref[which : which + 1, :]
        for at in head_blocks(width, head_dim):
            head = qkv[:, which * width + at.start : which * width + at.stop]
            head = head * norm_scale(head) * gain
            turned = head * cosine + pltpu.roll(head, head_dim // 2, 1) * sine
            to_ref = query_ref if which == 0 else group_ref
            to_ref[:, at] = turned.astype(bf16)
    group_ref[:, width : 2 * width] = qkv[:, 2 * width :].astype(bf16)
    rest = group_ref.shape[1] - 2 * width
    group_ref[:, 2 * width :] = jnp.broadcast_to(
        segment_ref[...], (segment_ref.shape[0], rest)
    ).astype(bf16)


def project_back(
    query_grad_ref,
    group_grad_ref,
    pre_ref,
    cosine_ref,
    sine_ref,
    head_gain_ref,
    weight_ref,
    input_ref,
    inverse_ref,
    gain_ref,
    grad_ref,
    part_ref,
    along_ref,
    terms_ref,
    head_terms_ref,
):
    width = query_grad_ref.shape[1]
    head_dim = cosine_ref.shape[1]
    cosine, sine = cosine_ref[...], sine_ref[...]

    @pl.when(pl.program_id(0) == 0)
    def _():
        terms_ref[...] = jnp.zeros_like(terms_ref)
        head_terms_ref[...] = jnp.zeros_like(head_terms_ref)

    for which in (0, 1):
        gain = head_gain_ref[which : which + 1, :]
        from_ref = query_grad_ref if which == 0 else group_grad_ref
        for at in head_blocks(width, head_dim):
            own = slice(which * width + at.start, which * width + at.stop)
            grad = from_ref[:, at].astype(f32)
            incoming = grad * cosine - pltpu.roll(grad, head_dim // 2, 1) * sine
            head = pre_ref[:, own]
            value_grad, gain_terms = norm_back(incoming, head, norm_scale(head), gain)
            grad_ref[:, own] = value_grad.astype(bf16)
            head_terms_ref[which : which + 1, :] += jnp.sum(gain_terms, axis=0, keepdims=True)
    grad_ref[:, 2 * width :] = group_grad_ref[:, width:]
    part = matmul_nt(grad_ref[...], weight_ref[...])
    part_ref[...] = part.astype(bf16)
    product = part * input_ref[...].astype(f32)
    terms_ref[...] += jnp.sum(product * inverse_ref[...], axis=0, keepdims=True)
    along_ref[...] = jnp.sum(product * gain_ref[...], axis=1, keepdims=True)


def run_project(input_b, gain, full, cosine, sine, head_gains, segment, width):
    rows, depth = input_b.shape
    head_dim = cosine.shape[1]
    block = min(rows, QUERY_BLOCK)
    by_rows = lambda columns: pl.BlockSpec((block, columns), lambda i: (i, 0))
    return pl.pallas_call(
        project,
        grid=(rows // block,),
        in_specs=[
            by_rows(depth),
            once((1, depth)),
            once((depth, 3 * width)),
            by_rows(head_dim),
            by_rows(head_dim),
            once((2, head_dim)),
            by_rows(1),
        ],
        out_specs=[
            by_rows(depth),
            by_rows(1),
            by_rows(2 * width),
            by_rows(width),
            by_rows(2 * width + EXTRA),
        ],
        out_shape=[
            jax.ShapeDtypeStruct((rows, depth), bf16),
            jax.ShapeDtypeStruct((rows, 1), f32),
            jax.ShapeDtypeStruct((rows, 2 * width), f32),
            jax.ShapeDtypeStruct((rows, width), bf16),
            jax.ShapeDtypeStruct((rows, 2 * width + EXTRA), bf16),
        ],
        compiler_params=params(1),
        cost_estimate=pl.CostEstimate(
            flops=6 * rows * depth * width, bytes_accessed=6 * depth * width, transcendentals=0
        ),
        name="project",
    )(input_b, gain, full, cosine, sine, head_gains, segment)


def run_project_back(
    query_grad, group_grad, pre, cosine, sine, head_gains, full, input_b, inverse, gain
):
    rows, depth = input_b.shape
    width = query_grad.shape[1]
    head_dim = cosine.shape[1]
    block = min(rows, QUERY_BLOCK)
    by_rows = lambda columns: pl.BlockSpec((block, columns), lambda i: (i, 0))
    whole = lambda shape: pl.BlockSpec(shape, lambda i: (0, 0))
    return pl.pallas_call(
        project_back,
        grid=(rows // block,),
        in_specs=[
            by_rows(width),
            by_rows(2 * width),
            by_rows(2 * width),
            by_rows(head_dim),
            by_rows(head_dim),
            once((2, head_dim)),
            once((depth, 3 * width)),
            by_rows(depth),
            by_rows(1),
            once((1, depth)),
        ],
        out_specs=[
            by_rows(3 * width),
            by_rows(depth),
            by_rows(1),
            whole((1, depth)),
            whole((2, head_dim)),
        ],
        out_shape=[
            jax.ShapeDtypeStruct((rows, 3 * width), bf16),
            jax.ShapeDtypeStruct((rows, depth), bf16),
            jax.ShapeDtypeStruct((rows, 1), f32),
            jax.ShapeDtypeStruct((1, depth), f32),
            jax.ShapeDtypeStruct((2, head_dim), f32),
        ],
        compiler_params=params(1),
        cost_estimate=pl.CostEstimate(
            flops=6 * rows * depth * width, bytes_accessed=8 * depth * width, transcendentals=0
        ),
        name="project_back",
    )(query_grad, group_grad, pre, cosine, sine, head_gains, full, input_b, inverse, gain)


def split_three(values):
    high = values.astype(bf16)
    rest = values - high.astype(f32)
    middle = rest.astype(bf16)
    return (high, middle, (rest - middle.astype(f32)).astype(bf16))


def on_device(
    layer_input,
    token_order,
    doc_lengths,
    expert_routes,
    attn_gain,
    query_weight,
    key_weight,
    value_weight,
    query_gain,
    key_gain,
    out_weight,
    moe_gain,
    router_weight,
    gate_weight,
    up_weight,
    down_weight,
    out_grad,
):
    tp_index = lax.axis_index("tp")
    ctx_size = lax.axis_size("ctx")
    fc_size = lax.axis_size("fsdp") * ctx_size
    fc_index = lax.axis_index("fsdp") * ctx_size + lax.axis_index("ctx")
    tok_count, quarter = layer_input.shape
    share = tok_count // lax.axis_size("tp")
    head_dim = query_gain.shape[0]
    head_width = query_weight.shape[1]
    heads = head_width // head_dim
    scale = head_dim ** (-0.5)
    experts = router_weight.shape[1]
    top = expert_routes.shape[1]
    local_experts = gate_weight.shape[0]
    capacity = tok_count * top * 5 // (4 * experts)
    own_rows = lambda values: lax.dynamic_slice_in_dim(values, tp_index * share, share, 0)
    own_width = lambda values: lax.dynamic_slice_in_dim(values, tp_index * quarter, quarter, 1)

    packed = jnp.concatenate(
        [
            query_weight,
            key_weight,
            value_weight,
            out_weight.T,
            router_weight,
            attn_gain[:, None],
            moe_gain[:, None],
            jnp.zeros((attn_gain.shape[0], EXTRA - experts - 2), bf16),
        ],
        axis=1,
    )
    full = lax.all_gather(packed, ROWS, axis=0, tiled=True)
    expert_ids = jnp.arange(experts, dtype=jnp.int32)
    named = jnp.any(expert_routes[:, :, None] == expert_ids[None, None, :], axis=1)
    earlier = jnp.tri(tok_count, tok_count, -1, dtype=bf16)
    before = matmul(earlier, named.astype(bf16))
    first_slot = (lax.rem(fc_index, CHUNK // tok_count) * capacity).astype(f32)
    ranks = jnp.where(named, before + first_slot, -1.0).astype(bf16)
    input_b = gather_tp(layer_input, True, 0)
    out_grad, full, input_b = lax.optimization_barrier((out_grad, full, input_b))
    grad_rows_b = lax.all_gather(out_grad, "tp", axis=1, tiled=True)
    side = 3 * head_width
    qkv_weight = full[:, :side]
    full_out = full[:, side : side + head_width]
    side = side + head_width
    full_router = full[:, side : side + experts]
    attn_gain_f = full[:, side + experts].astype(f32)
    moe_gain_f = full[:, side + experts + 1].astype(f32)
    width = input_b.shape[1]
    segment, position = doc_places(token_order[0], doc_lengths[0])
    cosine, sine = rope_tables(position, head_dim)
    head_gains = jnp.stack([query_gain, key_gain])
    attn_gain_row = attn_gain_f[None, :]
    normed, inverse_one, heads_pre, query_rows, group_part = run_project(
        input_b,
        attn_gain_row,
        full,
        cosine,
        sine,
        head_gains,
        segment.astype(f32)[:, None],
        head_width,
    )
    group = gather_ctx(group_part, 1)
    after_group, group = lax.optimization_barrier((grad_rows_b, group))
    grad_packed = jnp.concatenate(
        [after_group, ranks, jnp.zeros((tok_count, EXTRA - experts), bf16)], axis=1
    )
    grad_all = lax.all_gather(grad_packed, ROWS, axis=0, tiled=True)
    chunks = grad_all.shape[0] // CHUNK
    first_expert = fc_index * local_experts
    local_ranks = lax.dynamic_slice_in_dim(
        grad_all[:, width:], first_expert, local_experts, 1
    ).astype(jnp.int32)
    ids = chunk_order(chunks)
    rank_columns = jnp.stack(
        [
            lax.dynamic_slice_in_dim(local_ranks, ids[at] * CHUNK, CHUNK, 0)
            for at in range(chunks)
        ]
    )
    rank_rows = jnp.transpose(rank_columns, (0, 2, 1))[:, :, None, :]

    seg_rows = segment.astype(f32).reshape(-1, 1, min(tok_count, QUERY_BLOCK))
    seg_columns = group[:, 2 * head_width : 2 * head_width + 1].astype(f32)
    attn_b, log_total = run_attend(query_rows, group, seg_rows, seg_columns, heads, scale)
    attn_part = matmul_nt(attn_b, full_out).astype(bf16)
    attn_out = scatter_tp(attn_part, False, 2)
    resid = own_rows(input_b).astype(f32) + attn_out
    inverse_two = norm_scale(resid)
    moe_in = (resid * inverse_two * moe_gain_f).astype(bf16)
    logits = matmul(moe_in, full_router)
    own_named = own_rows(named)
    chosen = jnp.where(own_named, logits, -jnp.inf)
    gates = jax.nn.softmax(chosen, axis=-1)
    own_tokens = gather_tp(
        jnp.concatenate(
            [moe_in, *split_three(gates), jnp.zeros((share, EXTRA - 3 * experts), bf16)], axis=1
        ),
        False,
        3,
    )
    kept, grad_slots, back_sum, out_part = expert_steps(
        ids,
        own_tokens,
        grad_all,
        rank_rows,
        rank_columns,
        first_expert.reshape(1),
        (gate_weight, up_weight, down_weight),
    )
    token_slots, hidden_rows, gate_act_grad, up_act_grad, route_part = kept
    hit = jnp.arange(chunks, dtype=jnp.int32)[:, None] == ids[None, :]
    route_all = jnp.sum(
        jnp.where(hit[:, :, None, None], route_part[None, :, :, 0, :], 0.0), axis=1
    )
    route_all = jnp.transpose(route_all, (1, 0, 2)).reshape(
        local_experts, fc_size, tok_count
    )
    route_all = lax.all_to_all(
        jnp.transpose(route_all, (1, 0, 2)), ROWS, split_axis=0, concat_axis=0, tiled=True
    ).reshape(experts, tok_count)

    back_rows, ((grad_gate, gate_grad), grad_up, grad_down) = scatter_line(
        back_sum,
        (
            lambda: (weight_grad(token_slots, gate_act_grad), rotated_sum(route_all)),
            lambda: weight_grad(token_slots, up_act_grad),
            lambda: weight_grad(hidden_rows, grad_slots),
        ),
    )
    parts = own_tokens[:, width : width + 3 * experts].astype(f32)
    all_gates = parts[:, :experts] + parts[:, experts : 2 * experts] + parts[:, 2 * experts :]
    gate_grad = gate_grad.T
    logit_grad = all_gates * (
        gate_grad - jnp.sum(all_gates * gate_grad, axis=-1, keepdims=True)
    )
    grad_router = lax.dot_general(
        own_tokens[:, :width].astype(f32),
        logit_grad,
        (((0,), (0,)), ((), ())),
        precision=highest,
    )
    own_logit_grad = own_rows(logit_grad)
    router_back = lax.dot_general(
        own_logit_grad, full_router.astype(f32), (((1,), (1,)), ((), ())), precision=highest
    )
    moe_in_grad = (
        back_rows + router_back
    )
    resid_norm_grad, gain_terms = norm_back(moe_in_grad, resid, inverse_two, moe_gain_f)
    grad_moe_gain = jnp.sum(gain_terms, axis=0)
    resid_grad = own_rows(grad_rows_b).astype(f32) + resid_norm_grad
    resid_grad_b = gather_tp(resid_grad.astype(bf16), False, 5)

    out_sum = lax.psum_scatter(out_part, ROWS, scatter_dimension=0, tiled=True)

    grad_out = lax.dot_general(
        resid_grad_b, attn_b, (((0,), (0,)), ((), ())), preferred_element_type=f32
    )
    attn_grad = matmul(resid_grad_b, full_out).astype(bf16)
    query_rot_grad, key_part, value_part = run_attend_back(
        query_rows, group, seg_rows, seg_columns, attn_b, log_total, attn_grad, heads, scale
    )
    out_sum, key_part = lax.optimization_barrier((out_sum, key_part))
    out_sum = lax.psum_scatter(out_sum, "tp", scatter_dimension=0, tiled=True).astype(f32)
    group_grad = scatter_ctx(jnp.concatenate([key_part, value_part], axis=1), 6)
    qkv_grad, normed_part, along, attn_terms, head_terms = run_project_back(
        query_rot_grad,
        group_grad,
        heads_pre,
        cosine,
        sine,
        head_gains,
        full,
        input_b,
        inverse_one,
        attn_gain_row,
    )
    along = along[:, 0]
    gains = jnp.concatenate([attn_terms[0], grad_moe_gain, head_terms[0], head_terms[1]])
    normed_grad, gains, along = close_tp(normed_part, gains, along, 7)
    along = along[:, None] / width
    normed_grad, out_sum = lax.optimization_barrier((normed_grad, out_sum))
    layer_sum = resid + out_sum
    layer_output = lax.all_to_all(
        layer_sum.astype(bf16), "tp", split_axis=1, concat_axis=0, tiled=True
    )
    input_quarter = layer_input.astype(f32)
    gain_quarter = lax.dynamic_slice_in_dim(attn_gain_f, tp_index * quarter, quarter, 0)
    grad_input = own_width(resid_grad_b).astype(f32) + inverse_one * (
        normed_grad * gain_quarter - input_quarter * inverse_one * inverse_one * along
    )
    grad_qkv = lax.dot_general(
        normed, qkv_grad, (((0,), (0,)), ((), ())), preferred_element_type=f32
    )
    owned_out = lax.psum_scatter(
        jnp.concatenate(
            [grad_out, grad_router, jnp.zeros((width, EXTRA - experts), f32)], axis=1
        ).astype(bf16),
        ROWS,
        scatter_dimension=0,
        tiled=True,
    )
    (owned_out,) = then(normed_grad, owned_out)
    owned_out = owned_out.astype(f32)
    owned_qkv = lax.psum_scatter(
        grad_qkv.astype(bf16), ROWS, scatter_dimension=0, tiled=True
    ).astype(f32)
    owned_gain = attn_gain.shape[0]
    own_gain = lambda at: lax.dynamic_slice_in_dim(
        gains, at * width + fc_index * owned_gain, owned_gain, 0
    )
    return (
        layer_output,
        grad_input,
        own_gain(0),
        owned_qkv[:, :head_width],
        owned_qkv[:, head_width : 2 * head_width],
        owned_qkv[:, 2 * head_width :],
        gains[2 * width : 2 * width + head_dim],
        gains[2 * width + head_dim :],
        owned_out[:, :head_width].T,
        own_gain(1),
        owned_out[:, head_width : head_width + experts],
        grad_gate,
        grad_up,
        grad_down,
    )


def solution(mesh):
    in_specs = (
        P(("fsdp", "ctx"), "tp"),
        P("fsdp", "ctx"),
        P("fsdp", None),
        P(("fsdp", "ctx"), None),
        P(("fsdp", "ctx")),
        P(("fsdp", "ctx"), "tp"),
        P(("fsdp", "ctx"), "tp"),
        P(("fsdp", "ctx"), "tp"),
        P(),
        P(),
        P("tp", ("fsdp", "ctx")),
        P(("fsdp", "ctx")),
        P(("fsdp", "ctx"), None),
        P(("fsdp", "ctx"), None, "tp"),
        P(("fsdp", "ctx"), None, "tp"),
        P(("fsdp", "ctx"), "tp", None),
        P(("fsdp", "ctx"), "tp"),
    )
    out_specs = (
        P(("fsdp", "ctx"), "tp"),
        P(("fsdp", "ctx"), "tp"),
        P(("fsdp", "ctx")),
        P(("fsdp", "ctx"), "tp"),
        P(("fsdp", "ctx"), "tp"),
        P(("fsdp", "ctx"), "tp"),
        P(),
        P(),
        P("tp", ("fsdp", "ctx")),
        P(("fsdp", "ctx")),
        P(("fsdp", "ctx"), None),
        P(("fsdp", "ctx"), None, "tp"),
        P(("fsdp", "ctx"), None, "tp"),
        P(("fsdp", "ctx"), "tp", None),
    )
    return jax.shard_map(
        on_device, mesh=mesh, in_specs=in_specs, out_specs=out_specs, check_vma=False
    )
```

```python
import functools

import jax
import jax.numpy as jnp
from jax import lax
from jax.experimental import pallas as pl
from jax.experimental.pallas import tpu as pltpu
from jax.sharding import PartitionSpec as P

QUERY_BLOCK = 256
CHUNK = 768
SLOTS = 256
EXTRA = 128
VMEM_BYTES = 60 * 1024 * 1024


epsilon = 1e-05
rope_base = 50000.0
masked_score = -1e30
highest = lax.Precision.HIGHEST
bf16 = jnp.bfloat16
f32 = jnp.float32
ROWS = ("fsdp", "ctx")
ALL = ("fsdp", "ctx", "tp")
MESH = pl.DeviceIdType.MESH


def doc_places(order_row, length_row):
    ends = jnp.cumsum(length_row, dtype=jnp.int32)
    passed = (order_row[:, None] >= ends[None, :]).astype(jnp.int32)
    segment = jnp.sum(passed, axis=1, dtype=jnp.int32)
    start = jnp.sum(passed * length_row[None, :], axis=1, dtype=jnp.int32)
    return (segment, order_row - start)


def rope_tables(position, head_dim):
    half = head_dim // 2
    freqs = rope_base ** (-(jnp.arange(half, dtype=jnp.float32) * (2.0 / head_dim)))
    angles = position.astype(jnp.float32)[:, None] * freqs[None, :]
    cosine, sine = jnp.cos(angles), jnp.sin(angles)
    return jnp.concatenate([cosine, cosine], axis=1), jnp.concatenate([-sine, sine], axis=1)


def norm_scale(values):
    return lax.rsqrt(jnp.mean(values * values, axis=-1, keepdims=True) + epsilon)


def norm_back(incoming, values, inverse, gain):
    scaled = incoming * gain
    value_grad = inverse * (
        scaled - values * inverse * inverse * jnp.mean(scaled * values, axis=-1, keepdims=True)
    )
    return (value_grad, incoming * values * inverse)


def matmul(left, right):
    return jnp.dot(left, right, preferred_element_type=f32)


def matmul_nt(left, right):
    return lax.dot_general(left, right, (((1,), (1,)), ((), ())), preferred_element_type=f32)


def slot_rows(rank_row):
    slots = lax.broadcasted_iota(jnp.int32, (SLOTS, rank_row.shape[1]), 0)
    return slots == rank_row


def slot_columns(rank_column):
    slots = lax.broadcasted_iota(jnp.int32, (rank_column.shape[0], SLOTS), 1)
    return jnp.where(slots == rank_column, 1.0, 0.0).astype(bf16)


def as_one_hot(mask):
    return jnp.where(mask, 1.0, 0.0).astype(bf16)


def select_grads(ids_ref, rank_ref, grad_ref, down_ref, rows_ref, product_ref):
    expert = pl.program_id(1)
    rows = matmul(as_one_hot(slot_rows(rank_ref[...])), grad_ref[...]).astype(bf16)
    rows_ref[...] = rows
    product_ref[...] = matmul_nt(rows, down_ref[expert])


def expert_step(
    expert,
    named,
    rank_ref,
    tokens,
    product_ref,
    gate_ref,
    up_ref,
    await_weights,
    rows_ref,
    hidden_ref,
    gate_grad_ref,
    up_grad_ref,
    route_ref,
    held_ref,
):
    width = rows_ref.shape[1]
    mask = slot_rows(rank_ref[...])
    picked = matmul(as_one_hot(mask), tokens)
    rows = picked[:, :width].astype(bf16)
    rows_ref[...] = rows
    lane = lax.broadcasted_iota(jnp.int32, (SLOTS, EXTRA), 1)
    mine = jnp.logical_and(lax.rem(lane, 32) == named, lane < 96)
    gate = jnp.sum(jnp.where(mine, picked[:, width:], 0.0), axis=1, keepdims=True)
    await_weights()
    gate_act = matmul(rows, gate_ref[expert])
    up_act = matmul(rows, up_ref[expert])
    sigmoid_g = 1.0 / (1.0 + jnp.exp(-gate_act))
    silu_g = gate_act * sigmoid_g
    hidden = silu_g * up_act
    hidden_ref[...] = (gate * hidden).astype(bf16)
    product = product_ref[...]
    route = jnp.sum(hidden.astype(bf16).astype(f32) * product, axis=1, keepdims=True)
    route_ref[...] = jnp.sum(jnp.where(mask, route, 0.0), axis=0, keepdims=True)
    hidden_grad = gate * product
    gate_grad = (
        hidden_grad * up_act * sigmoid_g * (1.0 + gate_act * (1.0 - sigmoid_g))
    ).astype(bf16)
    up_grad = (hidden_grad * silu_g).astype(bf16)
    gate_grad_ref[...] = gate_grad
    up_grad_ref[...] = up_grad
    back = matmul_nt(gate_grad, gate_ref[expert]) + matmul_nt(up_grad, up_ref[expert])
    held_ref[pl.ds(pl.multiple_of(expert * SLOTS, SLOTS), SLOTS), :] = back.astype(bf16)


def chunk_places(column_ref):
    columns = column_ref[...]
    return jnp.concatenate(
        [slot_columns(columns[:, e : e + 1]) for e in range(columns.shape[1])], axis=1
    )


def expert_pass(
    ids_ref,
    first_ref,
    rank_ref,
    column_ref,
    near_ref,
    far_ref,
    product_ref,
    gate_in_ref,
    up_in_ref,
    *refs,
):
    (
        rows_ref,
        hidden_ref,
        gate_grad_ref,
        up_grad_ref,
        route_ref,
        near_back_ref,
        far_back_ref,
        token_ref,
        gate_ref,
        up_ref,
        held_ref,
        back_ref,
        token_sem,
        gate_sem,
        up_sem,
        back_sem,
    ) = refs[-16:]
    chunk, expert = pl.program_id(0), pl.program_id(1)
    local = gate_ref.shape[0]
    width = rows_ref.shape[1]
    tiles = back_sem.shape[1]
    tile = width // tiles
    loads = [
        pltpu.make_async_copy(source, token_ref.at[at], token_sem.at[at])
        for at, source in enumerate((near_ref, far_ref))
    ]

    def weight_load(source, held, sem, at):
        return pltpu.make_async_copy(source.at[at], held.at[at], sem.at[at])

    def back_store(to, at, step):
        columns = pl.ds(step * tile, tile)
        return pltpu.make_async_copy(
            back_ref.at[at, :, columns], to.at[:, columns], back_sem.at[at, step]
        )

    @pl.when(jnp.logical_and(chunk == 0, expert == 0))
    def _():
        loads[0].start()
        for at in range(local):
            weight_load(gate_in_ref, gate_ref, gate_sem, at).start()
            weight_load(up_in_ref, up_ref, up_sem, at).start()
        loads[1].start()
        loads[0].wait()

    @pl.when(jnp.logical_and(chunk == 1, expert == 0))
    def _():
        loads[1].wait()

    def await_weights():
        @pl.when(chunk == 0)
        def _():
            weight_load(gate_in_ref, gate_ref, gate_sem, expert).wait()
            weight_load(up_in_ref, up_ref, up_sem, expert).wait()

    expert_step(
        expert,
        first_ref[0] + expert,
        rank_ref,
        token_ref[chunk],
        product_ref,
        gate_ref,
        up_ref,
        await_weights,
        rows_ref,
        hidden_ref,
        gate_grad_ref,
        up_grad_ref,
        route_ref,
        held_ref,
    )

    @pl.when(expert == local - 1)
    def _():
        places = chunk_places(column_ref)
        for step in range(tiles):
            at = pl.ds(step * tile, tile)
            back_ref[chunk, :, at] = matmul(places, held_ref[:, at]).astype(bf16)

            @pl.when(chunk == 0)
            def _():
                back_store(near_back_ref, 0, step).start()

            @pl.when(chunk == 1)
            def _():
                back_store(far_back_ref, 1, step).start()

    @pl.when(jnp.logical_and(chunk == 1, expert == local - 1))
    def _():
        for step in range(tiles):
            back_store(near_back_ref, 0, step).wait()
            back_store(far_back_ref, 1, step).wait()


def exchange_pass(
    rank_ref,
    column_ref,
    product_ref,
    gate_in_ref,
    up_in_ref,
    down_in_ref,
    own_ref,
    sibling_ref,
    from_across_ref,
    from_other_ref,
    rows_ref,
    hidden_ref,
    gate_grad_ref,
    up_grad_ref,
    route_ref,
    sum_ref,
    out_ref,
    inbox_ref,
    landing_ref,
    token_ref,
    gate_ref,
    up_ref,
    down_ref,
    hidden_held_ref,
    held_ref,
    far_ref,
    beside_ref,
    chip_ref,
    corner_ref,
    token_sem,
    gate_sem,
    up_sem,
    pass_send,
    pass_recv,
    far_send,
    far_recv,
    link_send,
    link_recv,
    store_sem,
    down_sem,
    out_sem,
    landing_sem,
):
    step, expert = pl.program_id(0), pl.program_id(1)
    local = gate_ref.shape[0]
    rows, width = far_ref.shape
    half = rows // 2
    fsdp, ctx = lax.axis_index("fsdp"), lax.axis_index("ctx")
    beside_id = {"fsdp": fsdp + 1 - 2 * lax.rem(fsdp, 2)}
    across_id = {"fsdp": lax.rem(fsdp + 2, 4)}
    other_id = {"ctx": 1 - ctx}
    last = expert == local - 1
    low, high = pl.ds(0, half), pl.ds(half, half)
    sources = (
        inbox_ref.at[0],
        from_across_ref,
        inbox_ref.at[1],
        from_other_ref,
        inbox_ref.at[3],
        inbox_ref.at[2],
        sibling_ref,
        own_ref,
    )

    def token_load(at):
        slot = at % 2
        return pltpu.make_async_copy(sources[at], token_ref.at[slot], token_sem.at[slot])

    def weight_load(source, held, sem, at):
        return pltpu.make_async_copy(source.at[at], held.at[at], sem.at[at])

    def pass_copy(number):
        source, to, peer = (
            (from_across_ref, inbox_ref.at[0], beside_id),
            (from_other_ref, inbox_ref.at[1], beside_id),
            (from_other_ref.at[low], inbox_ref.at[2, low], across_id),
            (from_across_ref.at[high], inbox_ref.at[2, high], other_id),
            (inbox_ref.at[2], inbox_ref.at[3], beside_id),
        )[number]
        return pltpu.make_async_remote_copy(
            src_ref=source,
            dst_ref=to,
            send_sem=pass_send.at[number],
            recv_sem=pass_recv.at[number],
            device_id=peer,
            device_id_type=MESH,
        )

    def far_copy(turn):
        return pltpu.make_async_remote_copy(
            src_ref=far_ref,
            dst_ref=beside_ref.at[turn % 2],
            send_sem=far_send.at[turn],
            recv_sem=far_recv.at[turn],
            device_id=beside_id,
            device_id_type=MESH,
        )

    def link_copy(number):
        source, to, peer = (
            (chip_ref.at[0, high], landing_ref.at[0, high], across_id),
            (chip_ref.at[1, low], landing_ref.at[1, low], other_id),
            (chip_ref.at[2, low], corner_ref.at[0], other_id),
            (chip_ref.at[2, high], corner_ref.at[1], across_id),
            (chip_ref.at[1, high], landing_ref.at[1, high], other_id),
            (chip_ref.at[0, low], landing_ref.at[0, low], across_id),
        )[number]
        return pltpu.make_async_remote_copy(
            src_ref=source,
            dst_ref=to,
            send_sem=link_send.at[number],
            recv_sem=link_recv.at[number],
            device_id=peer,
            device_id_type=MESH,
        )

    @pl.when(jnp.logical_and(step == 0, expert == 0))
    def _():
        barrier = pltpu.get_barrier_semaphore()
        for peer in (beside_id, across_id, other_id):
            pl.semaphore_signal(barrier, inc=1, device_id=peer, device_id_type=MESH)
        pl.semaphore_wait(barrier, 3)
        for number in range(4):
            pass_copy(number).start()
        for at in range(local):
            weight_load(gate_in_ref, gate_ref, gate_sem, at).start()
            weight_load(up_in_ref, up_ref, up_sem, at).start()
        down_load = pltpu.make_async_copy(down_in_ref, down_ref, down_sem)
        down_load.start()
        pass_copy(0).wait_recv()
        token_load(0).start()

    @pl.when(jnp.logical_and(step == 3, expert == 0))
    def _():
        pass_copy(2).wait_recv()
        pass_copy(3).wait_recv()
        pass_copy(4).start()

    for at in range(8):

        @pl.when(jnp.logical_and(step == at, expert == 0))
        def _():
            token_load(at).wait()

        if at < 7:

            @pl.when(jnp.logical_and(step == at, last))
            def _():
                if at == 1:
                    pass_copy(1).wait_recv()
                if at == 3:
                    pass_copy(4).wait_recv()
                token_load(at + 1).start()

    def await_weights():
        @pl.when(step == 0)
        def _():
            weight_load(gate_in_ref, gate_ref, gate_sem, expert).wait()
            weight_load(up_in_ref, up_ref, up_sem, expert).wait()

    first = (fsdp * 2 + ctx) * local

    @pl.when(step < 8)
    def _():
        expert_step(
            expert,
            first + expert,
            rank_ref,
            token_ref[lax.rem(step, 2)],
            product_ref,
            gate_ref,
            up_ref,
            await_weights,
            rows_ref,
            hidden_ref,
            gate_grad_ref,
            up_grad_ref,
            route_ref,
            held_ref,
        )
        hidden_held_ref[step, expert] = hidden_ref[...]

    tile = 512

    def tiles():
        for at in range(0, width, tile):
            yield pl.ds(at, tile)

    def add_half(turn, part, landed):
        total = chip_ref[turn, part, :].astype(f32) + corner_ref[landed].astype(f32)
        chip_ref[turn, part, :] = total.astype(bf16)

    for turn in range(4):

        @pl.when(jnp.logical_and(step == 2 * turn, last))
        def _():
            if turn > 0:
                far_copy(turn - 1).wait_send()
            places = chunk_places(column_ref)
            for at in tiles():
                far_ref[:, at] = matmul(places, held_ref[:, at]).astype(bf16)
            far_copy(turn).start()

        @pl.when(jnp.logical_and(step == 2 * turn + 1, last))
        def _():
            far_copy(turn).wait_recv()
            if turn == 3:
                far_copy(3).wait_send()
            places = chunk_places(column_ref)
            for at in tiles():
                total = matmul(places, held_ref[:, at]) + beside_ref[turn % 2, :, at].astype(f32)
                if turn < 3:
                    chip_ref[turn, :, at] = total.astype(bf16)
                else:
                    far_ref[:, at] = total.astype(bf16)
            if turn < 2:
                link_copy(turn).start()
            if turn == 2:
                link_copy(2).start()
                link_copy(3).start()


    number = step - 8
    turn = number // 2
    chip = lax.rem(fsdp + 2 * (1 - lax.rem(turn, 2)), 4)
    core = chip + (1 - lax.rem(number, 2)) * (1 - 2 * lax.rem(fsdp, 2))
    line = lax.rem(ctx + lax.rem((turn + 1) // 2, 2), 2)
    places_at = (core * 2 + line) * rows
    slot = lax.rem(step, 2)
    columns_of = width // local
    hidden = gate_ref.shape[2]

    def out_store(at, which):
        columns = pl.ds(pl.multiple_of(which * columns_of, columns_of), columns_of)
        return pltpu.make_async_copy(
            token_ref.at[slot, :, columns],
            out_ref.at[pl.ds(pl.multiple_of(at, rows), rows), columns],
            out_sem.at[slot, which],
        )

    @pl.when(step >= 8)
    def _():
        @pl.when(jnp.logical_and(step == 8, expert == 0))
        def _():
            pltpu.make_async_copy(down_in_ref, down_ref, down_sem).wait()

        @pl.when(expert == 0)
        def _():
            columns = column_ref[...]
            for e in range(local):
                held_ref[pl.ds(0, rows), pl.ds(e * hidden, hidden)] = matmul(
                    slot_columns(columns[:, e : e + 1]), hidden_held_ref[number, e]
                ).astype(bf16)

        @pl.when(step >= 10)
        def _():
            out_store(places_at, expert).wait()

        at = pl.ds(pl.multiple_of(expert * columns_of, columns_of), columns_of)
        token_ref[slot, :, at] = matmul(
            held_ref[pl.ds(0, rows), pl.ds(0, local * hidden)], down_ref[:, at]
        ).astype(bf16)
        out_store(places_at, expert).start()

    @pl.when(jnp.logical_and(step == 9, expert == 1))
    def _():
        link_copy(3).wait_recv()
        add_half(1, high, 1)
        link_copy(4).start()
        link_copy(2).wait_recv()
        add_half(0, low, 0)
        link_copy(5).start()

    @pl.when(jnp.logical_and(step == 15, last))
    def _():
        landing = []
        for way, numbers in enumerate(((0, 5), (1, 4))):
            for number in numbers:
                link_copy(number).wait_recv()
            copy = pltpu.make_async_copy(
                landing_ref.at[way], beside_ref.at[way], landing_sem.at[way]
            )
            copy.start()
            landing.append(copy)
        for copy in landing:
            copy.wait()
        for part in (low, high):
            held_ref[part, :] = (
                far_ref[part, :].astype(f32)
                + beside_ref[0, part, :].astype(f32)
                + beside_ref[1, part, :].astype(f32)
            ).astype(bf16)
        store = pltpu.make_async_copy(held_ref.at[pl.ds(0, rows)], sum_ref, store_sem)
        store.start()
        for number in range(5):
            pass_copy(number).wait_send()
        for number in range(6):
            link_copy(number).wait_send()
        for other_slot in (0, 1):
            for which in range(local):
                columns = pl.ds(which * columns_of, columns_of)
                pltpu.make_async_copy(
                    token_ref.at[other_slot, :, columns],
                    out_ref.at[pl.ds(0, rows), columns],
                    out_sem.at[other_slot, which],
                ).wait()
        store.wait()


def expert_sums(ids_ref, column_ref, hidden_ref, down_ref, out_ref):
    columns = column_ref[...]
    dense = [
        matmul(slot_columns(columns[:, e : e + 1]), hidden_ref[e]).astype(bf16)
        for e in range(columns.shape[1])
    ]
    out_ref[...] = matmul(jnp.concatenate(dense, axis=1), down_ref[...]).astype(bf16)


def params(dims):
    return pltpu.CompilerParams(
        dimension_semantics=("arbitrary",) * dims, vmem_limit_bytes=VMEM_BYTES
    )


def once(shape):
    return pl.BlockSpec(
        shape, lambda *ids: (0,) * len(shape), pipeline_mode=pl.Buffered(1)
    )


def run_select_grads(ids, rank_rows, grad_all, down_weight):
    chunks, local = rank_rows.shape[:2]
    hidden, width = down_weight.shape[1:]
    slots = chunks * local * SLOTS
    place = lambda g, e, ids: (g, e, 0, 0)
    return pl.pallas_call(
        select_grads,
        grid_spec=pltpu.PrefetchScalarGridSpec(
            num_scalar_prefetch=1,
            grid=(chunks, local),
            in_specs=[
                pl.BlockSpec((None, None, 1, CHUNK), place),
                pl.BlockSpec((CHUNK, width), lambda g, e, ids: (ids[g], 0)),
                once(down_weight.shape),
            ],
            out_specs=[
                pl.BlockSpec((None, None, SLOTS, width), place),
                pl.BlockSpec((None, None, SLOTS, hidden), place),
            ],
        ),
        out_shape=[
            jax.ShapeDtypeStruct((chunks, local, SLOTS, width), bf16),
            jax.ShapeDtypeStruct((chunks, local, SLOTS, hidden), f32),
        ],
        compiler_params=params(2),
        cost_estimate=pl.CostEstimate(
            flops=2 * slots * width * (CHUNK + hidden),
            bytes_accessed=2 * (chunks * CHUNK + slots) * width,
            transcendentals=0,
        ),
        name="select_grads",
    )(ids, rank_rows, grad_all, down_weight)


def run_exchange_pass(rank_rows, rank_columns, product, weights, sources):
    gate_weight, up_weight, down_weight = weights
    chunks, local = rank_rows.shape[:2]
    width, hidden = gate_weight.shape[1:]
    slots = chunks * local * SLOTS
    flat_down = down_weight.reshape(local * hidden, width)

    def per_expert(g, e):
        return (jnp.minimum(g, chunks - 1), jnp.where(g < chunks, e, local - 1), 0, 0)

    narrow = pl.BlockSpec((None, None, SLOTS, hidden), per_expert)
    anywhere = pl.BlockSpec(memory_space=pl.ANY)
    half = (2, CHUNK // 2, width)
    narrow_shape = jax.ShapeDtypeStruct((chunks, local, SLOTS, hidden), bf16)
    outs = pl.pallas_call(
        exchange_pass,
        grid=(2 * chunks, local),
        in_specs=[
            pl.BlockSpec((None, None, 1, CHUNK), per_expert),
            pl.BlockSpec((None, CHUNK, local), lambda g, e: (lax.rem(g, chunks), 0, 0)),
            narrow,
            *[anywhere] * 7,
        ],
        out_specs=[
            pl.BlockSpec((None, None, SLOTS, width), per_expert),
            narrow,
            narrow,
            narrow,
            pl.BlockSpec((None, None, 1, CHUNK), per_expert),
            *[anywhere] * 4,
        ],
        out_shape=[
            jax.ShapeDtypeStruct((chunks, local, SLOTS, width), bf16),
            narrow_shape,
            narrow_shape,
            narrow_shape,
            jax.ShapeDtypeStruct((chunks, local, 1, CHUNK), f32),
            jax.ShapeDtypeStruct((CHUNK, width), bf16),
            jax.ShapeDtypeStruct((chunks * CHUNK, width), bf16),
            jax.ShapeDtypeStruct((4, *sources[0].shape), bf16),
            jax.ShapeDtypeStruct((2, CHUNK, width), bf16),
        ],
        scratch_shapes=[
            pltpu.VMEM((2, CHUNK, width + EXTRA), bf16),
            pltpu.VMEM(gate_weight.shape, bf16),
            pltpu.VMEM(up_weight.shape, bf16),
            pltpu.VMEM(flat_down.shape, bf16),
            pltpu.VMEM((chunks, local, SLOTS, hidden), bf16),
            pltpu.VMEM((local * SLOTS, width), bf16),
            pltpu.VMEM((CHUNK, width), bf16),
            pltpu.VMEM((2, CHUNK, width), bf16),
            pltpu.VMEM((3, CHUNK, width), bf16),
            pltpu.VMEM(half, bf16),
            pltpu.SemaphoreType.DMA((2,)),
            pltpu.SemaphoreType.DMA((local,)),
            pltpu.SemaphoreType.DMA((local,)),
            pltpu.SemaphoreType.DMA((5,)),
            pltpu.SemaphoreType.DMA((5,)),
            pltpu.SemaphoreType.DMA((4,)),
            pltpu.SemaphoreType.DMA((4,)),
            pltpu.SemaphoreType.DMA((6,)),
            pltpu.SemaphoreType.DMA((6,)),
            pltpu.SemaphoreType.DMA,
            pltpu.SemaphoreType.DMA,
            pltpu.SemaphoreType.DMA((2, local)),
            pltpu.SemaphoreType.DMA((2,)),
        ],
        compiler_params=pltpu.CompilerParams(
            dimension_semantics=("arbitrary",) * 2,
            collective_id=9,
            has_side_effects=True,
            vmem_limit_bytes=VMEM_BYTES,
        ),
        cost_estimate=pl.CostEstimate(
            flops=2 * slots * width * (2 * CHUNK + 4 * hidden),
            bytes_accessed=2 * (12 * CHUNK + slots) * width,
            transcendentals=slots * hidden,
        ),
        name="exchange_pass",
    )(rank_rows, rank_columns, product, gate_weight, up_weight, flat_down, *sources)
    return outs[:5], outs[5], outs[6]


def run_expert_pass(
    ids, first, rank_rows, rank_columns, near, far, product, gate_weight, up_weight, kept
):
    chunks, local = rank_rows.shape[:2]
    width, hidden = gate_weight.shape[1:]
    slots = 2 * local * SLOTS
    per_expert = lambda g, e, ids: (ids[g], e, 0, 0)
    narrow = pl.BlockSpec((None, None, SLOTS, hidden), per_expert)
    in_specs = [
        pl.BlockSpec(memory_space=pltpu.SMEM),
        pl.BlockSpec((None, None, 1, CHUNK), per_expert),
        pl.BlockSpec((None, CHUNK, local), lambda g, e, ids: (ids[g], 0, 0)),
        pl.BlockSpec(memory_space=pl.ANY),
        pl.BlockSpec(memory_space=pl.ANY),
        narrow,
        pl.BlockSpec(memory_space=pl.ANY),
        pl.BlockSpec(memory_space=pl.ANY),
    ]
    kept_shapes = [
        jax.ShapeDtypeStruct((chunks, local, SLOTS, width), bf16),
        jax.ShapeDtypeStruct((chunks, local, SLOTS, hidden), bf16),
        jax.ShapeDtypeStruct((chunks, local, SLOTS, hidden), bf16),
        jax.ShapeDtypeStruct((chunks, local, SLOTS, hidden), bf16),
        jax.ShapeDtypeStruct((chunks, local, 1, CHUNK), f32),
    ]
    outs = pl.pallas_call(
        expert_pass,
        grid_spec=pltpu.PrefetchScalarGridSpec(
            num_scalar_prefetch=1,
            grid=(2, local),
            in_specs=in_specs + [pl.BlockSpec(memory_space=pl.ANY)] * len(kept),
            out_specs=[
                pl.BlockSpec((None, None, SLOTS, width), per_expert),
                narrow,
                narrow,
                narrow,
                pl.BlockSpec((None, None, 1, CHUNK), per_expert),
                pl.BlockSpec(memory_space=pl.ANY),
                pl.BlockSpec(memory_space=pl.ANY),
            ],
            scratch_shapes=[
                pltpu.VMEM((2, CHUNK, width + EXTRA), bf16),
                pltpu.VMEM(gate_weight.shape, bf16),
                pltpu.VMEM(up_weight.shape, bf16),
                pltpu.VMEM((local * SLOTS, width), bf16),
                pltpu.VMEM((2, CHUNK, width), bf16),
                pltpu.SemaphoreType.DMA((2,)),
                pltpu.SemaphoreType.DMA((local,)),
                pltpu.SemaphoreType.DMA((local,)),
                pltpu.SemaphoreType.DMA((2, 4)),
            ],
        ),
        out_shape=kept_shapes + [jax.ShapeDtypeStruct((CHUNK, width), bf16)] * 2,
        input_output_aliases={9 + at: at for at in range(len(kept))},
        compiler_params=params(2),
        cost_estimate=pl.CostEstimate(
            flops=2 * slots * width * (2 * CHUNK + 4 * hidden),
            bytes_accessed=2 * (4 * CHUNK + slots) * width,
            transcendentals=slots * hidden,
        ),
        name="expert_pass",
    )(ids, first, rank_rows, rank_columns, near, far, product, gate_weight, up_weight, *kept)
    return outs[:5], outs[5], outs[6]


def run_expert_sums(ids, rank_columns, hidden_rows, down_weight):
    chunks, local, unused, hidden = hidden_rows.shape
    width = down_weight.shape[2]
    flat = down_weight.reshape(local * hidden, width)
    return pl.pallas_call(
        expert_sums,
        grid_spec=pltpu.PrefetchScalarGridSpec(
            num_scalar_prefetch=1,
            grid=(chunks,),
            in_specs=[
                pl.BlockSpec((None, CHUNK, local), lambda g, ids: (g, 0, 0)),
                pl.BlockSpec((None, local, SLOTS, hidden), lambda g, ids: (g, 0, 0, 0)),
                once(flat.shape),
            ],
            out_specs=pl.BlockSpec((CHUNK, width), lambda g, ids: (ids[g], 0)),
        ),
        out_shape=jax.ShapeDtypeStruct((chunks * CHUNK, width), bf16),
        compiler_params=params(1),
        cost_estimate=pl.CostEstimate(
            flops=2 * chunks * CHUNK * local * hidden * (width + SLOTS),
            bytes_accessed=2 * chunks * CHUNK * width,
            transcendentals=0,
        ),
        name="expert_sums",
    )(ids, rank_columns, hidden_rows, flat)


def line_barrier(size):
    place = lax.axis_index("tp")
    barrier = pltpu.get_barrier_semaphore()

    @pl.when(place > 0)
    def _():
        pl.semaphore_signal(barrier, inc=1, device_id={"tp": place - 1}, device_id_type=MESH)

    @pl.when(place < size - 1)
    def _():
        pl.semaphore_signal(barrier, inc=1, device_id={"tp": place + 1}, device_id_type=MESH)

    has_left = jnp.where(place > 0, 1, 0)
    has_right = jnp.where(place < size - 1, 1, 0)
    pl.semaphore_wait(barrier, has_left + has_right)


def line_gather(size, columns, in_ref, out_ref, own_sem, send_sem, recv_sem):
    place = lax.axis_index("tp")
    extent = in_ref.shape[1] if columns else in_ref.shape[0]

    def block(index):
        at = pl.ds(pl.multiple_of(index * extent, extent), extent)
        return out_ref.at[:, at] if columns else out_ref.at[at, :]

    line_barrier(size)
    own = pltpu.make_async_copy(in_ref, block(place), own_sem)
    own.start()

    def sending(way, step):
        source = place - step if way == 0 else place + step
        to = place + 1 if way == 0 else place - 1
        return pltpu.make_async_remote_copy(
            src_ref=in_ref if step == 0 else block(source),
            dst_ref=block(source),
            send_sem=send_sem.at[way, step],
            recv_sem=recv_sem.at[way, step],
            device_id={"tp": to},
            device_id_type=MESH,
        )

    def sends(way, step):
        if way == 0:
            return jnp.logical_and(place >= step, place < size - 1)
        return jnp.logical_and(place + step < size, place > 0)

    def receiving(way, step):
        source = place - 1 - step if way == 0 else place + 1 + step
        origin = place - 1 if way == 0 else place + 1
        return pltpu.make_async_remote_copy(
            src_ref=block(source),
            dst_ref=block(source),
            send_sem=send_sem.at[way, step],
            recv_sem=recv_sem.at[way, step],
            device_id={"tp": origin},
            device_id_type=MESH,
        )

    def receives(way, step):
        return place > step if way == 0 else place + 1 + step < size

    for step in range(size - 1):
        for way in (0, 1):

            @pl.when(sends(way, step))
            def _():
                sending(way, step).start()

        for way in (0, 1):

            @pl.when(receives(way, step))
            def _():
                receiving(way, step).wait_recv()

    for step in range(size - 1):
        for way in (0, 1):

            @pl.when(sends(way, step))
            def _():
                sending(way, step).wait_send()

    own.wait()


def line_scatter(
    size, columns, in_ref, out_ref, staged_ref, landed_ref, send_sem, recv_sem, stages=()
):
    place = lax.axis_index("tp")
    extent = out_ref.shape[1] if columns else out_ref.shape[0]

    def block(index):
        at = pl.ds(pl.multiple_of(index * extent, extent), extent)
        values = in_ref[:, at] if columns else in_ref[at, :]
        return values.astype(f32)

    if not stages:
        line_barrier(size)

    def copying(way, step, to):
        return pltpu.make_async_remote_copy(
            src_ref=staged_ref.at[way, step],
            dst_ref=landed_ref.at[way, step],
            send_sem=send_sem.at[way, step],
            recv_sem=recv_sem.at[way, step],
            device_id={"tp": to},
            device_id_type=MESH,
        )

    for step in range(size - 1):
        for way in (0, 1):
            rank = place if way == 0 else size - 1 - place
            target = size - 1 - step + place if way == 0 else place - (size - 1 - step)
            to = place + 1 if way == 0 else place - 1
            active = jnp.logical_and(rank <= step, rank < size - 1)

            @pl.when(active)
            def _():
                values = block(target)
                if step == 0:
                    staged_ref[way, step] = values.astype(bf16)
                else:

                    @pl.when(rank == 0)
                    def _():
                        staged_ref[way, step] = values.astype(bf16)

                    @pl.when(rank > 0)
                    def _():
                        landed = landed_ref[way, step - 1].astype(f32)
                        staged_ref[way, step] = (values + landed).astype(bf16)

                copying(way, step, to).start()

        if step < len(stages):
            stages[step]()

        for way in (0, 1):
            rank = place if way == 0 else size - 1 - place
            origin = place - 1 if way == 0 else place + 1

            @pl.when(jnp.logical_and(rank > 0, rank - 1 <= step))
            def _():
                copying(way, step, origin).wait_recv()

    for stage in stages[size - 1 :]:
        stage()
    out_ref[...] = block(place)
    for way in (0, 1):
        rank = place if way == 0 else size - 1 - place

        @pl.when(rank > 0)
        def _():
            out_ref[...] += landed_ref[way, size - 2].astype(f32)

    for step in range(size - 1):
        for way in (0, 1):
            rank = place if way == 0 else size - 1 - place
            to = place + 1 if way == 0 else place - 1

            @pl.when(jnp.logical_and(rank <= step, rank < size - 1))
            def _():
                copying(way, step, to).wait_send()


def closing_sums(
    sizes,
    narrow,
    in_ref,
    small_ref,
    out_ref,
    every_ref,
    line_ref,
    staged_ref,
    landed_ref,
    total_ref,
    small_tp_ref,
    small_ctx_ref,
    small_fsdp_ref,
    send_sem,
    recv_sem,
    small_send_sem,
    small_recv_sem,
):
    axes = ("tp", "ctx", "fsdp")
    barrier = pltpu.get_barrier_semaphore()
    for axis, size in zip(axes, sizes):
        place = lax.axis_index(axis)
        for offset in range(1, size):
            peer = lax.rem(place + offset, size)
            pl.semaphore_signal(barrier, inc=1, device_id={axis: peer}, device_id_type=MESH)
    pl.semaphore_wait(barrier, sum(sizes) - len(sizes))
    landings = (small_tp_ref, small_ctx_ref, small_fsdp_ref)

    def copying(axis, offset, peer):
        return pltpu.make_async_remote_copy(
            src_ref=small_ref if axis == 0 else total_ref.at[axis - 1],
            dst_ref=landings[axis].at[offset - 1],
            send_sem=small_send_sem.at[axis, offset - 1],
            recv_sem=small_recv_sem.at[axis, offset - 1],
            device_id={axes[axis]: peer},
            device_id_type=MESH,
        )

    def each(axis):
        size, place = sizes[axis], lax.axis_index(axes[axis])
        for offset in range(1, size):
            yield (
                offset,
                lax.rem(place + offset, size),
                lax.rem(place + size - offset, size),
            )

    def start(axis):
        for offset, to, origin in each(axis):
            copying(axis, offset, to).start()

    def finish(axis):
        total = small_ref[...] if axis == 0 else total_ref[axis - 1]
        for offset, to, origin in each(axis):
            copying(axis, offset, origin).wait_recv()
            total = total + landings[axis][offset - 1]
        for offset, to, origin in each(axis):
            copying(axis, offset, to).wait_send()
        return total

    def first():
        start(0)

    def second():
        total = finish(0)
        total_ref[0] = total
        line_ref[...] = total[:, narrow:]
        start(1)

    def third():
        total_ref[1] = finish(1)
        start(2)

    def last():
        every_ref[...] = finish(2)[:, :narrow]

    line_scatter(
        sizes[0],
        True,
        in_ref,
        out_ref,
        staged_ref,
        landed_ref,
        send_sem,
        recv_sem,
        stages=(first, second, third, last),
    )


def peer_barrier(axis, size):
    place = lax.axis_index(axis)
    barrier = pltpu.get_barrier_semaphore()
    for offset in range(1, size):
        peer = lax.rem(place + offset, size)
        pl.semaphore_signal(barrier, inc=1, device_id={axis: peer}, device_id_type=MESH)
    pl.semaphore_wait(barrier, size - 1)


def peer_gather(size, in_ref, out_ref, own_sem, send_sem, recv_sem):
    place = lax.axis_index("ctx")
    rows = in_ref.shape[0]

    def block(index):
        return out_ref.at[pl.ds(pl.multiple_of(index * rows, rows), rows), :]

    def copying(offset, source, peer):
        return pltpu.make_async_remote_copy(
            src_ref=in_ref,
            dst_ref=block(source),
            send_sem=send_sem.at[offset - 1],
            recv_sem=recv_sem.at[offset - 1],
            device_id={"ctx": peer},
            device_id_type=MESH,
        )

    peer_barrier("ctx", size)
    own = pltpu.make_async_copy(in_ref, block(place), own_sem)
    own.start()
    for offset in range(1, size):
        copying(offset, place, lax.rem(place + offset, size)).start()
    for offset in range(1, size):
        origin = lax.rem(place + size - offset, size)
        copying(offset, origin, origin).wait_recv()
    for offset in range(1, size):
        copying(offset, place, lax.rem(place + offset, size)).wait_send()
    own.wait()


def peer_scatter(size, in_ref, out_ref, landed_ref, send_sem, recv_sem):
    place = lax.axis_index("ctx")
    rows = out_ref.shape[0]

    def at(index):
        return pl.ds(pl.multiple_of(index * rows, rows), rows)

    def copying(offset, peer):
        return pltpu.make_async_remote_copy(
            src_ref=in_ref.at[at(peer), :],
            dst_ref=landed_ref.at[offset - 1],
            send_sem=send_sem.at[offset - 1],
            recv_sem=recv_sem.at[offset - 1],
            device_id={"ctx": peer},
            device_id_type=MESH,
        )

    peer_barrier("ctx", size)
    for offset in range(1, size):
        copying(offset, lax.rem(place + offset, size)).start()
    total = in_ref[at(place), :].astype(f32)
    for offset in range(1, size):
        origin = lax.rem(place + size - offset, size)
        copying(offset, origin).wait_recv()
        total = total + landed_ref[offset - 1].astype(f32)
    out_ref[...] = total.astype(bf16)
    for offset in range(1, size):
        copying(offset, lax.rem(place + offset, size)).wait_send()


def remote_params(number):
    return pltpu.CompilerParams(
        collective_id=number, has_side_effects=True, vmem_limit_bytes=VMEM_BYTES
    )


def gather_tp(values, columns, number):
    size = lax.axis_size("tp")
    rows, width = values.shape
    shape = (rows, size * width) if columns else (size * rows, width)
    return pl.pallas_call(
        functools.partial(line_gather, size, columns),
        in_specs=[pl.BlockSpec(memory_space=pl.ANY)],
        out_specs=pl.BlockSpec(memory_space=pl.ANY),
        out_shape=jax.ShapeDtypeStruct(shape, values.dtype),
        scratch_shapes=[
            pltpu.SemaphoreType.DMA,
            pltpu.SemaphoreType.DMA((2, size - 1)),
            pltpu.SemaphoreType.DMA((2, size - 1)),
        ],
        compiler_params=remote_params(number),
        cost_estimate=pl.CostEstimate(flops=0, bytes_accessed=150_000_000, transcendentals=0),
        name="gather_tp",
    )(values)


def scatter_tp(values, columns, number):
    size = lax.axis_size("tp")
    rows, width = values.shape
    shape = (rows, width // size) if columns else (rows // size, width)
    return pl.pallas_call(
        functools.partial(line_scatter, size, columns),
        in_specs=[pl.BlockSpec(memory_space=pltpu.VMEM)],
        out_specs=pl.BlockSpec(memory_space=pltpu.VMEM),
        out_shape=jax.ShapeDtypeStruct(shape, f32),
        scratch_shapes=[
            pltpu.VMEM((2, size - 1, *shape), bf16),
            pltpu.VMEM((2, size - 1, *shape), bf16),
            pltpu.SemaphoreType.DMA((2, size - 1)),
            pltpu.SemaphoreType.DMA((2, size - 1)),
        ],
        compiler_params=remote_params(number),
        cost_estimate=pl.CostEstimate(flops=0, bytes_accessed=150_000_000, transcendentals=0),
        name="scatter_tp",
    )(values)


def close_tp(values, gains, along, number):
    sizes = tuple(lax.axis_size(axis) for axis in ("tp", "ctx", "fsdp"))
    rows, width = values.shape
    shape = (rows, width // sizes[0])
    pad = lambda row: jnp.pad(row, (0, -row.shape[0] % 1024)).reshape(8, -1)
    gains_b, along_b = pad(gains), pad(along)
    narrow, wide = gains_b.shape[1], along_b.shape[1]
    small = jnp.concatenate([gains_b, along_b], axis=1)
    peers = max(sizes) - 1
    out, every, line = pl.pallas_call(
        functools.partial(closing_sums, sizes, narrow),
        in_specs=[pl.BlockSpec(memory_space=pltpu.VMEM)] * 2,
        out_specs=[pl.BlockSpec(memory_space=pltpu.VMEM)] * 3,
        out_shape=[
            jax.ShapeDtypeStruct(shape, f32),
            jax.ShapeDtypeStruct((8, narrow), f32),
            jax.ShapeDtypeStruct((8, wide), f32),
        ],
        scratch_shapes=[
            pltpu.VMEM((2, sizes[0] - 1, *shape), bf16),
            pltpu.VMEM((2, sizes[0] - 1, *shape), bf16),
            pltpu.VMEM((2, *small.shape), f32),
            *[pltpu.VMEM((size - 1, *small.shape), f32) for size in sizes],
            pltpu.SemaphoreType.DMA((2, sizes[0] - 1)),
            pltpu.SemaphoreType.DMA((2, sizes[0] - 1)),
            pltpu.SemaphoreType.DMA((3, peers)),
            pltpu.SemaphoreType.DMA((3, peers)),
        ],
        compiler_params=remote_params(number),
        cost_estimate=pl.CostEstimate(flops=0, bytes_accessed=150_000_000, transcendentals=0),
        name="close_tp",
    )(values, small)
    return out, every.reshape(-1)[: gains.shape[0]], line.reshape(-1)[: along.shape[0]]


def gather_ctx(values, number):
    size = lax.axis_size("ctx")
    rows, width = values.shape
    return pl.pallas_call(
        functools.partial(peer_gather, size),
        in_specs=[pl.BlockSpec(memory_space=pl.ANY)],
        out_specs=pl.BlockSpec(memory_space=pl.ANY),
        out_shape=jax.ShapeDtypeStruct((size * rows, width), values.dtype),
        scratch_shapes=[
            pltpu.SemaphoreType.DMA,
            pltpu.SemaphoreType.DMA((size - 1,)),
            pltpu.SemaphoreType.DMA((size - 1,)),
        ],
        compiler_params=remote_params(number),
        cost_estimate=pl.CostEstimate(flops=0, bytes_accessed=100_000_000, transcendentals=0),
        name="gather_ctx",
    )(values)


def scatter_ctx(values, number):
    size = lax.axis_size("ctx")
    rows, width = values.shape
    shape = (rows // size, width)
    return pl.pallas_call(
        functools.partial(peer_scatter, size),
        in_specs=[pl.BlockSpec(memory_space=pltpu.VMEM)],
        out_specs=pl.BlockSpec(memory_space=pltpu.VMEM),
        out_shape=jax.ShapeDtypeStruct(shape, values.dtype),
        scratch_shapes=[
            pltpu.VMEM((size - 1, *shape), bf16),
            pltpu.SemaphoreType.DMA((size - 1,)),
            pltpu.SemaphoreType.DMA((size - 1,)),
        ],
        compiler_params=remote_params(number),
        cost_estimate=pl.CostEstimate(flops=0, bytes_accessed=100_000_000, transcendentals=0),
        name="scatter_ctx",
    )(values)


def attend(scale, query_ref, key_ref, value_ref, seg_row_ref, seg_column_ref, out_ref, total_ref):
    scores = matmul_nt(key_ref[...], query_ref[...]) * scale
    scores = jnp.where(seg_column_ref[...] == seg_row_ref[...], scores, masked_score)
    most = jnp.max(scores, axis=0, keepdims=True)
    probs = jnp.exp(scores - most)
    total = jnp.sum(probs, axis=0, keepdims=True)
    mixed = matmul(value_ref[...].T, probs.astype(bf16)) / total
    out_ref[...] = mixed.T.astype(bf16)
    total_ref[...] = most + jnp.log(total)


def attend_back(
    scale,
    query_ref,
    key_ref,
    value_ref,
    seg_row_ref,
    seg_column_ref,
    out_ref,
    total_ref,
    grad_ref,
    query_grad_ref,
    key_grad_ref,
    value_grad_ref,
    key_sum_ref,
    value_sum_ref,
):
    step = pl.program_id(1)
    query, key, grad = query_ref[...], key_ref[...], grad_ref[...]
    scores = matmul_nt(key, query) * scale
    scores = jnp.where(seg_column_ref[...] == seg_row_ref[...], scores, masked_score)
    probs = jnp.exp(scores - total_ref[...])
    products = grad.astype(f32) * out_ref[...].astype(f32)
    delta = jnp.sum(products.T, axis=0, keepdims=True)
    score_grad = (probs * (matmul_nt(value_ref[...], grad) - delta)).astype(bf16)
    query_grad_ref[...] = (matmul(key.T, score_grad) * scale).T
    key_part = matmul(score_grad, query) * scale
    value_part = matmul(probs.astype(bf16), grad)

    @pl.when(step == 0)
    def _():
        key_sum_ref[...] = key_part
        value_sum_ref[...] = value_part

    @pl.when(step > 0)
    def _():
        key_sum_ref[...] += key_part
        value_sum_ref[...] += value_part

    @pl.when(step == pl.num_programs(1) - 1)
    def _():
        key_grad_ref[...] = key_sum_ref[...].astype(bf16)
        value_grad_ref[...] = value_sum_ref[...].astype(bf16)


def attention_specs(rows, keys, heads, head_dim):
    block = min(rows, QUERY_BLOCK)
    query = pl.BlockSpec((block, head_dim), lambda h, i: (i, h))
    return (
        (heads, rows // block),
        [
            query,
            pl.BlockSpec((keys, head_dim), lambda h, i: (0, h)),
            pl.BlockSpec((keys, head_dim), lambda h, i: (0, h + heads)),
            pl.BlockSpec((None, 1, block), lambda h, i: (i, 0, 0)),
            pl.BlockSpec((keys, 1), lambda h, i: (0, 0)),
        ],
        query,
        pl.BlockSpec((None, None, 1, block), lambda h, i: (h, i, 0, 0)),
        pl.BlockSpec((keys, head_dim), lambda h, i: (0, h)),
    )


def run_attend(query_b, group, seg_rows, seg_columns, heads, scale):
    rows, keys = query_b.shape[0], group.shape[0]
    head_dim = query_b.shape[1] // heads
    grid, specs, query, total, unused = attention_specs(rows, keys, heads, head_dim)
    work = heads * rows * keys
    return pl.pallas_call(
        functools.partial(attend, scale),
        grid=grid,
        in_specs=specs,
        out_specs=[query, total],
        out_shape=[
            jax.ShapeDtypeStruct(query_b.shape, bf16),
            jax.ShapeDtypeStruct((*grid, 1, rows // grid[1]), f32),
        ],
        compiler_params=params(2),
        cost_estimate=pl.CostEstimate(
            flops=4 * work * head_dim, bytes_accessed=8 * query_b.size, transcendentals=work
        ),
        name="attend",
    )(query_b, group, group, seg_rows, seg_columns)


def run_attend_back(query_b, group, seg_rows, seg_columns, out_b, total, grad_b, heads, scale):
    rows, keys = query_b.shape[0], group.shape[0]
    head_dim = query_b.shape[1] // heads
    grid, specs, query, total_spec, key = attention_specs(rows, keys, heads, head_dim)
    work = heads * rows * keys
    return pl.pallas_call(
        functools.partial(attend_back, scale),
        grid=grid,
        in_specs=[*specs, query, total_spec, query],
        out_specs=[query, key, key],
        out_shape=[
            jax.ShapeDtypeStruct(query_b.shape, f32),
            jax.ShapeDtypeStruct((keys, query_b.shape[1]), bf16),
            jax.ShapeDtypeStruct((keys, query_b.shape[1]), bf16),
        ],
        scratch_shapes=[pltpu.VMEM((keys, head_dim), f32)] * 2,
        compiler_params=params(2),
        cost_estimate=pl.CostEstimate(
            flops=10 * work * head_dim, bytes_accessed=16 * query_b.size, transcendentals=work
        ),
        name="attend_back",
    )(query_b, group, group, seg_rows, seg_columns, out_b, total, grad_b)


def beside(values):
    return lax.ppermute(values, "fsdp", [(0, 1), (1, 0), (2, 3), (3, 2)])


def across(values):
    return lax.ppermute(values, "fsdp", [(0, 2), (1, 3), (2, 0), (3, 1)])


def other(values):
    return lax.ppermute(values, "ctx", [(0, 1), (1, 0)])


def added(*values):
    total = values[0].astype(f32)
    for value in values[1:]:
        total = total + value.astype(f32)
    return total.astype(bf16)


def then(first, *values):
    return lax.optimization_barrier((first, *values))[1:]


def weight_grad(left, right):
    return jnp.einsum("gesa,gesb->eab", left, right, preferred_element_type=f32)


def by_chips():
    return lax.axis_size("fsdp") == 4 and lax.axis_size("ctx") == 2


def chunk_order(chunks):
    if not by_chips():
        return jnp.arange(chunks, dtype=jnp.int32)
    fsdp, ctx = lax.axis_index("fsdp"), lax.axis_index("ctx")
    sibling = fsdp + 1 - 2 * lax.rem(fsdp, 2)
    flip = lambda core: lax.rem(core + 2, 4)
    places = (
        (flip(sibling), ctx),
        (flip(fsdp), ctx),
        (sibling, 1 - ctx),
        (fsdp, 1 - ctx),
        (flip(sibling), 1 - ctx),
        (flip(fsdp), 1 - ctx),
        (sibling, ctx),
        (fsdp, ctx),
    )
    return jnp.stack([jnp.asarray(2 * f + c, jnp.int32) for f, c in places])


def expert_steps(ids, own_tokens, grad_all, rank_rows, rank_columns, first, weights):
    gate_weight, up_weight, down_weight = weights
    chunks = rank_rows.shape[0]

    def one_pass(at, near, far, product, kept):
        return run_expert_pass(
            jnp.array([at, at + 1], jnp.int32),
            first,
            rank_rows,
            rank_columns,
            near,
            far,
            product,
            gate_weight,
            up_weight,
            kept,
        )

    if not by_chips():
        token_all = lax.all_gather(own_tokens, ROWS, axis=0, tiled=True)
        blocks = token_all.reshape(chunks, CHUNK, -1)
        grad_slots, product = run_select_grads(ids, rank_rows, grad_all, down_weight)
        kept, backs = (), []
        for at in range(0, chunks, 2):
            kept, near, far = one_pass(at, blocks[at], blocks[at + 1], product, kept)
            backs += [near, far]
        back_sum = lax.psum_scatter(
            jnp.concatenate(backs), ROWS, scatter_dimension=0, tiled=True
        )
        out_part = run_expert_sums(ids, rank_columns, kept[1], down_weight)
        return kept, grad_slots, back_sum, out_part

    from_across, from_other = across(own_tokens), other(own_tokens)
    from_beside = beside(own_tokens)
    grad_slots, product = run_select_grads(ids, rank_rows, grad_all, down_weight)
    from_across, from_other = then(product, from_across, from_other)
    kept, back_sum, out_part = run_exchange_pass(
        rank_rows,
        rank_columns,
        product,
        weights,
        (own_tokens, from_beside, from_across, from_other),
    )
    return kept, grad_slots, back_sum, out_part


def rotated_sum(values):
    size = lax.axis_size("tp")
    total = values
    for offset in range(1, size):
        pairs = [(at, (at + offset) % size) for at in range(size)]
        total = total + lax.ppermute(values, "tp", pairs)
    return total


def scatter_line(values, beside_steps):
    size, place = lax.axis_size("tp"), lax.axis_index("tp")
    rows = values.shape[0] // size
    block = lambda at: lax.dynamic_slice_in_dim(
        values, jnp.clip(at, 0, size - 1) * rows, rows, 0
    )
    right, left, made = None, None, []
    for step in range(size - 1):
        to_right = block(size - 1 - step + place)
        to_left = block(place - (size - 1 - step))
        if step > 0:
            to_right, to_left = added(to_right, right), added(to_left, left)
        right = lax.ppermute(
            to_right, "tp", [(at, at + 1) for at in range(size - 1) if at <= step]
        )
        left = lax.ppermute(
            to_left, "tp", [(at, at - 1) for at in range(1, size) if size - 1 - at <= step]
        )
        if step < len(beside_steps):
            made.append(beside_steps[step](made))
            right, left = then(made[-1], right, left)
    total = block(place).astype(f32) + right.astype(f32) + left.astype(f32)
    return total, made


def head_blocks(width, head_dim):
    for at in range(0, width, head_dim):
        yield slice(at, at + head_dim)


def project(
    input_ref,
    gain_ref,
    weight_ref,
    cosine_ref,
    sine_ref,
    head_gain_ref,
    normed_ref,
    inverse_ref,
    pre_ref,
    query_ref,
    group_ref,
):
    values = input_ref[...].astype(f32)
    inverse = norm_scale(values)
    normed = (values * inverse * gain_ref[...]).astype(bf16)
    normed_ref[...] = normed
    inverse_ref[...] = inverse
    qkv = matmul(normed, weight_ref[...])
    width = query_ref.shape[1]
    head_dim = cosine_ref.shape[1]
    pre_ref[...] = qkv[:, : 2 * width]
    cosine, sine = cosine_ref[...], sine_ref[...]
    for which in (0, 1):
        gain = head_gain_ref[which : which + 1, :]
        for at in head_blocks(width, head_dim):
            head = qkv[:, which * width + at.start : which * width + at.stop]
            head = head * norm_scale(head) * gain
            turned = head * cosine + pltpu.roll(head, head_dim // 2, 1) * sine
            to_ref = query_ref if which == 0 else group_ref
            to_ref[:, at] = turned.astype(bf16)
    group_ref[:, width : 2 * width] = qkv[:, 2 * width :].astype(bf16)


def project_back(
    query_grad_ref,
    group_grad_ref,
    pre_ref,
    cosine_ref,
    sine_ref,
    head_gain_ref,
    weight_ref,
    input_ref,
    inverse_ref,
    gain_ref,
    grad_ref,
    part_ref,
    along_ref,
    terms_ref,
    head_terms_ref,
):
    width = query_grad_ref.shape[1]
    head_dim = cosine_ref.shape[1]
    cosine, sine = cosine_ref[...], sine_ref[...]

    @pl.when(pl.program_id(0) == 0)
    def _():
        terms_ref[...] = jnp.zeros_like(terms_ref)
        head_terms_ref[...] = jnp.zeros_like(head_terms_ref)

    for which in (0, 1):
        gain = head_gain_ref[which : which + 1, :]
        from_ref = query_grad_ref if which == 0 else group_grad_ref
        for at in head_blocks(width, head_dim):
            own = slice(which * width + at.start, which * width + at.stop)
            grad = from_ref[:, at].astype(f32)
            incoming = grad * cosine - pltpu.roll(grad, head_dim // 2, 1) * sine
            head = pre_ref[:, own]
            value_grad, gain_terms = norm_back(incoming, head, norm_scale(head), gain)
            grad_ref[:, own] = value_grad.astype(bf16)
            head_terms_ref[which : which + 1, :] += jnp.sum(gain_terms, axis=0, keepdims=True)
    grad_ref[:, 2 * width :] = group_grad_ref[:, width:]
    part = matmul_nt(grad_ref[...], weight_ref[...])
    part_ref[...] = part.astype(bf16)
    product = part * input_ref[...].astype(f32)
    terms_ref[...] += jnp.sum(product * inverse_ref[...], axis=0, keepdims=True)
    along_ref[...] = jnp.sum(product * gain_ref[...], axis=1, keepdims=True)


def run_project(input_b, gain, full, cosine, sine, head_gains, width):
    rows, depth = input_b.shape
    head_dim = cosine.shape[1]
    block = min(rows, QUERY_BLOCK)
    by_rows = lambda columns: pl.BlockSpec((block, columns), lambda i: (i, 0))
    return pl.pallas_call(
        project,
        grid=(rows // block,),
        in_specs=[
            by_rows(depth),
            once((1, depth)),
            once((depth, 3 * width)),
            by_rows(head_dim),
            by_rows(head_dim),
            once((2, head_dim)),
        ],
        out_specs=[
            by_rows(depth),
            by_rows(1),
            by_rows(2 * width),
            by_rows(width),
            by_rows(2 * width),
        ],
        out_shape=[
            jax.ShapeDtypeStruct((rows, depth), bf16),
            jax.ShapeDtypeStruct((rows, 1), f32),
            jax.ShapeDtypeStruct((rows, 2 * width), f32),
            jax.ShapeDtypeStruct((rows, width), bf16),
            jax.ShapeDtypeStruct((rows, 2 * width), bf16),
        ],
        compiler_params=params(1),
        cost_estimate=pl.CostEstimate(
            flops=6 * rows * depth * width, bytes_accessed=6 * depth * width, transcendentals=0
        ),
        name="project",
    )(input_b, gain, full, cosine, sine, head_gains)


def run_project_back(
    query_grad, group_grad, pre, cosine, sine, head_gains, full, input_b, inverse, gain
):
    rows, depth = input_b.shape
    width = query_grad.shape[1]
    head_dim = cosine.shape[1]
    block = min(rows, QUERY_BLOCK)
    by_rows = lambda columns: pl.BlockSpec((block, columns), lambda i: (i, 0))
    whole = lambda shape: pl.BlockSpec(shape, lambda i: (0, 0))
    return pl.pallas_call(
        project_back,
        grid=(rows // block,),
        in_specs=[
            by_rows(width),
            by_rows(2 * width),
            by_rows(2 * width),
            by_rows(head_dim),
            by_rows(head_dim),
            once((2, head_dim)),
            once((depth, 3 * width)),
            by_rows(depth),
            by_rows(1),
            once((1, depth)),
        ],
        out_specs=[
            by_rows(3 * width),
            by_rows(depth),
            by_rows(1),
            whole((1, depth)),
            whole((2, head_dim)),
        ],
        out_shape=[
            jax.ShapeDtypeStruct((rows, 3 * width), bf16),
            jax.ShapeDtypeStruct((rows, depth), bf16),
            jax.ShapeDtypeStruct((rows, 1), f32),
            jax.ShapeDtypeStruct((1, depth), f32),
            jax.ShapeDtypeStruct((2, head_dim), f32),
        ],
        compiler_params=params(1),
        cost_estimate=pl.CostEstimate(
            flops=6 * rows * depth * width, bytes_accessed=8 * depth * width, transcendentals=0
        ),
        name="project_back",
    )(query_grad, group_grad, pre, cosine, sine, head_gains, full, input_b, inverse, gain)


def split_three(values):
    high = values.astype(bf16)
    rest = values - high.astype(f32)
    middle = rest.astype(bf16)
    return (high, middle, (rest - middle.astype(f32)).astype(bf16))


def on_device(
    layer_input,
    token_order,
    doc_lengths,
    expert_routes,
    attn_gain,
    query_weight,
    key_weight,
    value_weight,
    query_gain,
    key_gain,
    out_weight,
    moe_gain,
    router_weight,
    gate_weight,
    up_weight,
    down_weight,
    out_grad,
):
    tp_index = lax.axis_index("tp")
    ctx_size = lax.axis_size("ctx")
    fc_size = lax.axis_size("fsdp") * ctx_size
    fc_index = lax.axis_index("fsdp") * ctx_size + lax.axis_index("ctx")
    tok_count, quarter = layer_input.shape
    share = tok_count // lax.axis_size("tp")
    head_dim = query_gain.shape[0]
    head_width = query_weight.shape[1]
    heads = head_width // head_dim
    scale = head_dim ** (-0.5)
    experts = router_weight.shape[1]
    top = expert_routes.shape[1]
    local_experts = gate_weight.shape[0]
    capacity = tok_count * top * 5 // (4 * experts)
    own_rows = lambda values: lax.dynamic_slice_in_dim(values, tp_index * share, share, 0)
    own_width = lambda values: lax.dynamic_slice_in_dim(values, tp_index * quarter, quarter, 1)

    packed = jnp.concatenate(
        [
            query_weight,
            key_weight,
            value_weight,
            out_weight.T,
            router_weight,
            attn_gain[:, None],
            moe_gain[:, None],
            jnp.zeros((attn_gain.shape[0], EXTRA - experts - 2), bf16),
        ],
        axis=1,
    )
    full = lax.all_gather(packed, ROWS, axis=0, tiled=True)
    expert_ids = jnp.arange(experts, dtype=jnp.int32)
    named = jnp.any(expert_routes[:, :, None] == expert_ids[None, None, :], axis=1)
    earlier = jnp.tri(tok_count, tok_count, -1, dtype=bf16)
    before = matmul(earlier, named.astype(bf16))
    first_slot = (lax.rem(fc_index, CHUNK // tok_count) * capacity).astype(f32)
    ranks = jnp.where(named, before + first_slot, -1.0).astype(bf16)
    input_b = gather_tp(layer_input, True, 0)
    segment, position = doc_places(token_order[0], doc_lengths[0])
    ctx_index = lax.axis_index("ctx")
    seg_columns = jnp.zeros((ctx_size, tok_count), f32)
    for offset in range(ctx_size):
        piece = segment.astype(f32)[None, :]
        if offset > 0:
            pairs = [(at, (at + offset) % ctx_size) for at in range(ctx_size)]
            piece = lax.ppermute(piece, "ctx", pairs)
        origin = lax.rem(ctx_index + ctx_size - offset, ctx_size)
        seg_columns = lax.dynamic_update_slice_in_dim(seg_columns, piece, origin, 0)
    out_grad, full, input_b, seg_columns = lax.optimization_barrier(
        (out_grad, full, input_b, seg_columns)
    )
    grad_rows_b = lax.all_gather(out_grad, "tp", axis=1, tiled=True)
    side = 3 * head_width
    qkv_weight = full[:, :side]
    full_out = full[:, side : side + head_width]
    side = side + head_width
    full_router = full[:, side : side + experts]
    attn_gain_f = full[:, side + experts].astype(f32)
    moe_gain_f = full[:, side + experts + 1].astype(f32)
    width = input_b.shape[1]
    cosine, sine = rope_tables(position, head_dim)
    head_gains = jnp.stack([query_gain, key_gain])
    attn_gain_row = attn_gain_f[None, :]
    normed, inverse_one, heads_pre, query_rows, group_part = run_project(
        input_b,
        attn_gain_row,
        full,
        cosine,
        sine,
        head_gains,
        head_width,
    )
    group = gather_ctx(group_part, 1)
    after_group, group = lax.optimization_barrier((grad_rows_b, group))
    grad_packed = jnp.concatenate(
        [after_group, ranks, jnp.zeros((tok_count, EXTRA - experts), bf16)], axis=1
    )
    grad_all = lax.all_gather(grad_packed, ROWS, axis=0, tiled=True)
    chunks = grad_all.shape[0] // CHUNK
    first_expert = fc_index * local_experts
    local_ranks = lax.dynamic_slice_in_dim(
        grad_all[:, width:], first_expert, local_experts, 1
    ).astype(jnp.int32)
    ids = chunk_order(chunks)
    rank_columns = jnp.stack(
        [
            lax.dynamic_slice_in_dim(local_ranks, ids[at] * CHUNK, CHUNK, 0)
            for at in range(chunks)
        ]
    )
    rank_rows = jnp.transpose(rank_columns, (0, 2, 1))[:, :, None, :]

    seg_rows = segment.astype(f32).reshape(-1, 1, min(tok_count, QUERY_BLOCK))
    seg_columns = seg_columns.reshape(-1, 1)
    attn_b, log_total = run_attend(query_rows, group, seg_rows, seg_columns, heads, scale)
    attn_part = matmul_nt(attn_b, full_out).astype(bf16)
    attn_out = scatter_tp(attn_part, False, 2)
    resid = own_rows(input_b).astype(f32) + attn_out
    inverse_two = norm_scale(resid)
    moe_in = (resid * inverse_two * moe_gain_f).astype(bf16)
    logits = matmul(moe_in, full_router)
    own_named = own_rows(named)
    chosen = jnp.where(own_named, logits, -jnp.inf)
    gates = jax.nn.softmax(chosen, axis=-1)
    own_tokens = gather_tp(
        jnp.concatenate(
            [moe_in, *split_three(gates), jnp.zeros((share, EXTRA - 3 * experts), bf16)], axis=1
        ),
        False,
        3,
    )
    kept, grad_slots, back_sum, out_part = expert_steps(
        ids,
        own_tokens,
        grad_all,
        rank_rows,
        rank_columns,
        first_expert.reshape(1),
        (gate_weight, up_weight, down_weight),
    )
    token_slots, hidden_rows, gate_act_grad, up_act_grad, route_part = kept
    hit = jnp.arange(chunks, dtype=jnp.int32)[:, None] == ids[None, :]
    route_all = jnp.sum(
        jnp.where(hit[:, :, None, None], route_part[None, :, :, 0, :], 0.0), axis=1
    )
    route_all = jnp.transpose(route_all, (1, 0, 2)).reshape(
        local_experts, fc_size, tok_count
    )
    route_all = lax.all_to_all(
        jnp.transpose(route_all, (1, 0, 2)), ROWS, split_axis=0, concat_axis=0, tiled=True
    ).reshape(experts, tok_count)

    back_rows, ((grad_gate, route_all), (grad_up, gate_grad), grad_down) = scatter_line(
        back_sum,
        (
            lambda made: (weight_grad(token_slots, gate_act_grad), route_all),
            lambda made: (weight_grad(token_slots, up_act_grad), rotated_sum(made[0][1])),
            lambda made: weight_grad(hidden_rows, grad_slots),
        ),
    )
    parts = own_tokens[:, width : width + 3 * experts].astype(f32)
    all_gates = parts[:, :experts] + parts[:, experts : 2 * experts] + parts[:, 2 * experts :]
    gate_grad = gate_grad.T
    logit_grad = all_gates * (
        gate_grad - jnp.sum(all_gates * gate_grad, axis=-1, keepdims=True)
    )
    grad_router = lax.dot_general(
        own_tokens[:, :width].astype(f32),
        logit_grad,
        (((0,), (0,)), ((), ())),
        precision=highest,
    )
    own_logit_grad = own_rows(logit_grad)
    router_back = lax.dot_general(
        own_logit_grad, full_router.astype(f32), (((1,), (1,)), ((), ())), precision=highest
    )
    moe_in_grad = (
        back_rows + router_back
    )
    resid_norm_grad, gain_terms = norm_back(moe_in_grad, resid, inverse_two, moe_gain_f)
    grad_moe_gain = jnp.sum(gain_terms, axis=0)
    resid_grad = own_rows(grad_rows_b).astype(f32) + resid_norm_grad
    resid_grad_b = gather_tp(resid_grad.astype(bf16), False, 5)

    out_sum = lax.psum_scatter(out_part, ROWS, scatter_dimension=0, tiled=True)

    grad_out = lax.dot_general(
        resid_grad_b, attn_b, (((0,), (0,)), ((), ())), preferred_element_type=f32
    )
    attn_grad = matmul(resid_grad_b, full_out).astype(bf16)
    query_rot_grad, key_part, value_part = run_attend_back(
        query_rows, group, seg_rows, seg_columns, attn_b, log_total, attn_grad, heads, scale
    )
    out_sum, key_part = lax.optimization_barrier((out_sum, key_part))
    out_sum = lax.psum_scatter(out_sum, "tp", scatter_dimension=0, tiled=True).astype(f32)
    group_grad = scatter_ctx(jnp.concatenate([key_part, value_part], axis=1), 6)
    qkv_grad, normed_part, along, attn_terms, head_terms = run_project_back(
        query_rot_grad,
        group_grad,
        heads_pre,
        cosine,
        sine,
        head_gains,
        full,
        input_b,
        inverse_one,
        attn_gain_row,
    )
    along = along[:, 0]
    gains = jnp.concatenate([attn_terms[0], grad_moe_gain, head_terms[0], head_terms[1]])
    normed_grad, gains, along = close_tp(normed_part, gains, along, 7)
    along = along[:, None] / width
    normed_grad, out_sum = lax.optimization_barrier((normed_grad, out_sum))
    layer_sum = resid + out_sum
    layer_output = lax.all_to_all(
        layer_sum.astype(bf16), "tp", split_axis=1, concat_axis=0, tiled=True
    )
    input_quarter = layer_input.astype(f32)
    gain_quarter = lax.dynamic_slice_in_dim(attn_gain_f, tp_index * quarter, quarter, 0)
    grad_input = own_width(resid_grad_b).astype(f32) + inverse_one * (
        normed_grad * gain_quarter - input_quarter * inverse_one * inverse_one * along
    )
    grad_qkv = lax.dot_general(
        normed, qkv_grad, (((0,), (0,)), ((), ())), preferred_element_type=f32
    )
    owned_out = lax.psum_scatter(
        jnp.concatenate(
            [grad_out, grad_router, jnp.zeros((width, EXTRA - experts), f32)], axis=1
        ).astype(bf16),
        ROWS,
        scatter_dimension=0,
        tiled=True,
    )
    (owned_out,) = then(normed_grad, owned_out)
    owned_out = owned_out.astype(f32)
    owned_qkv = lax.psum_scatter(
        grad_qkv.astype(bf16), ROWS, scatter_dimension=0, tiled=True
    ).astype(f32)
    owned_gain = attn_gain.shape[0]
    own_gain = lambda at: lax.dynamic_slice_in_dim(
        gains, at * width + fc_index * owned_gain, owned_gain, 0
    )
    return (
        layer_output,
        grad_input,
        own_gain(0),
        owned_qkv[:, :head_width],
        owned_qkv[:, head_width : 2 * head_width],
        owned_qkv[:, 2 * head_width :],
        gains[2 * width : 2 * width + head_dim],
        gains[2 * width + head_dim :],
        owned_out[:, :head_width].T,
        own_gain(1),
        owned_out[:, head_width : head_width + experts],
        grad_gate,
        grad_up,
        grad_down,
    )


def solution(mesh):
    in_specs = (
        P(("fsdp", "ctx"), "tp"),
        P("fsdp", "ctx"),
        P("fsdp", None),
        P(("fsdp", "ctx"), None),
        P(("fsdp", "ctx")),
        P(("fsdp", "ctx"), "tp"),
        P(("fsdp", "ctx"), "tp"),
        P(("fsdp", "ctx"), "tp"),
        P(),
        P(),
        P("tp", ("fsdp", "ctx")),
        P(("fsdp", "ctx")),
        P(("fsdp", "ctx"), None),
        P(("fsdp", "ctx"), None, "tp"),
        P(("fsdp", "ctx"), None, "tp"),
        P(("fsdp", "ctx"), "tp", None),
        P(("fsdp", "ctx"), "tp"),
    )
    out_specs = (
        P(("fsdp", "ctx"), "tp"),
        P(("fsdp", "ctx"), "tp"),
        P(("fsdp", "ctx")),
        P(("fsdp", "ctx"), "tp"),
        P(("fsdp", "ctx"), "tp"),
        P(("fsdp", "ctx"), "tp"),
        P(),
        P(),
        P("tp", ("fsdp", "ctx")),
        P(("fsdp", "ctx")),
        P(("fsdp", "ctx"), None),
        P(("fsdp", "ctx"), None, "tp"),
        P(("fsdp", "ctx"), None, "tp"),
        P(("fsdp", "ctx"), "tp", None),
    )
    return jax.shard_map(
        on_device, mesh=mesh, in_specs=in_specs, out_specs=out_specs, check_vma=False
    )
```

```python
import functools

import jax
import jax.numpy as jnp
from jax import lax
from jax.experimental import pallas as pl
from jax.experimental.pallas import tpu as pltpu
from jax.sharding import PartitionSpec as P

QUERY_BLOCK = 256
CHUNK = 768
SLOTS = 256
EXTRA = 128
VMEM_BYTES = 60 * 1024 * 1024


epsilon = 1e-05
rope_base = 50000.0
masked_score = -1e30
highest = lax.Precision.HIGHEST
bf16 = jnp.bfloat16
f32 = jnp.float32
ROWS = ("fsdp", "ctx")
ALL = ("fsdp", "ctx", "tp")
MESH = pl.DeviceIdType.MESH


def doc_places(order_row, length_row):
    ends = jnp.cumsum(length_row, dtype=jnp.int32)
    passed = (order_row[:, None] >= ends[None, :]).astype(jnp.int32)
    segment = jnp.sum(passed, axis=1, dtype=jnp.int32)
    start = jnp.sum(passed * length_row[None, :], axis=1, dtype=jnp.int32)
    return (segment, order_row - start)


def rope_tables(position, head_dim):
    half = head_dim // 2
    freqs = rope_base ** (-(jnp.arange(half, dtype=jnp.float32) * (2.0 / head_dim)))
    angles = position.astype(jnp.float32)[:, None] * freqs[None, :]
    cosine, sine = jnp.cos(angles), jnp.sin(angles)
    return jnp.concatenate([cosine, cosine], axis=1), jnp.concatenate([-sine, sine], axis=1)


def norm_scale(values):
    return lax.rsqrt(jnp.mean(values * values, axis=-1, keepdims=True) + epsilon)


def norm_back(incoming, values, inverse, gain):
    scaled = incoming * gain
    value_grad = inverse * (
        scaled - values * inverse * inverse * jnp.mean(scaled * values, axis=-1, keepdims=True)
    )
    return (value_grad, incoming * values * inverse)


def matmul(left, right):
    return jnp.dot(left, right, preferred_element_type=f32)


def matmul_nt(left, right):
    return lax.dot_general(left, right, (((1,), (1,)), ((), ())), preferred_element_type=f32)


def slot_rows(rank_row):
    slots = lax.broadcasted_iota(jnp.int32, (SLOTS, rank_row.shape[1]), 0)
    return slots == rank_row


def slot_columns(rank_column):
    slots = lax.broadcasted_iota(jnp.int32, (rank_column.shape[0], SLOTS), 1)
    return jnp.where(slots == rank_column, 1.0, 0.0).astype(bf16)


def as_one_hot(mask):
    return jnp.where(mask, 1.0, 0.0).astype(bf16)


def select_grads(ids_ref, rank_ref, grad_ref, down_ref, rows_ref, product_ref):
    expert = pl.program_id(1)
    rows = matmul(as_one_hot(slot_rows(rank_ref[...])), grad_ref[...]).astype(bf16)
    rows_ref[...] = rows
    product_ref[...] = matmul_nt(rows, down_ref[expert])


def expert_step(
    expert,
    named,
    rank_ref,
    tokens,
    product_ref,
    gate_ref,
    up_ref,
    await_weights,
    rows_ref,
    hidden_ref,
    gate_grad_ref,
    up_grad_ref,
    route_ref,
    held_ref,
):
    width = rows_ref.shape[1]
    mask = slot_rows(rank_ref[...])
    picked = matmul(as_one_hot(mask), tokens)
    rows = picked[:, :width].astype(bf16)
    rows_ref[...] = rows
    lane = lax.broadcasted_iota(jnp.int32, (SLOTS, EXTRA), 1)
    mine = jnp.logical_and(lax.rem(lane, 32) == named, lane < 96)
    gate = jnp.sum(jnp.where(mine, picked[:, width:], 0.0), axis=1, keepdims=True)
    await_weights()
    gate_act = matmul(rows, gate_ref[expert])
    up_act = matmul(rows, up_ref[expert])
    sigmoid_g = 1.0 / (1.0 + jnp.exp(-gate_act))
    silu_g = gate_act * sigmoid_g
    hidden = silu_g * up_act
    hidden_ref[...] = (gate * hidden).astype(bf16)
    product = product_ref[...]
    route = jnp.sum(hidden.astype(bf16).astype(f32) * product, axis=1, keepdims=True)
    route_ref[...] = jnp.sum(jnp.where(mask, route, 0.0), axis=0, keepdims=True)
    hidden_grad = gate * product
    gate_grad = (
        hidden_grad * up_act * sigmoid_g * (1.0 + gate_act * (1.0 - sigmoid_g))
    ).astype(bf16)
    up_grad = (hidden_grad * silu_g).astype(bf16)
    gate_grad_ref[...] = gate_grad
    up_grad_ref[...] = up_grad
    back = matmul_nt(gate_grad, gate_ref[expert]) + matmul_nt(up_grad, up_ref[expert])
    held_ref[pl.ds(pl.multiple_of(expert * SLOTS, SLOTS), SLOTS), :] = back.astype(bf16)


def chunk_places(column_ref):
    columns = column_ref[...]
    return jnp.concatenate(
        [slot_columns(columns[:, e : e + 1]) for e in range(columns.shape[1])], axis=1
    )


def expert_pass(
    ids_ref,
    first_ref,
    rank_ref,
    column_ref,
    near_ref,
    far_ref,
    product_ref,
    gate_in_ref,
    up_in_ref,
    *refs,
):
    (
        rows_ref,
        hidden_ref,
        gate_grad_ref,
        up_grad_ref,
        route_ref,
        near_back_ref,
        far_back_ref,
        token_ref,
        gate_ref,
        up_ref,
        held_ref,
        back_ref,
        token_sem,
        gate_sem,
        up_sem,
        back_sem,
    ) = refs[-16:]
    chunk, expert = pl.program_id(0), pl.program_id(1)
    local = gate_ref.shape[0]
    width = rows_ref.shape[1]
    tiles = back_sem.shape[1]
    tile = width // tiles
    loads = [
        pltpu.make_async_copy(source, token_ref.at[at], token_sem.at[at])
        for at, source in enumerate((near_ref, far_ref))
    ]

    def weight_load(source, held, sem, at):
        return pltpu.make_async_copy(source.at[at], held.at[at], sem.at[at])

    def back_store(to, at, step):
        columns = pl.ds(step * tile, tile)
        return pltpu.make_async_copy(
            back_ref.at[at, :, columns], to.at[:, columns], back_sem.at[at, step]
        )

    @pl.when(jnp.logical_and(chunk == 0, expert == 0))
    def _():
        loads[0].start()
        for at in range(local):
            weight_load(gate_in_ref, gate_ref, gate_sem, at).start()
            weight_load(up_in_ref, up_ref, up_sem, at).start()
        loads[1].start()
        loads[0].wait()

    @pl.when(jnp.logical_and(chunk == 1, expert == 0))
    def _():
        loads[1].wait()

    def await_weights():
        @pl.when(chunk == 0)
        def _():
            weight_load(gate_in_ref, gate_ref, gate_sem, expert).wait()
            weight_load(up_in_ref, up_ref, up_sem, expert).wait()

    expert_step(
        expert,
        first_ref[0] + expert,
        rank_ref,
        token_ref[chunk],
        product_ref,
        gate_ref,
        up_ref,
        await_weights,
        rows_ref,
        hidden_ref,
        gate_grad_ref,
        up_grad_ref,
        route_ref,
        held_ref,
    )

    @pl.when(expert == local - 1)
    def _():
        places = chunk_places(column_ref)
        for step in range(tiles):
            at = pl.ds(step * tile, tile)
            back_ref[chunk, :, at] = matmul(places, held_ref[:, at]).astype(bf16)

            @pl.when(chunk == 0)
            def _():
                back_store(near_back_ref, 0, step).start()

            @pl.when(chunk == 1)
            def _():
                back_store(far_back_ref, 1, step).start()

    @pl.when(jnp.logical_and(chunk == 1, expert == local - 1))
    def _():
        for step in range(tiles):
            back_store(near_back_ref, 0, step).wait()
            back_store(far_back_ref, 1, step).wait()


def exchange_pass(
    rank_ref,
    column_ref,
    product_ref,
    gate_in_ref,
    up_in_ref,
    down_in_ref,
    own_ref,
    sibling_ref,
    from_across_ref,
    from_other_ref,
    rows_ref,
    hidden_ref,
    gate_grad_ref,
    up_grad_ref,
    route_ref,
    sum_ref,
    out_ref,
    inbox_ref,
    landing_ref,
    token_ref,
    gate_ref,
    up_ref,
    down_ref,
    hidden_held_ref,
    held_ref,
    far_ref,
    beside_ref,
    chip_ref,
    corner_ref,
    token_sem,
    gate_sem,
    up_sem,
    pass_send,
    pass_recv,
    far_send,
    far_recv,
    link_send,
    link_recv,
    store_sem,
    down_sem,
    out_sem,
    landing_sem,
):
    step, expert = pl.program_id(0), pl.program_id(1)
    local = gate_ref.shape[0]
    rows, width = far_ref.shape
    half = rows // 2
    fsdp, ctx = lax.axis_index("fsdp"), lax.axis_index("ctx")
    beside_id = {"fsdp": fsdp + 1 - 2 * lax.rem(fsdp, 2)}
    across_id = {"fsdp": lax.rem(fsdp + 2, 4)}
    other_id = {"ctx": 1 - ctx}
    last = expert == local - 1
    low, high = pl.ds(0, half), pl.ds(half, half)
    sources = (
        inbox_ref.at[0],
        from_across_ref,
        inbox_ref.at[1],
        from_other_ref,
        inbox_ref.at[3],
        inbox_ref.at[2],
        sibling_ref,
        own_ref,
    )

    def token_load(at):
        slot = at % 2
        return pltpu.make_async_copy(sources[at], token_ref.at[slot], token_sem.at[slot])

    def weight_load(source, held, sem, at):
        return pltpu.make_async_copy(source.at[at], held.at[at], sem.at[at])

    def pass_copy(number):
        source, to, peer = (
            (from_across_ref, inbox_ref.at[0], beside_id),
            (from_other_ref, inbox_ref.at[1], beside_id),
            (from_other_ref.at[low], inbox_ref.at[2, low], across_id),
            (from_across_ref.at[high], inbox_ref.at[2, high], other_id),
            (inbox_ref.at[2], inbox_ref.at[3], beside_id),
        )[number]
        return pltpu.make_async_remote_copy(
            src_ref=source,
            dst_ref=to,
            send_sem=pass_send.at[number],
            recv_sem=pass_recv.at[number],
            device_id=peer,
            device_id_type=MESH,
        )

    def far_copy(turn):
        return pltpu.make_async_remote_copy(
            src_ref=far_ref,
            dst_ref=beside_ref.at[turn % 2],
            send_sem=far_send.at[turn],
            recv_sem=far_recv.at[turn],
            device_id=beside_id,
            device_id_type=MESH,
        )

    def link_copy(number):
        source, to, peer = (
            (chip_ref.at[0, high], landing_ref.at[0, high], across_id),
            (chip_ref.at[1, low], landing_ref.at[1, low], other_id),
            (chip_ref.at[2, low], corner_ref.at[0], other_id),
            (chip_ref.at[2, high], corner_ref.at[1], across_id),
            (chip_ref.at[1, high], landing_ref.at[1, high], other_id),
            (chip_ref.at[0, low], landing_ref.at[0, low], across_id),
        )[number]
        return pltpu.make_async_remote_copy(
            src_ref=source,
            dst_ref=to,
            send_sem=link_send.at[number],
            recv_sem=link_recv.at[number],
            device_id=peer,
            device_id_type=MESH,
        )

    @pl.when(jnp.logical_and(step == 0, expert == 0))
    def _():
        barrier = pltpu.get_barrier_semaphore()
        for peer in (beside_id, across_id, other_id):
            pl.semaphore_signal(barrier, inc=1, device_id=peer, device_id_type=MESH)
        pl.semaphore_wait(barrier, 3)
        for number in range(4):
            pass_copy(number).start()
        for at in range(local):
            weight_load(gate_in_ref, gate_ref, gate_sem, at).start()
            weight_load(up_in_ref, up_ref, up_sem, at).start()
        down_load = pltpu.make_async_copy(down_in_ref, down_ref, down_sem)
        down_load.start()
        pass_copy(0).wait_recv()
        token_load(0).start()

    @pl.when(jnp.logical_and(step == 3, expert == 0))
    def _():
        pass_copy(2).wait_recv()
        pass_copy(3).wait_recv()
        pass_copy(4).start()

    for at in range(8):

        @pl.when(jnp.logical_and(step == at, expert == 0))
        def _():
            token_load(at).wait()

        if at < 7:

            @pl.when(jnp.logical_and(step == at, last))
            def _():
                if at == 1:
                    pass_copy(1).wait_recv()
                if at == 3:
                    pass_copy(4).wait_recv()
                token_load(at + 1).start()

    def await_weights():
        @pl.when(step == 0)
        def _():
            weight_load(gate_in_ref, gate_ref, gate_sem, expert).wait()
            weight_load(up_in_ref, up_ref, up_sem, expert).wait()

    first = (fsdp * 2 + ctx) * local

    @pl.when(step < 8)
    def _():
        expert_step(
            expert,
            first + expert,
            rank_ref,
            token_ref[lax.rem(step, 2)],
            product_ref,
            gate_ref,
            up_ref,
            await_weights,
            rows_ref,
            hidden_ref,
            gate_grad_ref,
            up_grad_ref,
            route_ref,
            held_ref,
        )
        hidden_held_ref[step, expert] = hidden_ref[...]

    tile = 512

    def tiles():
        for at in range(0, width, tile):
            yield pl.ds(at, tile)

    def add_half(turn, part, landed):
        total = chip_ref[turn, part, :].astype(f32) + corner_ref[landed].astype(f32)
        chip_ref[turn, part, :] = total.astype(bf16)

    for turn in range(4):

        @pl.when(jnp.logical_and(step == 2 * turn, last))
        def _():
            if turn > 0:
                far_copy(turn - 1).wait_send()
            places = chunk_places(column_ref)
            for at in tiles():
                far_ref[:, at] = matmul(places, held_ref[:, at]).astype(bf16)
            far_copy(turn).start()

        @pl.when(jnp.logical_and(step == 2 * turn + 1, last))
        def _():
            far_copy(turn).wait_recv()
            if turn == 3:
                far_copy(3).wait_send()
            places = chunk_places(column_ref)
            for at in tiles():
                total = matmul(places, held_ref[:, at]) + beside_ref[turn % 2, :, at].astype(f32)
                if turn < 3:
                    chip_ref[turn, :, at] = total.astype(bf16)
                else:
                    far_ref[:, at] = total.astype(bf16)
            if turn < 2:
                link_copy(turn).start()
            if turn == 2:
                link_copy(2).start()
                link_copy(3).start()


    number = step - 8
    turn = number // 2
    chip = lax.rem(fsdp + 2 * (1 - lax.rem(turn, 2)), 4)
    core = chip + (1 - lax.rem(number, 2)) * (1 - 2 * lax.rem(fsdp, 2))
    line = lax.rem(ctx + lax.rem((turn + 1) // 2, 2), 2)
    places_at = (core * 2 + line) * rows
    slot = lax.rem(step, 2)
    columns_of = width // local
    hidden = gate_ref.shape[2]

    def out_store(at, which):
        columns = pl.ds(pl.multiple_of(which * columns_of, columns_of), columns_of)
        return pltpu.make_async_copy(
            token_ref.at[slot, :, columns],
            out_ref.at[pl.ds(pl.multiple_of(at, rows), rows), columns],
            out_sem.at[slot, which],
        )

    @pl.when(step >= 8)
    def _():
        @pl.when(jnp.logical_and(step == 8, expert == 0))
        def _():
            pltpu.make_async_copy(down_in_ref, down_ref, down_sem).wait()

        @pl.when(expert == 0)
        def _():
            columns = column_ref[...]
            for e in range(local):
                held_ref[pl.ds(0, rows), pl.ds(e * hidden, hidden)] = matmul(
                    slot_columns(columns[:, e : e + 1]), hidden_held_ref[number, e]
                ).astype(bf16)

        @pl.when(step >= 10)
        def _():
            out_store(places_at, expert).wait()

        at = pl.ds(pl.multiple_of(expert * columns_of, columns_of), columns_of)
        token_ref[slot, :, at] = matmul(
            held_ref[pl.ds(0, rows), pl.ds(0, local * hidden)], down_ref[:, at]
        ).astype(bf16)
        out_store(places_at, expert).start()

    @pl.when(jnp.logical_and(step == 9, expert == 1))
    def _():
        link_copy(3).wait_recv()
        add_half(1, high, 1)
        link_copy(4).start()
        link_copy(2).wait_recv()
        add_half(0, low, 0)
        link_copy(5).start()

    @pl.when(jnp.logical_and(step == 15, last))
    def _():
        landing = []
        for way, numbers in enumerate(((0, 5), (1, 4))):
            for number in numbers:
                link_copy(number).wait_recv()
            copy = pltpu.make_async_copy(
                landing_ref.at[way], beside_ref.at[way], landing_sem.at[way]
            )
            copy.start()
            landing.append(copy)
        for copy in landing:
            copy.wait()
        for part in (low, high):
            held_ref[part, :] = (
                far_ref[part, :].astype(f32)
                + beside_ref[0, part, :].astype(f32)
                + beside_ref[1, part, :].astype(f32)
            ).astype(bf16)
        store = pltpu.make_async_copy(held_ref.at[pl.ds(0, rows)], sum_ref, store_sem)
        store.start()
        for number in range(5):
            pass_copy(number).wait_send()
        for number in range(6):
            link_copy(number).wait_send()
        for other_slot in (0, 1):
            for which in range(local):
                columns = pl.ds(which * columns_of, columns_of)
                pltpu.make_async_copy(
                    token_ref.at[other_slot, :, columns],
                    out_ref.at[pl.ds(0, rows), columns],
                    out_sem.at[other_slot, which],
                ).wait()
        store.wait()


def expert_sums(ids_ref, column_ref, hidden_ref, down_ref, out_ref):
    columns = column_ref[...]
    dense = [
        matmul(slot_columns(columns[:, e : e + 1]), hidden_ref[e]).astype(bf16)
        for e in range(columns.shape[1])
    ]
    out_ref[...] = matmul(jnp.concatenate(dense, axis=1), down_ref[...]).astype(bf16)


def params(dims):
    return pltpu.CompilerParams(
        dimension_semantics=("arbitrary",) * dims, vmem_limit_bytes=VMEM_BYTES
    )


def once(shape):
    return pl.BlockSpec(
        shape, lambda *ids: (0,) * len(shape), pipeline_mode=pl.Buffered(1)
    )


def run_select_grads(ids, rank_rows, grad_all, down_weight):
    chunks, local = rank_rows.shape[:2]
    hidden, width = down_weight.shape[1:]
    slots = chunks * local * SLOTS
    place = lambda g, e, ids: (g, e, 0, 0)
    return pl.pallas_call(
        select_grads,
        grid_spec=pltpu.PrefetchScalarGridSpec(
            num_scalar_prefetch=1,
            grid=(chunks, local),
            in_specs=[
                pl.BlockSpec((None, None, 1, CHUNK), place),
                pl.BlockSpec((CHUNK, width), lambda g, e, ids: (ids[g], 0)),
                once(down_weight.shape),
            ],
            out_specs=[
                pl.BlockSpec((None, None, SLOTS, width), place),
                pl.BlockSpec((None, None, SLOTS, hidden), place),
            ],
        ),
        out_shape=[
            jax.ShapeDtypeStruct((chunks, local, SLOTS, width), bf16),
            jax.ShapeDtypeStruct((chunks, local, SLOTS, hidden), f32),
        ],
        compiler_params=params(2),
        cost_estimate=pl.CostEstimate(
            flops=2 * slots * width * (CHUNK + hidden),
            bytes_accessed=2 * (chunks * CHUNK + slots) * width,
            transcendentals=0,
        ),
        name="select_grads",
    )(ids, rank_rows, grad_all, down_weight)


def run_exchange_pass(rank_rows, rank_columns, product, weights, sources):
    gate_weight, up_weight, down_weight = weights
    chunks, local = rank_rows.shape[:2]
    width, hidden = gate_weight.shape[1:]
    slots = chunks * local * SLOTS
    flat_down = down_weight.reshape(local * hidden, width)

    def per_expert(g, e):
        return (jnp.minimum(g, chunks - 1), jnp.where(g < chunks, e, local - 1), 0, 0)

    narrow = pl.BlockSpec((None, None, SLOTS, hidden), per_expert)
    anywhere = pl.BlockSpec(memory_space=pl.ANY)
    half = (2, CHUNK // 2, width)
    narrow_shape = jax.ShapeDtypeStruct((chunks, local, SLOTS, hidden), bf16)
    outs = pl.pallas_call(
        exchange_pass,
        grid=(2 * chunks, local),
        in_specs=[
            pl.BlockSpec((None, None, 1, CHUNK), per_expert),
            pl.BlockSpec((None, CHUNK, local), lambda g, e: (lax.rem(g, chunks), 0, 0)),
            narrow,
            *[anywhere] * 7,
        ],
        out_specs=[
            pl.BlockSpec((None, None, SLOTS, width), per_expert),
            narrow,
            narrow,
            narrow,
            pl.BlockSpec((None, None, 1, CHUNK), per_expert),
            *[anywhere] * 4,
        ],
        out_shape=[
            jax.ShapeDtypeStruct((chunks, local, SLOTS, width), bf16),
            narrow_shape,
            narrow_shape,
            narrow_shape,
            jax.ShapeDtypeStruct((chunks, local, 1, CHUNK), f32),
            jax.ShapeDtypeStruct((CHUNK, width), bf16),
            jax.ShapeDtypeStruct((chunks * CHUNK, width), bf16),
            jax.ShapeDtypeStruct((4, *sources[0].shape), bf16),
            jax.ShapeDtypeStruct((2, CHUNK, width), bf16),
        ],
        scratch_shapes=[
            pltpu.VMEM((2, CHUNK, width + EXTRA), bf16),
            pltpu.VMEM(gate_weight.shape, bf16),
            pltpu.VMEM(up_weight.shape, bf16),
            pltpu.VMEM(flat_down.shape, bf16),
            pltpu.VMEM((chunks, local, SLOTS, hidden), bf16),
            pltpu.VMEM((local * SLOTS, width), bf16),
            pltpu.VMEM((CHUNK, width), bf16),
            pltpu.VMEM((2, CHUNK, width), bf16),
            pltpu.VMEM((3, CHUNK, width), bf16),
            pltpu.VMEM(half, bf16),
            pltpu.SemaphoreType.DMA((2,)),
            pltpu.SemaphoreType.DMA((local,)),
            pltpu.SemaphoreType.DMA((local,)),
            pltpu.SemaphoreType.DMA((5,)),
            pltpu.SemaphoreType.DMA((5,)),
            pltpu.SemaphoreType.DMA((4,)),
            pltpu.SemaphoreType.DMA((4,)),
            pltpu.SemaphoreType.DMA((6,)),
            pltpu.SemaphoreType.DMA((6,)),
            pltpu.SemaphoreType.DMA,
            pltpu.SemaphoreType.DMA,
            pltpu.SemaphoreType.DMA((2, local)),
            pltpu.SemaphoreType.DMA((2,)),
        ],
        compiler_params=pltpu.CompilerParams(
            dimension_semantics=("arbitrary",) * 2,
            collective_id=9,
            has_side_effects=True,
            vmem_limit_bytes=VMEM_BYTES,
        ),
        cost_estimate=pl.CostEstimate(
            flops=2 * slots * width * (2 * CHUNK + 4 * hidden),
            bytes_accessed=2 * (12 * CHUNK + slots) * width,
            transcendentals=slots * hidden,
        ),
        name="exchange_pass",
    )(rank_rows, rank_columns, product, gate_weight, up_weight, flat_down, *sources)
    return outs[:5], outs[5], outs[6]


def run_expert_pass(
    ids, first, rank_rows, rank_columns, near, far, product, gate_weight, up_weight, kept
):
    chunks, local = rank_rows.shape[:2]
    width, hidden = gate_weight.shape[1:]
    slots = 2 * local * SLOTS
    per_expert = lambda g, e, ids: (ids[g], e, 0, 0)
    narrow = pl.BlockSpec((None, None, SLOTS, hidden), per_expert)
    in_specs = [
        pl.BlockSpec(memory_space=pltpu.SMEM),
        pl.BlockSpec((None, None, 1, CHUNK), per_expert),
        pl.BlockSpec((None, CHUNK, local), lambda g, e, ids: (ids[g], 0, 0)),
        pl.BlockSpec(memory_space=pl.ANY),
        pl.BlockSpec(memory_space=pl.ANY),
        narrow,
        pl.BlockSpec(memory_space=pl.ANY),
        pl.BlockSpec(memory_space=pl.ANY),
    ]
    kept_shapes = [
        jax.ShapeDtypeStruct((chunks, local, SLOTS, width), bf16),
        jax.ShapeDtypeStruct((chunks, local, SLOTS, hidden), bf16),
        jax.ShapeDtypeStruct((chunks, local, SLOTS, hidden), bf16),
        jax.ShapeDtypeStruct((chunks, local, SLOTS, hidden), bf16),
        jax.ShapeDtypeStruct((chunks, local, 1, CHUNK), f32),
    ]
    outs = pl.pallas_call(
        expert_pass,
        grid_spec=pltpu.PrefetchScalarGridSpec(
            num_scalar_prefetch=1,
            grid=(2, local),
            in_specs=in_specs + [pl.BlockSpec(memory_space=pl.ANY)] * len(kept),
            out_specs=[
                pl.BlockSpec((None, None, SLOTS, width), per_expert),
                narrow,
                narrow,
                narrow,
                pl.BlockSpec((None, None, 1, CHUNK), per_expert),
                pl.BlockSpec(memory_space=pl.ANY),
                pl.BlockSpec(memory_space=pl.ANY),
            ],
            scratch_shapes=[
                pltpu.VMEM((2, CHUNK, width + EXTRA), bf16),
                pltpu.VMEM(gate_weight.shape, bf16),
                pltpu.VMEM(up_weight.shape, bf16),
                pltpu.VMEM((local * SLOTS, width), bf16),
                pltpu.VMEM((2, CHUNK, width), bf16),
                pltpu.SemaphoreType.DMA((2,)),
                pltpu.SemaphoreType.DMA((local,)),
                pltpu.SemaphoreType.DMA((local,)),
                pltpu.SemaphoreType.DMA((2, 4)),
            ],
        ),
        out_shape=kept_shapes + [jax.ShapeDtypeStruct((CHUNK, width), bf16)] * 2,
        input_output_aliases={9 + at: at for at in range(len(kept))},
        compiler_params=params(2),
        cost_estimate=pl.CostEstimate(
            flops=2 * slots * width * (2 * CHUNK + 4 * hidden),
            bytes_accessed=2 * (4 * CHUNK + slots) * width,
            transcendentals=slots * hidden,
        ),
        name="expert_pass",
    )(ids, first, rank_rows, rank_columns, near, far, product, gate_weight, up_weight, *kept)
    return outs[:5], outs[5], outs[6]


def run_expert_sums(ids, rank_columns, hidden_rows, down_weight):
    chunks, local, unused, hidden = hidden_rows.shape
    width = down_weight.shape[2]
    flat = down_weight.reshape(local * hidden, width)
    return pl.pallas_call(
        expert_sums,
        grid_spec=pltpu.PrefetchScalarGridSpec(
            num_scalar_prefetch=1,
            grid=(chunks,),
            in_specs=[
                pl.BlockSpec((None, CHUNK, local), lambda g, ids: (g, 0, 0)),
                pl.BlockSpec((None, local, SLOTS, hidden), lambda g, ids: (g, 0, 0, 0)),
                once(flat.shape),
            ],
            out_specs=pl.BlockSpec((CHUNK, width), lambda g, ids: (ids[g], 0)),
        ),
        out_shape=jax.ShapeDtypeStruct((chunks * CHUNK, width), bf16),
        compiler_params=params(1),
        cost_estimate=pl.CostEstimate(
            flops=2 * chunks * CHUNK * local * hidden * (width + SLOTS),
            bytes_accessed=2 * chunks * CHUNK * width,
            transcendentals=0,
        ),
        name="expert_sums",
    )(ids, rank_columns, hidden_rows, flat)


def line_barrier(size):
    place = lax.axis_index("tp")
    barrier = pltpu.get_barrier_semaphore()

    @pl.when(place > 0)
    def _():
        pl.semaphore_signal(barrier, inc=1, device_id={"tp": place - 1}, device_id_type=MESH)

    @pl.when(place < size - 1)
    def _():
        pl.semaphore_signal(barrier, inc=1, device_id={"tp": place + 1}, device_id_type=MESH)

    has_left = jnp.where(place > 0, 1, 0)
    has_right = jnp.where(place < size - 1, 1, 0)
    pl.semaphore_wait(barrier, has_left + has_right)


def line_gather(size, columns, in_ref, out_ref, own_sem, send_sem, recv_sem):
    place = lax.axis_index("tp")
    extent = in_ref.shape[1] if columns else in_ref.shape[0]

    def block(index):
        at = pl.ds(pl.multiple_of(index * extent, extent), extent)
        return out_ref.at[:, at] if columns else out_ref.at[at, :]

    line_barrier(size)
    own = pltpu.make_async_copy(in_ref, block(place), own_sem)
    own.start()

    def sending(way, step):
        source = place - step if way == 0 else place + step
        to = place + 1 if way == 0 else place - 1
        return pltpu.make_async_remote_copy(
            src_ref=in_ref if step == 0 else block(source),
            dst_ref=block(source),
            send_sem=send_sem.at[way, step],
            recv_sem=recv_sem.at[way, step],
            device_id={"tp": to},
            device_id_type=MESH,
        )

    def sends(way, step):
        if way == 0:
            return jnp.logical_and(place >= step, place < size - 1)
        return jnp.logical_and(place + step < size, place > 0)

    def receiving(way, step):
        source = place - 1 - step if way == 0 else place + 1 + step
        origin = place - 1 if way == 0 else place + 1
        return pltpu.make_async_remote_copy(
            src_ref=block(source),
            dst_ref=block(source),
            send_sem=send_sem.at[way, step],
            recv_sem=recv_sem.at[way, step],
            device_id={"tp": origin},
            device_id_type=MESH,
        )

    def receives(way, step):
        return place > step if way == 0 else place + 1 + step < size

    for step in range(size - 1):
        for way in (0, 1):

            @pl.when(sends(way, step))
            def _():
                sending(way, step).start()

        for way in (0, 1):

            @pl.when(receives(way, step))
            def _():
                receiving(way, step).wait_recv()

    for step in range(size - 1):
        for way in (0, 1):

            @pl.when(sends(way, step))
            def _():
                sending(way, step).wait_send()

    own.wait()


def line_scatter(
    size, columns, in_ref, out_ref, staged_ref, landed_ref, send_sem, recv_sem, stages=()
):
    place = lax.axis_index("tp")
    extent = out_ref.shape[1] if columns else out_ref.shape[0]

    def block(index):
        at = pl.ds(pl.multiple_of(index * extent, extent), extent)
        values = in_ref[:, at] if columns else in_ref[at, :]
        return values.astype(f32)

    if not stages:
        line_barrier(size)

    def copying(way, step, to):
        return pltpu.make_async_remote_copy(
            src_ref=staged_ref.at[way, step],
            dst_ref=landed_ref.at[way, step],
            send_sem=send_sem.at[way, step],
            recv_sem=recv_sem.at[way, step],
            device_id={"tp": to},
            device_id_type=MESH,
        )

    for step in range(size - 1):
        for way in (0, 1):
            rank = place if way == 0 else size - 1 - place
            target = size - 1 - step + place if way == 0 else place - (size - 1 - step)
            to = place + 1 if way == 0 else place - 1
            active = jnp.logical_and(rank <= step, rank < size - 1)

            @pl.when(active)
            def _():
                values = block(target)
                if step == 0:
                    staged_ref[way, step] = values.astype(bf16)
                else:

                    @pl.when(rank == 0)
                    def _():
                        staged_ref[way, step] = values.astype(bf16)

                    @pl.when(rank > 0)
                    def _():
                        landed = landed_ref[way, step - 1].astype(f32)
                        staged_ref[way, step] = (values + landed).astype(bf16)

                copying(way, step, to).start()

        if step < len(stages):
            stages[step]()

        for way in (0, 1):
            rank = place if way == 0 else size - 1 - place
            origin = place - 1 if way == 0 else place + 1

            @pl.when(jnp.logical_and(rank > 0, rank - 1 <= step))
            def _():
                copying(way, step, origin).wait_recv()

    for stage in stages[size - 1 :]:
        stage()
    out_ref[...] = block(place)
    for way in (0, 1):
        rank = place if way == 0 else size - 1 - place

        @pl.when(rank > 0)
        def _():
            out_ref[...] += landed_ref[way, size - 2].astype(f32)

    for step in range(size - 1):
        for way in (0, 1):
            rank = place if way == 0 else size - 1 - place
            to = place + 1 if way == 0 else place - 1

            @pl.when(jnp.logical_and(rank <= step, rank < size - 1))
            def _():
                copying(way, step, to).wait_send()


def closing_sums(
    sizes,
    narrow,
    in_ref,
    small_ref,
    out_ref,
    every_ref,
    line_ref,
    staged_ref,
    landed_ref,
    total_ref,
    small_tp_ref,
    small_ctx_ref,
    small_fsdp_ref,
    send_sem,
    recv_sem,
    small_send_sem,
    small_recv_sem,
):
    axes = ("tp", "ctx", "fsdp")
    barrier = pltpu.get_barrier_semaphore()
    for axis, size in zip(axes, sizes):
        place = lax.axis_index(axis)
        for offset in range(1, size):
            peer = lax.rem(place + offset, size)
            pl.semaphore_signal(barrier, inc=1, device_id={axis: peer}, device_id_type=MESH)
    pl.semaphore_wait(barrier, sum(sizes) - len(sizes))
    landings = (small_tp_ref, small_ctx_ref, small_fsdp_ref)

    def copying(axis, offset, peer):
        return pltpu.make_async_remote_copy(
            src_ref=small_ref if axis == 0 else total_ref.at[axis - 1],
            dst_ref=landings[axis].at[offset - 1],
            send_sem=small_send_sem.at[axis, offset - 1],
            recv_sem=small_recv_sem.at[axis, offset - 1],
            device_id={axes[axis]: peer},
            device_id_type=MESH,
        )

    def each(axis):
        size, place = sizes[axis], lax.axis_index(axes[axis])
        for offset in range(1, size):
            yield (
                offset,
                lax.rem(place + offset, size),
                lax.rem(place + size - offset, size),
            )

    def start(axis):
        for offset, to, origin in each(axis):
            copying(axis, offset, to).start()

    def finish(axis):
        total = small_ref[...] if axis == 0 else total_ref[axis - 1]
        for offset, to, origin in each(axis):
            copying(axis, offset, origin).wait_recv()
            total = total + landings[axis][offset - 1]
        for offset, to, origin in each(axis):
            copying(axis, offset, to).wait_send()
        return total

    def first():
        start(0)

    def second():
        total = finish(0)
        total_ref[0] = total
        line_ref[...] = total[:, narrow:]
        start(1)

    def third():
        total_ref[1] = finish(1)
        start(2)

    def last():
        every_ref[...] = finish(2)[:, :narrow]

    line_scatter(
        sizes[0],
        True,
        in_ref,
        out_ref,
        staged_ref,
        landed_ref,
        send_sem,
        recv_sem,
        stages=(first, second, third, last),
    )


def peer_barrier(axis, size):
    place = lax.axis_index(axis)
    barrier = pltpu.get_barrier_semaphore()
    for offset in range(1, size):
        peer = lax.rem(place + offset, size)
        pl.semaphore_signal(barrier, inc=1, device_id={axis: peer}, device_id_type=MESH)
    pl.semaphore_wait(barrier, size - 1)


def peer_gather(size, in_ref, out_ref, own_sem, send_sem, recv_sem):
    place = lax.axis_index("ctx")
    rows = in_ref.shape[0]

    def block(index):
        return out_ref.at[pl.ds(pl.multiple_of(index * rows, rows), rows), :]

    def copying(offset, source, peer):
        return pltpu.make_async_remote_copy(
            src_ref=in_ref,
            dst_ref=block(source),
            send_sem=send_sem.at[offset - 1],
            recv_sem=recv_sem.at[offset - 1],
            device_id={"ctx": peer},
            device_id_type=MESH,
        )

    peer_barrier("ctx", size)
    own = pltpu.make_async_copy(in_ref, block(place), own_sem)
    own.start()
    for offset in range(1, size):
        copying(offset, place, lax.rem(place + offset, size)).start()
    for offset in range(1, size):
        origin = lax.rem(place + size - offset, size)
        copying(offset, origin, origin).wait_recv()
    for offset in range(1, size):
        copying(offset, place, lax.rem(place + offset, size)).wait_send()
    own.wait()


def peer_scatter(size, in_ref, out_ref, landed_ref, send_sem, recv_sem):
    place = lax.axis_index("ctx")
    rows = out_ref.shape[0]

    def at(index):
        return pl.ds(pl.multiple_of(index * rows, rows), rows)

    def copying(offset, peer):
        return pltpu.make_async_remote_copy(
            src_ref=in_ref.at[at(peer), :],
            dst_ref=landed_ref.at[offset - 1],
            send_sem=send_sem.at[offset - 1],
            recv_sem=recv_sem.at[offset - 1],
            device_id={"ctx": peer},
            device_id_type=MESH,
        )

    peer_barrier("ctx", size)
    for offset in range(1, size):
        copying(offset, lax.rem(place + offset, size)).start()
    total = in_ref[at(place), :].astype(f32)
    for offset in range(1, size):
        origin = lax.rem(place + size - offset, size)
        copying(offset, origin).wait_recv()
        total = total + landed_ref[offset - 1].astype(f32)
    out_ref[...] = total.astype(bf16)
    for offset in range(1, size):
        copying(offset, lax.rem(place + offset, size)).wait_send()


def remote_params(number):
    return pltpu.CompilerParams(
        collective_id=number, has_side_effects=True, vmem_limit_bytes=VMEM_BYTES
    )


def gather_tp(values, columns, number):
    size = lax.axis_size("tp")
    rows, width = values.shape
    shape = (rows, size * width) if columns else (size * rows, width)
    return pl.pallas_call(
        functools.partial(line_gather, size, columns),
        in_specs=[pl.BlockSpec(memory_space=pl.ANY)],
        out_specs=pl.BlockSpec(memory_space=pl.ANY),
        out_shape=jax.ShapeDtypeStruct(shape, values.dtype),
        scratch_shapes=[
            pltpu.SemaphoreType.DMA,
            pltpu.SemaphoreType.DMA((2, size - 1)),
            pltpu.SemaphoreType.DMA((2, size - 1)),
        ],
        compiler_params=remote_params(number),
        cost_estimate=pl.CostEstimate(flops=0, bytes_accessed=150_000_000, transcendentals=0),
        name="gather_tp",
    )(values)


def scatter_tp(values, columns, number):
    size = lax.axis_size("tp")
    rows, width = values.shape
    shape = (rows, width // size) if columns else (rows // size, width)
    return pl.pallas_call(
        functools.partial(line_scatter, size, columns),
        in_specs=[pl.BlockSpec(memory_space=pltpu.VMEM)],
        out_specs=pl.BlockSpec(memory_space=pltpu.VMEM),
        out_shape=jax.ShapeDtypeStruct(shape, f32),
        scratch_shapes=[
            pltpu.VMEM((2, size - 1, *shape), bf16),
            pltpu.VMEM((2, size - 1, *shape), bf16),
            pltpu.SemaphoreType.DMA((2, size - 1)),
            pltpu.SemaphoreType.DMA((2, size - 1)),
        ],
        compiler_params=remote_params(number),
        cost_estimate=pl.CostEstimate(flops=0, bytes_accessed=150_000_000, transcendentals=0),
        name="scatter_tp",
    )(values)


def close_tp(values, gains, along, number):
    sizes = tuple(lax.axis_size(axis) for axis in ("tp", "ctx", "fsdp"))
    rows, width = values.shape
    shape = (rows, width // sizes[0])
    pad = lambda row: jnp.pad(row, (0, -row.shape[0] % 1024)).reshape(8, -1)
    gains_b, along_b = pad(gains), pad(along)
    narrow, wide = gains_b.shape[1], along_b.shape[1]
    small = jnp.concatenate([gains_b, along_b], axis=1)
    peers = max(sizes) - 1
    out, every, line = pl.pallas_call(
        functools.partial(closing_sums, sizes, narrow),
        in_specs=[pl.BlockSpec(memory_space=pltpu.VMEM)] * 2,
        out_specs=[pl.BlockSpec(memory_space=pltpu.VMEM)] * 3,
        out_shape=[
            jax.ShapeDtypeStruct(shape, f32),
            jax.ShapeDtypeStruct((8, narrow), f32),
            jax.ShapeDtypeStruct((8, wide), f32),
        ],
        scratch_shapes=[
            pltpu.VMEM((2, sizes[0] - 1, *shape), bf16),
            pltpu.VMEM((2, sizes[0] - 1, *shape), bf16),
            pltpu.VMEM((2, *small.shape), f32),
            *[pltpu.VMEM((size - 1, *small.shape), f32) for size in sizes],
            pltpu.SemaphoreType.DMA((2, sizes[0] - 1)),
            pltpu.SemaphoreType.DMA((2, sizes[0] - 1)),
            pltpu.SemaphoreType.DMA((3, peers)),
            pltpu.SemaphoreType.DMA((3, peers)),
        ],
        compiler_params=remote_params(number),
        cost_estimate=pl.CostEstimate(flops=0, bytes_accessed=150_000_000, transcendentals=0),
        name="close_tp",
    )(values, small)
    return out, every.reshape(-1)[: gains.shape[0]], line.reshape(-1)[: along.shape[0]]


def gather_ctx(values, number):
    size = lax.axis_size("ctx")
    rows, width = values.shape
    return pl.pallas_call(
        functools.partial(peer_gather, size),
        in_specs=[pl.BlockSpec(memory_space=pl.ANY)],
        out_specs=pl.BlockSpec(memory_space=pl.ANY),
        out_shape=jax.ShapeDtypeStruct((size * rows, width), values.dtype),
        scratch_shapes=[
            pltpu.SemaphoreType.DMA,
            pltpu.SemaphoreType.DMA((size - 1,)),
            pltpu.SemaphoreType.DMA((size - 1,)),
        ],
        compiler_params=remote_params(number),
        cost_estimate=pl.CostEstimate(flops=0, bytes_accessed=100_000_000, transcendentals=0),
        name="gather_ctx",
    )(values)


def scatter_ctx(values, number):
    size = lax.axis_size("ctx")
    rows, width = values.shape
    shape = (rows // size, width)
    return pl.pallas_call(
        functools.partial(peer_scatter, size),
        in_specs=[pl.BlockSpec(memory_space=pltpu.VMEM)],
        out_specs=pl.BlockSpec(memory_space=pltpu.VMEM),
        out_shape=jax.ShapeDtypeStruct(shape, values.dtype),
        scratch_shapes=[
            pltpu.VMEM((size - 1, *shape), bf16),
            pltpu.SemaphoreType.DMA((size - 1,)),
            pltpu.SemaphoreType.DMA((size - 1,)),
        ],
        compiler_params=remote_params(number),
        cost_estimate=pl.CostEstimate(flops=0, bytes_accessed=100_000_000, transcendentals=0),
        name="scatter_ctx",
    )(values)


def attend(scale, query_ref, key_ref, value_ref, seg_row_ref, seg_column_ref, out_ref, total_ref):
    scores = matmul_nt(key_ref[...], query_ref[...]) * scale
    scores = jnp.where(seg_column_ref[...] == seg_row_ref[...], scores, masked_score)
    most = jnp.max(scores, axis=0, keepdims=True)
    probs = jnp.exp(scores - most)
    total = jnp.sum(probs, axis=0, keepdims=True)
    mixed = matmul(value_ref[...].T, probs.astype(bf16)) / total
    out_ref[...] = mixed.T.astype(bf16)
    total_ref[...] = most + jnp.log(total)


def attend_back(
    scale,
    query_ref,
    key_ref,
    value_ref,
    seg_row_ref,
    seg_column_ref,
    out_ref,
    total_ref,
    grad_ref,
    query_grad_ref,
    key_grad_ref,
    value_grad_ref,
    key_sum_ref,
    value_sum_ref,
):
    step = pl.program_id(1)
    query, key, grad = query_ref[...], key_ref[...], grad_ref[...]
    scores = matmul_nt(key, query) * scale
    scores = jnp.where(seg_column_ref[...] == seg_row_ref[...], scores, masked_score)
    probs = jnp.exp(scores - total_ref[...])
    products = grad.astype(f32) * out_ref[...].astype(f32)
    delta = jnp.sum(products.T, axis=0, keepdims=True)
    score_grad = (probs * (matmul_nt(value_ref[...], grad) - delta)).astype(bf16)
    query_grad_ref[...] = (matmul(key.T, score_grad) * scale).T
    key_part = matmul(score_grad, query) * scale
    value_part = matmul(probs.astype(bf16), grad)

    @pl.when(step == 0)
    def _():
        key_sum_ref[...] = key_part
        value_sum_ref[...] = value_part

    @pl.when(step > 0)
    def _():
        key_sum_ref[...] += key_part
        value_sum_ref[...] += value_part

    @pl.when(step == pl.num_programs(1) - 1)
    def _():
        key_grad_ref[...] = key_sum_ref[...].astype(bf16)
        value_grad_ref[...] = value_sum_ref[...].astype(bf16)


def attention_specs(rows, keys, heads, head_dim):
    block = min(rows, QUERY_BLOCK)
    query = pl.BlockSpec((block, head_dim), lambda h, i: (i, h))
    return (
        (heads, rows // block),
        [
            query,
            pl.BlockSpec((keys, head_dim), lambda h, i: (0, h)),
            pl.BlockSpec((keys, head_dim), lambda h, i: (0, h + heads)),
            pl.BlockSpec((None, 1, block), lambda h, i: (i, 0, 0)),
            pl.BlockSpec((keys, 1), lambda h, i: (0, 0)),
        ],
        query,
        pl.BlockSpec((None, None, 1, block), lambda h, i: (h, i, 0, 0)),
        pl.BlockSpec((keys, head_dim), lambda h, i: (0, h)),
    )


def run_attend(query_b, group, seg_rows, seg_columns, heads, scale):
    rows, keys = query_b.shape[0], group.shape[0]
    head_dim = query_b.shape[1] // heads
    grid, specs, query, total, unused = attention_specs(rows, keys, heads, head_dim)
    work = heads * rows * keys
    return pl.pallas_call(
        functools.partial(attend, scale),
        grid=grid,
        in_specs=specs,
        out_specs=[query, total],
        out_shape=[
            jax.ShapeDtypeStruct(query_b.shape, bf16),
            jax.ShapeDtypeStruct((*grid, 1, rows // grid[1]), f32),
        ],
        compiler_params=params(2),
        cost_estimate=pl.CostEstimate(
            flops=4 * work * head_dim, bytes_accessed=8 * query_b.size, transcendentals=work
        ),
        name="attend",
    )(query_b, group, group, seg_rows, seg_columns)


def run_attend_back(query_b, group, seg_rows, seg_columns, out_b, total, grad_b, heads, scale):
    rows, keys = query_b.shape[0], group.shape[0]
    head_dim = query_b.shape[1] // heads
    grid, specs, query, total_spec, key = attention_specs(rows, keys, heads, head_dim)
    work = heads * rows * keys
    return pl.pallas_call(
        functools.partial(attend_back, scale),
        grid=grid,
        in_specs=[*specs, query, total_spec, query],
        out_specs=[query, key, key],
        out_shape=[
            jax.ShapeDtypeStruct(query_b.shape, f32),
            jax.ShapeDtypeStruct((keys, query_b.shape[1]), bf16),
            jax.ShapeDtypeStruct((keys, query_b.shape[1]), bf16),
        ],
        scratch_shapes=[pltpu.VMEM((keys, head_dim), f32)] * 2,
        compiler_params=params(2),
        cost_estimate=pl.CostEstimate(
            flops=10 * work * head_dim, bytes_accessed=16 * query_b.size, transcendentals=work
        ),
        name="attend_back",
    )(query_b, group, group, seg_rows, seg_columns, out_b, total, grad_b)


def beside(values):
    return lax.ppermute(values, "fsdp", [(0, 1), (1, 0), (2, 3), (3, 2)])


def across(values):
    return lax.ppermute(values, "fsdp", [(0, 2), (1, 3), (2, 0), (3, 1)])


def other(values):
    return lax.ppermute(values, "ctx", [(0, 1), (1, 0)])


def added(*values):
    total = values[0].astype(f32)
    for value in values[1:]:
        total = total + value.astype(f32)
    return total.astype(bf16)


def then(first, *values):
    return lax.optimization_barrier((first, *values))[1:]


def by_chips():
    return lax.axis_size("fsdp") == 4 and lax.axis_size("ctx") == 2


def chunk_order(chunks):
    if not by_chips():
        return jnp.arange(chunks, dtype=jnp.int32)
    fsdp, ctx = lax.axis_index("fsdp"), lax.axis_index("ctx")
    sibling = fsdp + 1 - 2 * lax.rem(fsdp, 2)
    flip = lambda core: lax.rem(core + 2, 4)
    places = (
        (flip(sibling), ctx),
        (flip(fsdp), ctx),
        (sibling, 1 - ctx),
        (fsdp, 1 - ctx),
        (flip(sibling), 1 - ctx),
        (flip(fsdp), 1 - ctx),
        (sibling, ctx),
        (fsdp, ctx),
    )
    return jnp.stack([jnp.asarray(2 * f + c, jnp.int32) for f, c in places])


def expert_steps(ids, own_tokens, grad_all, rank_rows, rank_columns, first, weights):
    gate_weight, up_weight, down_weight = weights
    chunks = rank_rows.shape[0]

    def one_pass(at, near, far, product, kept):
        return run_expert_pass(
            jnp.array([at, at + 1], jnp.int32),
            first,
            rank_rows,
            rank_columns,
            near,
            far,
            product,
            gate_weight,
            up_weight,
            kept,
        )

    if not by_chips():
        token_all = lax.all_gather(own_tokens, ROWS, axis=0, tiled=True)
        blocks = token_all.reshape(chunks, CHUNK, -1)
        grad_slots, product = run_select_grads(ids, rank_rows, grad_all, down_weight)
        kept, backs = (), []
        for at in range(0, chunks, 2):
            kept, near, far = one_pass(at, blocks[at], blocks[at + 1], product, kept)
            backs += [near, far]
        back_sum = lax.psum_scatter(
            jnp.concatenate(backs), ROWS, scatter_dimension=0, tiled=True
        )
        out_part = run_expert_sums(ids, rank_columns, kept[1], down_weight)
        return kept, grad_slots, back_sum, out_part

    from_across, from_other = across(own_tokens), other(own_tokens)
    from_beside = beside(own_tokens)
    grad_slots, product = run_select_grads(ids, rank_rows, grad_all, down_weight)
    from_across, from_other = then(product, from_across, from_other)
    kept, back_sum, out_part = run_exchange_pass(
        rank_rows,
        rank_columns,
        product,
        weights,
        (own_tokens, from_beside, from_across, from_other),
    )
    return kept, grad_slots, back_sum, out_part


def head_blocks(width, head_dim):
    for at in range(0, width, head_dim):
        yield slice(at, at + head_dim)


def project(
    input_ref,
    gain_ref,
    weight_ref,
    cosine_ref,
    sine_ref,
    head_gain_ref,
    normed_ref,
    inverse_ref,
    pre_ref,
    query_ref,
    group_ref,
):
    values = input_ref[...].astype(f32)
    inverse = norm_scale(values)
    normed = (values * inverse * gain_ref[...]).astype(bf16)
    normed_ref[...] = normed
    inverse_ref[...] = inverse
    qkv = matmul(normed, weight_ref[...])
    width = query_ref.shape[1]
    head_dim = cosine_ref.shape[1]
    pre_ref[...] = qkv[:, : 2 * width]
    cosine, sine = cosine_ref[...], sine_ref[...]
    for which in (0, 1):
        gain = head_gain_ref[which : which + 1, :]
        for at in head_blocks(width, head_dim):
            head = qkv[:, which * width + at.start : which * width + at.stop]
            head = head * norm_scale(head) * gain
            turned = head * cosine + pltpu.roll(head, head_dim // 2, 1) * sine
            to_ref = query_ref if which == 0 else group_ref
            to_ref[:, at] = turned.astype(bf16)
    group_ref[:, width : 2 * width] = qkv[:, 2 * width :].astype(bf16)


def project_back(
    query_grad_ref,
    group_grad_ref,
    pre_ref,
    cosine_ref,
    sine_ref,
    head_gain_ref,
    weight_ref,
    input_ref,
    inverse_ref,
    gain_ref,
    grad_ref,
    part_ref,
    along_ref,
    terms_ref,
    head_terms_ref,
):
    width = query_grad_ref.shape[1]
    head_dim = cosine_ref.shape[1]
    cosine, sine = cosine_ref[...], sine_ref[...]

    @pl.when(pl.program_id(0) == 0)
    def _():
        terms_ref[...] = jnp.zeros_like(terms_ref)
        head_terms_ref[...] = jnp.zeros_like(head_terms_ref)

    for which in (0, 1):
        gain = head_gain_ref[which : which + 1, :]
        from_ref = query_grad_ref if which == 0 else group_grad_ref
        for at in head_blocks(width, head_dim):
            own = slice(which * width + at.start, which * width + at.stop)
            grad = from_ref[:, at].astype(f32)
            incoming = grad * cosine - pltpu.roll(grad, head_dim // 2, 1) * sine
            head = pre_ref[:, own]
            value_grad, gain_terms = norm_back(incoming, head, norm_scale(head), gain)
            grad_ref[:, own] = value_grad.astype(bf16)
            head_terms_ref[which : which + 1, :] += jnp.sum(gain_terms, axis=0, keepdims=True)
    grad_ref[:, 2 * width :] = group_grad_ref[:, width:]
    part = matmul_nt(grad_ref[...], weight_ref[...])
    part_ref[...] = part.astype(bf16)
    product = part * input_ref[...].astype(f32)
    terms_ref[...] += jnp.sum(product * inverse_ref[...], axis=0, keepdims=True)
    along_ref[...] = jnp.sum(product * gain_ref[...], axis=1, keepdims=True)


def run_project(input_b, gain, full, cosine, sine, head_gains, width):
    rows, depth = input_b.shape
    head_dim = cosine.shape[1]
    block = min(rows, QUERY_BLOCK)
    by_rows = lambda columns: pl.BlockSpec((block, columns), lambda i: (i, 0))
    return pl.pallas_call(
        project,
        grid=(rows // block,),
        in_specs=[
            by_rows(depth),
            once((1, depth)),
            once((depth, 3 * width)),
            by_rows(head_dim),
            by_rows(head_dim),
            once((2, head_dim)),
        ],
        out_specs=[
            by_rows(depth),
            by_rows(1),
            by_rows(2 * width),
            by_rows(width),
            by_rows(2 * width),
        ],
        out_shape=[
            jax.ShapeDtypeStruct((rows, depth), bf16),
            jax.ShapeDtypeStruct((rows, 1), f32),
            jax.ShapeDtypeStruct((rows, 2 * width), f32),
            jax.ShapeDtypeStruct((rows, width), bf16),
            jax.ShapeDtypeStruct((rows, 2 * width), bf16),
        ],
        compiler_params=params(1),
        cost_estimate=pl.CostEstimate(
            flops=6 * rows * depth * width, bytes_accessed=6 * depth * width, transcendentals=0
        ),
        name="project",
    )(input_b, gain, full, cosine, sine, head_gains)


def run_project_back(
    query_grad, group_grad, pre, cosine, sine, head_gains, full, input_b, inverse, gain
):
    rows, depth = input_b.shape
    width = query_grad.shape[1]
    head_dim = cosine.shape[1]
    block = min(rows, QUERY_BLOCK)
    by_rows = lambda columns: pl.BlockSpec((block, columns), lambda i: (i, 0))
    whole = lambda shape: pl.BlockSpec(shape, lambda i: (0, 0))
    return pl.pallas_call(
        project_back,
        grid=(rows // block,),
        in_specs=[
            by_rows(width),
            by_rows(2 * width),
            by_rows(2 * width),
            by_rows(head_dim),
            by_rows(head_dim),
            once((2, head_dim)),
            once((depth, 3 * width)),
            by_rows(depth),
            by_rows(1),
            once((1, depth)),
        ],
        out_specs=[
            by_rows(3 * width),
            by_rows(depth),
            by_rows(1),
            whole((1, depth)),
            whole((2, head_dim)),
        ],
        out_shape=[
            jax.ShapeDtypeStruct((rows, 3 * width), bf16),
            jax.ShapeDtypeStruct((rows, depth), bf16),
            jax.ShapeDtypeStruct((rows, 1), f32),
            jax.ShapeDtypeStruct((1, depth), f32),
            jax.ShapeDtypeStruct((2, head_dim), f32),
        ],
        compiler_params=params(1),
        cost_estimate=pl.CostEstimate(
            flops=6 * rows * depth * width, bytes_accessed=8 * depth * width, transcendentals=0
        ),
        name="project_back",
    )(query_grad, group_grad, pre, cosine, sine, head_gains, full, input_b, inverse, gain)


def grads_scatter(
    size,
    local,
    in_ref,
    small_ref,
    rows_ref,
    grad_rows_ref,
    gate_grad_ref,
    up_grad_ref,
    hidden_ref,
    out_ref,
    total_ref,
    gate_out_ref,
    up_out_ref,
    down_out_ref,
    staged_ref,
    landed_ref,
    small_landed_ref,
    first_ref,
    second_ref,
    send_sem,
    recv_sem,
    small_send_sem,
    small_recv_sem,
):
    step, part = pl.program_id(0), pl.program_id(1)
    place = lax.axis_index("tp")
    extent = out_ref.shape[0]

    def block(index):
        return in_ref[pl.ds(pl.multiple_of(index * extent, extent), extent), :].astype(f32)

    def copying(way, stage, to):
        return pltpu.make_async_remote_copy(
            src_ref=staged_ref.at[way, stage],
            dst_ref=landed_ref.at[way, stage],
            send_sem=send_sem.at[way, stage],
            recv_sem=recv_sem.at[way, stage],
            device_id={"tp": to},
            device_id_type=MESH,
        )

    def small_copy(offset, peer):
        return pltpu.make_async_remote_copy(
            src_ref=small_ref,
            dst_ref=small_landed_ref.at[offset - 1],
            send_sem=small_send_sem.at[offset - 1],
            recv_sem=small_recv_sem.at[offset - 1],
            device_id={"tp": peer},
            device_id_type=MESH,
        )

    def ways():
        yield 0, place, place + 1, place - 1
        yield 1, size - 1 - place, place - 1, place + 1

    def send(stage):
        for way, rank, to, origin in ways():
            target = size - 1 - stage + place if way == 0 else place - (size - 1 - stage)

            @pl.when(jnp.logical_and(rank <= stage, rank < size - 1))
            def _():
                values = block(target)
                if stage == 0:
                    staged_ref[way, stage] = values.astype(bf16)
                else:

                    @pl.when(rank == 0)
                    def _():
                        staged_ref[way, stage] = values.astype(bf16)

                    @pl.when(rank > 0)
                    def _():
                        landed = landed_ref[way, stage - 1].astype(f32)
                        staged_ref[way, stage] = (values + landed).astype(bf16)

                copying(way, stage, to).start()

    def receive(stage):
        for way, rank, to, origin in ways():

            @pl.when(jnp.logical_and(rank > 0, rank - 1 <= stage))
            def _():
                copying(way, stage, origin).wait_recv()

    @pl.when(jnp.logical_and(step == 0, part == 0))
    def _():
        peer_barrier("tp", size)
        for offset in range(1, size):
            small_copy(offset, lax.rem(place + offset, size)).start()
        send(0)

    for stage in range(1, size - 1):

        @pl.when(jnp.logical_and(step == min(2 * stage, 2 * local - 1), part == 0))
        def _():
            receive(stage - 1)
            send(stage)

    def flat(ref):
        return ref[...].reshape(ref.shape[0] * ref.shape[1], ref.shape[2])

    def collect(sum_ref, values):
        @pl.when(part == 0)
        def _():
            sum_ref[...] = values

        @pl.when(part == 1)
        def _():
            sum_ref[...] += values

    @pl.when(step < local)
    def _():
        rows = flat(rows_ref)
        collect(first_ref, matmul(flat(gate_grad_ref).T, rows))
        collect(second_ref, matmul(flat(up_grad_ref).T, rows))

        @pl.when(part == 1)
        def _():
            gate_out_ref[...] = first_ref[...].T
            up_out_ref[...] = second_ref[...].T

    @pl.when(step >= local)
    def _():
        collect(down_out_ref, matmul(flat(hidden_ref).T, flat(grad_rows_ref)))

    @pl.when(jnp.logical_and(step == 2 * local - 1, part == 1))
    def _():
        total = small_ref[...]
        for offset in range(1, size):
            small_copy(offset, lax.rem(place + size - offset, size)).wait_recv()
            total = total + small_landed_ref[offset - 1]
        total_ref[...] = total
        receive(size - 2)
        out_ref[...] = block(place)
        for way, rank, to, origin in ways():

            @pl.when(rank > 0)
            def _():
                out_ref[...] += landed_ref[way, size - 2].astype(f32)

        for offset in range(1, size):
            small_copy(offset, lax.rem(place + offset, size)).wait_send()
        for stage in range(size - 1):
            for way, rank, to, origin in ways():

                @pl.when(jnp.logical_and(rank <= stage, rank < size - 1))
                def _():
                    copying(way, stage, to).wait_send()


def run_grads_scatter(values, small, token_slots, grad_slots, gate_grad, up_grad, hidden_rows):
    size = lax.axis_size("tp")
    rows, width = values.shape
    shape = (rows // size, width)
    chunks, local, slots, hidden = hidden_rows.shape
    half = chunks // 2
    early = lambda i, k: jnp.minimum(i, local - 1)
    late = lambda i, k: jnp.maximum(i - local, 0)
    early_part = lambda i, k: jnp.where(i < local, k, 1)
    late_part = lambda i, k: jnp.where(i < local, 0, k)
    wide = lambda at, part: pl.BlockSpec(
        (half, None, slots, width), lambda i, k: (part(i, k), at(i, k), 0, 0)
    )
    thin = lambda at, part: pl.BlockSpec(
        (half, None, slots, hidden), lambda i, k: (part(i, k), at(i, k), 0, 0)
    )
    tall = pl.BlockSpec((None, width, hidden), lambda i, k: (early(i, k), 0, 0))
    fixed = lambda form: pl.BlockSpec(form, lambda i, k: (0,) * len(form))
    return pl.pallas_call(
        functools.partial(grads_scatter, size, local),
        grid=(2 * local, 2),
        in_specs=[
            once(values.shape),
            once(small.shape),
            wide(early, early_part),
            wide(late, late_part),
            thin(early, early_part),
            thin(early, early_part),
            thin(late, late_part),
        ],
        out_specs=[
            fixed(shape),
            fixed(small.shape),
            tall,
            tall,
            pl.BlockSpec((None, hidden, width), lambda i, k: (late(i, k), 0, 0)),
        ],
        out_shape=[
            jax.ShapeDtypeStruct(shape, f32),
            jax.ShapeDtypeStruct(small.shape, f32),
            jax.ShapeDtypeStruct((local, width, hidden), f32),
            jax.ShapeDtypeStruct((local, width, hidden), f32),
            jax.ShapeDtypeStruct((local, hidden, width), f32),
        ],
        scratch_shapes=[
            pltpu.VMEM((2, size - 1, *shape), bf16),
            pltpu.VMEM((2, size - 1, *shape), bf16),
            pltpu.VMEM((size - 1, *small.shape), f32),
            pltpu.VMEM((hidden, width), f32),
            pltpu.VMEM((hidden, width), f32),
            pltpu.SemaphoreType.DMA((2, size - 1)),
            pltpu.SemaphoreType.DMA((2, size - 1)),
            pltpu.SemaphoreType.DMA((size - 1,)),
            pltpu.SemaphoreType.DMA((size - 1,)),
        ],
        compiler_params=pltpu.CompilerParams(
            dimension_semantics=("arbitrary",) * 2,
            collective_id=10,
            has_side_effects=True,
            vmem_limit_bytes=VMEM_BYTES,
        ),
        cost_estimate=pl.CostEstimate(
            flops=6 * chunks * local * slots * width * hidden,
            bytes_accessed=150_000_000,
            transcendentals=0,
        ),
        name="grads_scatter",
    )(values, small, token_slots, grad_slots, gate_grad, up_grad, hidden_rows)


def split_three(values):
    high = values.astype(bf16)
    rest = values - high.astype(f32)
    middle = rest.astype(bf16)
    return (high, middle, (rest - middle.astype(f32)).astype(bf16))


def on_device(
    layer_input,
    token_order,
    doc_lengths,
    expert_routes,
    attn_gain,
    query_weight,
    key_weight,
    value_weight,
    query_gain,
    key_gain,
    out_weight,
    moe_gain,
    router_weight,
    gate_weight,
    up_weight,
    down_weight,
    out_grad,
):
    tp_index = lax.axis_index("tp")
    ctx_size = lax.axis_size("ctx")
    fc_size = lax.axis_size("fsdp") * ctx_size
    fc_index = lax.axis_index("fsdp") * ctx_size + lax.axis_index("ctx")
    tok_count, quarter = layer_input.shape
    share = tok_count // lax.axis_size("tp")
    head_dim = query_gain.shape[0]
    head_width = query_weight.shape[1]
    heads = head_width // head_dim
    scale = head_dim ** (-0.5)
    experts = router_weight.shape[1]
    top = expert_routes.shape[1]
    local_experts = gate_weight.shape[0]
    capacity = tok_count * top * 5 // (4 * experts)
    own_rows = lambda values: lax.dynamic_slice_in_dim(values, tp_index * share, share, 0)
    own_width = lambda values: lax.dynamic_slice_in_dim(values, tp_index * quarter, quarter, 1)

    packed = jnp.concatenate(
        [
            query_weight,
            key_weight,
            value_weight,
            out_weight.T,
            router_weight,
            attn_gain[:, None],
            moe_gain[:, None],
            jnp.zeros((attn_gain.shape[0], EXTRA - experts - 2), bf16),
        ],
        axis=1,
    )
    full = lax.all_gather(packed, ROWS, axis=0, tiled=True)
    expert_ids = jnp.arange(experts, dtype=jnp.int32)
    named = jnp.any(expert_routes[:, :, None] == expert_ids[None, None, :], axis=1)
    earlier = jnp.tri(tok_count, tok_count, -1, dtype=bf16)
    before = matmul(earlier, named.astype(bf16))
    first_slot = (lax.rem(fc_index, CHUNK // tok_count) * capacity).astype(f32)
    ranks = jnp.where(named, before + first_slot, -1.0).astype(bf16)
    input_b = gather_tp(layer_input, True, 0)
    segment, position = doc_places(token_order[0], doc_lengths[0])
    ctx_index = lax.axis_index("ctx")
    seg_columns = jnp.zeros((ctx_size, tok_count), f32)
    for offset in range(ctx_size):
        piece = segment.astype(f32)[None, :]
        if offset > 0:
            pairs = [(at, (at + offset) % ctx_size) for at in range(ctx_size)]
            piece = lax.ppermute(piece, "ctx", pairs)
        origin = lax.rem(ctx_index + ctx_size - offset, ctx_size)
        seg_columns = lax.dynamic_update_slice_in_dim(seg_columns, piece, origin, 0)
    out_grad, full, input_b, seg_columns = lax.optimization_barrier(
        (out_grad, full, input_b, seg_columns)
    )
    grad_rows_b = lax.all_gather(out_grad, "tp", axis=1, tiled=True)
    side = 3 * head_width
    qkv_weight = full[:, :side]
    full_out = full[:, side : side + head_width]
    side = side + head_width
    full_router = full[:, side : side + experts]
    attn_gain_f = full[:, side + experts].astype(f32)
    moe_gain_f = full[:, side + experts + 1].astype(f32)
    width = input_b.shape[1]
    cosine, sine = rope_tables(position, head_dim)
    head_gains = jnp.stack([query_gain, key_gain])
    attn_gain_row = attn_gain_f[None, :]
    normed, inverse_one, heads_pre, query_rows, group_part = run_project(
        input_b,
        attn_gain_row,
        full,
        cosine,
        sine,
        head_gains,
        head_width,
    )
    group = gather_ctx(group_part, 1)
    after_group, group = lax.optimization_barrier((grad_rows_b, group))
    grad_packed = jnp.concatenate(
        [after_group, ranks, jnp.zeros((tok_count, EXTRA - experts), bf16)], axis=1
    )
    grad_all = lax.all_gather(grad_packed, ROWS, axis=0, tiled=True)
    chunks = grad_all.shape[0] // CHUNK
    first_expert = fc_index * local_experts
    local_ranks = lax.dynamic_slice_in_dim(
        grad_all[:, width:], first_expert, local_experts, 1
    ).astype(jnp.int32)
    ids = chunk_order(chunks)
    rank_columns = jnp.stack(
        [
            lax.dynamic_slice_in_dim(local_ranks, ids[at] * CHUNK, CHUNK, 0)
            for at in range(chunks)
        ]
    )
    rank_rows = jnp.transpose(rank_columns, (0, 2, 1))[:, :, None, :]

    seg_rows = segment.astype(f32).reshape(-1, 1, min(tok_count, QUERY_BLOCK))
    seg_columns = seg_columns.reshape(-1, 1)
    attn_b, log_total = run_attend(query_rows, group, seg_rows, seg_columns, heads, scale)
    attn_part = matmul_nt(attn_b, full_out).astype(bf16)
    attn_out = scatter_tp(attn_part, False, 2)
    resid = own_rows(input_b).astype(f32) + attn_out
    inverse_two = norm_scale(resid)
    moe_in = (resid * inverse_two * moe_gain_f).astype(bf16)
    logits = matmul(moe_in, full_router)
    own_named = own_rows(named)
    chosen = jnp.where(own_named, logits, -jnp.inf)
    gates = jax.nn.softmax(chosen, axis=-1)
    own_tokens = gather_tp(
        jnp.concatenate(
            [moe_in, *split_three(gates), jnp.zeros((share, EXTRA - 3 * experts), bf16)], axis=1
        ),
        False,
        3,
    )
    kept, grad_slots, back_sum, out_part = expert_steps(
        ids,
        own_tokens,
        grad_all,
        rank_rows,
        rank_columns,
        first_expert.reshape(1),
        (gate_weight, up_weight, down_weight),
    )
    token_slots, hidden_rows, gate_act_grad, up_act_grad, route_part = kept
    hit = jnp.arange(chunks, dtype=jnp.int32)[:, None] == ids[None, :]
    route_all = jnp.sum(
        jnp.where(hit[:, :, None, None], route_part[None, :, :, 0, :], 0.0), axis=1
    )
    route_all = jnp.transpose(route_all, (1, 0, 2)).reshape(
        local_experts, fc_size, tok_count
    )
    route_all = lax.all_to_all(
        jnp.transpose(route_all, (1, 0, 2)), ROWS, split_axis=0, concat_axis=0, tiled=True
    ).reshape(experts, tok_count)

    back_rows, gate_grad, grad_gate, grad_up, grad_down = run_grads_scatter(
        back_sum, route_all, token_slots, grad_slots, gate_act_grad, up_act_grad, hidden_rows
    )
    parts = own_tokens[:, width : width + 3 * experts].astype(f32)
    all_gates = parts[:, :experts] + parts[:, experts : 2 * experts] + parts[:, 2 * experts :]
    gate_grad = gate_grad.T
    logit_grad = all_gates * (
        gate_grad - jnp.sum(all_gates * gate_grad, axis=-1, keepdims=True)
    )
    grad_router = lax.dot_general(
        own_tokens[:, :width].astype(f32),
        logit_grad,
        (((0,), (0,)), ((), ())),
        precision=highest,
    )
    own_logit_grad = own_rows(logit_grad)
    router_back = lax.dot_general(
        own_logit_grad, full_router.astype(f32), (((1,), (1,)), ((), ())), precision=highest
    )
    moe_in_grad = (
        back_rows + router_back
    )
    resid_norm_grad, gain_terms = norm_back(moe_in_grad, resid, inverse_two, moe_gain_f)
    grad_moe_gain = jnp.sum(gain_terms, axis=0)
    resid_grad = own_rows(grad_rows_b).astype(f32) + resid_norm_grad
    resid_grad_b = gather_tp(resid_grad.astype(bf16), False, 5)

    out_sum = lax.psum_scatter(out_part, ROWS, scatter_dimension=0, tiled=True)

    grad_out = lax.dot_general(
        resid_grad_b, attn_b, (((0,), (0,)), ((), ())), preferred_element_type=f32
    )
    attn_grad = matmul(resid_grad_b, full_out).astype(bf16)
    query_rot_grad, key_part, value_part = run_attend_back(
        query_rows, group, seg_rows, seg_columns, attn_b, log_total, attn_grad, heads, scale
    )
    out_sum, key_part = lax.optimization_barrier((out_sum, key_part))
    out_sum = lax.psum_scatter(out_sum, "tp", scatter_dimension=0, tiled=True).astype(f32)
    group_grad = scatter_ctx(jnp.concatenate([key_part, value_part], axis=1), 6)
    qkv_grad, normed_part, along, attn_terms, head_terms = run_project_back(
        query_rot_grad,
        group_grad,
        heads_pre,
        cosine,
        sine,
        head_gains,
        full,
        input_b,
        inverse_one,
        attn_gain_row,
    )
    along = along[:, 0]
    gains = jnp.concatenate([attn_terms[0], grad_moe_gain, head_terms[0], head_terms[1]])
    normed_grad, gains, along = close_tp(normed_part, gains, along, 7)
    along = along[:, None] / width
    normed_grad, out_sum = lax.optimization_barrier((normed_grad, out_sum))
    layer_sum = resid + out_sum
    layer_output = lax.all_to_all(
        layer_sum.astype(bf16), "tp", split_axis=1, concat_axis=0, tiled=True
    )
    input_quarter = layer_input.astype(f32)
    gain_quarter = lax.dynamic_slice_in_dim(attn_gain_f, tp_index * quarter, quarter, 0)
    grad_input = own_width(resid_grad_b).astype(f32) + inverse_one * (
        normed_grad * gain_quarter - input_quarter * inverse_one * inverse_one * along
    )
    grad_qkv = lax.dot_general(
        normed, qkv_grad, (((0,), (0,)), ((), ())), preferred_element_type=f32
    )
    owned_out = lax.psum_scatter(
        jnp.concatenate(
            [grad_out, grad_router, jnp.zeros((width, EXTRA - experts), f32)], axis=1
        ).astype(bf16),
        ROWS,
        scatter_dimension=0,
        tiled=True,
    )
    (owned_out,) = then(normed_grad, owned_out)
    owned_out = owned_out.astype(f32)
    owned_qkv = lax.psum_scatter(
        grad_qkv.astype(bf16), ROWS, scatter_dimension=0, tiled=True
    ).astype(f32)
    owned_gain = attn_gain.shape[0]
    own_gain = lambda at: lax.dynamic_slice_in_dim(
        gains, at * width + fc_index * owned_gain, owned_gain, 0
    )
    return (
        layer_output,
        grad_input,
        own_gain(0),
        owned_qkv[:, :head_width],
        owned_qkv[:, head_width : 2 * head_width],
        owned_qkv[:, 2 * head_width :],
        gains[2 * width : 2 * width + head_dim],
        gains[2 * width + head_dim :],
        owned_out[:, :head_width].T,
        own_gain(1),
        owned_out[:, head_width : head_width + experts],
        grad_gate,
        grad_up,
        grad_down,
    )


def solution(mesh):
    in_specs = (
        P(("fsdp", "ctx"), "tp"),
        P("fsdp", "ctx"),
        P("fsdp", None),
        P(("fsdp", "ctx"), None),
        P(("fsdp", "ctx")),
        P(("fsdp", "ctx"), "tp"),
        P(("fsdp", "ctx"), "tp"),
        P(("fsdp", "ctx"), "tp"),
        P(),
        P(),
        P("tp", ("fsdp", "ctx")),
        P(("fsdp", "ctx")),
        P(("fsdp", "ctx"), None),
        P(("fsdp", "ctx"), None, "tp"),
        P(("fsdp", "ctx"), None, "tp"),
        P(("fsdp", "ctx"), "tp", None),
        P(("fsdp", "ctx"), "tp"),
    )
    out_specs = (
        P(("fsdp", "ctx"), "tp"),
        P(("fsdp", "ctx"), "tp"),
        P(("fsdp", "ctx")),
        P(("fsdp", "ctx"), "tp"),
        P(("fsdp", "ctx"), "tp"),
        P(("fsdp", "ctx"), "tp"),
        P(),
        P(),
        P("tp", ("fsdp", "ctx")),
        P(("fsdp", "ctx")),
        P(("fsdp", "ctx"), None),
        P(("fsdp", "ctx"), None, "tp"),
        P(("fsdp", "ctx"), None, "tp"),
        P(("fsdp", "ctx"), "tp", None),
    )
    return jax.shard_map(
        on_device, mesh=mesh, in_specs=in_specs, out_specs=out_specs, check_vma=False
    )
```

```python
import functools

import jax
import jax.numpy as jnp
from jax import lax
from jax.experimental import pallas as pl
from jax.experimental.pallas import tpu as pltpu
from jax.sharding import PartitionSpec as P

QUERY_BLOCK = 256
CHUNK = 768
SLOTS = 256
EXTRA = 128
VMEM_BYTES = 60 * 1024 * 1024


epsilon = 1e-05
rope_base = 50000.0
masked_score = -1e30
highest = lax.Precision.HIGHEST
bf16 = jnp.bfloat16
f32 = jnp.float32
ROWS = ("fsdp", "ctx")
ALL = ("fsdp", "ctx", "tp")
MESH = pl.DeviceIdType.MESH


def doc_places(order_row, length_row):
    ends = jnp.cumsum(length_row, dtype=jnp.int32)
    passed = (order_row[:, None] >= ends[None, :]).astype(jnp.int32)
    segment = jnp.sum(passed, axis=1, dtype=jnp.int32)
    start = jnp.sum(passed * length_row[None, :], axis=1, dtype=jnp.int32)
    return (segment, order_row - start)


def rope_tables(position, head_dim):
    half = head_dim // 2
    freqs = rope_base ** (-(jnp.arange(half, dtype=jnp.float32) * (2.0 / head_dim)))
    angles = position.astype(jnp.float32)[:, None] * freqs[None, :]
    cosine, sine = jnp.cos(angles), jnp.sin(angles)
    return jnp.concatenate([cosine, cosine], axis=1), jnp.concatenate([-sine, sine], axis=1)


def norm_scale(values):
    return lax.rsqrt(jnp.mean(values * values, axis=-1, keepdims=True) + epsilon)


def norm_back(incoming, values, inverse, gain):
    scaled = incoming * gain
    value_grad = inverse * (
        scaled - values * inverse * inverse * jnp.mean(scaled * values, axis=-1, keepdims=True)
    )
    return (value_grad, incoming * values * inverse)


def matmul(left, right):
    return jnp.dot(left, right, preferred_element_type=f32)


def matmul_nt(left, right):
    return lax.dot_general(left, right, (((1,), (1,)), ((), ())), preferred_element_type=f32)


def slot_rows(rank_row):
    slots = lax.broadcasted_iota(jnp.int32, (SLOTS, rank_row.shape[1]), 0)
    return slots == rank_row


def slot_columns(rank_column):
    slots = lax.broadcasted_iota(jnp.int32, (rank_column.shape[0], SLOTS), 1)
    return jnp.where(slots == rank_column, 1.0, 0.0).astype(bf16)


def as_one_hot(mask):
    return jnp.where(mask, 1.0, 0.0).astype(bf16)


def select_grads(ids_ref, rank_ref, grad_ref, down_ref, rows_ref, product_ref):
    expert = pl.program_id(1)
    rows = matmul(as_one_hot(slot_rows(rank_ref[...])), grad_ref[...]).astype(bf16)
    rows_ref[...] = rows
    product_ref[...] = matmul_nt(rows, down_ref[expert])


def expert_step(
    expert,
    named,
    rank_ref,
    tokens,
    product_ref,
    gate_ref,
    up_ref,
    await_weights,
    rows_ref,
    hidden_ref,
    gate_grad_ref,
    up_grad_ref,
    route_ref,
    held_ref,
):
    width = rows_ref.shape[1]
    mask = slot_rows(rank_ref[...])
    picked = matmul(as_one_hot(mask), tokens)
    rows = picked[:, :width].astype(bf16)
    rows_ref[...] = rows
    lane = lax.broadcasted_iota(jnp.int32, (SLOTS, EXTRA), 1)
    mine = jnp.logical_and(lax.rem(lane, 32) == named, lane < 96)
    gate = jnp.sum(jnp.where(mine, picked[:, width:], 0.0), axis=1, keepdims=True)
    await_weights()
    gate_act = matmul(rows, gate_ref[expert])
    up_act = matmul(rows, up_ref[expert])
    sigmoid_g = 1.0 / (1.0 + jnp.exp(-gate_act))
    silu_g = gate_act * sigmoid_g
    hidden = silu_g * up_act
    hidden_ref[...] = (gate * hidden).astype(bf16)
    product = product_ref[...]
    route = jnp.sum(hidden.astype(bf16).astype(f32) * product, axis=1, keepdims=True)
    route_ref[...] = jnp.sum(jnp.where(mask, route, 0.0), axis=0, keepdims=True)
    hidden_grad = gate * product
    gate_grad = (
        hidden_grad * up_act * sigmoid_g * (1.0 + gate_act * (1.0 - sigmoid_g))
    ).astype(bf16)
    up_grad = (hidden_grad * silu_g).astype(bf16)
    gate_grad_ref[...] = gate_grad
    up_grad_ref[...] = up_grad
    back = matmul_nt(gate_grad, gate_ref[expert]) + matmul_nt(up_grad, up_ref[expert])
    held_ref[pl.ds(pl.multiple_of(expert * SLOTS, SLOTS), SLOTS), :] = back.astype(bf16)


def chunk_places(column_ref):
    columns = column_ref[...]
    return jnp.concatenate(
        [slot_columns(columns[:, e : e + 1]) for e in range(columns.shape[1])], axis=1
    )


def expert_pass(
    ids_ref,
    first_ref,
    rank_ref,
    column_ref,
    near_ref,
    far_ref,
    product_ref,
    gate_in_ref,
    up_in_ref,
    *refs,
):
    (
        rows_ref,
        hidden_ref,
        gate_grad_ref,
        up_grad_ref,
        route_ref,
        near_back_ref,
        far_back_ref,
        token_ref,
        gate_ref,
        up_ref,
        held_ref,
        back_ref,
        token_sem,
        gate_sem,
        up_sem,
        back_sem,
    ) = refs[-16:]
    chunk, expert = pl.program_id(0), pl.program_id(1)
    local = gate_ref.shape[0]
    width = rows_ref.shape[1]
    tiles = back_sem.shape[1]
    tile = width // tiles
    loads = [
        pltpu.make_async_copy(source, token_ref.at[at], token_sem.at[at])
        for at, source in enumerate((near_ref, far_ref))
    ]

    def weight_load(source, held, sem, at):
        return pltpu.make_async_copy(source.at[at], held.at[at], sem.at[at])

    def back_store(to, at, step):
        columns = pl.ds(step * tile, tile)
        return pltpu.make_async_copy(
            back_ref.at[at, :, columns], to.at[:, columns], back_sem.at[at, step]
        )

    @pl.when(jnp.logical_and(chunk == 0, expert == 0))
    def _():
        loads[0].start()
        for at in range(local):
            weight_load(gate_in_ref, gate_ref, gate_sem, at).start()
            weight_load(up_in_ref, up_ref, up_sem, at).start()
        loads[1].start()
        loads[0].wait()

    @pl.when(jnp.logical_and(chunk == 1, expert == 0))
    def _():
        loads[1].wait()

    def await_weights():
        @pl.when(chunk == 0)
        def _():
            weight_load(gate_in_ref, gate_ref, gate_sem, expert).wait()
            weight_load(up_in_ref, up_ref, up_sem, expert).wait()

    expert_step(
        expert,
        first_ref[0] + expert,
        rank_ref,
        token_ref[chunk],
        product_ref,
        gate_ref,
        up_ref,
        await_weights,
        rows_ref,
        hidden_ref,
        gate_grad_ref,
        up_grad_ref,
        route_ref,
        held_ref,
    )

    @pl.when(expert == local - 1)
    def _():
        places = chunk_places(column_ref)
        for step in range(tiles):
            at = pl.ds(step * tile, tile)
            back_ref[chunk, :, at] = matmul(places, held_ref[:, at]).astype(bf16)

            @pl.when(chunk == 0)
            def _():
                back_store(near_back_ref, 0, step).start()

            @pl.when(chunk == 1)
            def _():
                back_store(far_back_ref, 1, step).start()

    @pl.when(jnp.logical_and(chunk == 1, expert == local - 1))
    def _():
        for step in range(tiles):
            back_store(near_back_ref, 0, step).wait()
            back_store(far_back_ref, 1, step).wait()


def exchange_pass(
    rank_ref,
    column_ref,
    product_ref,
    gate_in_ref,
    up_in_ref,
    down_in_ref,
    own_ref,
    sibling_ref,
    from_across_ref,
    from_other_ref,
    rows_ref,
    hidden_ref,
    gate_grad_ref,
    up_grad_ref,
    route_ref,
    sum_ref,
    out_ref,
    inbox_ref,
    landing_ref,
    token_ref,
    gate_ref,
    up_ref,
    down_ref,
    hidden_held_ref,
    held_ref,
    far_ref,
    beside_ref,
    chip_ref,
    corner_ref,
    token_sem,
    gate_sem,
    up_sem,
    pass_send,
    pass_recv,
    far_send,
    far_recv,
    link_send,
    link_recv,
    store_sem,
    down_sem,
    out_sem,
    landing_sem,
):
    step, expert = pl.program_id(0), pl.program_id(1)
    local = gate_ref.shape[0]
    rows, width = far_ref.shape
    half = rows // 2
    fsdp, ctx = lax.axis_index("fsdp"), lax.axis_index("ctx")
    beside_id = {"fsdp": fsdp + 1 - 2 * lax.rem(fsdp, 2)}
    across_id = {"fsdp": lax.rem(fsdp + 2, 4)}
    other_id = {"ctx": 1 - ctx}
    last = expert == local - 1
    low, high = pl.ds(0, half), pl.ds(half, half)
    sources = (
        inbox_ref.at[0],
        from_across_ref,
        inbox_ref.at[1],
        from_other_ref,
        inbox_ref.at[3],
        inbox_ref.at[2],
        sibling_ref,
        own_ref,
    )

    def token_load(at):
        slot = at % 2
        return pltpu.make_async_copy(sources[at], token_ref.at[slot], token_sem.at[slot])

    def weight_load(source, held, sem, at):
        return pltpu.make_async_copy(source.at[at], held.at[at], sem.at[at])

    def pass_copy(number):
        source, to, peer = (
            (from_across_ref, inbox_ref.at[0], beside_id),
            (from_other_ref, inbox_ref.at[1], beside_id),
            (from_other_ref.at[low], inbox_ref.at[2, low], across_id),
            (from_across_ref.at[high], inbox_ref.at[2, high], other_id),
            (inbox_ref.at[2], inbox_ref.at[3], beside_id),
        )[number]
        return pltpu.make_async_remote_copy(
            src_ref=source,
            dst_ref=to,
            send_sem=pass_send.at[number],
            recv_sem=pass_recv.at[number],
            device_id=peer,
            device_id_type=MESH,
        )

    def far_copy(turn):
        return pltpu.make_async_remote_copy(
            src_ref=far_ref,
            dst_ref=beside_ref.at[turn % 2],
            send_sem=far_send.at[turn],
            recv_sem=far_recv.at[turn],
            device_id=beside_id,
            device_id_type=MESH,
        )

    def link_copy(number):
        source, to, peer = (
            (chip_ref.at[0, high], landing_ref.at[0, high], across_id),
            (chip_ref.at[1, low], landing_ref.at[1, low], other_id),
            (chip_ref.at[2, low], corner_ref.at[0], other_id),
            (chip_ref.at[2, high], corner_ref.at[1], across_id),
            (chip_ref.at[1, high], landing_ref.at[1, high], other_id),
            (chip_ref.at[0, low], landing_ref.at[0, low], across_id),
        )[number]
        return pltpu.make_async_remote_copy(
            src_ref=source,
            dst_ref=to,
            send_sem=link_send.at[number],
            recv_sem=link_recv.at[number],
            device_id=peer,
            device_id_type=MESH,
        )

    @pl.when(jnp.logical_and(step == 0, expert == 0))
    def _():
        barrier = pltpu.get_barrier_semaphore()
        for peer in (beside_id, across_id, other_id):
            pl.semaphore_signal(barrier, inc=1, device_id=peer, device_id_type=MESH)
        pl.semaphore_wait(barrier, 3)
        for number in range(4):
            pass_copy(number).start()
        for at in range(local):
            weight_load(gate_in_ref, gate_ref, gate_sem, at).start()
            weight_load(up_in_ref, up_ref, up_sem, at).start()
        down_load = pltpu.make_async_copy(down_in_ref, down_ref, down_sem)
        down_load.start()
        pass_copy(0).wait_recv()
        token_load(0).start()

    @pl.when(jnp.logical_and(step == 3, expert == 0))
    def _():
        pass_copy(2).wait_recv()
        pass_copy(3).wait_recv()
        pass_copy(4).start()

    for at in range(8):

        @pl.when(jnp.logical_and(step == at, expert == 0))
        def _():
            token_load(at).wait()

        if at < 7:

            @pl.when(jnp.logical_and(step == at, last))
            def _():
                if at == 1:
                    pass_copy(1).wait_recv()
                if at == 3:
                    pass_copy(4).wait_recv()
                token_load(at + 1).start()

    def await_weights():
        @pl.when(step == 0)
        def _():
            weight_load(gate_in_ref, gate_ref, gate_sem, expert).wait()
            weight_load(up_in_ref, up_ref, up_sem, expert).wait()

    first = (fsdp * 2 + ctx) * local

    @pl.when(step < 8)
    def _():
        expert_step(
            expert,
            first + expert,
            rank_ref,
            token_ref[lax.rem(step, 2)],
            product_ref,
            gate_ref,
            up_ref,
            await_weights,
            rows_ref,
            hidden_ref,
            gate_grad_ref,
            up_grad_ref,
            route_ref,
            held_ref,
        )
        hidden_held_ref[step, expert] = hidden_ref[...]

    tile = 512

    def tiles():
        for at in range(0, width, tile):
            yield pl.ds(at, tile)

    def add_half(turn, part, landed):
        total = chip_ref[turn, part, :].astype(f32) + corner_ref[landed].astype(f32)
        chip_ref[turn, part, :] = total.astype(bf16)

    for turn in range(4):

        @pl.when(jnp.logical_and(step == 2 * turn, last))
        def _():
            if turn > 0:
                far_copy(turn - 1).wait_send()
            places = chunk_places(column_ref)
            for at in tiles():
                far_ref[:, at] = matmul(places, held_ref[:, at]).astype(bf16)
            far_copy(turn).start()

        @pl.when(jnp.logical_and(step == 2 * turn + 1, last))
        def _():
            far_copy(turn).wait_recv()
            if turn == 3:
                far_copy(3).wait_send()
            places = chunk_places(column_ref)
            for at in tiles():
                total = matmul(places, held_ref[:, at]) + beside_ref[turn % 2, :, at].astype(f32)
                if turn < 3:
                    chip_ref[turn, :, at] = total.astype(bf16)
                else:
                    far_ref[:, at] = total.astype(bf16)
            if turn < 2:
                link_copy(turn).start()
            if turn == 2:
                link_copy(2).start()
                link_copy(3).start()


    number = step - 8
    turn = number // 2
    chip = lax.rem(fsdp + 2 * (1 - lax.rem(turn, 2)), 4)
    core = chip + (1 - lax.rem(number, 2)) * (1 - 2 * lax.rem(fsdp, 2))
    line = lax.rem(ctx + lax.rem((turn + 1) // 2, 2), 2)
    places_at = (core * 2 + line) * rows
    slot = lax.rem(step, 2)
    columns_of = width // local
    hidden = gate_ref.shape[2]

    def out_store(at, which):
        columns = pl.ds(pl.multiple_of(which * columns_of, columns_of), columns_of)
        return pltpu.make_async_copy(
            token_ref.at[slot, :, columns],
            out_ref.at[pl.ds(pl.multiple_of(at, rows), rows), columns],
            out_sem.at[slot, which],
        )

    @pl.when(step >= 8)
    def _():
        @pl.when(jnp.logical_and(step == 8, expert == 0))
        def _():
            pltpu.make_async_copy(down_in_ref, down_ref, down_sem).wait()

        @pl.when(expert == 0)
        def _():
            columns = column_ref[...]
            for e in range(local):
                held_ref[pl.ds(0, rows), pl.ds(e * hidden, hidden)] = matmul(
                    slot_columns(columns[:, e : e + 1]), hidden_held_ref[number, e]
                ).astype(bf16)

        @pl.when(step >= 10)
        def _():
            out_store(places_at, expert).wait()

        at = pl.ds(pl.multiple_of(expert * columns_of, columns_of), columns_of)
        token_ref[slot, :, at] = matmul(
            held_ref[pl.ds(0, rows), pl.ds(0, local * hidden)], down_ref[:, at]
        ).astype(bf16)
        out_store(places_at, expert).start()

    @pl.when(jnp.logical_and(step == 9, expert == 1))
    def _():
        link_copy(3).wait_recv()
        add_half(1, high, 1)
        link_copy(4).start()
        link_copy(2).wait_recv()
        add_half(0, low, 0)
        link_copy(5).start()

    @pl.when(jnp.logical_and(step == 15, last))
    def _():
        landing = []
        for way, numbers in enumerate(((0, 5), (1, 4))):
            for number in numbers:
                link_copy(number).wait_recv()
            copy = pltpu.make_async_copy(
                landing_ref.at[way], beside_ref.at[way], landing_sem.at[way]
            )
            copy.start()
            landing.append(copy)
        for copy in landing:
            copy.wait()
        for part in (low, high):
            held_ref[part, :] = (
                far_ref[part, :].astype(f32)
                + beside_ref[0, part, :].astype(f32)
                + beside_ref[1, part, :].astype(f32)
            ).astype(bf16)
        store = pltpu.make_async_copy(held_ref.at[pl.ds(0, rows)], sum_ref, store_sem)
        store.start()
        for number in range(5):
            pass_copy(number).wait_send()
        for number in range(6):
            link_copy(number).wait_send()
        for other_slot in (0, 1):
            for which in range(local):
                columns = pl.ds(which * columns_of, columns_of)
                pltpu.make_async_copy(
                    token_ref.at[other_slot, :, columns],
                    out_ref.at[pl.ds(0, rows), columns],
                    out_sem.at[other_slot, which],
                ).wait()
        store.wait()


def expert_sums(ids_ref, column_ref, hidden_ref, down_ref, out_ref):
    columns = column_ref[...]
    dense = [
        matmul(slot_columns(columns[:, e : e + 1]), hidden_ref[e]).astype(bf16)
        for e in range(columns.shape[1])
    ]
    out_ref[...] = matmul(jnp.concatenate(dense, axis=1), down_ref[...]).astype(bf16)


def params(dims):
    return pltpu.CompilerParams(
        dimension_semantics=("arbitrary",) * dims, vmem_limit_bytes=VMEM_BYTES
    )


def once(shape):
    return pl.BlockSpec(
        shape, lambda *ids: (0,) * len(shape), pipeline_mode=pl.Buffered(1)
    )


def run_select_grads(ids, rank_rows, grad_all, down_weight):
    chunks, local = rank_rows.shape[:2]
    hidden, width = down_weight.shape[1:]
    slots = chunks * local * SLOTS
    place = lambda g, e, ids: (g, e, 0, 0)
    return pl.pallas_call(
        select_grads,
        grid_spec=pltpu.PrefetchScalarGridSpec(
            num_scalar_prefetch=1,
            grid=(chunks, local),
            in_specs=[
                pl.BlockSpec((None, None, 1, CHUNK), place),
                pl.BlockSpec((CHUNK, width), lambda g, e, ids: (ids[g], 0)),
                once(down_weight.shape),
            ],
            out_specs=[
                pl.BlockSpec((None, None, SLOTS, width), place),
                pl.BlockSpec((None, None, SLOTS, hidden), place),
            ],
        ),
        out_shape=[
            jax.ShapeDtypeStruct((chunks, local, SLOTS, width), bf16),
            jax.ShapeDtypeStruct((chunks, local, SLOTS, hidden), f32),
        ],
        compiler_params=params(2),
        cost_estimate=pl.CostEstimate(
            flops=2 * slots * width * (CHUNK + hidden),
            bytes_accessed=2 * (chunks * CHUNK + slots) * width,
            transcendentals=0,
        ),
        name="select_grads",
    )(ids, rank_rows, grad_all, down_weight)


def run_exchange_pass(rank_rows, rank_columns, product, weights, sources):
    gate_weight, up_weight, down_weight = weights
    chunks, local = rank_rows.shape[:2]
    width, hidden = gate_weight.shape[1:]
    slots = chunks * local * SLOTS
    flat_down = down_weight.reshape(local * hidden, width)

    def per_expert(g, e):
        return (jnp.minimum(g, chunks - 1), jnp.where(g < chunks, e, local - 1), 0, 0)

    narrow = pl.BlockSpec((None, None, SLOTS, hidden), per_expert)
    anywhere = pl.BlockSpec(memory_space=pl.ANY)
    half = (2, CHUNK // 2, width)
    narrow_shape = jax.ShapeDtypeStruct((chunks, local, SLOTS, hidden), bf16)
    outs = pl.pallas_call(
        exchange_pass,
        grid=(2 * chunks, local),
        in_specs=[
            pl.BlockSpec((None, None, 1, CHUNK), per_expert),
            pl.BlockSpec((None, CHUNK, local), lambda g, e: (lax.rem(g, chunks), 0, 0)),
            narrow,
            *[anywhere] * 7,
        ],
        out_specs=[
            pl.BlockSpec((None, None, SLOTS, width), per_expert),
            narrow,
            narrow,
            narrow,
            pl.BlockSpec((None, None, 1, CHUNK), per_expert),
            *[anywhere] * 4,
        ],
        out_shape=[
            jax.ShapeDtypeStruct((chunks, local, SLOTS, width), bf16),
            narrow_shape,
            narrow_shape,
            narrow_shape,
            jax.ShapeDtypeStruct((chunks, local, 1, CHUNK), f32),
            jax.ShapeDtypeStruct((CHUNK, width), bf16),
            jax.ShapeDtypeStruct((chunks * CHUNK, width), bf16),
            jax.ShapeDtypeStruct((4, *sources[0].shape), bf16),
            jax.ShapeDtypeStruct((2, CHUNK, width), bf16),
        ],
        scratch_shapes=[
            pltpu.VMEM((2, CHUNK, width + EXTRA), bf16),
            pltpu.VMEM(gate_weight.shape, bf16),
            pltpu.VMEM(up_weight.shape, bf16),
            pltpu.VMEM(flat_down.shape, bf16),
            pltpu.VMEM((chunks, local, SLOTS, hidden), bf16),
            pltpu.VMEM((local * SLOTS, width), bf16),
            pltpu.VMEM((CHUNK, width), bf16),
            pltpu.VMEM((2, CHUNK, width), bf16),
            pltpu.VMEM((3, CHUNK, width), bf16),
            pltpu.VMEM(half, bf16),
            pltpu.SemaphoreType.DMA((2,)),
            pltpu.SemaphoreType.DMA((local,)),
            pltpu.SemaphoreType.DMA((local,)),
            pltpu.SemaphoreType.DMA((5,)),
            pltpu.SemaphoreType.DMA((5,)),
            pltpu.SemaphoreType.DMA((4,)),
            pltpu.SemaphoreType.DMA((4,)),
            pltpu.SemaphoreType.DMA((6,)),
            pltpu.SemaphoreType.DMA((6,)),
            pltpu.SemaphoreType.DMA,
            pltpu.SemaphoreType.DMA,
            pltpu.SemaphoreType.DMA((2, local)),
            pltpu.SemaphoreType.DMA((2,)),
        ],
        compiler_params=pltpu.CompilerParams(
            dimension_semantics=("arbitrary",) * 2,
            collective_id=9,
            has_side_effects=True,
            vmem_limit_bytes=VMEM_BYTES,
        ),
        cost_estimate=pl.CostEstimate(
            flops=2 * slots * width * (2 * CHUNK + 4 * hidden),
            bytes_accessed=2 * (12 * CHUNK + slots) * width,
            transcendentals=slots * hidden,
        ),
        name="exchange_pass",
    )(rank_rows, rank_columns, product, gate_weight, up_weight, flat_down, *sources)
    return outs[:5], outs[5], outs[6]


def run_expert_pass(
    ids, first, rank_rows, rank_columns, near, far, product, gate_weight, up_weight, kept
):
    chunks, local = rank_rows.shape[:2]
    width, hidden = gate_weight.shape[1:]
    slots = 2 * local * SLOTS
    per_expert = lambda g, e, ids: (ids[g], e, 0, 0)
    narrow = pl.BlockSpec((None, None, SLOTS, hidden), per_expert)
    in_specs = [
        pl.BlockSpec(memory_space=pltpu.SMEM),
        pl.BlockSpec((None, None, 1, CHUNK), per_expert),
        pl.BlockSpec((None, CHUNK, local), lambda g, e, ids: (ids[g], 0, 0)),
        pl.BlockSpec(memory_space=pl.ANY),
        pl.BlockSpec(memory_space=pl.ANY),
        narrow,
        pl.BlockSpec(memory_space=pl.ANY),
        pl.BlockSpec(memory_space=pl.ANY),
    ]
    kept_shapes = [
        jax.ShapeDtypeStruct((chunks, local, SLOTS, width), bf16),
        jax.ShapeDtypeStruct((chunks, local, SLOTS, hidden), bf16),
        jax.ShapeDtypeStruct((chunks, local, SLOTS, hidden), bf16),
        jax.ShapeDtypeStruct((chunks, local, SLOTS, hidden), bf16),
        jax.ShapeDtypeStruct((chunks, local, 1, CHUNK), f32),
    ]
    outs = pl.pallas_call(
        expert_pass,
        grid_spec=pltpu.PrefetchScalarGridSpec(
            num_scalar_prefetch=1,
            grid=(2, local),
            in_specs=in_specs + [pl.BlockSpec(memory_space=pl.ANY)] * len(kept),
            out_specs=[
                pl.BlockSpec((None, None, SLOTS, width), per_expert),
                narrow,
                narrow,
                narrow,
                pl.BlockSpec((None, None, 1, CHUNK), per_expert),
                pl.BlockSpec(memory_space=pl.ANY),
                pl.BlockSpec(memory_space=pl.ANY),
            ],
            scratch_shapes=[
                pltpu.VMEM((2, CHUNK, width + EXTRA), bf16),
                pltpu.VMEM(gate_weight.shape, bf16),
                pltpu.VMEM(up_weight.shape, bf16),
                pltpu.VMEM((local * SLOTS, width), bf16),
                pltpu.VMEM((2, CHUNK, width), bf16),
                pltpu.SemaphoreType.DMA((2,)),
                pltpu.SemaphoreType.DMA((local,)),
                pltpu.SemaphoreType.DMA((local,)),
                pltpu.SemaphoreType.DMA((2, 4)),
            ],
        ),
        out_shape=kept_shapes + [jax.ShapeDtypeStruct((CHUNK, width), bf16)] * 2,
        input_output_aliases={9 + at: at for at in range(len(kept))},
        compiler_params=params(2),
        cost_estimate=pl.CostEstimate(
            flops=2 * slots * width * (2 * CHUNK + 4 * hidden),
            bytes_accessed=2 * (4 * CHUNK + slots) * width,
            transcendentals=slots * hidden,
        ),
        name="expert_pass",
    )(ids, first, rank_rows, rank_columns, near, far, product, gate_weight, up_weight, *kept)
    return outs[:5], outs[5], outs[6]


def run_expert_sums(ids, rank_columns, hidden_rows, down_weight):
    chunks, local, unused, hidden = hidden_rows.shape
    width = down_weight.shape[2]
    flat = down_weight.reshape(local * hidden, width)
    return pl.pallas_call(
        expert_sums,
        grid_spec=pltpu.PrefetchScalarGridSpec(
            num_scalar_prefetch=1,
            grid=(chunks,),
            in_specs=[
                pl.BlockSpec((None, CHUNK, local), lambda g, ids: (g, 0, 0)),
                pl.BlockSpec((None, local, SLOTS, hidden), lambda g, ids: (g, 0, 0, 0)),
                once(flat.shape),
            ],
            out_specs=pl.BlockSpec((CHUNK, width), lambda g, ids: (ids[g], 0)),
        ),
        out_shape=jax.ShapeDtypeStruct((chunks * CHUNK, width), bf16),
        compiler_params=params(1),
        cost_estimate=pl.CostEstimate(
            flops=2 * chunks * CHUNK * local * hidden * (width + SLOTS),
            bytes_accessed=2 * chunks * CHUNK * width,
            transcendentals=0,
        ),
        name="expert_sums",
    )(ids, rank_columns, hidden_rows, flat)


def line_barrier(size):
    place = lax.axis_index("tp")
    barrier = pltpu.get_barrier_semaphore()

    @pl.when(place > 0)
    def _():
        pl.semaphore_signal(barrier, inc=1, device_id={"tp": place - 1}, device_id_type=MESH)

    @pl.when(place < size - 1)
    def _():
        pl.semaphore_signal(barrier, inc=1, device_id={"tp": place + 1}, device_id_type=MESH)

    has_left = jnp.where(place > 0, 1, 0)
    has_right = jnp.where(place < size - 1, 1, 0)
    pl.semaphore_wait(barrier, has_left + has_right)


def line_gather(size, columns, in_ref, out_ref, own_sem, send_sem, recv_sem):
    place = lax.axis_index("tp")
    extent = in_ref.shape[1] if columns else in_ref.shape[0]

    def block(index):
        at = pl.ds(pl.multiple_of(index * extent, extent), extent)
        return out_ref.at[:, at] if columns else out_ref.at[at, :]

    line_barrier(size)
    own = pltpu.make_async_copy(in_ref, block(place), own_sem)
    own.start()

    def sending(way, step):
        source = place - step if way == 0 else place + step
        to = place + 1 if way == 0 else place - 1
        return pltpu.make_async_remote_copy(
            src_ref=in_ref if step == 0 else block(source),
            dst_ref=block(source),
            send_sem=send_sem.at[way, step],
            recv_sem=recv_sem.at[way, step],
            device_id={"tp": to},
            device_id_type=MESH,
        )

    def sends(way, step):
        if way == 0:
            return jnp.logical_and(place >= step, place < size - 1)
        return jnp.logical_and(place + step < size, place > 0)

    def receiving(way, step):
        source = place - 1 - step if way == 0 else place + 1 + step
        origin = place - 1 if way == 0 else place + 1
        return pltpu.make_async_remote_copy(
            src_ref=block(source),
            dst_ref=block(source),
            send_sem=send_sem.at[way, step],
            recv_sem=recv_sem.at[way, step],
            device_id={"tp": origin},
            device_id_type=MESH,
        )

    def receives(way, step):
        return place > step if way == 0 else place + 1 + step < size

    for step in range(size - 1):
        for way in (0, 1):

            @pl.when(sends(way, step))
            def _():
                sending(way, step).start()

        for way in (0, 1):

            @pl.when(receives(way, step))
            def _():
                receiving(way, step).wait_recv()

    for step in range(size - 1):
        for way in (0, 1):

            @pl.when(sends(way, step))
            def _():
                sending(way, step).wait_send()

    own.wait()


def line_scatter(
    size, columns, in_ref, out_ref, staged_ref, landed_ref, send_sem, recv_sem, stages=()
):
    place = lax.axis_index("tp")
    extent = out_ref.shape[1] if columns else out_ref.shape[0]

    def block(index):
        at = pl.ds(pl.multiple_of(index * extent, extent), extent)
        values = in_ref[:, at] if columns else in_ref[at, :]
        return values.astype(f32)

    if not stages:
        line_barrier(size)

    def copying(way, step, to):
        return pltpu.make_async_remote_copy(
            src_ref=staged_ref.at[way, step],
            dst_ref=landed_ref.at[way, step],
            send_sem=send_sem.at[way, step],
            recv_sem=recv_sem.at[way, step],
            device_id={"tp": to},
            device_id_type=MESH,
        )

    for step in range(size - 1):
        for way in (0, 1):
            rank = place if way == 0 else size - 1 - place
            target = size - 1 - step + place if way == 0 else place - (size - 1 - step)
            to = place + 1 if way == 0 else place - 1
            active = jnp.logical_and(rank <= step, rank < size - 1)

            @pl.when(active)
            def _():
                values = block(target)
                if step == 0:
                    staged_ref[way, step] = values.astype(bf16)
                else:

                    @pl.when(rank == 0)
                    def _():
                        staged_ref[way, step] = values.astype(bf16)

                    @pl.when(rank > 0)
                    def _():
                        landed = landed_ref[way, step - 1].astype(f32)
                        staged_ref[way, step] = (values + landed).astype(bf16)

                copying(way, step, to).start()

        if step < len(stages):
            stages[step]()

        for way in (0, 1):
            rank = place if way == 0 else size - 1 - place
            origin = place - 1 if way == 0 else place + 1

            @pl.when(jnp.logical_and(rank > 0, rank - 1 <= step))
            def _():
                copying(way, step, origin).wait_recv()

    for stage in stages[size - 1 :]:
        stage()
    out_ref[...] = block(place)
    for way in (0, 1):
        rank = place if way == 0 else size - 1 - place

        @pl.when(rank > 0)
        def _():
            out_ref[...] += landed_ref[way, size - 2].astype(f32)

    for step in range(size - 1):
        for way in (0, 1):
            rank = place if way == 0 else size - 1 - place
            to = place + 1 if way == 0 else place - 1

            @pl.when(jnp.logical_and(rank <= step, rank < size - 1))
            def _():
                copying(way, step, to).wait_send()


def closing_sums(
    sizes,
    narrow,
    in_ref,
    small_ref,
    out_ref,
    every_ref,
    line_ref,
    staged_ref,
    landed_ref,
    total_ref,
    small_tp_ref,
    small_ctx_ref,
    small_fsdp_ref,
    send_sem,
    recv_sem,
    small_send_sem,
    small_recv_sem,
):
    axes = ("tp", "ctx", "fsdp")
    barrier = pltpu.get_barrier_semaphore()
    for axis, size in zip(axes, sizes):
        place = lax.axis_index(axis)
        for offset in range(1, size):
            peer = lax.rem(place + offset, size)
            pl.semaphore_signal(barrier, inc=1, device_id={axis: peer}, device_id_type=MESH)
    pl.semaphore_wait(barrier, sum(sizes) - len(sizes))
    landings = (small_tp_ref, small_ctx_ref, small_fsdp_ref)

    def copying(axis, offset, peer):
        return pltpu.make_async_remote_copy(
            src_ref=small_ref if axis == 0 else total_ref.at[axis - 1],
            dst_ref=landings[axis].at[offset - 1],
            send_sem=small_send_sem.at[axis, offset - 1],
            recv_sem=small_recv_sem.at[axis, offset - 1],
            device_id={axes[axis]: peer},
            device_id_type=MESH,
        )

    def each(axis):
        size, place = sizes[axis], lax.axis_index(axes[axis])
        for offset in range(1, size):
            yield (
                offset,
                lax.rem(place + offset, size),
                lax.rem(place + size - offset, size),
            )

    def start(axis):
        for offset, to, origin in each(axis):
            copying(axis, offset, to).start()

    def finish(axis):
        total = small_ref[...] if axis == 0 else total_ref[axis - 1]
        for offset, to, origin in each(axis):
            copying(axis, offset, origin).wait_recv()
            total = total + landings[axis][offset - 1]
        for offset, to, origin in each(axis):
            copying(axis, offset, to).wait_send()
        return total

    def first():
        start(0)

    def second():
        total = finish(0)
        total_ref[0] = total
        line_ref[...] = total[:, narrow:]
        start(1)

    def third():
        total_ref[1] = finish(1)
        start(2)

    def last():
        every_ref[...] = finish(2)[:, :narrow]

    line_scatter(
        sizes[0],
        True,
        in_ref,
        out_ref,
        staged_ref,
        landed_ref,
        send_sem,
        recv_sem,
        stages=(first, second, third, last),
    )


def peer_barrier(axis, size):
    place = lax.axis_index(axis)
    barrier = pltpu.get_barrier_semaphore()
    for offset in range(1, size):
        peer = lax.rem(place + offset, size)
        pl.semaphore_signal(barrier, inc=1, device_id={axis: peer}, device_id_type=MESH)
    pl.semaphore_wait(barrier, size - 1)


def peer_gather(size, in_ref, out_ref, own_sem, send_sem, recv_sem):
    place = lax.axis_index("ctx")
    rows = in_ref.shape[0]

    def block(index):
        return out_ref.at[pl.ds(pl.multiple_of(index * rows, rows), rows), :]

    def copying(offset, source, peer):
        return pltpu.make_async_remote_copy(
            src_ref=in_ref,
            dst_ref=block(source),
            send_sem=send_sem.at[offset - 1],
            recv_sem=recv_sem.at[offset - 1],
            device_id={"ctx": peer},
            device_id_type=MESH,
        )

    peer_barrier("ctx", size)
    own = pltpu.make_async_copy(in_ref, block(place), own_sem)
    own.start()
    for offset in range(1, size):
        copying(offset, place, lax.rem(place + offset, size)).start()
    for offset in range(1, size):
        origin = lax.rem(place + size - offset, size)
        copying(offset, origin, origin).wait_recv()
    for offset in range(1, size):
        copying(offset, place, lax.rem(place + offset, size)).wait_send()
    own.wait()


def peer_scatter(size, in_ref, out_ref, landed_ref, send_sem, recv_sem):
    place = lax.axis_index("ctx")
    rows = out_ref.shape[0]

    def at(index):
        return pl.ds(pl.multiple_of(index * rows, rows), rows)

    def copying(offset, peer):
        return pltpu.make_async_remote_copy(
            src_ref=in_ref.at[at(peer), :],
            dst_ref=landed_ref.at[offset - 1],
            send_sem=send_sem.at[offset - 1],
            recv_sem=recv_sem.at[offset - 1],
            device_id={"ctx": peer},
            device_id_type=MESH,
        )

    peer_barrier("ctx", size)
    for offset in range(1, size):
        copying(offset, lax.rem(place + offset, size)).start()
    total = in_ref[at(place), :].astype(f32)
    for offset in range(1, size):
        origin = lax.rem(place + size - offset, size)
        copying(offset, origin).wait_recv()
        total = total + landed_ref[offset - 1].astype(f32)
    out_ref[...] = total.astype(bf16)
    for offset in range(1, size):
        copying(offset, lax.rem(place + offset, size)).wait_send()


def remote_params(number):
    return pltpu.CompilerParams(
        collective_id=number, has_side_effects=True, vmem_limit_bytes=VMEM_BYTES
    )


def gather_tp(values, columns, number):
    size = lax.axis_size("tp")
    rows, width = values.shape
    shape = (rows, size * width) if columns else (size * rows, width)
    return pl.pallas_call(
        functools.partial(line_gather, size, columns),
        in_specs=[pl.BlockSpec(memory_space=pl.ANY)],
        out_specs=pl.BlockSpec(memory_space=pl.ANY),
        out_shape=jax.ShapeDtypeStruct(shape, values.dtype),
        scratch_shapes=[
            pltpu.SemaphoreType.DMA,
            pltpu.SemaphoreType.DMA((2, size - 1)),
            pltpu.SemaphoreType.DMA((2, size - 1)),
        ],
        compiler_params=remote_params(number),
        cost_estimate=pl.CostEstimate(flops=0, bytes_accessed=150_000_000, transcendentals=0),
        name="gather_tp",
    )(values)


def scatter_tp(values, columns, number):
    size = lax.axis_size("tp")
    rows, width = values.shape
    shape = (rows, width // size) if columns else (rows // size, width)
    return pl.pallas_call(
        functools.partial(line_scatter, size, columns),
        in_specs=[pl.BlockSpec(memory_space=pltpu.VMEM)],
        out_specs=pl.BlockSpec(memory_space=pltpu.VMEM),
        out_shape=jax.ShapeDtypeStruct(shape, f32),
        scratch_shapes=[
            pltpu.VMEM((2, size - 1, *shape), bf16),
            pltpu.VMEM((2, size - 1, *shape), bf16),
            pltpu.SemaphoreType.DMA((2, size - 1)),
            pltpu.SemaphoreType.DMA((2, size - 1)),
        ],
        compiler_params=remote_params(number),
        cost_estimate=pl.CostEstimate(flops=0, bytes_accessed=150_000_000, transcendentals=0),
        name="scatter_tp",
    )(values)


def close_tp(values, gains, along, number):
    sizes = tuple(lax.axis_size(axis) for axis in ("tp", "ctx", "fsdp"))
    rows, width = values.shape
    shape = (rows, width // sizes[0])
    pad = lambda row: jnp.pad(row, (0, -row.shape[0] % 1024)).reshape(8, -1)
    gains_b, along_b = pad(gains), pad(along)
    narrow, wide = gains_b.shape[1], along_b.shape[1]
    small = jnp.concatenate([gains_b, along_b], axis=1)
    peers = max(sizes) - 1
    out, every, line = pl.pallas_call(
        functools.partial(closing_sums, sizes, narrow),
        in_specs=[pl.BlockSpec(memory_space=pltpu.VMEM)] * 2,
        out_specs=[pl.BlockSpec(memory_space=pltpu.VMEM)] * 3,
        out_shape=[
            jax.ShapeDtypeStruct(shape, f32),
            jax.ShapeDtypeStruct((8, narrow), f32),
            jax.ShapeDtypeStruct((8, wide), f32),
        ],
        scratch_shapes=[
            pltpu.VMEM((2, sizes[0] - 1, *shape), bf16),
            pltpu.VMEM((2, sizes[0] - 1, *shape), bf16),
            pltpu.VMEM((2, *small.shape), f32),
            *[pltpu.VMEM((size - 1, *small.shape), f32) for size in sizes],
            pltpu.SemaphoreType.DMA((2, sizes[0] - 1)),
            pltpu.SemaphoreType.DMA((2, sizes[0] - 1)),
            pltpu.SemaphoreType.DMA((3, peers)),
            pltpu.SemaphoreType.DMA((3, peers)),
        ],
        compiler_params=remote_params(number),
        cost_estimate=pl.CostEstimate(flops=0, bytes_accessed=150_000_000, transcendentals=0),
        name="close_tp",
    )(values, small)
    return out, every.reshape(-1)[: gains.shape[0]], line.reshape(-1)[: along.shape[0]]


def gather_ctx(values, number):
    size = lax.axis_size("ctx")
    rows, width = values.shape
    return pl.pallas_call(
        functools.partial(peer_gather, size),
        in_specs=[pl.BlockSpec(memory_space=pl.ANY)],
        out_specs=pl.BlockSpec(memory_space=pl.ANY),
        out_shape=jax.ShapeDtypeStruct((size * rows, width), values.dtype),
        scratch_shapes=[
            pltpu.SemaphoreType.DMA,
            pltpu.SemaphoreType.DMA((size - 1,)),
            pltpu.SemaphoreType.DMA((size - 1,)),
        ],
        compiler_params=remote_params(number),
        cost_estimate=pl.CostEstimate(flops=0, bytes_accessed=100_000_000, transcendentals=0),
        name="gather_ctx",
    )(values)


def scatter_ctx(values, number):
    size = lax.axis_size("ctx")
    rows, width = values.shape
    shape = (rows // size, width)
    return pl.pallas_call(
        functools.partial(peer_scatter, size),
        in_specs=[pl.BlockSpec(memory_space=pltpu.VMEM)],
        out_specs=pl.BlockSpec(memory_space=pltpu.VMEM),
        out_shape=jax.ShapeDtypeStruct(shape, values.dtype),
        scratch_shapes=[
            pltpu.VMEM((size - 1, *shape), bf16),
            pltpu.SemaphoreType.DMA((size - 1,)),
            pltpu.SemaphoreType.DMA((size - 1,)),
        ],
        compiler_params=remote_params(number),
        cost_estimate=pl.CostEstimate(flops=0, bytes_accessed=100_000_000, transcendentals=0),
        name="scatter_ctx",
    )(values)


def attend(scale, query_ref, key_ref, value_ref, seg_row_ref, seg_column_ref, out_ref, total_ref):
    scores = matmul_nt(key_ref[...], query_ref[...]) * scale
    scores = jnp.where(seg_column_ref[...] == seg_row_ref[...], scores, masked_score)
    most = jnp.max(scores, axis=0, keepdims=True)
    probs = jnp.exp(scores - most)
    total = jnp.sum(probs, axis=0, keepdims=True)
    mixed = matmul(value_ref[...].T, probs.astype(bf16)) / total
    out_ref[...] = mixed.T.astype(bf16)
    total_ref[...] = most + jnp.log(total)


def attend_back(
    scale,
    query_ref,
    key_ref,
    value_ref,
    seg_row_ref,
    seg_column_ref,
    out_ref,
    total_ref,
    grad_ref,
    query_grad_ref,
    key_grad_ref,
    value_grad_ref,
    key_sum_ref,
    value_sum_ref,
):
    step = pl.program_id(1)
    query, key, grad = query_ref[...], key_ref[...], grad_ref[...]
    scores = matmul_nt(key, query) * scale
    scores = jnp.where(seg_column_ref[...] == seg_row_ref[...], scores, masked_score)
    probs = jnp.exp(scores - total_ref[...])
    products = grad.astype(f32) * out_ref[...].astype(f32)
    delta = jnp.sum(products.T, axis=0, keepdims=True)
    score_grad = (probs * (matmul_nt(value_ref[...], grad) - delta)).astype(bf16)
    query_grad_ref[...] = (matmul(key.T, score_grad) * scale).T
    key_part = matmul(score_grad, query) * scale
    value_part = matmul(probs.astype(bf16), grad)

    @pl.when(step == 0)
    def _():
        key_sum_ref[...] = key_part
        value_sum_ref[...] = value_part

    @pl.when(step > 0)
    def _():
        key_sum_ref[...] += key_part
        value_sum_ref[...] += value_part

    @pl.when(step == pl.num_programs(1) - 1)
    def _():
        key_grad_ref[...] = key_sum_ref[...].astype(bf16)
        value_grad_ref[...] = value_sum_ref[...].astype(bf16)


def attention_specs(rows, keys, heads, head_dim):
    block = min(rows, QUERY_BLOCK)
    query = pl.BlockSpec((block, head_dim), lambda h, i: (i, h))
    return (
        (heads, rows // block),
        [
            query,
            pl.BlockSpec((keys, head_dim), lambda h, i: (0, h)),
            pl.BlockSpec((keys, head_dim), lambda h, i: (0, h + heads)),
            pl.BlockSpec((None, 1, block), lambda h, i: (i, 0, 0)),
            pl.BlockSpec((keys, 1), lambda h, i: (0, 0)),
        ],
        query,
        pl.BlockSpec((None, None, 1, block), lambda h, i: (h, i, 0, 0)),
        pl.BlockSpec((keys, head_dim), lambda h, i: (0, h)),
    )


def run_attend(query_b, group, seg_rows, seg_columns, heads, scale):
    rows, keys = query_b.shape[0], group.shape[0]
    head_dim = query_b.shape[1] // heads
    grid, specs, query, total, unused = attention_specs(rows, keys, heads, head_dim)
    work = heads * rows * keys
    return pl.pallas_call(
        functools.partial(attend, scale),
        grid=grid,
        in_specs=specs,
        out_specs=[query, total],
        out_shape=[
            jax.ShapeDtypeStruct(query_b.shape, bf16),
            jax.ShapeDtypeStruct((*grid, 1, rows // grid[1]), f32),
        ],
        compiler_params=params(2),
        cost_estimate=pl.CostEstimate(
            flops=4 * work * head_dim, bytes_accessed=8 * query_b.size, transcendentals=work
        ),
        name="attend",
    )(query_b, group, group, seg_rows, seg_columns)


def run_attend_back(query_b, group, seg_rows, seg_columns, out_b, total, grad_b, heads, scale):
    rows, keys = query_b.shape[0], group.shape[0]
    head_dim = query_b.shape[1] // heads
    grid, specs, query, total_spec, key = attention_specs(rows, keys, heads, head_dim)
    work = heads * rows * keys
    return pl.pallas_call(
        functools.partial(attend_back, scale),
        grid=grid,
        in_specs=[*specs, query, total_spec, query],
        out_specs=[query, key, key],
        out_shape=[
            jax.ShapeDtypeStruct(query_b.shape, f32),
            jax.ShapeDtypeStruct((keys, query_b.shape[1]), bf16),
            jax.ShapeDtypeStruct((keys, query_b.shape[1]), bf16),
        ],
        scratch_shapes=[pltpu.VMEM((keys, head_dim), f32)] * 2,
        compiler_params=params(2),
        cost_estimate=pl.CostEstimate(
            flops=10 * work * head_dim, bytes_accessed=16 * query_b.size, transcendentals=work
        ),
        name="attend_back",
    )(query_b, group, group, seg_rows, seg_columns, out_b, total, grad_b)


def beside(values):
    return lax.ppermute(values, "fsdp", [(0, 1), (1, 0), (2, 3), (3, 2)])


def across(values):
    return lax.ppermute(values, "fsdp", [(0, 2), (1, 3), (2, 0), (3, 1)])


def other(values):
    return lax.ppermute(values, "ctx", [(0, 1), (1, 0)])


def added(*values):
    total = values[0].astype(f32)
    for value in values[1:]:
        total = total + value.astype(f32)
    return total.astype(bf16)


def then(first, *values):
    return lax.optimization_barrier((first, *values))[1:]


def by_chips():
    return lax.axis_size("fsdp") == 4 and lax.axis_size("ctx") == 2


def chunk_order(chunks):
    if not by_chips():
        return jnp.arange(chunks, dtype=jnp.int32)
    fsdp, ctx = lax.axis_index("fsdp"), lax.axis_index("ctx")
    sibling = fsdp + 1 - 2 * lax.rem(fsdp, 2)
    flip = lambda core: lax.rem(core + 2, 4)
    places = (
        (flip(sibling), ctx),
        (flip(fsdp), ctx),
        (sibling, 1 - ctx),
        (fsdp, 1 - ctx),
        (flip(sibling), 1 - ctx),
        (flip(fsdp), 1 - ctx),
        (sibling, ctx),
        (fsdp, ctx),
    )
    return jnp.stack([jnp.asarray(2 * f + c, jnp.int32) for f, c in places])


def expert_steps(ids, own_tokens, grad_all, rank_rows, rank_columns, first, weights):
    gate_weight, up_weight, down_weight = weights
    chunks = rank_rows.shape[0]

    def one_pass(at, near, far, product, kept):
        return run_expert_pass(
            jnp.array([at, at + 1], jnp.int32),
            first,
            rank_rows,
            rank_columns,
            near,
            far,
            product,
            gate_weight,
            up_weight,
            kept,
        )

    if not by_chips():
        token_all = lax.all_gather(own_tokens, ROWS, axis=0, tiled=True)
        blocks = token_all.reshape(chunks, CHUNK, -1)
        grad_slots, product = run_select_grads(ids, rank_rows, grad_all, down_weight)
        kept, backs = (), []
        for at in range(0, chunks, 2):
            kept, near, far = one_pass(at, blocks[at], blocks[at + 1], product, kept)
            backs += [near, far]
        back_sum = lax.psum_scatter(
            jnp.concatenate(backs), ROWS, scatter_dimension=0, tiled=True
        )
        out_part = run_expert_sums(ids, rank_columns, kept[1], down_weight)
        return kept, grad_slots, back_sum, out_part

    from_across, from_other = across(own_tokens), other(own_tokens)
    from_beside = beside(own_tokens)
    grad_slots, product = run_select_grads(ids, rank_rows, grad_all, down_weight)
    from_across, from_other = then(product, from_across, from_other)
    kept, back_sum, out_part = run_exchange_pass(
        rank_rows,
        rank_columns,
        product,
        weights,
        (own_tokens, from_beside, from_across, from_other),
    )
    return kept, grad_slots, back_sum, out_part


def head_blocks(width, head_dim):
    for at in range(0, width, head_dim):
        yield slice(at, at + head_dim)


def project(
    input_ref,
    gain_ref,
    weight_ref,
    cosine_ref,
    sine_ref,
    head_gain_ref,
    normed_ref,
    inverse_ref,
    pre_ref,
    query_ref,
    group_ref,
):
    values = input_ref[...].astype(f32)
    inverse = norm_scale(values)
    normed = (values * inverse * gain_ref[...]).astype(bf16)
    normed_ref[...] = normed
    inverse_ref[...] = inverse
    qkv = matmul(normed, weight_ref[...])
    width = query_ref.shape[1]
    head_dim = cosine_ref.shape[1]
    pre_ref[...] = qkv[:, : 2 * width]
    cosine, sine = cosine_ref[...], sine_ref[...]
    for which in (0, 1):
        gain = head_gain_ref[which : which + 1, :]
        for at in head_blocks(width, head_dim):
            head = qkv[:, which * width + at.start : which * width + at.stop]
            head = head * norm_scale(head) * gain
            turned = head * cosine + pltpu.roll(head, head_dim // 2, 1) * sine
            to_ref = query_ref if which == 0 else group_ref
            to_ref[:, at] = turned.astype(bf16)
    group_ref[:, width : 2 * width] = qkv[:, 2 * width :].astype(bf16)


def project_back(
    query_grad_ref,
    group_grad_ref,
    pre_ref,
    cosine_ref,
    sine_ref,
    head_gain_ref,
    weight_ref,
    input_ref,
    inverse_ref,
    gain_ref,
    grad_ref,
    part_ref,
    along_ref,
    terms_ref,
    head_terms_ref,
):
    width = query_grad_ref.shape[1]
    head_dim = cosine_ref.shape[1]
    cosine, sine = cosine_ref[...], sine_ref[...]

    @pl.when(pl.program_id(0) == 0)
    def _():
        terms_ref[...] = jnp.zeros_like(terms_ref)
        head_terms_ref[...] = jnp.zeros_like(head_terms_ref)

    for which in (0, 1):
        gain = head_gain_ref[which : which + 1, :]
        from_ref = query_grad_ref if which == 0 else group_grad_ref
        for at in head_blocks(width, head_dim):
            own = slice(which * width + at.start, which * width + at.stop)
            grad = from_ref[:, at].astype(f32)
            incoming = grad * cosine - pltpu.roll(grad, head_dim // 2, 1) * sine
            head = pre_ref[:, own]
            value_grad, gain_terms = norm_back(incoming, head, norm_scale(head), gain)
            grad_ref[:, own] = value_grad.astype(bf16)
            head_terms_ref[which : which + 1, :] += jnp.sum(gain_terms, axis=0, keepdims=True)
    grad_ref[:, 2 * width :] = group_grad_ref[:, width:]
    part = matmul_nt(grad_ref[...], weight_ref[...])
    part_ref[...] = part.astype(bf16)
    product = part * input_ref[...].astype(f32)
    terms_ref[...] += jnp.sum(product * inverse_ref[...], axis=0, keepdims=True)
    along_ref[...] = jnp.sum(product * gain_ref[...], axis=1, keepdims=True)


def run_project(input_b, gain, full, cosine, sine, head_gains, width):
    rows, depth = input_b.shape
    head_dim = cosine.shape[1]
    block = min(rows, QUERY_BLOCK)
    by_rows = lambda columns: pl.BlockSpec((block, columns), lambda i: (i, 0))
    return pl.pallas_call(
        project,
        grid=(rows // block,),
        in_specs=[
            by_rows(depth),
            once((1, depth)),
            once((depth, 3 * width)),
            by_rows(head_dim),
            by_rows(head_dim),
            once((2, head_dim)),
        ],
        out_specs=[
            by_rows(depth),
            by_rows(1),
            by_rows(2 * width),
            by_rows(width),
            by_rows(2 * width),
        ],
        out_shape=[
            jax.ShapeDtypeStruct((rows, depth), bf16),
            jax.ShapeDtypeStruct((rows, 1), f32),
            jax.ShapeDtypeStruct((rows, 2 * width), f32),
            jax.ShapeDtypeStruct((rows, width), bf16),
            jax.ShapeDtypeStruct((rows, 2 * width), bf16),
        ],
        compiler_params=params(1),
        cost_estimate=pl.CostEstimate(
            flops=6 * rows * depth * width, bytes_accessed=6 * depth * width, transcendentals=0
        ),
        name="project",
    )(input_b, gain, full, cosine, sine, head_gains)


def run_project_back(
    query_grad, group_grad, pre, cosine, sine, head_gains, full, input_b, inverse, gain
):
    rows, depth = input_b.shape
    width = query_grad.shape[1]
    head_dim = cosine.shape[1]
    block = min(rows, QUERY_BLOCK)
    by_rows = lambda columns: pl.BlockSpec((block, columns), lambda i: (i, 0))
    whole = lambda shape: pl.BlockSpec(shape, lambda i: (0, 0))
    return pl.pallas_call(
        project_back,
        grid=(rows // block,),
        in_specs=[
            by_rows(width),
            by_rows(2 * width),
            by_rows(2 * width),
            by_rows(head_dim),
            by_rows(head_dim),
            once((2, head_dim)),
            once((depth, 3 * width)),
            by_rows(depth),
            by_rows(1),
            once((1, depth)),
        ],
        out_specs=[
            by_rows(3 * width),
            by_rows(depth),
            by_rows(1),
            whole((1, depth)),
            whole((2, head_dim)),
        ],
        out_shape=[
            jax.ShapeDtypeStruct((rows, 3 * width), bf16),
            jax.ShapeDtypeStruct((rows, depth), bf16),
            jax.ShapeDtypeStruct((rows, 1), f32),
            jax.ShapeDtypeStruct((1, depth), f32),
            jax.ShapeDtypeStruct((2, head_dim), f32),
        ],
        compiler_params=params(1),
        cost_estimate=pl.CostEstimate(
            flops=6 * rows * depth * width, bytes_accessed=8 * depth * width, transcendentals=0
        ),
        name="project_back",
    )(query_grad, group_grad, pre, cosine, sine, head_gains, full, input_b, inverse, gain)


def grads_scatter(
    size,
    local,
    in_ref,
    small_ref,
    rows_ref,
    grad_rows_ref,
    gate_grad_ref,
    up_grad_ref,
    hidden_ref,
    out_ref,
    total_ref,
    gate_out_ref,
    up_out_ref,
    down_out_ref,
    staged_ref,
    landed_ref,
    small_landed_ref,
    first_ref,
    second_ref,
    send_sem,
    recv_sem,
    small_send_sem,
    small_recv_sem,
):
    step, part = pl.program_id(0), pl.program_id(1)
    place = lax.axis_index("tp")
    extent = out_ref.shape[0]

    def block(index):
        return in_ref[pl.ds(pl.multiple_of(index * extent, extent), extent), :].astype(f32)

    def copying(way, stage, to):
        return pltpu.make_async_remote_copy(
            src_ref=staged_ref.at[way, stage],
            dst_ref=landed_ref.at[way, stage],
            send_sem=send_sem.at[way, stage],
            recv_sem=recv_sem.at[way, stage],
            device_id={"tp": to},
            device_id_type=MESH,
        )

    def small_copy(offset, peer):
        return pltpu.make_async_remote_copy(
            src_ref=small_ref,
            dst_ref=small_landed_ref.at[offset - 1],
            send_sem=small_send_sem.at[offset - 1],
            recv_sem=small_recv_sem.at[offset - 1],
            device_id={"tp": peer},
            device_id_type=MESH,
        )

    def ways():
        yield 0, place, place + 1, place - 1
        yield 1, size - 1 - place, place - 1, place + 1

    def send(stage):
        for way, rank, to, origin in ways():
            target = size - 1 - stage + place if way == 0 else place - (size - 1 - stage)

            @pl.when(jnp.logical_and(rank <= stage, rank < size - 1))
            def _():
                values = block(target)
                if stage == 0:
                    staged_ref[way, stage] = values.astype(bf16)
                else:

                    @pl.when(rank == 0)
                    def _():
                        staged_ref[way, stage] = values.astype(bf16)

                    @pl.when(rank > 0)
                    def _():
                        landed = landed_ref[way, stage - 1].astype(f32)
                        staged_ref[way, stage] = (values + landed).astype(bf16)

                copying(way, stage, to).start()

    def receive(stage):
        for way, rank, to, origin in ways():

            @pl.when(jnp.logical_and(rank > 0, rank - 1 <= stage))
            def _():
                copying(way, stage, origin).wait_recv()

    @pl.when(jnp.logical_and(step == 0, part == 0))
    def _():
        peer_barrier("tp", size)
        for offset in range(1, size):
            small_copy(offset, lax.rem(place + offset, size)).start()
        send(0)

    for stage in range(1, size - 1):

        @pl.when(jnp.logical_and(step == min(2 * stage, 2 * local - 1), part == 0))
        def _():
            receive(stage - 1)
            send(stage)

    def flat(ref):
        return ref[...].reshape(ref.shape[0] * ref.shape[1], ref.shape[2])

    def collect(sum_ref, values):
        @pl.when(part == 0)
        def _():
            sum_ref[...] = values

        @pl.when(part == 1)
        def _():
            sum_ref[...] += values

    @pl.when(step < local)
    def _():
        rows = flat(rows_ref)
        collect(first_ref, matmul(flat(gate_grad_ref).T, rows))
        collect(second_ref, matmul(flat(up_grad_ref).T, rows))

        @pl.when(part == 1)
        def _():
            gate_out_ref[...] = first_ref[...].T
            up_out_ref[...] = second_ref[...].T

    @pl.when(step >= local)
    def _():
        collect(down_out_ref, matmul(flat(hidden_ref).T, flat(grad_rows_ref)))

    @pl.when(jnp.logical_and(step == 2 * local - 1, part == 1))
    def _():
        total = small_ref[...]
        for offset in range(1, size):
            small_copy(offset, lax.rem(place + size - offset, size)).wait_recv()
            total = total + small_landed_ref[offset - 1]
        total_ref[...] = total
        receive(size - 2)
        out_ref[...] = block(place)
        for way, rank, to, origin in ways():

            @pl.when(rank > 0)
            def _():
                out_ref[...] += landed_ref[way, size - 2].astype(f32)

        for offset in range(1, size):
            small_copy(offset, lax.rem(place + offset, size)).wait_send()
        for stage in range(size - 1):
            for way, rank, to, origin in ways():

                @pl.when(jnp.logical_and(rank <= stage, rank < size - 1))
                def _():
                    copying(way, stage, to).wait_send()


def run_grads_scatter(values, small, token_slots, grad_slots, gate_grad, up_grad, hidden_rows):
    size = lax.axis_size("tp")
    rows, width = values.shape
    shape = (rows // size, width)
    chunks, local, slots, hidden = hidden_rows.shape
    half = chunks // 2
    early = lambda i, k: jnp.minimum(i, local - 1)
    late = lambda i, k: jnp.maximum(i - local, 0)
    early_part = lambda i, k: jnp.where(i < local, k, 1)
    late_part = lambda i, k: jnp.where(i < local, 0, k)
    wide = lambda at, part: pl.BlockSpec(
        (half, None, slots, width), lambda i, k: (part(i, k), at(i, k), 0, 0)
    )
    thin = lambda at, part: pl.BlockSpec(
        (half, None, slots, hidden), lambda i, k: (part(i, k), at(i, k), 0, 0)
    )
    tall = pl.BlockSpec((None, width, hidden), lambda i, k: (early(i, k), 0, 0))
    fixed = lambda form: pl.BlockSpec(form, lambda i, k: (0,) * len(form))
    return pl.pallas_call(
        functools.partial(grads_scatter, size, local),
        grid=(2 * local, 2),
        in_specs=[
            once(values.shape),
            once(small.shape),
            wide(early, early_part),
            wide(late, late_part),
            thin(early, early_part),
            thin(early, early_part),
            thin(late, late_part),
        ],
        out_specs=[
            fixed(shape),
            fixed(small.shape),
            tall,
            tall,
            pl.BlockSpec((None, hidden, width), lambda i, k: (late(i, k), 0, 0)),
        ],
        out_shape=[
            jax.ShapeDtypeStruct(shape, f32),
            jax.ShapeDtypeStruct(small.shape, f32),
            jax.ShapeDtypeStruct((local, width, hidden), f32),
            jax.ShapeDtypeStruct((local, width, hidden), f32),
            jax.ShapeDtypeStruct((local, hidden, width), f32),
        ],
        scratch_shapes=[
            pltpu.VMEM((2, size - 1, *shape), bf16),
            pltpu.VMEM((2, size - 1, *shape), bf16),
            pltpu.VMEM((size - 1, *small.shape), f32),
            pltpu.VMEM((hidden, width), f32),
            pltpu.VMEM((hidden, width), f32),
            pltpu.SemaphoreType.DMA((2, size - 1)),
            pltpu.SemaphoreType.DMA((2, size - 1)),
            pltpu.SemaphoreType.DMA((size - 1,)),
            pltpu.SemaphoreType.DMA((size - 1,)),
        ],
        compiler_params=pltpu.CompilerParams(
            dimension_semantics=("arbitrary",) * 2,
            collective_id=10,
            has_side_effects=True,
            vmem_limit_bytes=VMEM_BYTES,
        ),
        cost_estimate=pl.CostEstimate(
            flops=6 * chunks * local * slots * width * hidden,
            bytes_accessed=150_000_000,
            transcendentals=0,
        ),
        name="grads_scatter",
    )(values, small, token_slots, grad_slots, gate_grad, up_grad, hidden_rows)


def split_three(values):
    high = values.astype(bf16)
    rest = values - high.astype(f32)
    middle = rest.astype(bf16)
    return (high, middle, (rest - middle.astype(f32)).astype(bf16))


def on_device(
    layer_input,
    token_order,
    doc_lengths,
    expert_routes,
    attn_gain,
    query_weight,
    key_weight,
    value_weight,
    query_gain,
    key_gain,
    out_weight,
    moe_gain,
    router_weight,
    gate_weight,
    up_weight,
    down_weight,
    out_grad,
):
    tp_index = lax.axis_index("tp")
    ctx_size = lax.axis_size("ctx")
    fc_size = lax.axis_size("fsdp") * ctx_size
    fc_index = lax.axis_index("fsdp") * ctx_size + lax.axis_index("ctx")
    tok_count, quarter = layer_input.shape
    share = tok_count // lax.axis_size("tp")
    head_dim = query_gain.shape[0]
    head_width = query_weight.shape[1]
    heads = head_width // head_dim
    scale = head_dim ** (-0.5)
    experts = router_weight.shape[1]
    top = expert_routes.shape[1]
    local_experts = gate_weight.shape[0]
    capacity = tok_count * top * 5 // (4 * experts)
    own_rows = lambda values: lax.dynamic_slice_in_dim(values, tp_index * share, share, 0)
    own_width = lambda values: lax.dynamic_slice_in_dim(values, tp_index * quarter, quarter, 1)

    packed = jnp.concatenate(
        [
            query_weight,
            key_weight,
            value_weight,
            out_weight.T,
            router_weight,
            attn_gain[:, None],
            moe_gain[:, None],
            jnp.zeros((attn_gain.shape[0], EXTRA - experts - 2), bf16),
        ],
        axis=1,
    )
    full = lax.all_gather(packed, ROWS, axis=0, tiled=True)
    expert_ids = jnp.arange(experts, dtype=jnp.int32)
    named = jnp.any(expert_routes[:, :, None] == expert_ids[None, None, :], axis=1)
    earlier = jnp.tri(tok_count, tok_count, -1, dtype=bf16)
    before = matmul(earlier, named.astype(bf16))
    first_slot = (lax.rem(fc_index, CHUNK // tok_count) * capacity).astype(f32)
    ranks = jnp.where(named, before + first_slot, -1.0).astype(bf16)
    input_b = gather_tp(layer_input, True, 0)
    segment, position = doc_places(token_order[0], doc_lengths[0])
    ctx_index = lax.axis_index("ctx")
    seg_columns = jnp.zeros((ctx_size, tok_count), f32)
    for offset in range(ctx_size):
        piece = segment.astype(f32)[None, :]
        if offset > 0:
            pairs = [(at, (at + offset) % ctx_size) for at in range(ctx_size)]
            piece = lax.ppermute(piece, "ctx", pairs)
        origin = lax.rem(ctx_index + ctx_size - offset, ctx_size)
        seg_columns = lax.dynamic_update_slice_in_dim(seg_columns, piece, origin, 0)
    out_grad, full, input_b, seg_columns = lax.optimization_barrier(
        (out_grad, full, input_b, seg_columns)
    )
    grad_rows_b = lax.all_gather(out_grad, "tp", axis=1, tiled=True)
    side = 3 * head_width
    qkv_weight = full[:, :side]
    full_out = full[:, side : side + head_width]
    side = side + head_width
    full_router = full[:, side : side + experts]
    attn_gain_f = full[:, side + experts].astype(f32)
    moe_gain_f = full[:, side + experts + 1].astype(f32)
    width = input_b.shape[1]
    cosine, sine = rope_tables(position, head_dim)
    head_gains = jnp.stack([query_gain, key_gain])
    attn_gain_row = attn_gain_f[None, :]
    normed, inverse_one, heads_pre, query_rows, group_part = run_project(
        input_b,
        attn_gain_row,
        full,
        cosine,
        sine,
        head_gains,
        head_width,
    )
    group = gather_ctx(group_part, 1)
    after_group, group = lax.optimization_barrier((grad_rows_b, group))
    grad_packed = jnp.concatenate(
        [after_group, ranks, jnp.zeros((tok_count, EXTRA - experts), bf16)], axis=1
    )
    grad_all = lax.all_gather(grad_packed, ROWS, axis=0, tiled=True)
    chunks = grad_all.shape[0] // CHUNK
    first_expert = fc_index * local_experts
    local_ranks = lax.dynamic_slice_in_dim(
        grad_all[:, width:], first_expert, local_experts, 1
    ).astype(jnp.int32)
    ids = chunk_order(chunks)
    rank_columns = jnp.stack(
        [
            lax.dynamic_slice_in_dim(local_ranks, ids[at] * CHUNK, CHUNK, 0)
            for at in range(chunks)
        ]
    )
    rank_rows = jnp.transpose(rank_columns, (0, 2, 1))[:, :, None, :]

    seg_rows = segment.astype(f32).reshape(-1, 1, min(tok_count, QUERY_BLOCK))
    seg_columns = seg_columns.reshape(-1, 1)
    attn_b, log_total = run_attend(query_rows, group, seg_rows, seg_columns, heads, scale)
    attn_part = matmul_nt(attn_b, full_out).astype(bf16)
    attn_out = scatter_tp(attn_part, False, 2)
    resid = own_rows(input_b).astype(f32) + attn_out
    inverse_two = norm_scale(resid)
    moe_in = (resid * inverse_two * moe_gain_f).astype(bf16)
    logits = matmul(moe_in, full_router)
    own_named = own_rows(named)
    chosen = jnp.where(own_named, logits, -jnp.inf)
    gates = jax.nn.softmax(chosen, axis=-1)
    own_tokens = gather_tp(
        jnp.concatenate(
            [moe_in, *split_three(gates), jnp.zeros((share, EXTRA - 3 * experts), bf16)], axis=1
        ),
        False,
        3,
    )
    kept, grad_slots, back_sum, out_part = expert_steps(
        ids,
        own_tokens,
        grad_all,
        rank_rows,
        rank_columns,
        first_expert.reshape(1),
        (gate_weight, up_weight, down_weight),
    )
    token_slots, hidden_rows, gate_act_grad, up_act_grad, route_part = kept
    hit = jnp.arange(chunks, dtype=jnp.int32)[:, None] == ids[None, :]
    route_all = jnp.sum(
        jnp.where(hit[:, :, None, None], route_part[None, :, :, 0, :], 0.0), axis=1
    )
    route_all = jnp.transpose(route_all, (1, 0, 2)).reshape(
        local_experts, fc_size, tok_count
    )
    route_all = lax.all_to_all(
        jnp.transpose(route_all, (1, 0, 2)), ROWS, split_axis=0, concat_axis=0, tiled=True
    ).reshape(experts, tok_count)

    back_rows, gate_grad, grad_gate, grad_up, grad_down = run_grads_scatter(
        back_sum, route_all, token_slots, grad_slots, gate_act_grad, up_act_grad, hidden_rows
    )
    parts = own_tokens[:, width : width + 3 * experts].astype(f32)
    all_gates = parts[:, :experts] + parts[:, experts : 2 * experts] + parts[:, 2 * experts :]
    gate_grad = gate_grad.T
    logit_grad = all_gates * (
        gate_grad - jnp.sum(all_gates * gate_grad, axis=-1, keepdims=True)
    )
    grad_router = lax.dot_general(
        own_tokens[:, :width].astype(f32),
        logit_grad,
        (((0,), (0,)), ((), ())),
        precision=highest,
    )
    own_logit_grad = own_rows(logit_grad)
    router_back = lax.dot_general(
        own_logit_grad, full_router.astype(f32), (((1,), (1,)), ((), ())), precision=highest
    )
    moe_in_grad = (
        back_rows + router_back
    )
    resid_norm_grad, gain_terms = norm_back(moe_in_grad, resid, inverse_two, moe_gain_f)
    grad_moe_gain = jnp.sum(gain_terms, axis=0)
    resid_grad = own_rows(grad_rows_b).astype(f32) + resid_norm_grad
    resid_grad_b = gather_tp(resid_grad.astype(bf16), False, 5)

    out_sum = lax.psum_scatter(out_part, ROWS, scatter_dimension=0, tiled=True)

    grad_out = lax.dot_general(
        resid_grad_b, attn_b, (((0,), (0,)), ((), ())), preferred_element_type=f32
    )
    attn_grad = matmul(resid_grad_b, full_out).astype(bf16)
    query_rot_grad, key_part, value_part = run_attend_back(
        query_rows, group, seg_rows, seg_columns, attn_b, log_total, attn_grad, heads, scale
    )
    out_sum, key_part = lax.optimization_barrier((out_sum, key_part))
    out_sum = lax.psum_scatter(out_sum, "tp", scatter_dimension=0, tiled=True).astype(f32)
    group_grad = scatter_ctx(jnp.concatenate([key_part, value_part], axis=1), 6)
    qkv_grad, normed_part, along, attn_terms, head_terms = run_project_back(
        query_rot_grad,
        group_grad,
        heads_pre,
        cosine,
        sine,
        head_gains,
        full,
        input_b,
        inverse_one,
        attn_gain_row,
    )
    along = along[:, 0]
    gains = jnp.concatenate([attn_terms[0], grad_moe_gain, head_terms[0], head_terms[1]])
    normed_grad, gains, along = close_tp(normed_part, gains, along, 7)
    along = along[:, None] / width
    normed_grad, out_sum = lax.optimization_barrier((normed_grad, out_sum))
    grad_gate, grad_up, grad_down = then(normed_grad, grad_gate, grad_up, grad_down)
    grad_gate, grad_up, grad_down = [
        lax.clamp(jnp.float32(-jnp.inf), grad, jnp.float32(jnp.inf))
        for grad in (grad_gate, grad_up, grad_down)
    ]
    layer_sum = resid + out_sum
    layer_output = lax.all_to_all(
        layer_sum.astype(bf16), "tp", split_axis=1, concat_axis=0, tiled=True
    )
    input_quarter = layer_input.astype(f32)
    gain_quarter = lax.dynamic_slice_in_dim(attn_gain_f, tp_index * quarter, quarter, 0)
    grad_input = own_width(resid_grad_b).astype(f32) + inverse_one * (
        normed_grad * gain_quarter - input_quarter * inverse_one * inverse_one * along
    )
    grad_qkv = lax.dot_general(
        normed, qkv_grad, (((0,), (0,)), ((), ())), preferred_element_type=f32
    )
    owned_out = lax.psum_scatter(
        jnp.concatenate(
            [grad_out, grad_router, jnp.zeros((width, EXTRA - experts), f32)], axis=1
        ).astype(bf16),
        ROWS,
        scatter_dimension=0,
        tiled=True,
    )
    (owned_out,) = then(normed_grad, owned_out)
    owned_out = owned_out.astype(f32)
    owned_qkv = lax.psum_scatter(
        grad_qkv.astype(bf16), ROWS, scatter_dimension=0, tiled=True
    ).astype(f32)
    owned_gain = attn_gain.shape[0]
    own_gain = lambda at: lax.dynamic_slice_in_dim(
        gains, at * width + fc_index * owned_gain, owned_gain, 0
    )
    return (
        layer_output,
        grad_input,
        own_gain(0),
        owned_qkv[:, :head_width],
        owned_qkv[:, head_width : 2 * head_width],
        owned_qkv[:, 2 * head_width :],
        gains[2 * width : 2 * width + head_dim],
        gains[2 * width + head_dim :],
        owned_out[:, :head_width].T,
        own_gain(1),
        owned_out[:, head_width : head_width + experts],
        grad_gate,
        grad_up,
        grad_down,
    )


def solution(mesh):
    in_specs = (
        P(("fsdp", "ctx"), "tp"),
        P("fsdp", "ctx"),
        P("fsdp", None),
        P(("fsdp", "ctx"), None),
        P(("fsdp", "ctx")),
        P(("fsdp", "ctx"), "tp"),
        P(("fsdp", "ctx"), "tp"),
        P(("fsdp", "ctx"), "tp"),
        P(),
        P(),
        P("tp", ("fsdp", "ctx")),
        P(("fsdp", "ctx")),
        P(("fsdp", "ctx"), None),
        P(("fsdp", "ctx"), None, "tp"),
        P(("fsdp", "ctx"), None, "tp"),
        P(("fsdp", "ctx"), "tp", None),
        P(("fsdp", "ctx"), "tp"),
    )
    out_specs = (
        P(("fsdp", "ctx"), "tp"),
        P(("fsdp", "ctx"), "tp"),
        P(("fsdp", "ctx")),
        P(("fsdp", "ctx"), "tp"),
        P(("fsdp", "ctx"), "tp"),
        P(("fsdp", "ctx"), "tp"),
        P(),
        P(),
        P("tp", ("fsdp", "ctx")),
        P(("fsdp", "ctx")),
        P(("fsdp", "ctx"), None),
        P(("fsdp", "ctx"), None, "tp"),
        P(("fsdp", "ctx"), None, "tp"),
        P(("fsdp", "ctx"), "tp", None),
    )
    return jax.shard_map(
        on_device, mesh=mesh, in_specs=in_specs, out_specs=out_specs, check_vma=False
    )
```

```python
import functools

import jax
import jax.numpy as jnp
from jax import lax
from jax.experimental import pallas as pl
from jax.experimental.pallas import tpu as pltpu
from jax.sharding import PartitionSpec as P

QUERY_BLOCK = 256
CHUNK = 768
SLOTS = 256
EXTRA = 128
VMEM_BYTES = 60 * 1024 * 1024


epsilon = 1e-05
rope_base = 50000.0
masked_score = -1e30
highest = lax.Precision.HIGHEST
bf16 = jnp.bfloat16
f32 = jnp.float32
ROWS = ("fsdp", "ctx")
ALL = ("fsdp", "ctx", "tp")
MESH = pl.DeviceIdType.MESH


def doc_places(order_row, length_row):
    ends = jnp.cumsum(length_row, dtype=jnp.int32)
    passed = (order_row[:, None] >= ends[None, :]).astype(jnp.int32)
    segment = jnp.sum(passed, axis=1, dtype=jnp.int32)
    start = jnp.sum(passed * length_row[None, :], axis=1, dtype=jnp.int32)
    return (segment, order_row - start)


def rope_tables(position, head_dim):
    half = head_dim // 2
    freqs = rope_base ** (-(jnp.arange(half, dtype=jnp.float32) * (2.0 / head_dim)))
    angles = position.astype(jnp.float32)[:, None] * freqs[None, :]
    cosine, sine = jnp.cos(angles), jnp.sin(angles)
    return jnp.concatenate([cosine, cosine], axis=1), jnp.concatenate([-sine, sine], axis=1)


def norm_scale(values):
    return lax.rsqrt(jnp.mean(values * values, axis=-1, keepdims=True) + epsilon)


def norm_back(incoming, values, inverse, gain):
    scaled = incoming * gain
    value_grad = inverse * (
        scaled - values * inverse * inverse * jnp.mean(scaled * values, axis=-1, keepdims=True)
    )
    return (value_grad, incoming * values * inverse)


def matmul(left, right):
    return jnp.dot(left, right, preferred_element_type=f32)


def matmul_nt(left, right):
    return lax.dot_general(left, right, (((1,), (1,)), ((), ())), preferred_element_type=f32)


def slot_rows(rank_row):
    slots = lax.broadcasted_iota(jnp.int32, (SLOTS, rank_row.shape[1]), 0)
    return slots == rank_row


def slot_columns(rank_column):
    slots = lax.broadcasted_iota(jnp.int32, (rank_column.shape[0], SLOTS), 1)
    return jnp.where(slots == rank_column, 1.0, 0.0).astype(bf16)


def as_one_hot(mask):
    return jnp.where(mask, 1.0, 0.0).astype(bf16)


def select_grads(ids_ref, rank_ref, grad_ref, down_ref, rows_ref, product_ref):
    expert = pl.program_id(1)
    rows = matmul(as_one_hot(slot_rows(rank_ref[...])), grad_ref[...]).astype(bf16)
    rows_ref[...] = rows
    product_ref[...] = matmul_nt(rows, down_ref[expert])


def expert_step(
    expert,
    named,
    rank_ref,
    tokens,
    product_ref,
    gate_ref,
    up_ref,
    await_weights,
    rows_ref,
    hidden_ref,
    gate_grad_ref,
    up_grad_ref,
    route_ref,
    held_ref,
):
    width = rows_ref.shape[1]
    mask = slot_rows(rank_ref[...])
    picked = matmul(as_one_hot(mask), tokens)
    rows = picked[:, :width].astype(bf16)
    rows_ref[...] = rows
    lane = lax.broadcasted_iota(jnp.int32, (SLOTS, EXTRA), 1)
    mine = jnp.logical_and(lax.rem(lane, 32) == named, lane < 96)
    gate = jnp.sum(jnp.where(mine, picked[:, width:], 0.0), axis=1, keepdims=True)
    await_weights()
    gate_act = matmul(rows, gate_ref[expert])
    up_act = matmul(rows, up_ref[expert])
    sigmoid_g = 1.0 / (1.0 + jnp.exp(-gate_act))
    silu_g = gate_act * sigmoid_g
    hidden = silu_g * up_act
    hidden_ref[...] = (gate * hidden).astype(bf16)
    product = product_ref[...]
    route = jnp.sum(hidden.astype(bf16).astype(f32) * product, axis=1, keepdims=True)
    route_ref[...] = jnp.sum(jnp.where(mask, route, 0.0), axis=0, keepdims=True)
    hidden_grad = gate * product
    gate_grad = (
        hidden_grad * up_act * sigmoid_g * (1.0 + gate_act * (1.0 - sigmoid_g))
    ).astype(bf16)
    up_grad = (hidden_grad * silu_g).astype(bf16)
    gate_grad_ref[...] = gate_grad
    up_grad_ref[...] = up_grad
    back = matmul_nt(gate_grad, gate_ref[expert]) + matmul_nt(up_grad, up_ref[expert])
    held_ref[pl.ds(pl.multiple_of(expert * SLOTS, SLOTS), SLOTS), :] = back.astype(bf16)


def chunk_places(column_ref):
    columns = column_ref[...]
    return jnp.concatenate(
        [slot_columns(columns[:, e : e + 1]) for e in range(columns.shape[1])], axis=1
    )


def expert_pass(
    ids_ref,
    first_ref,
    rank_ref,
    column_ref,
    near_ref,
    far_ref,
    product_ref,
    gate_in_ref,
    up_in_ref,
    *refs,
):
    (
        rows_ref,
        hidden_ref,
        gate_grad_ref,
        up_grad_ref,
        route_ref,
        near_back_ref,
        far_back_ref,
        token_ref,
        gate_ref,
        up_ref,
        held_ref,
        back_ref,
        token_sem,
        gate_sem,
        up_sem,
        back_sem,
    ) = refs[-16:]
    chunk, expert = pl.program_id(0), pl.program_id(1)
    local = gate_ref.shape[0]
    width = rows_ref.shape[1]
    tiles = back_sem.shape[1]
    tile = width // tiles
    loads = [
        pltpu.make_async_copy(source, token_ref.at[at], token_sem.at[at])
        for at, source in enumerate((near_ref, far_ref))
    ]

    def weight_load(source, held, sem, at):
        return pltpu.make_async_copy(source.at[at], held.at[at], sem.at[at])

    def back_store(to, at, step):
        columns = pl.ds(step * tile, tile)
        return pltpu.make_async_copy(
            back_ref.at[at, :, columns], to.at[:, columns], back_sem.at[at, step]
        )

    @pl.when(jnp.logical_and(chunk == 0, expert == 0))
    def _():
        loads[0].start()
        for at in range(local):
            weight_load(gate_in_ref, gate_ref, gate_sem, at).start()
            weight_load(up_in_ref, up_ref, up_sem, at).start()
        loads[1].start()
        loads[0].wait()

    @pl.when(jnp.logical_and(chunk == 1, expert == 0))
    def _():
        loads[1].wait()

    def await_weights():
        @pl.when(chunk == 0)
        def _():
            weight_load(gate_in_ref, gate_ref, gate_sem, expert).wait()
            weight_load(up_in_ref, up_ref, up_sem, expert).wait()

    expert_step(
        expert,
        first_ref[0] + expert,
        rank_ref,
        token_ref[chunk],
        product_ref,
        gate_ref,
        up_ref,
        await_weights,
        rows_ref,
        hidden_ref,
        gate_grad_ref,
        up_grad_ref,
        route_ref,
        held_ref,
    )

    @pl.when(expert == local - 1)
    def _():
        places = chunk_places(column_ref)
        for step in range(tiles):
            at = pl.ds(step * tile, tile)
            back_ref[chunk, :, at] = matmul(places, held_ref[:, at]).astype(bf16)

            @pl.when(chunk == 0)
            def _():
                back_store(near_back_ref, 0, step).start()

            @pl.when(chunk == 1)
            def _():
                back_store(far_back_ref, 1, step).start()

    @pl.when(jnp.logical_and(chunk == 1, expert == local - 1))
    def _():
        for step in range(tiles):
            back_store(near_back_ref, 0, step).wait()
            back_store(far_back_ref, 1, step).wait()


def exchange_pass(
    rank_ref,
    column_ref,
    product_ref,
    gate_in_ref,
    up_in_ref,
    down_in_ref,
    own_ref,
    sibling_ref,
    from_across_ref,
    from_other_ref,
    rows_ref,
    hidden_ref,
    gate_grad_ref,
    up_grad_ref,
    route_ref,
    sum_ref,
    out_ref,
    inbox_ref,
    landing_ref,
    token_ref,
    gate_ref,
    up_ref,
    down_ref,
    hidden_held_ref,
    held_ref,
    far_ref,
    beside_ref,
    chip_ref,
    corner_ref,
    token_sem,
    gate_sem,
    up_sem,
    pass_send,
    pass_recv,
    far_send,
    far_recv,
    link_send,
    link_recv,
    store_sem,
    down_sem,
    out_sem,
    landing_sem,
):
    step, expert = pl.program_id(0), pl.program_id(1)
    local = gate_ref.shape[0]
    rows, width = far_ref.shape
    half = rows // 2
    fsdp, ctx = lax.axis_index("fsdp"), lax.axis_index("ctx")
    beside_id = {"fsdp": fsdp + 1 - 2 * lax.rem(fsdp, 2)}
    across_id = {"fsdp": lax.rem(fsdp + 2, 4)}
    other_id = {"ctx": 1 - ctx}
    last = expert == local - 1
    low, high = pl.ds(0, half), pl.ds(half, half)
    sources = (
        inbox_ref.at[0],
        from_across_ref,
        inbox_ref.at[1],
        from_other_ref,
        inbox_ref.at[3],
        inbox_ref.at[2],
        sibling_ref,
        own_ref,
    )

    def token_load(at):
        slot = at % 2
        return pltpu.make_async_copy(sources[at], token_ref.at[slot], token_sem.at[slot])

    def weight_load(source, held, sem, at):
        return pltpu.make_async_copy(source.at[at], held.at[at], sem.at[at])

    def pass_copy(number):
        source, to, peer = (
            (from_across_ref, inbox_ref.at[0], beside_id),
            (from_other_ref, inbox_ref.at[1], beside_id),
            (from_other_ref.at[low], inbox_ref.at[2, low], across_id),
            (from_across_ref.at[high], inbox_ref.at[2, high], other_id),
            (inbox_ref.at[2], inbox_ref.at[3], beside_id),
        )[number]
        return pltpu.make_async_remote_copy(
            src_ref=source,
            dst_ref=to,
            send_sem=pass_send.at[number],
            recv_sem=pass_recv.at[number],
            device_id=peer,
            device_id_type=MESH,
        )

    def far_copy(turn):
        return pltpu.make_async_remote_copy(
            src_ref=far_ref,
            dst_ref=beside_ref.at[turn % 2],
            send_sem=far_send.at[turn],
            recv_sem=far_recv.at[turn],
            device_id=beside_id,
            device_id_type=MESH,
        )

    def link_copy(number):
        source, to, peer = (
            (chip_ref.at[0, high], landing_ref.at[0, high], across_id),
            (chip_ref.at[1, low], landing_ref.at[1, low], other_id),
            (chip_ref.at[2, low], corner_ref.at[0], other_id),
            (chip_ref.at[2, high], corner_ref.at[1], across_id),
            (chip_ref.at[1, high], landing_ref.at[1, high], other_id),
            (chip_ref.at[0, low], landing_ref.at[0, low], across_id),
        )[number]
        return pltpu.make_async_remote_copy(
            src_ref=source,
            dst_ref=to,
            send_sem=link_send.at[number],
            recv_sem=link_recv.at[number],
            device_id=peer,
            device_id_type=MESH,
        )

    @pl.when(jnp.logical_and(step == 0, expert == 0))
    def _():
        barrier = pltpu.get_barrier_semaphore()
        for peer in (beside_id, across_id, other_id):
            pl.semaphore_signal(barrier, inc=1, device_id=peer, device_id_type=MESH)
        pl.semaphore_wait(barrier, 3)
        for number in (0, 2, 3):
            pass_copy(number).start()
        for at in range(local):
            weight_load(gate_in_ref, gate_ref, gate_sem, at).start()
            weight_load(up_in_ref, up_ref, up_sem, at).start()
        down_load = pltpu.make_async_copy(down_in_ref, down_ref, down_sem)
        down_load.start()
        pass_copy(0).wait_recv()
        token_load(0).start()
        pass_copy(1).start()

    @pl.when(jnp.logical_and(step == 3, expert == 0))
    def _():
        pass_copy(2).wait_recv()
        pass_copy(3).wait_recv()
        pass_copy(4).start()

    for at in range(8):

        @pl.when(jnp.logical_and(step == at, expert == 0))
        def _():
            token_load(at).wait()

        if at < 7:

            @pl.when(jnp.logical_and(step == at, last))
            def _():
                if at == 1:
                    pass_copy(1).wait_recv()
                if at == 3:
                    pass_copy(4).wait_recv()
                token_load(at + 1).start()

    def await_weights():
        @pl.when(step == 0)
        def _():
            weight_load(gate_in_ref, gate_ref, gate_sem, expert).wait()
            weight_load(up_in_ref, up_ref, up_sem, expert).wait()

    first = (fsdp * 2 + ctx) * local

    @pl.when(step < 8)
    def _():
        expert_step(
            expert,
            first + expert,
            rank_ref,
            token_ref[lax.rem(step, 2)],
            product_ref,
            gate_ref,
            up_ref,
            await_weights,
            rows_ref,
            hidden_ref,
            gate_grad_ref,
            up_grad_ref,
            route_ref,
            held_ref,
        )
        hidden_held_ref[step, expert] = hidden_ref[...]

    tile = 512

    def tiles():
        for at in range(0, width, tile):
            yield pl.ds(at, tile)

    def add_half(turn, part, landed):
        total = chip_ref[turn, part, :].astype(f32) + corner_ref[landed].astype(f32)
        chip_ref[turn, part, :] = total.astype(bf16)

    for turn in range(4):

        @pl.when(jnp.logical_and(step == 2 * turn, last))
        def _():
            if turn > 0:
                far_copy(turn - 1).wait_send()
            places = chunk_places(column_ref)
            for at in tiles():
                far_ref[:, at] = matmul(places, held_ref[:, at]).astype(bf16)
            far_copy(turn).start()

        @pl.when(jnp.logical_and(step == 2 * turn + 1, last))
        def _():
            far_copy(turn).wait_recv()
            if turn == 3:
                far_copy(3).wait_send()
            places = chunk_places(column_ref)
            for at in tiles():
                total = matmul(places, held_ref[:, at]) + beside_ref[turn % 2, :, at].astype(f32)
                if turn < 3:
                    chip_ref[turn, :, at] = total.astype(bf16)
                else:
                    far_ref[:, at] = total.astype(bf16)
            if turn < 2:
                link_copy(turn).start()
            if turn == 2:
                link_copy(2).start()
                link_copy(3).start()


    number = step - 8
    turn = number // 2
    chip = lax.rem(fsdp + 2 * (1 - lax.rem(turn, 2)), 4)
    core = chip + (1 - lax.rem(number, 2)) * (1 - 2 * lax.rem(fsdp, 2))
    line = lax.rem(ctx + lax.rem((turn + 1) // 2, 2), 2)
    places_at = (core * 2 + line) * rows
    slot = lax.rem(step, 2)
    columns_of = width // local
    hidden = gate_ref.shape[2]

    def out_store(at, which):
        columns = pl.ds(pl.multiple_of(which * columns_of, columns_of), columns_of)
        return pltpu.make_async_copy(
            token_ref.at[slot, :, columns],
            out_ref.at[pl.ds(pl.multiple_of(at, rows), rows), columns],
            out_sem.at[slot, which],
        )

    @pl.when(step >= 8)
    def _():
        @pl.when(jnp.logical_and(step == 8, expert == 0))
        def _():
            pltpu.make_async_copy(down_in_ref, down_ref, down_sem).wait()

        @pl.when(expert == 0)
        def _():
            columns = column_ref[...]
            for e in range(local):
                held_ref[pl.ds(0, rows), pl.ds(e * hidden, hidden)] = matmul(
                    slot_columns(columns[:, e : e + 1]), hidden_held_ref[number, e]
                ).astype(bf16)

        @pl.when(step >= 10)
        def _():
            out_store(places_at, expert).wait()

        at = pl.ds(pl.multiple_of(expert * columns_of, columns_of), columns_of)
        token_ref[slot, :, at] = matmul(
            held_ref[pl.ds(0, rows), pl.ds(0, local * hidden)], down_ref[:, at]
        ).astype(bf16)
        out_store(places_at, expert).start()

    @pl.when(jnp.logical_and(step == 9, expert == 1))
    def _():
        link_copy(3).wait_recv()
        add_half(1, high, 1)
        link_copy(4).start()
        link_copy(2).wait_recv()
        add_half(0, low, 0)
        link_copy(5).start()

    @pl.when(jnp.logical_and(step == 15, last))
    def _():
        landing = []
        for way, numbers in enumerate(((0, 5), (1, 4))):
            for number in numbers:
                link_copy(number).wait_recv()
            copy = pltpu.make_async_copy(
                landing_ref.at[way], beside_ref.at[way], landing_sem.at[way]
            )
            copy.start()
            landing.append(copy)
        for copy in landing:
            copy.wait()
        for part in (low, high):
            held_ref[part, :] = (
                far_ref[part, :].astype(f32)
                + beside_ref[0, part, :].astype(f32)
                + beside_ref[1, part, :].astype(f32)
            ).astype(bf16)
        store = pltpu.make_async_copy(held_ref.at[pl.ds(0, rows)], sum_ref, store_sem)
        store.start()
        for number in range(5):
            pass_copy(number).wait_send()
        for number in range(6):
            link_copy(number).wait_send()
        for other_slot in (0, 1):
            for which in range(local):
                columns = pl.ds(which * columns_of, columns_of)
                pltpu.make_async_copy(
                    token_ref.at[other_slot, :, columns],
                    out_ref.at[pl.ds(0, rows), columns],
                    out_sem.at[other_slot, which],
                ).wait()
        store.wait()


def expert_sums(ids_ref, column_ref, hidden_ref, down_ref, out_ref):
    columns = column_ref[...]
    dense = [
        matmul(slot_columns(columns[:, e : e + 1]), hidden_ref[e]).astype(bf16)
        for e in range(columns.shape[1])
    ]
    out_ref[...] = matmul(jnp.concatenate(dense, axis=1), down_ref[...]).astype(bf16)


def params(dims):
    return pltpu.CompilerParams(
        dimension_semantics=("arbitrary",) * dims, vmem_limit_bytes=VMEM_BYTES
    )


def once(shape):
    return pl.BlockSpec(
        shape, lambda *ids: (0,) * len(shape), pipeline_mode=pl.Buffered(1)
    )


def run_select_grads(ids, rank_rows, grad_all, down_weight):
    chunks, local = rank_rows.shape[:2]
    hidden, width = down_weight.shape[1:]
    slots = chunks * local * SLOTS
    place = lambda g, e, ids: (g, e, 0, 0)
    return pl.pallas_call(
        select_grads,
        grid_spec=pltpu.PrefetchScalarGridSpec(
            num_scalar_prefetch=1,
            grid=(chunks, local),
            in_specs=[
                pl.BlockSpec((None, None, 1, CHUNK), place),
                pl.BlockSpec((CHUNK, width), lambda g, e, ids: (ids[g], 0)),
                once(down_weight.shape),
            ],
            out_specs=[
                pl.BlockSpec((None, None, SLOTS, width), place),
                pl.BlockSpec((None, None, SLOTS, hidden), place),
            ],
        ),
        out_shape=[
            jax.ShapeDtypeStruct((chunks, local, SLOTS, width), bf16),
            jax.ShapeDtypeStruct((chunks, local, SLOTS, hidden), f32),
        ],
        compiler_params=params(2),
        cost_estimate=pl.CostEstimate(
            flops=2 * slots * width * (CHUNK + hidden),
            bytes_accessed=2 * (chunks * CHUNK + slots) * width,
            transcendentals=0,
        ),
        name="select_grads",
    )(ids, rank_rows, grad_all, down_weight)


def run_exchange_pass(rank_rows, rank_columns, product, weights, sources):
    gate_weight, up_weight, down_weight = weights
    chunks, local = rank_rows.shape[:2]
    width, hidden = gate_weight.shape[1:]
    slots = chunks * local * SLOTS
    flat_down = down_weight.reshape(local * hidden, width)

    def per_expert(g, e):
        return (jnp.minimum(g, chunks - 1), jnp.where(g < chunks, e, local - 1), 0, 0)

    narrow = pl.BlockSpec((None, None, SLOTS, hidden), per_expert)
    anywhere = pl.BlockSpec(memory_space=pl.ANY)
    half = (2, CHUNK // 2, width)
    narrow_shape = jax.ShapeDtypeStruct((chunks, local, SLOTS, hidden), bf16)
    outs = pl.pallas_call(
        exchange_pass,
        grid=(2 * chunks, local),
        in_specs=[
            pl.BlockSpec((None, None, 1, CHUNK), per_expert),
            pl.BlockSpec((None, CHUNK, local), lambda g, e: (lax.rem(g, chunks), 0, 0)),
            narrow,
            *[anywhere] * 7,
        ],
        out_specs=[
            pl.BlockSpec((None, None, SLOTS, width), per_expert),
            narrow,
            narrow,
            narrow,
            pl.BlockSpec((None, None, 1, CHUNK), per_expert),
            *[anywhere] * 4,
        ],
        out_shape=[
            jax.ShapeDtypeStruct((chunks, local, SLOTS, width), bf16),
            narrow_shape,
            narrow_shape,
            narrow_shape,
            jax.ShapeDtypeStruct((chunks, local, 1, CHUNK), f32),
            jax.ShapeDtypeStruct((CHUNK, width), bf16),
            jax.ShapeDtypeStruct((chunks * CHUNK, width), bf16),
            jax.ShapeDtypeStruct((4, *sources[0].shape), bf16),
            jax.ShapeDtypeStruct((2, CHUNK, width), bf16),
        ],
        scratch_shapes=[
            pltpu.VMEM((2, CHUNK, width + EXTRA), bf16),
            pltpu.VMEM(gate_weight.shape, bf16),
            pltpu.VMEM(up_weight.shape, bf16),
            pltpu.VMEM(flat_down.shape, bf16),
            pltpu.VMEM((chunks, local, SLOTS, hidden), bf16),
            pltpu.VMEM((local * SLOTS, width), bf16),
            pltpu.VMEM((CHUNK, width), bf16),
            pltpu.VMEM((2, CHUNK, width), bf16),
            pltpu.VMEM((3, CHUNK, width), bf16),
            pltpu.VMEM(half, bf16),
            pltpu.SemaphoreType.DMA((2,)),
            pltpu.SemaphoreType.DMA((local,)),
            pltpu.SemaphoreType.DMA((local,)),
            pltpu.SemaphoreType.DMA((5,)),
            pltpu.SemaphoreType.DMA((5,)),
            pltpu.SemaphoreType.DMA((4,)),
            pltpu.SemaphoreType.DMA((4,)),
            pltpu.SemaphoreType.DMA((6,)),
            pltpu.SemaphoreType.DMA((6,)),
            pltpu.SemaphoreType.DMA,
            pltpu.SemaphoreType.DMA,
            pltpu.SemaphoreType.DMA((2, local)),
            pltpu.SemaphoreType.DMA((2,)),
        ],
        compiler_params=pltpu.CompilerParams(
            dimension_semantics=("arbitrary",) * 2,
            collective_id=9,
            has_side_effects=True,
            vmem_limit_bytes=VMEM_BYTES,
        ),
        cost_estimate=pl.CostEstimate(
            flops=2 * slots * width * (2 * CHUNK + 4 * hidden),
            bytes_accessed=2 * (12 * CHUNK + slots) * width,
            transcendentals=slots * hidden,
        ),
        name="exchange_pass",
    )(rank_rows, rank_columns, product, gate_weight, up_weight, flat_down, *sources)
    return outs[:5], outs[5], outs[6]


def run_expert_pass(
    ids, first, rank_rows, rank_columns, near, far, product, gate_weight, up_weight, kept
):
    chunks, local = rank_rows.shape[:2]
    width, hidden = gate_weight.shape[1:]
    slots = 2 * local * SLOTS
    per_expert = lambda g, e, ids: (ids[g], e, 0, 0)
    narrow = pl.BlockSpec((None, None, SLOTS, hidden), per_expert)
    in_specs = [
        pl.BlockSpec(memory_space=pltpu.SMEM),
        pl.BlockSpec((None, None, 1, CHUNK), per_expert),
        pl.BlockSpec((None, CHUNK, local), lambda g, e, ids: (ids[g], 0, 0)),
        pl.BlockSpec(memory_space=pl.ANY),
        pl.BlockSpec(memory_space=pl.ANY),
        narrow,
        pl.BlockSpec(memory_space=pl.ANY),
        pl.BlockSpec(memory_space=pl.ANY),
    ]
    kept_shapes = [
        jax.ShapeDtypeStruct((chunks, local, SLOTS, width), bf16),
        jax.ShapeDtypeStruct((chunks, local, SLOTS, hidden), bf16),
        jax.ShapeDtypeStruct((chunks, local, SLOTS, hidden), bf16),
        jax.ShapeDtypeStruct((chunks, local, SLOTS, hidden), bf16),
        jax.ShapeDtypeStruct((chunks, local, 1, CHUNK), f32),
    ]
    outs = pl.pallas_call(
        expert_pass,
        grid_spec=pltpu.PrefetchScalarGridSpec(
            num_scalar_prefetch=1,
            grid=(2, local),
            in_specs=in_specs + [pl.BlockSpec(memory_space=pl.ANY)] * len(kept),
            out_specs=[
                pl.BlockSpec((None, None, SLOTS, width), per_expert),
                narrow,
                narrow,
                narrow,
                pl.BlockSpec((None, None, 1, CHUNK), per_expert),
                pl.BlockSpec(memory_space=pl.ANY),
                pl.BlockSpec(memory_space=pl.ANY),
            ],
            scratch_shapes=[
                pltpu.VMEM((2, CHUNK, width + EXTRA), bf16),
                pltpu.VMEM(gate_weight.shape, bf16),
                pltpu.VMEM(up_weight.shape, bf16),
                pltpu.VMEM((local * SLOTS, width), bf16),
                pltpu.VMEM((2, CHUNK, width), bf16),
                pltpu.SemaphoreType.DMA((2,)),
                pltpu.SemaphoreType.DMA((local,)),
                pltpu.SemaphoreType.DMA((local,)),
                pltpu.SemaphoreType.DMA((2, 4)),
            ],
        ),
        out_shape=kept_shapes + [jax.ShapeDtypeStruct((CHUNK, width), bf16)] * 2,
        input_output_aliases={9 + at: at for at in range(len(kept))},
        compiler_params=params(2),
        cost_estimate=pl.CostEstimate(
            flops=2 * slots * width * (2 * CHUNK + 4 * hidden),
            bytes_accessed=2 * (4 * CHUNK + slots) * width,
            transcendentals=slots * hidden,
        ),
        name="expert_pass",
    )(ids, first, rank_rows, rank_columns, near, far, product, gate_weight, up_weight, *kept)
    return outs[:5], outs[5], outs[6]


def run_expert_sums(ids, rank_columns, hidden_rows, down_weight):
    chunks, local, unused, hidden = hidden_rows.shape
    width = down_weight.shape[2]
    flat = down_weight.reshape(local * hidden, width)
    return pl.pallas_call(
        expert_sums,
        grid_spec=pltpu.PrefetchScalarGridSpec(
            num_scalar_prefetch=1,
            grid=(chunks,),
            in_specs=[
                pl.BlockSpec((None, CHUNK, local), lambda g, ids: (g, 0, 0)),
                pl.BlockSpec((None, local, SLOTS, hidden), lambda g, ids: (g, 0, 0, 0)),
                once(flat.shape),
            ],
            out_specs=pl.BlockSpec((CHUNK, width), lambda g, ids: (ids[g], 0)),
        ),
        out_shape=jax.ShapeDtypeStruct((chunks * CHUNK, width), bf16),
        compiler_params=params(1),
        cost_estimate=pl.CostEstimate(
            flops=2 * chunks * CHUNK * local * hidden * (width + SLOTS),
            bytes_accessed=2 * chunks * CHUNK * width,
            transcendentals=0,
        ),
        name="expert_sums",
    )(ids, rank_columns, hidden_rows, flat)


def line_barrier(size):
    place = lax.axis_index("tp")
    barrier = pltpu.get_barrier_semaphore()

    @pl.when(place > 0)
    def _():
        pl.semaphore_signal(barrier, inc=1, device_id={"tp": place - 1}, device_id_type=MESH)

    @pl.when(place < size - 1)
    def _():
        pl.semaphore_signal(barrier, inc=1, device_id={"tp": place + 1}, device_id_type=MESH)

    has_left = jnp.where(place > 0, 1, 0)
    has_right = jnp.where(place < size - 1, 1, 0)
    pl.semaphore_wait(barrier, has_left + has_right)


def line_gather(size, columns, in_ref, out_ref, own_sem, send_sem, recv_sem):
    place = lax.axis_index("tp")
    extent = in_ref.shape[1] if columns else in_ref.shape[0]

    def block(index):
        at = pl.ds(pl.multiple_of(index * extent, extent), extent)
        return out_ref.at[:, at] if columns else out_ref.at[at, :]

    line_barrier(size)
    own = pltpu.make_async_copy(in_ref, block(place), own_sem)
    own.start()

    def sending(way, step):
        source = place - step if way == 0 else place + step
        to = place + 1 if way == 0 else place - 1
        return pltpu.make_async_remote_copy(
            src_ref=in_ref if step == 0 else block(source),
            dst_ref=block(source),
            send_sem=send_sem.at[way, step],
            recv_sem=recv_sem.at[way, step],
            device_id={"tp": to},
            device_id_type=MESH,
        )

    def sends(way, step):
        if way == 0:
            return jnp.logical_and(place >= step, place < size - 1)
        return jnp.logical_and(place + step < size, place > 0)

    def receiving(way, step):
        source = place - 1 - step if way == 0 else place + 1 + step
        origin = place - 1 if way == 0 else place + 1
        return pltpu.make_async_remote_copy(
            src_ref=block(source),
            dst_ref=block(source),
            send_sem=send_sem.at[way, step],
            recv_sem=recv_sem.at[way, step],
            device_id={"tp": origin},
            device_id_type=MESH,
        )

    def receives(way, step):
        return place > step if way == 0 else place + 1 + step < size

    for step in range(size - 1):
        for way in (0, 1):

            @pl.when(sends(way, step))
            def _():
                sending(way, step).start()

        for way in (0, 1):

            @pl.when(receives(way, step))
            def _():
                receiving(way, step).wait_recv()

    for step in range(size - 1):
        for way in (0, 1):

            @pl.when(sends(way, step))
            def _():
                sending(way, step).wait_send()

    own.wait()


def line_scatter(
    size, columns, in_ref, out_ref, staged_ref, landed_ref, send_sem, recv_sem, stages=()
):
    place = lax.axis_index("tp")
    extent = out_ref.shape[1] if columns else out_ref.shape[0]

    def block(index):
        at = pl.ds(pl.multiple_of(index * extent, extent), extent)
        values = in_ref[:, at] if columns else in_ref[at, :]
        return values.astype(f32)

    if not stages:
        line_barrier(size)

    def copying(way, step, to):
        return pltpu.make_async_remote_copy(
            src_ref=staged_ref.at[way, step],
            dst_ref=landed_ref.at[way, step],
            send_sem=send_sem.at[way, step],
            recv_sem=recv_sem.at[way, step],
            device_id={"tp": to},
            device_id_type=MESH,
        )

    for step in range(size - 1):
        for way in (0, 1):
            rank = place if way == 0 else size - 1 - place
            target = size - 1 - step + place if way == 0 else place - (size - 1 - step)
            to = place + 1 if way == 0 else place - 1
            active = jnp.logical_and(rank <= step, rank < size - 1)

            @pl.when(active)
            def _():
                values = block(target)
                if step == 0:
                    staged_ref[way, step] = values.astype(bf16)
                else:

                    @pl.when(rank == 0)
                    def _():
                        staged_ref[way, step] = values.astype(bf16)

                    @pl.when(rank > 0)
                    def _():
                        landed = landed_ref[way, step - 1].astype(f32)
                        staged_ref[way, step] = (values + landed).astype(bf16)

                copying(way, step, to).start()

        if step < len(stages):
            stages[step]()

        for way in (0, 1):
            rank = place if way == 0 else size - 1 - place
            origin = place - 1 if way == 0 else place + 1

            @pl.when(jnp.logical_and(rank > 0, rank - 1 <= step))
            def _():
                copying(way, step, origin).wait_recv()

    for stage in stages[size - 1 :]:
        stage()
    out_ref[...] = block(place)
    for way in (0, 1):
        rank = place if way == 0 else size - 1 - place

        @pl.when(rank > 0)
        def _():
            out_ref[...] += landed_ref[way, size - 2].astype(f32)

    for step in range(size - 1):
        for way in (0, 1):
            rank = place if way == 0 else size - 1 - place
            to = place + 1 if way == 0 else place - 1

            @pl.when(jnp.logical_and(rank <= step, rank < size - 1))
            def _():
                copying(way, step, to).wait_send()


def closing_sums(
    sizes,
    narrow,
    in_ref,
    small_ref,
    out_ref,
    every_ref,
    line_ref,
    staged_ref,
    landed_ref,
    total_ref,
    small_tp_ref,
    small_ctx_ref,
    small_fsdp_ref,
    send_sem,
    recv_sem,
    small_send_sem,
    small_recv_sem,
):
    axes = ("tp", "ctx", "fsdp")
    barrier = pltpu.get_barrier_semaphore()
    for axis, size in zip(axes, sizes):
        place = lax.axis_index(axis)
        for offset in range(1, size):
            peer = lax.rem(place + offset, size)
            pl.semaphore_signal(barrier, inc=1, device_id={axis: peer}, device_id_type=MESH)
    pl.semaphore_wait(barrier, sum(sizes) - len(sizes))
    landings = (small_tp_ref, small_ctx_ref, small_fsdp_ref)

    def copying(axis, offset, peer):
        return pltpu.make_async_remote_copy(
            src_ref=small_ref if axis == 0 else total_ref.at[axis - 1],
            dst_ref=landings[axis].at[offset - 1],
            send_sem=small_send_sem.at[axis, offset - 1],
            recv_sem=small_recv_sem.at[axis, offset - 1],
            device_id={axes[axis]: peer},
            device_id_type=MESH,
        )

    def each(axis):
        size, place = sizes[axis], lax.axis_index(axes[axis])
        for offset in range(1, size):
            yield (
                offset,
                lax.rem(place + offset, size),
                lax.rem(place + size - offset, size),
            )

    def start(axis):
        for offset, to, origin in each(axis):
            copying(axis, offset, to).start()

    def finish(axis):
        total = small_ref[...] if axis == 0 else total_ref[axis - 1]
        for offset, to, origin in each(axis):
            copying(axis, offset, origin).wait_recv()
            total = total + landings[axis][offset - 1]
        for offset, to, origin in each(axis):
            copying(axis, offset, to).wait_send()
        return total

    def first():
        start(0)

    def second():
        total = finish(0)
        total_ref[0] = total
        line_ref[...] = total[:, narrow:]
        start(1)

    def third():
        total_ref[1] = finish(1)
        start(2)

    def last():
        every_ref[...] = finish(2)[:, :narrow]

    line_scatter(
        sizes[0],
        True,
        in_ref,
        out_ref,
        staged_ref,
        landed_ref,
        send_sem,
        recv_sem,
        stages=(first, second, third, last),
    )


def peer_barrier(axis, size):
    place = lax.axis_index(axis)
    barrier = pltpu.get_barrier_semaphore()
    for offset in range(1, size):
        peer = lax.rem(place + offset, size)
        pl.semaphore_signal(barrier, inc=1, device_id={axis: peer}, device_id_type=MESH)
    pl.semaphore_wait(barrier, size - 1)


def peer_gather(size, in_ref, out_ref, own_sem, send_sem, recv_sem):
    place = lax.axis_index("ctx")
    rows = in_ref.shape[0]

    def block(index):
        return out_ref.at[pl.ds(pl.multiple_of(index * rows, rows), rows), :]

    def copying(offset, source, peer):
        return pltpu.make_async_remote_copy(
            src_ref=in_ref,
            dst_ref=block(source),
            send_sem=send_sem.at[offset - 1],
            recv_sem=recv_sem.at[offset - 1],
            device_id={"ctx": peer},
            device_id_type=MESH,
        )

    peer_barrier("ctx", size)
    own = pltpu.make_async_copy(in_ref, block(place), own_sem)
    own.start()
    for offset in range(1, size):
        copying(offset, place, lax.rem(place + offset, size)).start()
    for offset in range(1, size):
        origin = lax.rem(place + size - offset, size)
        copying(offset, origin, origin).wait_recv()
    for offset in range(1, size):
        copying(offset, place, lax.rem(place + offset, size)).wait_send()
    own.wait()


def peer_scatter(size, in_ref, out_ref, landed_ref, send_sem, recv_sem):
    place = lax.axis_index("ctx")
    rows = out_ref.shape[0]

    def at(index):
        return pl.ds(pl.multiple_of(index * rows, rows), rows)

    def copying(offset, peer):
        return pltpu.make_async_remote_copy(
            src_ref=in_ref.at[at(peer), :],
            dst_ref=landed_ref.at[offset - 1],
            send_sem=send_sem.at[offset - 1],
            recv_sem=recv_sem.at[offset - 1],
            device_id={"ctx": peer},
            device_id_type=MESH,
        )

    peer_barrier("ctx", size)
    for offset in range(1, size):
        copying(offset, lax.rem(place + offset, size)).start()
    total = in_ref[at(place), :].astype(f32)
    for offset in range(1, size):
        origin = lax.rem(place + size - offset, size)
        copying(offset, origin).wait_recv()
        total = total + landed_ref[offset - 1].astype(f32)
    out_ref[...] = total.astype(bf16)
    for offset in range(1, size):
        copying(offset, lax.rem(place + offset, size)).wait_send()


def remote_params(number):
    return pltpu.CompilerParams(
        collective_id=number, has_side_effects=True, vmem_limit_bytes=VMEM_BYTES
    )


def gather_tp(values, columns, number):
    size = lax.axis_size("tp")
    rows, width = values.shape
    shape = (rows, size * width) if columns else (size * rows, width)
    return pl.pallas_call(
        functools.partial(line_gather, size, columns),
        in_specs=[pl.BlockSpec(memory_space=pl.ANY)],
        out_specs=pl.BlockSpec(memory_space=pl.ANY),
        out_shape=jax.ShapeDtypeStruct(shape, values.dtype),
        scratch_shapes=[
            pltpu.SemaphoreType.DMA,
            pltpu.SemaphoreType.DMA((2, size - 1)),
            pltpu.SemaphoreType.DMA((2, size - 1)),
        ],
        compiler_params=remote_params(number),
        cost_estimate=pl.CostEstimate(flops=0, bytes_accessed=150_000_000, transcendentals=0),
        name="gather_tp",
    )(values)


def scatter_tp(values, columns, number):
    size = lax.axis_size("tp")
    rows, width = values.shape
    shape = (rows, width // size) if columns else (rows // size, width)
    return pl.pallas_call(
        functools.partial(line_scatter, size, columns),
        in_specs=[pl.BlockSpec(memory_space=pltpu.VMEM)],
        out_specs=pl.BlockSpec(memory_space=pltpu.VMEM),
        out_shape=jax.ShapeDtypeStruct(shape, f32),
        scratch_shapes=[
            pltpu.VMEM((2, size - 1, *shape), bf16),
            pltpu.VMEM((2, size - 1, *shape), bf16),
            pltpu.SemaphoreType.DMA((2, size - 1)),
            pltpu.SemaphoreType.DMA((2, size - 1)),
        ],
        compiler_params=remote_params(number),
        cost_estimate=pl.CostEstimate(flops=0, bytes_accessed=150_000_000, transcendentals=0),
        name="scatter_tp",
    )(values)


def close_tp(values, gains, along, number):
    sizes = tuple(lax.axis_size(axis) for axis in ("tp", "ctx", "fsdp"))
    rows, width = values.shape
    shape = (rows, width // sizes[0])
    pad = lambda row: jnp.pad(row, (0, -row.shape[0] % 1024)).reshape(8, -1)
    gains_b, along_b = pad(gains), pad(along)
    narrow, wide = gains_b.shape[1], along_b.shape[1]
    small = jnp.concatenate([gains_b, along_b], axis=1)
    peers = max(sizes) - 1
    out, every, line = pl.pallas_call(
        functools.partial(closing_sums, sizes, narrow),
        in_specs=[pl.BlockSpec(memory_space=pltpu.VMEM)] * 2,
        out_specs=[pl.BlockSpec(memory_space=pltpu.VMEM)] * 3,
        out_shape=[
            jax.ShapeDtypeStruct(shape, f32),
            jax.ShapeDtypeStruct((8, narrow), f32),
            jax.ShapeDtypeStruct((8, wide), f32),
        ],
        scratch_shapes=[
            pltpu.VMEM((2, sizes[0] - 1, *shape), bf16),
            pltpu.VMEM((2, sizes[0] - 1, *shape), bf16),
            pltpu.VMEM((2, *small.shape), f32),
            *[pltpu.VMEM((size - 1, *small.shape), f32) for size in sizes],
            pltpu.SemaphoreType.DMA((2, sizes[0] - 1)),
            pltpu.SemaphoreType.DMA((2, sizes[0] - 1)),
            pltpu.SemaphoreType.DMA((3, peers)),
            pltpu.SemaphoreType.DMA((3, peers)),
        ],
        compiler_params=remote_params(number),
        cost_estimate=pl.CostEstimate(flops=0, bytes_accessed=150_000_000, transcendentals=0),
        name="close_tp",
    )(values, small)
    return out, every.reshape(-1)[: gains.shape[0]], line.reshape(-1)[: along.shape[0]]


def gather_ctx(values, number):
    size = lax.axis_size("ctx")
    rows, width = values.shape
    return pl.pallas_call(
        functools.partial(peer_gather, size),
        in_specs=[pl.BlockSpec(memory_space=pl.ANY)],
        out_specs=pl.BlockSpec(memory_space=pl.ANY),
        out_shape=jax.ShapeDtypeStruct((size * rows, width), values.dtype),
        scratch_shapes=[
            pltpu.SemaphoreType.DMA,
            pltpu.SemaphoreType.DMA((size - 1,)),
            pltpu.SemaphoreType.DMA((size - 1,)),
        ],
        compiler_params=remote_params(number),
        cost_estimate=pl.CostEstimate(flops=0, bytes_accessed=100_000_000, transcendentals=0),
        name="gather_ctx",
    )(values)


def scatter_ctx(values, number):
    size = lax.axis_size("ctx")
    rows, width = values.shape
    shape = (rows // size, width)
    return pl.pallas_call(
        functools.partial(peer_scatter, size),
        in_specs=[pl.BlockSpec(memory_space=pltpu.VMEM)],
        out_specs=pl.BlockSpec(memory_space=pltpu.VMEM),
        out_shape=jax.ShapeDtypeStruct(shape, values.dtype),
        scratch_shapes=[
            pltpu.VMEM((size - 1, *shape), bf16),
            pltpu.SemaphoreType.DMA((size - 1,)),
            pltpu.SemaphoreType.DMA((size - 1,)),
        ],
        compiler_params=remote_params(number),
        cost_estimate=pl.CostEstimate(flops=0, bytes_accessed=100_000_000, transcendentals=0),
        name="scatter_ctx",
    )(values)


def attend(scale, query_ref, key_ref, value_ref, seg_row_ref, seg_column_ref, out_ref, total_ref):
    scores = matmul_nt(key_ref[...], query_ref[...]) * scale
    scores = jnp.where(seg_column_ref[...] == seg_row_ref[...], scores, masked_score)
    most = jnp.max(scores, axis=0, keepdims=True)
    probs = jnp.exp(scores - most)
    total = jnp.sum(probs, axis=0, keepdims=True)
    mixed = matmul(value_ref[...].T, probs.astype(bf16)) / total
    out_ref[...] = mixed.T.astype(bf16)
    total_ref[...] = most + jnp.log(total)


def attend_back(
    scale,
    query_ref,
    key_ref,
    value_ref,
    seg_row_ref,
    seg_column_ref,
    out_ref,
    total_ref,
    grad_ref,
    query_grad_ref,
    key_grad_ref,
    value_grad_ref,
    key_sum_ref,
    value_sum_ref,
):
    step = pl.program_id(1)
    query, key, grad = query_ref[...], key_ref[...], grad_ref[...]
    scores = matmul_nt(key, query) * scale
    scores = jnp.where(seg_column_ref[...] == seg_row_ref[...], scores, masked_score)
    probs = jnp.exp(scores - total_ref[...])
    products = grad.astype(f32) * out_ref[...].astype(f32)
    delta = jnp.sum(products.T, axis=0, keepdims=True)
    score_grad = (probs * (matmul_nt(value_ref[...], grad) - delta)).astype(bf16)
    query_grad_ref[...] = (matmul(key.T, score_grad) * scale).T
    key_part = matmul(score_grad, query) * scale
    value_part = matmul(probs.astype(bf16), grad)

    @pl.when(step == 0)
    def _():
        key_sum_ref[...] = key_part
        value_sum_ref[...] = value_part

    @pl.when(step > 0)
    def _():
        key_sum_ref[...] += key_part
        value_sum_ref[...] += value_part

    @pl.when(step == pl.num_programs(1) - 1)
    def _():
        key_grad_ref[...] = key_sum_ref[...].astype(bf16)
        value_grad_ref[...] = value_sum_ref[...].astype(bf16)


def attention_specs(rows, keys, heads, head_dim):
    block = min(rows, QUERY_BLOCK)
    query = pl.BlockSpec((block, head_dim), lambda h, i: (i, h))
    return (
        (heads, rows // block),
        [
            query,
            pl.BlockSpec((keys, head_dim), lambda h, i: (0, h)),
            pl.BlockSpec((keys, head_dim), lambda h, i: (0, h + heads)),
            pl.BlockSpec((None, 1, block), lambda h, i: (i, 0, 0)),
            pl.BlockSpec((keys, 1), lambda h, i: (0, 0)),
        ],
        query,
        pl.BlockSpec((None, None, 1, block), lambda h, i: (h, i, 0, 0)),
        pl.BlockSpec((keys, head_dim), lambda h, i: (0, h)),
    )


def run_attend(query_b, group, seg_rows, seg_columns, heads, scale):
    rows, keys = query_b.shape[0], group.shape[0]
    head_dim = query_b.shape[1] // heads
    grid, specs, query, total, unused = attention_specs(rows, keys, heads, head_dim)
    work = heads * rows * keys
    return pl.pallas_call(
        functools.partial(attend, scale),
        grid=grid,
        in_specs=specs,
        out_specs=[query, total],
        out_shape=[
            jax.ShapeDtypeStruct(query_b.shape, bf16),
            jax.ShapeDtypeStruct((*grid, 1, rows // grid[1]), f32),
        ],
        compiler_params=params(2),
        cost_estimate=pl.CostEstimate(
            flops=4 * work * head_dim, bytes_accessed=8 * query_b.size, transcendentals=work
        ),
        name="attend",
    )(query_b, group, group, seg_rows, seg_columns)


def run_attend_back(query_b, group, seg_rows, seg_columns, out_b, total, grad_b, heads, scale):
    rows, keys = query_b.shape[0], group.shape[0]
    head_dim = query_b.shape[1] // heads
    grid, specs, query, total_spec, key = attention_specs(rows, keys, heads, head_dim)
    work = heads * rows * keys
    return pl.pallas_call(
        functools.partial(attend_back, scale),
        grid=grid,
        in_specs=[*specs, query, total_spec, query],
        out_specs=[query, key, key],
        out_shape=[
            jax.ShapeDtypeStruct(query_b.shape, f32),
            jax.ShapeDtypeStruct((keys, query_b.shape[1]), bf16),
            jax.ShapeDtypeStruct((keys, query_b.shape[1]), bf16),
        ],
        scratch_shapes=[pltpu.VMEM((keys, head_dim), f32)] * 2,
        compiler_params=params(2),
        cost_estimate=pl.CostEstimate(
            flops=10 * work * head_dim, bytes_accessed=16 * query_b.size, transcendentals=work
        ),
        name="attend_back",
    )(query_b, group, group, seg_rows, seg_columns, out_b, total, grad_b)


def beside(values):
    return lax.ppermute(values, "fsdp", [(0, 1), (1, 0), (2, 3), (3, 2)])


def across(values):
    return lax.ppermute(values, "fsdp", [(0, 2), (1, 3), (2, 0), (3, 1)])


def other(values):
    return lax.ppermute(values, "ctx", [(0, 1), (1, 0)])


def added(*values):
    total = values[0].astype(f32)
    for value in values[1:]:
        total = total + value.astype(f32)
    return total.astype(bf16)


def then(first, *values):
    return lax.optimization_barrier((first, *values))[1:]


def by_chips():
    return lax.axis_size("fsdp") == 4 and lax.axis_size("ctx") == 2


def chunk_order(chunks):
    if not by_chips():
        return jnp.arange(chunks, dtype=jnp.int32)
    fsdp, ctx = lax.axis_index("fsdp"), lax.axis_index("ctx")
    sibling = fsdp + 1 - 2 * lax.rem(fsdp, 2)
    flip = lambda core: lax.rem(core + 2, 4)
    places = (
        (flip(sibling), ctx),
        (flip(fsdp), ctx),
        (sibling, 1 - ctx),
        (fsdp, 1 - ctx),
        (flip(sibling), 1 - ctx),
        (flip(fsdp), 1 - ctx),
        (sibling, ctx),
        (fsdp, ctx),
    )
    return jnp.stack([jnp.asarray(2 * f + c, jnp.int32) for f, c in places])


def expert_steps(ids, own_tokens, grad_all, rank_rows, rank_columns, first, weights):
    gate_weight, up_weight, down_weight = weights
    chunks = rank_rows.shape[0]

    def one_pass(at, near, far, product, kept):
        return run_expert_pass(
            jnp.array([at, at + 1], jnp.int32),
            first,
            rank_rows,
            rank_columns,
            near,
            far,
            product,
            gate_weight,
            up_weight,
            kept,
        )

    if not by_chips():
        token_all = lax.all_gather(own_tokens, ROWS, axis=0, tiled=True)
        blocks = token_all.reshape(chunks, CHUNK, -1)
        grad_slots, product = run_select_grads(ids, rank_rows, grad_all, down_weight)
        kept, backs = (), []
        for at in range(0, chunks, 2):
            kept, near, far = one_pass(at, blocks[at], blocks[at + 1], product, kept)
            backs += [near, far]
        back_sum = lax.psum_scatter(
            jnp.concatenate(backs), ROWS, scatter_dimension=0, tiled=True
        )
        out_part = run_expert_sums(ids, rank_columns, kept[1], down_weight)
        return kept, grad_slots, back_sum, out_part

    from_across, from_other = across(own_tokens), other(own_tokens)
    from_beside = beside(own_tokens)
    grad_slots, product = run_select_grads(ids, rank_rows, grad_all, down_weight)
    from_across, from_other = then(product, from_across, from_other)
    kept, back_sum, out_part = run_exchange_pass(
        rank_rows,
        rank_columns,
        product,
        weights,
        (own_tokens, from_beside, from_across, from_other),
    )
    return kept, grad_slots, back_sum, out_part


def head_blocks(width, head_dim):
    for at in range(0, width, head_dim):
        yield slice(at, at + head_dim)


def project(
    input_ref,
    gain_ref,
    weight_ref,
    cosine_ref,
    sine_ref,
    head_gain_ref,
    normed_ref,
    inverse_ref,
    pre_ref,
    query_ref,
    group_ref,
):
    values = input_ref[...].astype(f32)
    inverse = norm_scale(values)
    normed = (values * inverse * gain_ref[...]).astype(bf16)
    normed_ref[...] = normed
    inverse_ref[...] = inverse
    qkv = matmul(normed, weight_ref[...])
    width = query_ref.shape[1]
    head_dim = cosine_ref.shape[1]
    pre_ref[...] = qkv[:, : 2 * width]
    cosine, sine = cosine_ref[...], sine_ref[...]
    for which in (0, 1):
        gain = head_gain_ref[which : which + 1, :]
        for at in head_blocks(width, head_dim):
            head = qkv[:, which * width + at.start : which * width + at.stop]
            head = head * norm_scale(head) * gain
            turned = head * cosine + pltpu.roll(head, head_dim // 2, 1) * sine
            to_ref = query_ref if which == 0 else group_ref
            to_ref[:, at] = turned.astype(bf16)
    group_ref[:, width : 2 * width] = qkv[:, 2 * width :].astype(bf16)


def project_back(
    query_grad_ref,
    group_grad_ref,
    pre_ref,
    cosine_ref,
    sine_ref,
    head_gain_ref,
    weight_ref,
    input_ref,
    inverse_ref,
    gain_ref,
    grad_ref,
    part_ref,
    along_ref,
    terms_ref,
    head_terms_ref,
):
    width = query_grad_ref.shape[1]
    head_dim = cosine_ref.shape[1]
    cosine, sine = cosine_ref[...], sine_ref[...]

    @pl.when(pl.program_id(0) == 0)
    def _():
        terms_ref[...] = jnp.zeros_like(terms_ref)
        head_terms_ref[...] = jnp.zeros_like(head_terms_ref)

    for which in (0, 1):
        gain = head_gain_ref[which : which + 1, :]
        from_ref = query_grad_ref if which == 0 else group_grad_ref
        for at in head_blocks(width, head_dim):
            own = slice(which * width + at.start, which * width + at.stop)
            grad = from_ref[:, at].astype(f32)
            incoming = grad * cosine - pltpu.roll(grad, head_dim // 2, 1) * sine
            head = pre_ref[:, own]
            value_grad, gain_terms = norm_back(incoming, head, norm_scale(head), gain)
            grad_ref[:, own] = value_grad.astype(bf16)
            head_terms_ref[which : which + 1, :] += jnp.sum(gain_terms, axis=0, keepdims=True)
    grad_ref[:, 2 * width :] = group_grad_ref[:, width:]
    part = matmul_nt(grad_ref[...], weight_ref[...])
    part_ref[...] = part.astype(bf16)
    product = part * input_ref[...].astype(f32)
    terms_ref[...] += jnp.sum(product * inverse_ref[...], axis=0, keepdims=True)
    along_ref[...] = jnp.sum(product * gain_ref[...], axis=1, keepdims=True)


def run_project(input_b, gain, full, cosine, sine, head_gains, width):
    rows, depth = input_b.shape
    head_dim = cosine.shape[1]
    block = min(rows, QUERY_BLOCK)
    by_rows = lambda columns: pl.BlockSpec((block, columns), lambda i: (i, 0))
    return pl.pallas_call(
        project,
        grid=(rows // block,),
        in_specs=[
            by_rows(depth),
            once((1, depth)),
            once((depth, 3 * width)),
            by_rows(head_dim),
            by_rows(head_dim),
            once((2, head_dim)),
        ],
        out_specs=[
            by_rows(depth),
            by_rows(1),
            by_rows(2 * width),
            by_rows(width),
            by_rows(2 * width),
        ],
        out_shape=[
            jax.ShapeDtypeStruct((rows, depth), bf16),
            jax.ShapeDtypeStruct((rows, 1), f32),
            jax.ShapeDtypeStruct((rows, 2 * width), f32),
            jax.ShapeDtypeStruct((rows, width), bf16),
            jax.ShapeDtypeStruct((rows, 2 * width), bf16),
        ],
        compiler_params=params(1),
        cost_estimate=pl.CostEstimate(
            flops=6 * rows * depth * width, bytes_accessed=6 * depth * width, transcendentals=0
        ),
        name="project",
    )(input_b, gain, full, cosine, sine, head_gains)


def run_project_back(
    query_grad, group_grad, pre, cosine, sine, head_gains, full, input_b, inverse, gain
):
    rows, depth = input_b.shape
    width = query_grad.shape[1]
    head_dim = cosine.shape[1]
    block = min(rows, QUERY_BLOCK)
    by_rows = lambda columns: pl.BlockSpec((block, columns), lambda i: (i, 0))
    whole = lambda shape: pl.BlockSpec(shape, lambda i: (0, 0))
    return pl.pallas_call(
        project_back,
        grid=(rows // block,),
        in_specs=[
            by_rows(width),
            by_rows(2 * width),
            by_rows(2 * width),
            by_rows(head_dim),
            by_rows(head_dim),
            once((2, head_dim)),
            once((depth, 3 * width)),
            by_rows(depth),
            by_rows(1),
            once((1, depth)),
        ],
        out_specs=[
            by_rows(3 * width),
            by_rows(depth),
            by_rows(1),
            whole((1, depth)),
            whole((2, head_dim)),
        ],
        out_shape=[
            jax.ShapeDtypeStruct((rows, 3 * width), bf16),
            jax.ShapeDtypeStruct((rows, depth), bf16),
            jax.ShapeDtypeStruct((rows, 1), f32),
            jax.ShapeDtypeStruct((1, depth), f32),
            jax.ShapeDtypeStruct((2, head_dim), f32),
        ],
        compiler_params=params(1),
        cost_estimate=pl.CostEstimate(
            flops=6 * rows * depth * width, bytes_accessed=8 * depth * width, transcendentals=0
        ),
        name="project_back",
    )(query_grad, group_grad, pre, cosine, sine, head_gains, full, input_b, inverse, gain)


def grads_scatter(
    size,
    local,
    in_ref,
    small_ref,
    rows_ref,
    grad_rows_ref,
    gate_grad_ref,
    up_grad_ref,
    hidden_ref,
    out_ref,
    total_ref,
    gate_out_ref,
    up_out_ref,
    down_out_ref,
    staged_ref,
    landed_ref,
    small_landed_ref,
    first_ref,
    second_ref,
    send_sem,
    recv_sem,
    small_send_sem,
    small_recv_sem,
):
    step, part = pl.program_id(0), pl.program_id(1)
    place = lax.axis_index("tp")
    extent = out_ref.shape[0]

    def block(index):
        return in_ref[pl.ds(pl.multiple_of(index * extent, extent), extent), :].astype(f32)

    def copying(way, stage, to):
        return pltpu.make_async_remote_copy(
            src_ref=staged_ref.at[way, stage],
            dst_ref=landed_ref.at[way, stage],
            send_sem=send_sem.at[way, stage],
            recv_sem=recv_sem.at[way, stage],
            device_id={"tp": to},
            device_id_type=MESH,
        )

    def small_copy(offset, peer):
        return pltpu.make_async_remote_copy(
            src_ref=small_ref,
            dst_ref=small_landed_ref.at[offset - 1],
            send_sem=small_send_sem.at[offset - 1],
            recv_sem=small_recv_sem.at[offset - 1],
            device_id={"tp": peer},
            device_id_type=MESH,
        )

    def ways():
        yield 0, place, place + 1, place - 1
        yield 1, size - 1 - place, place - 1, place + 1

    def send(stage):
        for way, rank, to, origin in ways():
            target = size - 1 - stage + place if way == 0 else place - (size - 1 - stage)

            @pl.when(jnp.logical_and(rank <= stage, rank < size - 1))
            def _():
                values = block(target)
                if stage == 0:
                    staged_ref[way, stage] = values.astype(bf16)
                else:

                    @pl.when(rank == 0)
                    def _():
                        staged_ref[way, stage] = values.astype(bf16)

                    @pl.when(rank > 0)
                    def _():
                        landed = landed_ref[way, stage - 1].astype(f32)
                        staged_ref[way, stage] = (values + landed).astype(bf16)

                copying(way, stage, to).start()

    def receive(stage):
        for way, rank, to, origin in ways():

            @pl.when(jnp.logical_and(rank > 0, rank - 1 <= stage))
            def _():
                copying(way, stage, origin).wait_recv()

    @pl.when(jnp.logical_and(step == 0, part == 0))
    def _():
        peer_barrier("tp", size)
        for offset in range(1, size):
            small_copy(offset, lax.rem(place + offset, size)).start()
        send(0)

    for stage in range(1, size - 1):

        @pl.when(2 * step + part == min(3 * stage, 4 * local - 1))
        def _():
            receive(stage - 1)
            send(stage)

    def flat(ref):
        return ref[...].reshape(ref.shape[0] * ref.shape[1], ref.shape[2])

    def collect(sum_ref, values):
        @pl.when(part == 0)
        def _():
            sum_ref[...] = values

        @pl.when(part == 1)
        def _():
            sum_ref[...] += values

    @pl.when(step < local)
    def _():
        rows = flat(rows_ref)
        collect(first_ref, matmul(flat(gate_grad_ref).T, rows))
        collect(second_ref, matmul(flat(up_grad_ref).T, rows))

        @pl.when(part == 1)
        def _():
            gate_out_ref[...] = first_ref[...].T
            up_out_ref[...] = second_ref[...].T

    @pl.when(step >= local)
    def _():
        collect(down_out_ref, matmul(flat(hidden_ref).T, flat(grad_rows_ref)))

    @pl.when(jnp.logical_and(step == 2 * local - 1, part == 1))
    def _():
        total = small_ref[...]
        for offset in range(1, size):
            small_copy(offset, lax.rem(place + size - offset, size)).wait_recv()
            total = total + small_landed_ref[offset - 1]
        total_ref[...] = total
        receive(size - 2)
        out_ref[...] = block(place)
        for way, rank, to, origin in ways():

            @pl.when(rank > 0)
            def _():
                out_ref[...] += landed_ref[way, size - 2].astype(f32)

        for offset in range(1, size):
            small_copy(offset, lax.rem(place + offset, size)).wait_send()
        for stage in range(size - 1):
            for way, rank, to, origin in ways():

                @pl.when(jnp.logical_and(rank <= stage, rank < size - 1))
                def _():
                    copying(way, stage, to).wait_send()


def run_grads_scatter(values, small, token_slots, grad_slots, gate_grad, up_grad, hidden_rows):
    size = lax.axis_size("tp")
    rows, width = values.shape
    shape = (rows // size, width)
    chunks, local, slots, hidden = hidden_rows.shape
    half = chunks // 2
    early = lambda i, k: jnp.minimum(i, local - 1)
    late = lambda i, k: jnp.maximum(i - local, 0)
    early_part = lambda i, k: jnp.where(i < local, k, 1)
    late_part = lambda i, k: jnp.where(i < local, 0, k)
    wide = lambda at, part: pl.BlockSpec(
        (half, None, slots, width), lambda i, k: (part(i, k), at(i, k), 0, 0)
    )
    thin = lambda at, part: pl.BlockSpec(
        (half, None, slots, hidden), lambda i, k: (part(i, k), at(i, k), 0, 0)
    )
    tall = pl.BlockSpec((None, width, hidden), lambda i, k: (early(i, k), 0, 0))
    fixed = lambda form: pl.BlockSpec(form, lambda i, k: (0,) * len(form))
    return pl.pallas_call(
        functools.partial(grads_scatter, size, local),
        grid=(2 * local, 2),
        in_specs=[
            once(values.shape),
            once(small.shape),
            wide(early, early_part),
            wide(late, late_part),
            thin(early, early_part),
            thin(early, early_part),
            thin(late, late_part),
        ],
        out_specs=[
            fixed(shape),
            fixed(small.shape),
            tall,
            tall,
            pl.BlockSpec((None, hidden, width), lambda i, k: (late(i, k), 0, 0)),
        ],
        out_shape=[
            jax.ShapeDtypeStruct(shape, f32),
            jax.ShapeDtypeStruct(small.shape, f32),
            jax.ShapeDtypeStruct((local, width, hidden), f32),
            jax.ShapeDtypeStruct((local, width, hidden), f32),
            jax.ShapeDtypeStruct((local, hidden, width), f32),
        ],
        scratch_shapes=[
            pltpu.VMEM((2, size - 1, *shape), bf16),
            pltpu.VMEM((2, size - 1, *shape), bf16),
            pltpu.VMEM((size - 1, *small.shape), f32),
            pltpu.VMEM((hidden, width), f32),
            pltpu.VMEM((hidden, width), f32),
            pltpu.SemaphoreType.DMA((2, size - 1)),
            pltpu.SemaphoreType.DMA((2, size - 1)),
            pltpu.SemaphoreType.DMA((size - 1,)),
            pltpu.SemaphoreType.DMA((size - 1,)),
        ],
        compiler_params=pltpu.CompilerParams(
            dimension_semantics=("arbitrary",) * 2,
            collective_id=10,
            has_side_effects=True,
            vmem_limit_bytes=VMEM_BYTES,
        ),
        cost_estimate=pl.CostEstimate(
            flops=6 * chunks * local * slots * width * hidden,
            bytes_accessed=150_000_000,
            transcendentals=0,
        ),
        name="grads_scatter",
    )(values, small, token_slots, grad_slots, gate_grad, up_grad, hidden_rows)


def split_three(values):
    high = values.astype(bf16)
    rest = values - high.astype(f32)
    middle = rest.astype(bf16)
    return (high, middle, (rest - middle.astype(f32)).astype(bf16))


def on_device(
    layer_input,
    token_order,
    doc_lengths,
    expert_routes,
    attn_gain,
    query_weight,
    key_weight,
    value_weight,
    query_gain,
    key_gain,
    out_weight,
    moe_gain,
    router_weight,
    gate_weight,
    up_weight,
    down_weight,
    out_grad,
):
    tp_index = lax.axis_index("tp")
    ctx_size = lax.axis_size("ctx")
    fc_size = lax.axis_size("fsdp") * ctx_size
    fc_index = lax.axis_index("fsdp") * ctx_size + lax.axis_index("ctx")
    tok_count, quarter = layer_input.shape
    share = tok_count // lax.axis_size("tp")
    head_dim = query_gain.shape[0]
    head_width = query_weight.shape[1]
    heads = head_width // head_dim
    scale = head_dim ** (-0.5)
    experts = router_weight.shape[1]
    top = expert_routes.shape[1]
    local_experts = gate_weight.shape[0]
    capacity = tok_count * top * 5 // (4 * experts)
    own_rows = lambda values: lax.dynamic_slice_in_dim(values, tp_index * share, share, 0)
    own_width = lambda values: lax.dynamic_slice_in_dim(values, tp_index * quarter, quarter, 1)

    packed = jnp.concatenate(
        [
            query_weight,
            key_weight,
            value_weight,
            out_weight.T,
            router_weight,
            attn_gain[:, None],
            moe_gain[:, None],
            jnp.zeros((attn_gain.shape[0], EXTRA - experts - 2), bf16),
        ],
        axis=1,
    )
    full = lax.all_gather(packed, ROWS, axis=0, tiled=True)
    expert_ids = jnp.arange(experts, dtype=jnp.int32)
    named = jnp.any(expert_routes[:, :, None] == expert_ids[None, None, :], axis=1)
    earlier = jnp.tri(tok_count, tok_count, -1, dtype=bf16)
    before = matmul(earlier, named.astype(bf16))
    first_slot = (lax.rem(fc_index, CHUNK // tok_count) * capacity).astype(f32)
    ranks = jnp.where(named, before + first_slot, -1.0).astype(bf16)
    input_b = gather_tp(layer_input, True, 0)
    segment, position = doc_places(token_order[0], doc_lengths[0])
    ctx_index = lax.axis_index("ctx")
    seg_columns = jnp.zeros((ctx_size, tok_count), f32)
    for offset in range(ctx_size):
        piece = segment.astype(f32)[None, :]
        if offset > 0:
            pairs = [(at, (at + offset) % ctx_size) for at in range(ctx_size)]
            piece = lax.ppermute(piece, "ctx", pairs)
        origin = lax.rem(ctx_index + ctx_size - offset, ctx_size)
        seg_columns = lax.dynamic_update_slice_in_dim(seg_columns, piece, origin, 0)
    out_grad, full, input_b, seg_columns = lax.optimization_barrier(
        (out_grad, full, input_b, seg_columns)
    )
    grad_rows_b = lax.all_gather(out_grad, "tp", axis=1, tiled=True)
    side = 3 * head_width
    qkv_weight = full[:, :side]
    full_out = full[:, side : side + head_width]
    side = side + head_width
    full_router = full[:, side : side + experts]
    attn_gain_f = full[:, side + experts].astype(f32)
    moe_gain_f = full[:, side + experts + 1].astype(f32)
    width = input_b.shape[1]
    cosine, sine = rope_tables(position, head_dim)
    head_gains = jnp.stack([query_gain, key_gain])
    attn_gain_row = attn_gain_f[None, :]
    normed, inverse_one, heads_pre, query_rows, group_part = run_project(
        input_b,
        attn_gain_row,
        full,
        cosine,
        sine,
        head_gains,
        head_width,
    )
    group = gather_ctx(group_part, 1)
    after_group, group = lax.optimization_barrier((grad_rows_b, group))
    grad_packed = jnp.concatenate(
        [after_group, ranks, jnp.zeros((tok_count, EXTRA - experts), bf16)], axis=1
    )
    grad_all = lax.all_gather(grad_packed, ROWS, axis=0, tiled=True)
    chunks = grad_all.shape[0] // CHUNK
    first_expert = fc_index * local_experts
    local_ranks = lax.dynamic_slice_in_dim(
        grad_all[:, width:], first_expert, local_experts, 1
    ).astype(jnp.int32)
    ids = chunk_order(chunks)
    rank_columns = jnp.stack(
        [
            lax.dynamic_slice_in_dim(local_ranks, ids[at] * CHUNK, CHUNK, 0)
            for at in range(chunks)
        ]
    )
    rank_rows = jnp.transpose(rank_columns, (0, 2, 1))[:, :, None, :]

    seg_rows = segment.astype(f32).reshape(-1, 1, min(tok_count, QUERY_BLOCK))
    seg_columns = seg_columns.reshape(-1, 1)
    attn_b, log_total = run_attend(query_rows, group, seg_rows, seg_columns, heads, scale)
    attn_part = matmul_nt(attn_b, full_out).astype(bf16)
    attn_out = scatter_tp(attn_part, False, 2)
    resid = own_rows(input_b).astype(f32) + attn_out
    inverse_two = norm_scale(resid)
    moe_in = (resid * inverse_two * moe_gain_f).astype(bf16)
    logits = matmul(moe_in, full_router)
    own_named = own_rows(named)
    chosen = jnp.where(own_named, logits, -jnp.inf)
    gates = jax.nn.softmax(chosen, axis=-1)
    own_tokens = gather_tp(
        jnp.concatenate(
            [moe_in, *split_three(gates), jnp.zeros((share, EXTRA - 3 * experts), bf16)], axis=1
        ),
        False,
        3,
    )
    kept, grad_slots, back_sum, out_part = expert_steps(
        ids,
        own_tokens,
        grad_all,
        rank_rows,
        rank_columns,
        first_expert.reshape(1),
        (gate_weight, up_weight, down_weight),
    )
    token_slots, hidden_rows, gate_act_grad, up_act_grad, route_part = kept
    hit = jnp.arange(chunks, dtype=jnp.int32)[:, None] == ids[None, :]
    route_all = jnp.sum(
        jnp.where(hit[:, :, None, None], route_part[None, :, :, 0, :], 0.0), axis=1
    )
    route_all = jnp.transpose(route_all, (1, 0, 2)).reshape(
        local_experts, fc_size, tok_count
    )
    route_all = lax.all_to_all(
        jnp.transpose(route_all, (1, 0, 2)), ROWS, split_axis=0, concat_axis=0, tiled=True
    ).reshape(experts, tok_count)

    back_rows, gate_grad, grad_gate, grad_up, grad_down = run_grads_scatter(
        back_sum, route_all, token_slots, grad_slots, gate_act_grad, up_act_grad, hidden_rows
    )
    parts = own_tokens[:, width : width + 3 * experts].astype(f32)
    all_gates = parts[:, :experts] + parts[:, experts : 2 * experts] + parts[:, 2 * experts :]
    gate_grad = gate_grad.T
    logit_grad = all_gates * (
        gate_grad - jnp.sum(all_gates * gate_grad, axis=-1, keepdims=True)
    )
    grad_router = lax.dot_general(
        own_tokens[:, :width].astype(f32),
        logit_grad,
        (((0,), (0,)), ((), ())),
        precision=highest,
    )
    own_logit_grad = own_rows(logit_grad)
    router_back = lax.dot_general(
        own_logit_grad, full_router.astype(f32), (((1,), (1,)), ((), ())), precision=highest
    )
    moe_in_grad = (
        back_rows + router_back
    )
    resid_norm_grad, gain_terms = norm_back(moe_in_grad, resid, inverse_two, moe_gain_f)
    grad_moe_gain = jnp.sum(gain_terms, axis=0)
    resid_grad = own_rows(grad_rows_b).astype(f32) + resid_norm_grad
    resid_grad_b = gather_tp(resid_grad.astype(bf16), False, 5)

    out_sum = lax.psum_scatter(out_part, ROWS, scatter_dimension=0, tiled=True)

    grad_out = lax.dot_general(
        resid_grad_b, attn_b, (((0,), (0,)), ((), ())), preferred_element_type=f32
    )
    attn_grad = matmul(resid_grad_b, full_out).astype(bf16)
    query_rot_grad, key_part, value_part = run_attend_back(
        query_rows, group, seg_rows, seg_columns, attn_b, log_total, attn_grad, heads, scale
    )
    out_sum, key_part = lax.optimization_barrier((out_sum, key_part))
    out_sum = lax.psum_scatter(out_sum, "tp", scatter_dimension=0, tiled=True).astype(f32)
    group_grad = scatter_ctx(jnp.concatenate([key_part, value_part], axis=1), 6)
    qkv_grad, normed_part, along, attn_terms, head_terms = run_project_back(
        query_rot_grad,
        group_grad,
        heads_pre,
        cosine,
        sine,
        head_gains,
        full,
        input_b,
        inverse_one,
        attn_gain_row,
    )
    along = along[:, 0]
    gains = jnp.concatenate([attn_terms[0], grad_moe_gain, head_terms[0], head_terms[1]])
    normed_grad, gains, along = close_tp(normed_part, gains, along, 7)
    along = along[:, None] / width
    normed_grad, out_sum = lax.optimization_barrier((normed_grad, out_sum))
    grad_gate, grad_up, grad_down = then(normed_grad, grad_gate, grad_up, grad_down)
    grad_gate, grad_up, grad_down = [
        lax.clamp(jnp.float32(-jnp.inf), grad, jnp.float32(jnp.inf))
        for grad in (grad_gate, grad_up, grad_down)
    ]
    layer_sum = resid + out_sum
    layer_output = lax.all_to_all(
        layer_sum.astype(bf16), "tp", split_axis=1, concat_axis=0, tiled=True
    )
    input_quarter = layer_input.astype(f32)
    gain_quarter = lax.dynamic_slice_in_dim(attn_gain_f, tp_index * quarter, quarter, 0)
    grad_input = own_width(resid_grad_b).astype(f32) + inverse_one * (
        normed_grad * gain_quarter - input_quarter * inverse_one * inverse_one * along
    )
    grad_qkv = lax.dot_general(
        normed, qkv_grad, (((0,), (0,)), ((), ())), preferred_element_type=f32
    )
    owned_out = lax.psum_scatter(
        jnp.concatenate(
            [grad_out, grad_router, jnp.zeros((width, EXTRA - experts), f32)], axis=1
        ).astype(bf16),
        ROWS,
        scatter_dimension=0,
        tiled=True,
    )
    (owned_out,) = then(normed_grad, owned_out)
    owned_out = owned_out.astype(f32)
    owned_qkv = lax.psum_scatter(
        grad_qkv.astype(bf16), ROWS, scatter_dimension=0, tiled=True
    ).astype(f32)
    owned_gain = attn_gain.shape[0]
    own_gain = lambda at: lax.dynamic_slice_in_dim(
        gains, at * width + fc_index * owned_gain, owned_gain, 0
    )
    return (
        layer_output,
        grad_input,
        own_gain(0),
        owned_qkv[:, :head_width],
        owned_qkv[:, head_width : 2 * head_width],
        owned_qkv[:, 2 * head_width :],
        gains[2 * width : 2 * width + head_dim],
        gains[2 * width + head_dim :],
        owned_out[:, :head_width].T,
        own_gain(1),
        owned_out[:, head_width : head_width + experts],
        grad_gate,
        grad_up,
        grad_down,
    )


def solution(mesh):
    in_specs = (
        P(("fsdp", "ctx"), "tp"),
        P("fsdp", "ctx"),
        P("fsdp", None),
        P(("fsdp", "ctx"), None),
        P(("fsdp", "ctx")),
        P(("fsdp", "ctx"), "tp"),
        P(("fsdp", "ctx"), "tp"),
        P(("fsdp", "ctx"), "tp"),
        P(),
        P(),
        P("tp", ("fsdp", "ctx")),
        P(("fsdp", "ctx")),
        P(("fsdp", "ctx"), None),
        P(("fsdp", "ctx"), None, "tp"),
        P(("fsdp", "ctx"), None, "tp"),
        P(("fsdp", "ctx"), "tp", None),
        P(("fsdp", "ctx"), "tp"),
    )
    out_specs = (
        P(("fsdp", "ctx"), "tp"),
        P(("fsdp", "ctx"), "tp"),
        P(("fsdp", "ctx")),
        P(("fsdp", "ctx"), "tp"),
        P(("fsdp", "ctx"), "tp"),
        P(("fsdp", "ctx"), "tp"),
        P(),
        P(),
        P("tp", ("fsdp", "ctx")),
        P(("fsdp", "ctx")),
        P(("fsdp", "ctx"), None),
        P(("fsdp", "ctx"), None, "tp"),
        P(("fsdp", "ctx"), None, "tp"),
        P(("fsdp", "ctx"), "tp", None),
    )
    return jax.shard_map(
        on_device, mesh=mesh, in_specs=in_specs, out_specs=out_specs, check_vma=False
    )
```

```python
import functools

import jax
import jax.numpy as jnp
from jax import lax
from jax.experimental import pallas as pl
from jax.experimental.pallas import tpu as pltpu
from jax.sharding import PartitionSpec as P

QUERY_BLOCK = 384
CHUNK = 768
SLOTS = 256
EXTRA = 128
VMEM_BYTES = 60 * 1024 * 1024


epsilon = 1e-05
rope_base = 50000.0
masked_score = -1e30
highest = lax.Precision.HIGHEST
bf16 = jnp.bfloat16
f32 = jnp.float32
ROWS = ("fsdp", "ctx")
ALL = ("fsdp", "ctx", "tp")
MESH = pl.DeviceIdType.MESH


def doc_places(order_row, length_row):
    ends = jnp.cumsum(length_row, dtype=jnp.int32)
    passed = (order_row[:, None] >= ends[None, :]).astype(jnp.int32)
    segment = jnp.sum(passed, axis=1, dtype=jnp.int32)
    start = jnp.sum(passed * length_row[None, :], axis=1, dtype=jnp.int32)
    return (segment, order_row - start)


def rope_tables(position, head_dim):
    half = head_dim // 2
    freqs = rope_base ** (-(jnp.arange(half, dtype=jnp.float32) * (2.0 / head_dim)))
    angles = position.astype(jnp.float32)[:, None] * freqs[None, :]
    cosine, sine = jnp.cos(angles), jnp.sin(angles)
    return jnp.concatenate([cosine, cosine], axis=1), jnp.concatenate([-sine, sine], axis=1)


def norm_scale(values):
    return lax.rsqrt(jnp.mean(values * values, axis=-1, keepdims=True) + epsilon)


def norm_back(incoming, values, inverse, gain):
    scaled = incoming * gain
    value_grad = inverse * (
        scaled - values * inverse * inverse * jnp.mean(scaled * values, axis=-1, keepdims=True)
    )
    return (value_grad, incoming * values * inverse)


def matmul(left, right):
    return jnp.dot(left, right, preferred_element_type=f32)


def matmul_nt(left, right):
    return lax.dot_general(left, right, (((1,), (1,)), ((), ())), preferred_element_type=f32)


def slot_rows(rank_row):
    slots = lax.broadcasted_iota(jnp.int32, (SLOTS, rank_row.shape[1]), 0)
    return slots == rank_row


def slot_columns(rank_column):
    slots = lax.broadcasted_iota(jnp.int32, (rank_column.shape[0], SLOTS), 1)
    return jnp.where(slots == rank_column, 1.0, 0.0).astype(bf16)


def as_one_hot(mask):
    return jnp.where(mask, 1.0, 0.0).astype(bf16)


def select_grads(ids_ref, rank_ref, grad_ref, down_ref, rows_ref, product_ref):
    expert = pl.program_id(1)
    rows = matmul(as_one_hot(slot_rows(rank_ref[...])), grad_ref[...]).astype(bf16)
    rows_ref[...] = rows
    product_ref[...] = matmul_nt(rows, down_ref[expert])


def expert_step(
    expert,
    named,
    rank_ref,
    tokens,
    product_ref,
    gate_ref,
    up_ref,
    await_weights,
    rows_ref,
    hidden_ref,
    gate_grad_ref,
    up_grad_ref,
    route_ref,
    held_ref,
):
    width = rows_ref.shape[1]
    mask = slot_rows(rank_ref[...])
    picked = matmul(as_one_hot(mask), tokens)
    rows = picked[:, :width].astype(bf16)
    rows_ref[...] = rows
    lane = lax.broadcasted_iota(jnp.int32, (SLOTS, EXTRA), 1)
    mine = jnp.logical_and(lax.rem(lane, 32) == named, lane < 96)
    gate = jnp.sum(jnp.where(mine, picked[:, width:], 0.0), axis=1, keepdims=True)
    await_weights()
    gate_act = matmul(rows, gate_ref[expert])
    up_act = matmul(rows, up_ref[expert])
    sigmoid_g = 1.0 / (1.0 + jnp.exp(-gate_act))
    silu_g = gate_act * sigmoid_g
    hidden = silu_g * up_act
    hidden_ref[...] = (gate * hidden).astype(bf16)
    product = product_ref[...]
    route = jnp.sum(hidden.astype(bf16).astype(f32) * product, axis=1, keepdims=True)
    route_ref[...] = jnp.sum(jnp.where(mask, route, 0.0), axis=0, keepdims=True)
    hidden_grad = gate * product
    gate_grad = (
        hidden_grad * up_act * sigmoid_g * (1.0 + gate_act * (1.0 - sigmoid_g))
    ).astype(bf16)
    up_grad = (hidden_grad * silu_g).astype(bf16)
    gate_grad_ref[...] = gate_grad
    up_grad_ref[...] = up_grad
    back = matmul_nt(gate_grad, gate_ref[expert]) + matmul_nt(up_grad, up_ref[expert])
    held_ref[pl.ds(pl.multiple_of(expert * SLOTS, SLOTS), SLOTS), :] = back.astype(bf16)


def chunk_places(column_ref):
    columns = column_ref[...]
    return jnp.concatenate(
        [slot_columns(columns[:, e : e + 1]) for e in range(columns.shape[1])], axis=1
    )


def expert_pass(
    ids_ref,
    first_ref,
    rank_ref,
    column_ref,
    near_ref,
    far_ref,
    product_ref,
    gate_in_ref,
    up_in_ref,
    *refs,
):
    (
        rows_ref,
        hidden_ref,
        gate_grad_ref,
        up_grad_ref,
        route_ref,
        near_back_ref,
        far_back_ref,
        token_ref,
        gate_ref,
        up_ref,
        held_ref,
        back_ref,
        token_sem,
        gate_sem,
        up_sem,
        back_sem,
    ) = refs[-16:]
    chunk, expert = pl.program_id(0), pl.program_id(1)
    local = gate_ref.shape[0]
    width = rows_ref.shape[1]
    tiles = back_sem.shape[1]
    tile = width // tiles
    loads = [
        pltpu.make_async_copy(source, token_ref.at[at], token_sem.at[at])
        for at, source in enumerate((near_ref, far_ref))
    ]

    def weight_load(source, held, sem, at):
        return pltpu.make_async_copy(source.at[at], held.at[at], sem.at[at])

    def back_store(to, at, step):
        columns = pl.ds(step * tile, tile)
        return pltpu.make_async_copy(
            back_ref.at[at, :, columns], to.at[:, columns], back_sem.at[at, step]
        )

    @pl.when(jnp.logical_and(chunk == 0, expert == 0))
    def _():
        loads[0].start()
        for at in range(local):
            weight_load(gate_in_ref, gate_ref, gate_sem, at).start()
            weight_load(up_in_ref, up_ref, up_sem, at).start()
        loads[1].start()
        loads[0].wait()

    @pl.when(jnp.logical_and(chunk == 1, expert == 0))
    def _():
        loads[1].wait()

    def await_weights():
        @pl.when(chunk == 0)
        def _():
            weight_load(gate_in_ref, gate_ref, gate_sem, expert).wait()
            weight_load(up_in_ref, up_ref, up_sem, expert).wait()

    expert_step(
        expert,
        first_ref[0] + expert,
        rank_ref,
        token_ref[chunk],
        product_ref,
        gate_ref,
        up_ref,
        await_weights,
        rows_ref,
        hidden_ref,
        gate_grad_ref,
        up_grad_ref,
        route_ref,
        held_ref,
    )

    @pl.when(expert == local - 1)
    def _():
        places = chunk_places(column_ref)
        for step in range(tiles):
            at = pl.ds(step * tile, tile)
            back_ref[chunk, :, at] = matmul(places, held_ref[:, at]).astype(bf16)

            @pl.when(chunk == 0)
            def _():
                back_store(near_back_ref, 0, step).start()

            @pl.when(chunk == 1)
            def _():
                back_store(far_back_ref, 1, step).start()

    @pl.when(jnp.logical_and(chunk == 1, expert == local - 1))
    def _():
        for step in range(tiles):
            back_store(near_back_ref, 0, step).wait()
            back_store(far_back_ref, 1, step).wait()


def exchange_pass(
    rank_ref,
    column_ref,
    product_ref,
    gate_in_ref,
    up_in_ref,
    down_in_ref,
    own_ref,
    sibling_ref,
    from_across_ref,
    from_other_ref,
    rows_ref,
    hidden_ref,
    gate_grad_ref,
    up_grad_ref,
    route_ref,
    sum_ref,
    out_ref,
    inbox_ref,
    landing_ref,
    token_ref,
    gate_ref,
    up_ref,
    down_ref,
    hidden_held_ref,
    held_ref,
    far_ref,
    beside_ref,
    chip_ref,
    corner_ref,
    token_sem,
    gate_sem,
    up_sem,
    pass_send,
    pass_recv,
    far_send,
    far_recv,
    link_send,
    link_recv,
    store_sem,
    down_sem,
    out_sem,
    landing_sem,
):
    step, expert = pl.program_id(0), pl.program_id(1)
    local = gate_ref.shape[0]
    rows, width = far_ref.shape
    half = rows // 2
    fsdp, ctx = lax.axis_index("fsdp"), lax.axis_index("ctx")
    beside_id = {"fsdp": fsdp + 1 - 2 * lax.rem(fsdp, 2)}
    across_id = {"fsdp": lax.rem(fsdp + 2, 4)}
    other_id = {"ctx": 1 - ctx}
    last = expert == local - 1
    low, high = pl.ds(0, half), pl.ds(half, half)
    sources = (
        inbox_ref.at[0],
        from_across_ref,
        inbox_ref.at[1],
        from_other_ref,
        inbox_ref.at[3],
        inbox_ref.at[2],
        sibling_ref,
        own_ref,
    )

    def token_load(at):
        slot = at % 2
        return pltpu.make_async_copy(sources[at], token_ref.at[slot], token_sem.at[slot])

    def weight_load(source, held, sem, at):
        return pltpu.make_async_copy(source.at[at], held.at[at], sem.at[at])

    def pass_copy(number):
        source, to, peer = (
            (from_across_ref, inbox_ref.at[0], beside_id),
            (from_other_ref, inbox_ref.at[1], beside_id),
            (from_other_ref.at[low], inbox_ref.at[2, low], across_id),
            (from_across_ref.at[high], inbox_ref.at[2, high], other_id),
            (inbox_ref.at[2], inbox_ref.at[3], beside_id),
        )[number]
        return pltpu.make_async_remote_copy(
            src_ref=source,
            dst_ref=to,
            send_sem=pass_send.at[number],
            recv_sem=pass_recv.at[number],
            device_id=peer,
            device_id_type=MESH,
        )

    def far_copy(turn):
        return pltpu.make_async_remote_copy(
            src_ref=far_ref,
            dst_ref=beside_ref.at[turn % 2],
            send_sem=far_send.at[turn],
            recv_sem=far_recv.at[turn],
            device_id=beside_id,
            device_id_type=MESH,
        )

    def link_copy(number):
        source, to, peer = (
            (chip_ref.at[0, high], landing_ref.at[0, high], across_id),
            (chip_ref.at[1, low], landing_ref.at[1, low], other_id),
            (chip_ref.at[2, low], corner_ref.at[0], other_id),
            (chip_ref.at[2, high], corner_ref.at[1], across_id),
            (chip_ref.at[1, high], landing_ref.at[1, high], other_id),
            (chip_ref.at[0, low], landing_ref.at[0, low], across_id),
        )[number]
        return pltpu.make_async_remote_copy(
            src_ref=source,
            dst_ref=to,
            send_sem=link_send.at[number],
            recv_sem=link_recv.at[number],
            device_id=peer,
            device_id_type=MESH,
        )

    @pl.when(jnp.logical_and(step == 0, expert == 0))
    def _():
        barrier = pltpu.get_barrier_semaphore()
        for peer in (beside_id, across_id, other_id):
            pl.semaphore_signal(barrier, inc=1, device_id=peer, device_id_type=MESH)
        pl.semaphore_wait(barrier, 3)
        for number in range(4):
            pass_copy(number).start()
        for at in range(local):
            weight_load(gate_in_ref, gate_ref, gate_sem, at).start()
            weight_load(up_in_ref, up_ref, up_sem, at).start()
        down_load = pltpu.make_async_copy(down_in_ref, down_ref, down_sem)
        down_load.start()
        pass_copy(0).wait_recv()
        token_load(0).start()

    @pl.when(jnp.logical_and(step == 3, expert == 0))
    def _():
        pass_copy(2).wait_recv()
        pass_copy(3).wait_recv()
        pass_copy(4).start()

    for at in range(8):

        @pl.when(jnp.logical_and(step == at, expert == 0))
        def _():
            token_load(at).wait()

        if at < 7:

            @pl.when(jnp.logical_and(step == at, last))
            def _():
                if at == 1:
                    pass_copy(1).wait_recv()
                if at == 3:
                    pass_copy(4).wait_recv()
                token_load(at + 1).start()

    def await_weights():
        @pl.when(step == 0)
        def _():
            weight_load(gate_in_ref, gate_ref, gate_sem, expert).wait()
            weight_load(up_in_ref, up_ref, up_sem, expert).wait()

    first = (fsdp * 2 + ctx) * local

    @pl.when(step < 8)
    def _():
        expert_step(
            expert,
            first + expert,
            rank_ref,
            token_ref[lax.rem(step, 2)],
            product_ref,
            gate_ref,
            up_ref,
            await_weights,
            rows_ref,
            hidden_ref,
            gate_grad_ref,
            up_grad_ref,
            route_ref,
            held_ref,
        )
        hidden_held_ref[step, expert] = hidden_ref[...]

    tile = 512

    def tiles():
        for at in range(0, width, tile):
            yield pl.ds(at, tile)

    def add_half(turn, part, landed):
        total = chip_ref[turn, part, :].astype(f32) + corner_ref[landed].astype(f32)
        chip_ref[turn, part, :] = total.astype(bf16)

    for turn in range(4):

        @pl.when(jnp.logical_and(step == 2 * turn, last))
        def _():
            if turn > 0:
                far_copy(turn - 1).wait_send()
            places = chunk_places(column_ref)
            for at in tiles():
                far_ref[:, at] = matmul(places, held_ref[:, at]).astype(bf16)
            far_copy(turn).start()

        @pl.when(jnp.logical_and(step == 2 * turn + 1, last))
        def _():
            far_copy(turn).wait_recv()
            if turn == 3:
                far_copy(3).wait_send()
            places = chunk_places(column_ref)
            for at in tiles():
                total = matmul(places, held_ref[:, at]) + beside_ref[turn % 2, :, at].astype(f32)
                if turn < 3:
                    chip_ref[turn, :, at] = total.astype(bf16)
                else:
                    far_ref[:, at] = total.astype(bf16)
            if turn < 2:
                link_copy(turn).start()
            if turn == 2:
                link_copy(2).start()
                link_copy(3).start()


    number = step - 8
    turn = number // 2
    chip = lax.rem(fsdp + 2 * (1 - lax.rem(turn, 2)), 4)
    core = chip + (1 - lax.rem(number, 2)) * (1 - 2 * lax.rem(fsdp, 2))
    line = lax.rem(ctx + lax.rem((turn + 1) // 2, 2), 2)
    places_at = (core * 2 + line) * rows
    slot = lax.rem(step, 2)
    columns_of = width // local
    hidden = gate_ref.shape[2]

    def out_store(at, which):
        columns = pl.ds(pl.multiple_of(which * columns_of, columns_of), columns_of)
        return pltpu.make_async_copy(
            token_ref.at[slot, :, columns],
            out_ref.at[pl.ds(pl.multiple_of(at, rows), rows), columns],
            out_sem.at[slot, which],
        )

    @pl.when(step >= 8)
    def _():
        @pl.when(jnp.logical_and(step == 8, expert == 0))
        def _():
            pltpu.make_async_copy(down_in_ref, down_ref, down_sem).wait()

        @pl.when(expert == 0)
        def _():
            columns = column_ref[...]
            for e in range(local):
                held_ref[pl.ds(0, rows), pl.ds(e * hidden, hidden)] = matmul(
                    slot_columns(columns[:, e : e + 1]), hidden_held_ref[number, e]
                ).astype(bf16)

        @pl.when(step >= 10)
        def _():
            out_store(places_at, expert).wait()

        at = pl.ds(pl.multiple_of(expert * columns_of, columns_of), columns_of)
        token_ref[slot, :, at] = matmul(
            held_ref[pl.ds(0, rows), pl.ds(0, local * hidden)], down_ref[:, at]
        ).astype(bf16)
        out_store(places_at, expert).start()

    @pl.when(jnp.logical_and(step == 9, expert == 1))
    def _():
        link_copy(3).wait_recv()
        add_half(1, high, 1)
        link_copy(4).start()
        link_copy(2).wait_recv()
        add_half(0, low, 0)
        link_copy(5).start()

    @pl.when(jnp.logical_and(step == 15, last))
    def _():
        landing = []
        for way, numbers in enumerate(((0, 5), (1, 4))):
            for number in numbers:
                link_copy(number).wait_recv()
            copy = pltpu.make_async_copy(
                landing_ref.at[way], beside_ref.at[way], landing_sem.at[way]
            )
            copy.start()
            landing.append(copy)
        for copy in landing:
            copy.wait()
        for part in (low, high):
            held_ref[part, :] = (
                far_ref[part, :].astype(f32)
                + beside_ref[0, part, :].astype(f32)
                + beside_ref[1, part, :].astype(f32)
            ).astype(bf16)
        store = pltpu.make_async_copy(held_ref.at[pl.ds(0, rows)], sum_ref, store_sem)
        store.start()
        for number in range(5):
            pass_copy(number).wait_send()
        for number in range(6):
            link_copy(number).wait_send()
        for other_slot in (0, 1):
            for which in range(local):
                columns = pl.ds(which * columns_of, columns_of)
                pltpu.make_async_copy(
                    token_ref.at[other_slot, :, columns],
                    out_ref.at[pl.ds(0, rows), columns],
                    out_sem.at[other_slot, which],
                ).wait()
        store.wait()


def expert_sums(ids_ref, column_ref, hidden_ref, down_ref, out_ref):
    columns = column_ref[...]
    dense = [
        matmul(slot_columns(columns[:, e : e + 1]), hidden_ref[e]).astype(bf16)
        for e in range(columns.shape[1])
    ]
    out_ref[...] = matmul(jnp.concatenate(dense, axis=1), down_ref[...]).astype(bf16)


def params(dims):
    return pltpu.CompilerParams(
        dimension_semantics=("arbitrary",) * dims, vmem_limit_bytes=VMEM_BYTES
    )


def once(shape):
    return pl.BlockSpec(
        shape, lambda *ids: (0,) * len(shape), pipeline_mode=pl.Buffered(1)
    )


def run_select_grads(ids, rank_rows, grad_all, down_weight):
    chunks, local = rank_rows.shape[:2]
    hidden, width = down_weight.shape[1:]
    slots = chunks * local * SLOTS
    place = lambda g, e, ids: (g, e, 0, 0)
    return pl.pallas_call(
        select_grads,
        grid_spec=pltpu.PrefetchScalarGridSpec(
            num_scalar_prefetch=1,
            grid=(chunks, local),
            in_specs=[
                pl.BlockSpec((None, None, 1, CHUNK), place),
                pl.BlockSpec((CHUNK, width), lambda g, e, ids: (ids[g], 0)),
                once(down_weight.shape),
            ],
            out_specs=[
                pl.BlockSpec((None, None, SLOTS, width), place),
                pl.BlockSpec((None, None, SLOTS, hidden), place),
            ],
        ),
        out_shape=[
            jax.ShapeDtypeStruct((chunks, local, SLOTS, width), bf16),
            jax.ShapeDtypeStruct((chunks, local, SLOTS, hidden), f32),
        ],
        compiler_params=params(2),
        cost_estimate=pl.CostEstimate(
            flops=2 * slots * width * (CHUNK + hidden),
            bytes_accessed=2 * (chunks * CHUNK + slots) * width,
            transcendentals=0,
        ),
        name="select_grads",
    )(ids, rank_rows, grad_all, down_weight)


def run_exchange_pass(rank_rows, rank_columns, product, weights, sources):
    gate_weight, up_weight, down_weight = weights
    chunks, local = rank_rows.shape[:2]
    width, hidden = gate_weight.shape[1:]
    slots = chunks * local * SLOTS
    flat_down = down_weight.reshape(local * hidden, width)

    def per_expert(g, e):
        return (jnp.minimum(g, chunks - 1), jnp.where(g < chunks, e, local - 1), 0, 0)

    narrow = pl.BlockSpec((None, None, SLOTS, hidden), per_expert)
    anywhere = pl.BlockSpec(memory_space=pl.ANY)
    half = (2, CHUNK // 2, width)
    narrow_shape = jax.ShapeDtypeStruct((chunks, local, SLOTS, hidden), bf16)
    outs = pl.pallas_call(
        exchange_pass,
        grid=(2 * chunks, local),
        in_specs=[
            pl.BlockSpec((None, None, 1, CHUNK), per_expert),
            pl.BlockSpec((None, CHUNK, local), lambda g, e: (lax.rem(g, chunks), 0, 0)),
            narrow,
            *[anywhere] * 7,
        ],
        out_specs=[
            pl.BlockSpec((None, None, SLOTS, width), per_expert),
            narrow,
            narrow,
            narrow,
            pl.BlockSpec((None, None, 1, CHUNK), per_expert),
            *[anywhere] * 4,
        ],
        out_shape=[
            jax.ShapeDtypeStruct((chunks, local, SLOTS, width), bf16),
            narrow_shape,
            narrow_shape,
            narrow_shape,
            jax.ShapeDtypeStruct((chunks, local, 1, CHUNK), f32),
            jax.ShapeDtypeStruct((CHUNK, width), bf16),
            jax.ShapeDtypeStruct((chunks * CHUNK, width), bf16),
            jax.ShapeDtypeStruct((4, *sources[0].shape), bf16),
            jax.ShapeDtypeStruct((2, CHUNK, width), bf16),
        ],
        scratch_shapes=[
            pltpu.VMEM((2, CHUNK, width + EXTRA), bf16),
            pltpu.VMEM(gate_weight.shape, bf16),
            pltpu.VMEM(up_weight.shape, bf16),
            pltpu.VMEM(flat_down.shape, bf16),
            pltpu.VMEM((chunks, local, SLOTS, hidden), bf16),
            pltpu.VMEM((local * SLOTS, width), bf16),
            pltpu.VMEM((CHUNK, width), bf16),
            pltpu.VMEM((2, CHUNK, width), bf16),
            pltpu.VMEM((3, CHUNK, width), bf16),
            pltpu.VMEM(half, bf16),
            pltpu.SemaphoreType.DMA((2,)),
            pltpu.SemaphoreType.DMA((local,)),
            pltpu.SemaphoreType.DMA((local,)),
            pltpu.SemaphoreType.DMA((5,)),
            pltpu.SemaphoreType.DMA((5,)),
            pltpu.SemaphoreType.DMA((4,)),
            pltpu.SemaphoreType.DMA((4,)),
            pltpu.SemaphoreType.DMA((6,)),
            pltpu.SemaphoreType.DMA((6,)),
            pltpu.SemaphoreType.DMA,
            pltpu.SemaphoreType.DMA,
            pltpu.SemaphoreType.DMA((2, local)),
            pltpu.SemaphoreType.DMA((2,)),
        ],
        compiler_params=pltpu.CompilerParams(
            dimension_semantics=("arbitrary",) * 2,
            collective_id=9,
            has_side_effects=True,
            vmem_limit_bytes=VMEM_BYTES,
        ),
        cost_estimate=pl.CostEstimate(
            flops=2 * slots * width * (2 * CHUNK + 4 * hidden),
            bytes_accessed=2 * (12 * CHUNK + slots) * width,
            transcendentals=slots * hidden,
        ),
        name="exchange_pass",
    )(rank_rows, rank_columns, product, gate_weight, up_weight, flat_down, *sources)
    return outs[:5], outs[5], outs[6]


def run_expert_pass(
    ids, first, rank_rows, rank_columns, near, far, product, gate_weight, up_weight, kept
):
    chunks, local = rank_rows.shape[:2]
    width, hidden = gate_weight.shape[1:]
    slots = 2 * local * SLOTS
    per_expert = lambda g, e, ids: (ids[g], e, 0, 0)
    narrow = pl.BlockSpec((None, None, SLOTS, hidden), per_expert)
    in_specs = [
        pl.BlockSpec(memory_space=pltpu.SMEM),
        pl.BlockSpec((None, None, 1, CHUNK), per_expert),
        pl.BlockSpec((None, CHUNK, local), lambda g, e, ids: (ids[g], 0, 0)),
        pl.BlockSpec(memory_space=pl.ANY),
        pl.BlockSpec(memory_space=pl.ANY),
        narrow,
        pl.BlockSpec(memory_space=pl.ANY),
        pl.BlockSpec(memory_space=pl.ANY),
    ]
    kept_shapes = [
        jax.ShapeDtypeStruct((chunks, local, SLOTS, width), bf16),
        jax.ShapeDtypeStruct((chunks, local, SLOTS, hidden), bf16),
        jax.ShapeDtypeStruct((chunks, local, SLOTS, hidden), bf16),
        jax.ShapeDtypeStruct((chunks, local, SLOTS, hidden), bf16),
        jax.ShapeDtypeStruct((chunks, local, 1, CHUNK), f32),
    ]
    outs = pl.pallas_call(
        expert_pass,
        grid_spec=pltpu.PrefetchScalarGridSpec(
            num_scalar_prefetch=1,
            grid=(2, local),
            in_specs=in_specs + [pl.BlockSpec(memory_space=pl.ANY)] * len(kept),
            out_specs=[
                pl.BlockSpec((None, None, SLOTS, width), per_expert),
                narrow,
                narrow,
                narrow,
                pl.BlockSpec((None, None, 1, CHUNK), per_expert),
                pl.BlockSpec(memory_space=pl.ANY),
                pl.BlockSpec(memory_space=pl.ANY),
            ],
            scratch_shapes=[
                pltpu.VMEM((2, CHUNK, width + EXTRA), bf16),
                pltpu.VMEM(gate_weight.shape, bf16),
                pltpu.VMEM(up_weight.shape, bf16),
                pltpu.VMEM((local * SLOTS, width), bf16),
                pltpu.VMEM((2, CHUNK, width), bf16),
                pltpu.SemaphoreType.DMA((2,)),
                pltpu.SemaphoreType.DMA((local,)),
                pltpu.SemaphoreType.DMA((local,)),
                pltpu.SemaphoreType.DMA((2, 4)),
            ],
        ),
        out_shape=kept_shapes + [jax.ShapeDtypeStruct((CHUNK, width), bf16)] * 2,
        input_output_aliases={9 + at: at for at in range(len(kept))},
        compiler_params=params(2),
        cost_estimate=pl.CostEstimate(
            flops=2 * slots * width * (2 * CHUNK + 4 * hidden),
            bytes_accessed=2 * (4 * CHUNK + slots) * width,
            transcendentals=slots * hidden,
        ),
        name="expert_pass",
    )(ids, first, rank_rows, rank_columns, near, far, product, gate_weight, up_weight, *kept)
    return outs[:5], outs[5], outs[6]


def run_expert_sums(ids, rank_columns, hidden_rows, down_weight):
    chunks, local, unused, hidden = hidden_rows.shape
    width = down_weight.shape[2]
    flat = down_weight.reshape(local * hidden, width)
    return pl.pallas_call(
        expert_sums,
        grid_spec=pltpu.PrefetchScalarGridSpec(
            num_scalar_prefetch=1,
            grid=(chunks,),
            in_specs=[
                pl.BlockSpec((None, CHUNK, local), lambda g, ids: (g, 0, 0)),
                pl.BlockSpec((None, local, SLOTS, hidden), lambda g, ids: (g, 0, 0, 0)),
                once(flat.shape),
            ],
            out_specs=pl.BlockSpec((CHUNK, width), lambda g, ids: (ids[g], 0)),
        ),
        out_shape=jax.ShapeDtypeStruct((chunks * CHUNK, width), bf16),
        compiler_params=params(1),
        cost_estimate=pl.CostEstimate(
            flops=2 * chunks * CHUNK * local * hidden * (width + SLOTS),
            bytes_accessed=2 * chunks * CHUNK * width,
            transcendentals=0,
        ),
        name="expert_sums",
    )(ids, rank_columns, hidden_rows, flat)


def line_barrier(size):
    place = lax.axis_index("tp")
    barrier = pltpu.get_barrier_semaphore()

    @pl.when(place > 0)
    def _():
        pl.semaphore_signal(barrier, inc=1, device_id={"tp": place - 1}, device_id_type=MESH)

    @pl.when(place < size - 1)
    def _():
        pl.semaphore_signal(barrier, inc=1, device_id={"tp": place + 1}, device_id_type=MESH)

    has_left = jnp.where(place > 0, 1, 0)
    has_right = jnp.where(place < size - 1, 1, 0)
    pl.semaphore_wait(barrier, has_left + has_right)


def line_gather(size, columns, in_ref, out_ref, own_sem, send_sem, recv_sem):
    place = lax.axis_index("tp")
    extent = in_ref.shape[1] if columns else in_ref.shape[0]

    def block(index):
        at = pl.ds(pl.multiple_of(index * extent, extent), extent)
        return out_ref.at[:, at] if columns else out_ref.at[at, :]

    line_barrier(size)
    own = pltpu.make_async_copy(in_ref, block(place), own_sem)
    own.start()

    def sending(way, step):
        source = place - step if way == 0 else place + step
        to = place + 1 if way == 0 else place - 1
        return pltpu.make_async_remote_copy(
            src_ref=in_ref if step == 0 else block(source),
            dst_ref=block(source),
            send_sem=send_sem.at[way, step],
            recv_sem=recv_sem.at[way, step],
            device_id={"tp": to},
            device_id_type=MESH,
        )

    def sends(way, step):
        if way == 0:
            return jnp.logical_and(place >= step, place < size - 1)
        return jnp.logical_and(place + step < size, place > 0)

    def receiving(way, step):
        source = place - 1 - step if way == 0 else place + 1 + step
        origin = place - 1 if way == 0 else place + 1
        return pltpu.make_async_remote_copy(
            src_ref=block(source),
            dst_ref=block(source),
            send_sem=send_sem.at[way, step],
            recv_sem=recv_sem.at[way, step],
            device_id={"tp": origin},
            device_id_type=MESH,
        )

    def receives(way, step):
        return place > step if way == 0 else place + 1 + step < size

    for step in range(size - 1):
        for way in (0, 1):

            @pl.when(sends(way, step))
            def _():
                sending(way, step).start()

        for way in (0, 1):

            @pl.when(receives(way, step))
            def _():
                receiving(way, step).wait_recv()

    for step in range(size - 1):
        for way in (0, 1):

            @pl.when(sends(way, step))
            def _():
                sending(way, step).wait_send()

    own.wait()


def line_scatter(
    size, columns, in_ref, out_ref, staged_ref, landed_ref, send_sem, recv_sem, stages=()
):
    place = lax.axis_index("tp")
    extent = out_ref.shape[1] if columns else out_ref.shape[0]

    def block(index):
        at = pl.ds(pl.multiple_of(index * extent, extent), extent)
        values = in_ref[:, at] if columns else in_ref[at, :]
        return values.astype(f32)

    if not stages:
        line_barrier(size)

    def copying(way, step, to):
        return pltpu.make_async_remote_copy(
            src_ref=staged_ref.at[way, step],
            dst_ref=landed_ref.at[way, step],
            send_sem=send_sem.at[way, step],
            recv_sem=recv_sem.at[way, step],
            device_id={"tp": to},
            device_id_type=MESH,
        )

    for step in range(size - 1):
        for way in (0, 1):
            rank = place if way == 0 else size - 1 - place
            target = size - 1 - step + place if way == 0 else place - (size - 1 - step)
            to = place + 1 if way == 0 else place - 1
            active = jnp.logical_and(rank <= step, rank < size - 1)

            @pl.when(active)
            def _():
                values = block(target)
                if step == 0:
                    staged_ref[way, step] = values.astype(bf16)
                else:

                    @pl.when(rank == 0)
                    def _():
                        staged_ref[way, step] = values.astype(bf16)

                    @pl.when(rank > 0)
                    def _():
                        landed = landed_ref[way, step - 1].astype(f32)
                        staged_ref[way, step] = (values + landed).astype(bf16)

                copying(way, step, to).start()

        if step < len(stages):
            stages[step]()

        for way in (0, 1):
            rank = place if way == 0 else size - 1 - place
            origin = place - 1 if way == 0 else place + 1

            @pl.when(jnp.logical_and(rank > 0, rank - 1 <= step))
            def _():
                copying(way, step, origin).wait_recv()

    for stage in stages[size - 1 :]:
        stage()
    out_ref[...] = block(place)
    for way in (0, 1):
        rank = place if way == 0 else size - 1 - place

        @pl.when(rank > 0)
        def _():
            out_ref[...] += landed_ref[way, size - 2].astype(f32)

    for step in range(size - 1):
        for way in (0, 1):
            rank = place if way == 0 else size - 1 - place
            to = place + 1 if way == 0 else place - 1

            @pl.when(jnp.logical_and(rank <= step, rank < size - 1))
            def _():
                copying(way, step, to).wait_send()


def closing_sums(
    sizes,
    narrow,
    in_ref,
    small_ref,
    out_ref,
    every_ref,
    line_ref,
    staged_ref,
    landed_ref,
    total_ref,
    small_tp_ref,
    small_ctx_ref,
    small_fsdp_ref,
    send_sem,
    recv_sem,
    small_send_sem,
    small_recv_sem,
):
    axes = ("tp", "ctx", "fsdp")
    barrier = pltpu.get_barrier_semaphore()
    for axis, size in zip(axes, sizes):
        place = lax.axis_index(axis)
        for offset in range(1, size):
            peer = lax.rem(place + offset, size)
            pl.semaphore_signal(barrier, inc=1, device_id={axis: peer}, device_id_type=MESH)
    pl.semaphore_wait(barrier, sum(sizes) - len(sizes))
    landings = (small_tp_ref, small_ctx_ref, small_fsdp_ref)

    def copying(axis, offset, peer):
        return pltpu.make_async_remote_copy(
            src_ref=small_ref if axis == 0 else total_ref.at[axis - 1],
            dst_ref=landings[axis].at[offset - 1],
            send_sem=small_send_sem.at[axis, offset - 1],
            recv_sem=small_recv_sem.at[axis, offset - 1],
            device_id={axes[axis]: peer},
            device_id_type=MESH,
        )

    def each(axis):
        size, place = sizes[axis], lax.axis_index(axes[axis])
        for offset in range(1, size):
            yield (
                offset,
                lax.rem(place + offset, size),
                lax.rem(place + size - offset, size),
            )

    def start(axis):
        for offset, to, origin in each(axis):
            copying(axis, offset, to).start()

    def finish(axis):
        total = small_ref[...] if axis == 0 else total_ref[axis - 1]
        for offset, to, origin in each(axis):
            copying(axis, offset, origin).wait_recv()
            total = total + landings[axis][offset - 1]
        for offset, to, origin in each(axis):
            copying(axis, offset, to).wait_send()
        return total

    def first():
        start(0)

    def second():
        total = finish(0)
        total_ref[0] = total
        line_ref[...] = total[:, narrow:]
        start(1)

    def third():
        total_ref[1] = finish(1)
        start(2)

    def last():
        every_ref[...] = finish(2)[:, :narrow]

    line_scatter(
        sizes[0],
        True,
        in_ref,
        out_ref,
        staged_ref,
        landed_ref,
        send_sem,
        recv_sem,
        stages=(first, second, third, last),
    )


def peer_barrier(axis, size):
    place = lax.axis_index(axis)
    barrier = pltpu.get_barrier_semaphore()
    for offset in range(1, size):
        peer = lax.rem(place + offset, size)
        pl.semaphore_signal(barrier, inc=1, device_id={axis: peer}, device_id_type=MESH)
    pl.semaphore_wait(barrier, size - 1)


def peer_gather(size, in_ref, out_ref, own_sem, send_sem, recv_sem):
    place = lax.axis_index("ctx")
    rows = in_ref.shape[0]

    def block(index):
        return out_ref.at[pl.ds(pl.multiple_of(index * rows, rows), rows), :]

    def copying(offset, source, peer):
        return pltpu.make_async_remote_copy(
            src_ref=in_ref,
            dst_ref=block(source),
            send_sem=send_sem.at[offset - 1],
            recv_sem=recv_sem.at[offset - 1],
            device_id={"ctx": peer},
            device_id_type=MESH,
        )

    peer_barrier("ctx", size)
    own = pltpu.make_async_copy(in_ref, block(place), own_sem)
    own.start()
    for offset in range(1, size):
        copying(offset, place, lax.rem(place + offset, size)).start()
    for offset in range(1, size):
        origin = lax.rem(place + size - offset, size)
        copying(offset, origin, origin).wait_recv()
    for offset in range(1, size):
        copying(offset, place, lax.rem(place + offset, size)).wait_send()
    own.wait()


def peer_scatter(size, in_ref, out_ref, landed_ref, send_sem, recv_sem):
    place = lax.axis_index("ctx")
    rows = out_ref.shape[0]

    def at(index):
        return pl.ds(pl.multiple_of(index * rows, rows), rows)

    def copying(offset, peer):
        return pltpu.make_async_remote_copy(
            src_ref=in_ref.at[at(peer), :],
            dst_ref=landed_ref.at[offset - 1],
            send_sem=send_sem.at[offset - 1],
            recv_sem=recv_sem.at[offset - 1],
            device_id={"ctx": peer},
            device_id_type=MESH,
        )

    peer_barrier("ctx", size)
    for offset in range(1, size):
        copying(offset, lax.rem(place + offset, size)).start()
    total = in_ref[at(place), :].astype(f32)
    for offset in range(1, size):
        origin = lax.rem(place + size - offset, size)
        copying(offset, origin).wait_recv()
        total = total + landed_ref[offset - 1].astype(f32)
    out_ref[...] = total.astype(bf16)
    for offset in range(1, size):
        copying(offset, lax.rem(place + offset, size)).wait_send()


def remote_params(number):
    return pltpu.CompilerParams(
        collective_id=number, has_side_effects=True, vmem_limit_bytes=VMEM_BYTES
    )


def gather_tp(values, columns, number):
    size = lax.axis_size("tp")
    rows, width = values.shape
    shape = (rows, size * width) if columns else (size * rows, width)
    return pl.pallas_call(
        functools.partial(line_gather, size, columns),
        in_specs=[pl.BlockSpec(memory_space=pl.ANY)],
        out_specs=pl.BlockSpec(memory_space=pl.ANY),
        out_shape=jax.ShapeDtypeStruct(shape, values.dtype),
        scratch_shapes=[
            pltpu.SemaphoreType.DMA,
            pltpu.SemaphoreType.DMA((2, size - 1)),
            pltpu.SemaphoreType.DMA((2, size - 1)),
        ],
        compiler_params=remote_params(number),
        cost_estimate=pl.CostEstimate(flops=0, bytes_accessed=150_000_000, transcendentals=0),
        name="gather_tp",
    )(values)


def scatter_tp(values, columns, number):
    size = lax.axis_size("tp")
    rows, width = values.shape
    shape = (rows, width // size) if columns else (rows // size, width)
    return pl.pallas_call(
        functools.partial(line_scatter, size, columns),
        in_specs=[pl.BlockSpec(memory_space=pltpu.VMEM)],
        out_specs=pl.BlockSpec(memory_space=pltpu.VMEM),
        out_shape=jax.ShapeDtypeStruct(shape, f32),
        scratch_shapes=[
            pltpu.VMEM((2, size - 1, *shape), bf16),
            pltpu.VMEM((2, size - 1, *shape), bf16),
            pltpu.SemaphoreType.DMA((2, size - 1)),
            pltpu.SemaphoreType.DMA((2, size - 1)),
        ],
        compiler_params=remote_params(number),
        cost_estimate=pl.CostEstimate(flops=0, bytes_accessed=150_000_000, transcendentals=0),
        name="scatter_tp",
    )(values)


def close_tp(values, gains, along, number):
    sizes = tuple(lax.axis_size(axis) for axis in ("tp", "ctx", "fsdp"))
    rows, width = values.shape
    shape = (rows, width // sizes[0])
    pad = lambda row: jnp.pad(row, (0, -row.shape[0] % 1024)).reshape(8, -1)
    gains_b, along_b = pad(gains), pad(along)
    narrow, wide = gains_b.shape[1], along_b.shape[1]
    small = jnp.concatenate([gains_b, along_b], axis=1)
    peers = max(sizes) - 1
    out, every, line = pl.pallas_call(
        functools.partial(closing_sums, sizes, narrow),
        in_specs=[pl.BlockSpec(memory_space=pltpu.VMEM)] * 2,
        out_specs=[pl.BlockSpec(memory_space=pltpu.VMEM)] * 3,
        out_shape=[
            jax.ShapeDtypeStruct(shape, f32),
            jax.ShapeDtypeStruct((8, narrow), f32),
            jax.ShapeDtypeStruct((8, wide), f32),
        ],
        scratch_shapes=[
            pltpu.VMEM((2, sizes[0] - 1, *shape), bf16),
            pltpu.VMEM((2, sizes[0] - 1, *shape), bf16),
            pltpu.VMEM((2, *small.shape), f32),
            *[pltpu.VMEM((size - 1, *small.shape), f32) for size in sizes],
            pltpu.SemaphoreType.DMA((2, sizes[0] - 1)),
            pltpu.SemaphoreType.DMA((2, sizes[0] - 1)),
            pltpu.SemaphoreType.DMA((3, peers)),
            pltpu.SemaphoreType.DMA((3, peers)),
        ],
        compiler_params=remote_params(number),
        cost_estimate=pl.CostEstimate(flops=0, bytes_accessed=150_000_000, transcendentals=0),
        name="close_tp",
    )(values, small)
    return out, every.reshape(-1)[: gains.shape[0]], line.reshape(-1)[: along.shape[0]]


def gather_ctx(values, number):
    size = lax.axis_size("ctx")
    rows, width = values.shape
    return pl.pallas_call(
        functools.partial(peer_gather, size),
        in_specs=[pl.BlockSpec(memory_space=pl.ANY)],
        out_specs=pl.BlockSpec(memory_space=pl.ANY),
        out_shape=jax.ShapeDtypeStruct((size * rows, width), values.dtype),
        scratch_shapes=[
            pltpu.SemaphoreType.DMA,
            pltpu.SemaphoreType.DMA((size - 1,)),
            pltpu.SemaphoreType.DMA((size - 1,)),
        ],
        compiler_params=remote_params(number),
        cost_estimate=pl.CostEstimate(flops=0, bytes_accessed=100_000_000, transcendentals=0),
        name="gather_ctx",
    )(values)


def scatter_ctx(values, number):
    size = lax.axis_size("ctx")
    rows, width = values.shape
    shape = (rows // size, width)
    return pl.pallas_call(
        functools.partial(peer_scatter, size),
        in_specs=[pl.BlockSpec(memory_space=pltpu.VMEM)],
        out_specs=pl.BlockSpec(memory_space=pltpu.VMEM),
        out_shape=jax.ShapeDtypeStruct(shape, values.dtype),
        scratch_shapes=[
            pltpu.VMEM((size - 1, *shape), bf16),
            pltpu.SemaphoreType.DMA((size - 1,)),
            pltpu.SemaphoreType.DMA((size - 1,)),
        ],
        compiler_params=remote_params(number),
        cost_estimate=pl.CostEstimate(flops=0, bytes_accessed=100_000_000, transcendentals=0),
        name="scatter_ctx",
    )(values)


def attend(scale, query_ref, key_ref, value_ref, seg_row_ref, seg_column_ref, out_ref, total_ref):
    scores = matmul_nt(key_ref[...], query_ref[...]) * scale
    scores = jnp.where(seg_column_ref[...] == seg_row_ref[...], scores, masked_score)
    most = jnp.max(scores, axis=0, keepdims=True)
    probs = jnp.exp(scores - most)
    total = jnp.sum(probs, axis=0, keepdims=True)
    mixed = matmul(value_ref[...].T, probs.astype(bf16)) / total
    out_ref[...] = mixed.T.astype(bf16)
    total_ref[...] = most + jnp.log(total)


def attend_back(
    scale,
    query_ref,
    key_ref,
    value_ref,
    seg_row_ref,
    seg_column_ref,
    out_ref,
    total_ref,
    grad_ref,
    query_grad_ref,
    key_grad_ref,
    value_grad_ref,
    key_sum_ref,
    value_sum_ref,
):
    step = pl.program_id(1)
    query, key, grad = query_ref[...], key_ref[...], grad_ref[...]
    scores = matmul_nt(key, query) * scale
    scores = jnp.where(seg_column_ref[...] == seg_row_ref[...], scores, masked_score)
    probs = jnp.exp(scores - total_ref[...])
    products = grad.astype(f32) * out_ref[...].astype(f32)
    delta = jnp.sum(products.T, axis=0, keepdims=True)
    score_grad = (probs * (matmul_nt(value_ref[...], grad) - delta)).astype(bf16)
    query_grad_ref[...] = (matmul(key.T, score_grad) * scale).T
    key_part = matmul(score_grad, query) * scale
    value_part = matmul(probs.astype(bf16), grad)

    @pl.when(step == 0)
    def _():
        key_sum_ref[...] = key_part
        value_sum_ref[...] = value_part

    @pl.when(step > 0)
    def _():
        key_sum_ref[...] += key_part
        value_sum_ref[...] += value_part

    @pl.when(step == pl.num_programs(1) - 1)
    def _():
        key_grad_ref[...] = key_sum_ref[...].astype(bf16)
        value_grad_ref[...] = value_sum_ref[...].astype(bf16)


def attention_specs(rows, keys, heads, head_dim):
    block = min(rows, QUERY_BLOCK)
    query = pl.BlockSpec((block, head_dim), lambda h, i: (i, h))
    return (
        (heads, rows // block),
        [
            query,
            pl.BlockSpec((keys, head_dim), lambda h, i: (0, h)),
            pl.BlockSpec((keys, head_dim), lambda h, i: (0, h + heads)),
            pl.BlockSpec((None, 1, block), lambda h, i: (i, 0, 0)),
            pl.BlockSpec((keys, 1), lambda h, i: (0, 0)),
        ],
        query,
        pl.BlockSpec((None, None, 1, block), lambda h, i: (h, i, 0, 0)),
        pl.BlockSpec((keys, head_dim), lambda h, i: (0, h)),
    )


def run_attend(query_b, group, seg_rows, seg_columns, heads, scale):
    rows, keys = query_b.shape[0], group.shape[0]
    head_dim = query_b.shape[1] // heads
    grid, specs, query, total, unused = attention_specs(rows, keys, heads, head_dim)
    work = heads * rows * keys
    return pl.pallas_call(
        functools.partial(attend, scale),
        grid=grid,
        in_specs=specs,
        out_specs=[query, total],
        out_shape=[
            jax.ShapeDtypeStruct(query_b.shape, bf16),
            jax.ShapeDtypeStruct((*grid, 1, rows // grid[1]), f32),
        ],
        compiler_params=params(2),
        cost_estimate=pl.CostEstimate(
            flops=4 * work * head_dim, bytes_accessed=8 * query_b.size, transcendentals=work
        ),
        name="attend",
    )(query_b, group, group, seg_rows, seg_columns)


def run_attend_back(query_b, group, seg_rows, seg_columns, out_b, total, grad_b, heads, scale):
    rows, keys = query_b.shape[0], group.shape[0]
    head_dim = query_b.shape[1] // heads
    grid, specs, query, total_spec, key = attention_specs(rows, keys, heads, head_dim)
    work = heads * rows * keys
    return pl.pallas_call(
        functools.partial(attend_back, scale),
        grid=grid,
        in_specs=[*specs, query, total_spec, query],
        out_specs=[query, key, key],
        out_shape=[
            jax.ShapeDtypeStruct(query_b.shape, f32),
            jax.ShapeDtypeStruct((keys, query_b.shape[1]), bf16),
            jax.ShapeDtypeStruct((keys, query_b.shape[1]), bf16),
        ],
        scratch_shapes=[pltpu.VMEM((keys, head_dim), f32)] * 2,
        compiler_params=params(2),
        cost_estimate=pl.CostEstimate(
            flops=10 * work * head_dim, bytes_accessed=16 * query_b.size, transcendentals=work
        ),
        name="attend_back",
    )(query_b, group, group, seg_rows, seg_columns, out_b, total, grad_b)


def beside(values):
    return lax.ppermute(values, "fsdp", [(0, 1), (1, 0), (2, 3), (3, 2)])


def across(values):
    return lax.ppermute(values, "fsdp", [(0, 2), (1, 3), (2, 0), (3, 1)])


def other(values):
    return lax.ppermute(values, "ctx", [(0, 1), (1, 0)])


def added(*values):
    total = values[0].astype(f32)
    for value in values[1:]:
        total = total + value.astype(f32)
    return total.astype(bf16)


def then(first, *values):
    return lax.optimization_barrier((first, *values))[1:]


def by_chips():
    return lax.axis_size("fsdp") == 4 and lax.axis_size("ctx") == 2


def chunk_order(chunks):
    if not by_chips():
        return jnp.arange(chunks, dtype=jnp.int32)
    fsdp, ctx = lax.axis_index("fsdp"), lax.axis_index("ctx")
    sibling = fsdp + 1 - 2 * lax.rem(fsdp, 2)
    flip = lambda core: lax.rem(core + 2, 4)
    places = (
        (flip(sibling), ctx),
        (flip(fsdp), ctx),
        (sibling, 1 - ctx),
        (fsdp, 1 - ctx),
        (flip(sibling), 1 - ctx),
        (flip(fsdp), 1 - ctx),
        (sibling, ctx),
        (fsdp, ctx),
    )
    return jnp.stack([jnp.asarray(2 * f + c, jnp.int32) for f, c in places])


def expert_steps(ids, own_tokens, grad_all, rank_rows, rank_columns, first, weights):
    gate_weight, up_weight, down_weight = weights
    chunks = rank_rows.shape[0]

    def one_pass(at, near, far, product, kept):
        return run_expert_pass(
            jnp.array([at, at + 1], jnp.int32),
            first,
            rank_rows,
            rank_columns,
            near,
            far,
            product,
            gate_weight,
            up_weight,
            kept,
        )

    if not by_chips():
        token_all = lax.all_gather(own_tokens, ROWS, axis=0, tiled=True)
        blocks = token_all.reshape(chunks, CHUNK, -1)
        grad_slots, product = run_select_grads(ids, rank_rows, grad_all, down_weight)
        kept, backs = (), []
        for at in range(0, chunks, 2):
            kept, near, far = one_pass(at, blocks[at], blocks[at + 1], product, kept)
            backs += [near, far]
        back_sum = lax.psum_scatter(
            jnp.concatenate(backs), ROWS, scatter_dimension=0, tiled=True
        )
        out_part = run_expert_sums(ids, rank_columns, kept[1], down_weight)
        return kept, grad_slots, back_sum, out_part

    from_across, from_other = across(own_tokens), other(own_tokens)
    from_beside = beside(own_tokens)
    grad_slots, product = run_select_grads(ids, rank_rows, grad_all, down_weight)
    from_across, from_other = then(product, from_across, from_other)
    kept, back_sum, out_part = run_exchange_pass(
        rank_rows,
        rank_columns,
        product,
        weights,
        (own_tokens, from_beside, from_across, from_other),
    )
    return kept, grad_slots, back_sum, out_part


def head_blocks(width, head_dim):
    for at in range(0, width, head_dim):
        yield slice(at, at + head_dim)


def project(
    input_ref,
    gain_ref,
    weight_ref,
    cosine_ref,
    sine_ref,
    head_gain_ref,
    normed_ref,
    inverse_ref,
    pre_ref,
    query_ref,
    group_ref,
):
    values = input_ref[...].astype(f32)
    inverse = norm_scale(values)
    normed = (values * inverse * gain_ref[...]).astype(bf16)
    normed_ref[...] = normed
    inverse_ref[...] = inverse
    qkv = matmul(normed, weight_ref[...])
    width = query_ref.shape[1]
    head_dim = cosine_ref.shape[1]
    pre_ref[...] = qkv[:, : 2 * width]
    cosine, sine = cosine_ref[...], sine_ref[...]
    for which in (0, 1):
        gain = head_gain_ref[which : which + 1, :]
        for at in head_blocks(width, head_dim):
            head = qkv[:, which * width + at.start : which * width + at.stop]
            head = head * norm_scale(head) * gain
            turned = head * cosine + pltpu.roll(head, head_dim // 2, 1) * sine
            to_ref = query_ref if which == 0 else group_ref
            to_ref[:, at] = turned.astype(bf16)
    group_ref[:, width : 2 * width] = qkv[:, 2 * width :].astype(bf16)


def project_back(
    query_grad_ref,
    group_grad_ref,
    pre_ref,
    cosine_ref,
    sine_ref,
    head_gain_ref,
    weight_ref,
    input_ref,
    inverse_ref,
    gain_ref,
    grad_ref,
    part_ref,
    along_ref,
    terms_ref,
    head_terms_ref,
):
    width = query_grad_ref.shape[1]
    head_dim = cosine_ref.shape[1]
    cosine, sine = cosine_ref[...], sine_ref[...]

    @pl.when(pl.program_id(0) == 0)
    def _():
        terms_ref[...] = jnp.zeros_like(terms_ref)
        head_terms_ref[...] = jnp.zeros_like(head_terms_ref)

    for which in (0, 1):
        gain = head_gain_ref[which : which + 1, :]
        from_ref = query_grad_ref if which == 0 else group_grad_ref
        for at in head_blocks(width, head_dim):
            own = slice(which * width + at.start, which * width + at.stop)
            grad = from_ref[:, at].astype(f32)
            incoming = grad * cosine - pltpu.roll(grad, head_dim // 2, 1) * sine
            head = pre_ref[:, own]
            value_grad, gain_terms = norm_back(incoming, head, norm_scale(head), gain)
            grad_ref[:, own] = value_grad.astype(bf16)
            head_terms_ref[which : which + 1, :] += jnp.sum(gain_terms, axis=0, keepdims=True)
    grad_ref[:, 2 * width :] = group_grad_ref[:, width:]
    part = matmul_nt(grad_ref[...], weight_ref[...])
    part_ref[...] = part.astype(bf16)
    product = part * input_ref[...].astype(f32)
    terms_ref[...] += jnp.sum(product * inverse_ref[...], axis=0, keepdims=True)
    along_ref[...] = jnp.sum(product * gain_ref[...], axis=1, keepdims=True)


def run_project(input_b, gain, full, cosine, sine, head_gains, width):
    rows, depth = input_b.shape
    head_dim = cosine.shape[1]
    block = min(rows, QUERY_BLOCK)
    by_rows = lambda columns: pl.BlockSpec((block, columns), lambda i: (i, 0))
    return pl.pallas_call(
        project,
        grid=(rows // block,),
        in_specs=[
            by_rows(depth),
            once((1, depth)),
            once((depth, 3 * width)),
            by_rows(head_dim),
            by_rows(head_dim),
            once((2, head_dim)),
        ],
        out_specs=[
            by_rows(depth),
            by_rows(1),
            by_rows(2 * width),
            by_rows(width),
            by_rows(2 * width),
        ],
        out_shape=[
            jax.ShapeDtypeStruct((rows, depth), bf16),
            jax.ShapeDtypeStruct((rows, 1), f32),
            jax.ShapeDtypeStruct((rows, 2 * width), f32),
            jax.ShapeDtypeStruct((rows, width), bf16),
            jax.ShapeDtypeStruct((rows, 2 * width), bf16),
        ],
        compiler_params=params(1),
        cost_estimate=pl.CostEstimate(
            flops=6 * rows * depth * width, bytes_accessed=6 * depth * width, transcendentals=0
        ),
        name="project",
    )(input_b, gain, full, cosine, sine, head_gains)


def run_project_back(
    query_grad, group_grad, pre, cosine, sine, head_gains, full, input_b, inverse, gain
):
    rows, depth = input_b.shape
    width = query_grad.shape[1]
    head_dim = cosine.shape[1]
    block = min(rows, QUERY_BLOCK)
    by_rows = lambda columns: pl.BlockSpec((block, columns), lambda i: (i, 0))
    whole = lambda shape: pl.BlockSpec(shape, lambda i: (0, 0))
    return pl.pallas_call(
        project_back,
        grid=(rows // block,),
        in_specs=[
            by_rows(width),
            by_rows(2 * width),
            by_rows(2 * width),
            by_rows(head_dim),
            by_rows(head_dim),
            once((2, head_dim)),
            once((depth, 3 * width)),
            by_rows(depth),
            by_rows(1),
            once((1, depth)),
        ],
        out_specs=[
            by_rows(3 * width),
            by_rows(depth),
            by_rows(1),
            whole((1, depth)),
            whole((2, head_dim)),
        ],
        out_shape=[
            jax.ShapeDtypeStruct((rows, 3 * width), bf16),
            jax.ShapeDtypeStruct((rows, depth), bf16),
            jax.ShapeDtypeStruct((rows, 1), f32),
            jax.ShapeDtypeStruct((1, depth), f32),
            jax.ShapeDtypeStruct((2, head_dim), f32),
        ],
        compiler_params=params(1),
        cost_estimate=pl.CostEstimate(
            flops=6 * rows * depth * width, bytes_accessed=8 * depth * width, transcendentals=0
        ),
        name="project_back",
    )(query_grad, group_grad, pre, cosine, sine, head_gains, full, input_b, inverse, gain)


def grads_scatter(
    size,
    local,
    in_ref,
    small_ref,
    rows_ref,
    grad_rows_ref,
    gate_grad_ref,
    up_grad_ref,
    hidden_ref,
    out_ref,
    total_ref,
    gate_out_ref,
    up_out_ref,
    down_out_ref,
    staged_ref,
    landed_ref,
    small_landed_ref,
    first_ref,
    second_ref,
    send_sem,
    recv_sem,
    small_send_sem,
    small_recv_sem,
):
    step, part = pl.program_id(0), pl.program_id(1)
    place = lax.axis_index("tp")
    extent = out_ref.shape[0]

    def block(index):
        return in_ref[pl.ds(pl.multiple_of(index * extent, extent), extent), :].astype(f32)

    def copying(way, stage, to):
        return pltpu.make_async_remote_copy(
            src_ref=staged_ref.at[way, stage],
            dst_ref=landed_ref.at[way, stage],
            send_sem=send_sem.at[way, stage],
            recv_sem=recv_sem.at[way, stage],
            device_id={"tp": to},
            device_id_type=MESH,
        )

    def small_copy(offset, peer):
        return pltpu.make_async_remote_copy(
            src_ref=small_ref,
            dst_ref=small_landed_ref.at[offset - 1],
            send_sem=small_send_sem.at[offset - 1],
            recv_sem=small_recv_sem.at[offset - 1],
            device_id={"tp": peer},
            device_id_type=MESH,
        )

    def ways():
        yield 0, place, place + 1, place - 1
        yield 1, size - 1 - place, place - 1, place + 1

    def send(stage):
        for way, rank, to, origin in ways():
            target = size - 1 - stage + place if way == 0 else place - (size - 1 - stage)

            @pl.when(jnp.logical_and(rank <= stage, rank < size - 1))
            def _():
                values = block(target)
                if stage == 0:
                    staged_ref[way, stage] = values.astype(bf16)
                else:

                    @pl.when(rank == 0)
                    def _():
                        staged_ref[way, stage] = values.astype(bf16)

                    @pl.when(rank > 0)
                    def _():
                        landed = landed_ref[way, stage - 1].astype(f32)
                        staged_ref[way, stage] = (values + landed).astype(bf16)

                copying(way, stage, to).start()

    def receive(stage):
        for way, rank, to, origin in ways():

            @pl.when(jnp.logical_and(rank > 0, rank - 1 <= stage))
            def _():
                copying(way, stage, origin).wait_recv()

    @pl.when(jnp.logical_and(step == 0, part == 0))
    def _():
        peer_barrier("tp", size)
        for offset in range(1, size):
            small_copy(offset, lax.rem(place + offset, size)).start()
        send(0)

    for stage in range(1, size - 1):

        @pl.when(jnp.logical_and(step == min(2 * stage, 2 * local - 1), part == 0))
        def _():
            receive(stage - 1)
            send(stage)

    def flat(ref):
        return ref[...].reshape(ref.shape[0] * ref.shape[1], ref.shape[2])

    def collect(sum_ref, values):
        @pl.when(part == 0)
        def _():
            sum_ref[...] = values

        @pl.when(part == 1)
        def _():
            sum_ref[...] += values

    @pl.when(step < local)
    def _():
        rows = flat(rows_ref)
        collect(first_ref, matmul(flat(gate_grad_ref).T, rows))
        collect(second_ref, matmul(flat(up_grad_ref).T, rows))

        @pl.when(part == 1)
        def _():
            gate_out_ref[...] = first_ref[...].T
            up_out_ref[...] = second_ref[...].T

    @pl.when(step >= local)
    def _():
        collect(down_out_ref, matmul(flat(hidden_ref).T, flat(grad_rows_ref)))

    @pl.when(jnp.logical_and(step == 2 * local - 1, part == 1))
    def _():
        total = small_ref[...]
        for offset in range(1, size):
            small_copy(offset, lax.rem(place + size - offset, size)).wait_recv()
            total = total + small_landed_ref[offset - 1]
        total_ref[...] = total
        receive(size - 2)
        out_ref[...] = block(place)
        for way, rank, to, origin in ways():

            @pl.when(rank > 0)
            def _():
                out_ref[...] += landed_ref[way, size - 2].astype(f32)

        for offset in range(1, size):
            small_copy(offset, lax.rem(place + offset, size)).wait_send()
        for stage in range(size - 1):
            for way, rank, to, origin in ways():

                @pl.when(jnp.logical_and(rank <= stage, rank < size - 1))
                def _():
                    copying(way, stage, to).wait_send()


def run_grads_scatter(values, small, token_slots, grad_slots, gate_grad, up_grad, hidden_rows):
    size = lax.axis_size("tp")
    rows, width = values.shape
    shape = (rows // size, width)
    chunks, local, slots, hidden = hidden_rows.shape
    half = chunks // 2
    early = lambda i, k: jnp.minimum(i, local - 1)
    late = lambda i, k: jnp.maximum(i - local, 0)
    early_part = lambda i, k: jnp.where(i < local, k, 1)
    late_part = lambda i, k: jnp.where(i < local, 0, k)
    wide = lambda at, part: pl.BlockSpec(
        (half, None, slots, width), lambda i, k: (part(i, k), at(i, k), 0, 0)
    )
    thin = lambda at, part: pl.BlockSpec(
        (half, None, slots, hidden), lambda i, k: (part(i, k), at(i, k), 0, 0)
    )
    tall = pl.BlockSpec((None, width, hidden), lambda i, k: (early(i, k), 0, 0))
    fixed = lambda form: pl.BlockSpec(form, lambda i, k: (0,) * len(form))
    return pl.pallas_call(
        functools.partial(grads_scatter, size, local),
        grid=(2 * local, 2),
        in_specs=[
            once(values.shape),
            once(small.shape),
            wide(early, early_part),
            wide(late, late_part),
            thin(early, early_part),
            thin(early, early_part),
            thin(late, late_part),
        ],
        out_specs=[
            fixed(shape),
            fixed(small.shape),
            tall,
            tall,
            pl.BlockSpec((None, hidden, width), lambda i, k: (late(i, k), 0, 0)),
        ],
        out_shape=[
            jax.ShapeDtypeStruct(shape, f32),
            jax.ShapeDtypeStruct(small.shape, f32),
            jax.ShapeDtypeStruct((local, width, hidden), f32),
            jax.ShapeDtypeStruct((local, width, hidden), f32),
            jax.ShapeDtypeStruct((local, hidden, width), f32),
        ],
        scratch_shapes=[
            pltpu.VMEM((2, size - 1, *shape), bf16),
            pltpu.VMEM((2, size - 1, *shape), bf16),
            pltpu.VMEM((size - 1, *small.shape), f32),
            pltpu.VMEM((hidden, width), f32),
            pltpu.VMEM((hidden, width), f32),
            pltpu.SemaphoreType.DMA((2, size - 1)),
            pltpu.SemaphoreType.DMA((2, size - 1)),
            pltpu.SemaphoreType.DMA((size - 1,)),
            pltpu.SemaphoreType.DMA((size - 1,)),
        ],
        compiler_params=pltpu.CompilerParams(
            dimension_semantics=("arbitrary",) * 2,
            collective_id=10,
            has_side_effects=True,
            vmem_limit_bytes=VMEM_BYTES,
        ),
        cost_estimate=pl.CostEstimate(
            flops=6 * chunks * local * slots * width * hidden,
            bytes_accessed=150_000_000,
            transcendentals=0,
        ),
        name="grads_scatter",
    )(values, small, token_slots, grad_slots, gate_grad, up_grad, hidden_rows)


def split_three(values):
    high = values.astype(bf16)
    rest = values - high.astype(f32)
    middle = rest.astype(bf16)
    return (high, middle, (rest - middle.astype(f32)).astype(bf16))


def on_device(
    layer_input,
    token_order,
    doc_lengths,
    expert_routes,
    attn_gain,
    query_weight,
    key_weight,
    value_weight,
    query_gain,
    key_gain,
    out_weight,
    moe_gain,
    router_weight,
    gate_weight,
    up_weight,
    down_weight,
    out_grad,
):
    tp_index = lax.axis_index("tp")
    ctx_size = lax.axis_size("ctx")
    fc_size = lax.axis_size("fsdp") * ctx_size
    fc_index = lax.axis_index("fsdp") * ctx_size + lax.axis_index("ctx")
    tok_count, quarter = layer_input.shape
    share = tok_count // lax.axis_size("tp")
    head_dim = query_gain.shape[0]
    head_width = query_weight.shape[1]
    heads = head_width // head_dim
    scale = head_dim ** (-0.5)
    experts = router_weight.shape[1]
    top = expert_routes.shape[1]
    local_experts = gate_weight.shape[0]
    capacity = tok_count * top * 5 // (4 * experts)
    own_rows = lambda values: lax.dynamic_slice_in_dim(values, tp_index * share, share, 0)
    own_width = lambda values: lax.dynamic_slice_in_dim(values, tp_index * quarter, quarter, 1)

    packed = jnp.concatenate(
        [
            query_weight,
            key_weight,
            value_weight,
            out_weight.T,
            router_weight,
            attn_gain[:, None],
            moe_gain[:, None],
            jnp.zeros((attn_gain.shape[0], EXTRA - experts - 2), bf16),
        ],
        axis=1,
    )
    full = lax.all_gather(packed, ROWS, axis=0, tiled=True)
    expert_ids = jnp.arange(experts, dtype=jnp.int32)
    named = jnp.any(expert_routes[:, :, None] == expert_ids[None, None, :], axis=1)
    earlier = jnp.tri(tok_count, tok_count, -1, dtype=bf16)
    before = matmul(earlier, named.astype(bf16))
    first_slot = (lax.rem(fc_index, CHUNK // tok_count) * capacity).astype(f32)
    ranks = jnp.where(named, before + first_slot, -1.0).astype(bf16)
    input_b = gather_tp(layer_input, True, 0)
    segment, position = doc_places(token_order[0], doc_lengths[0])
    ctx_index = lax.axis_index("ctx")
    seg_columns = jnp.zeros((ctx_size, tok_count), f32)
    for offset in range(ctx_size):
        piece = segment.astype(f32)[None, :]
        if offset > 0:
            pairs = [(at, (at + offset) % ctx_size) for at in range(ctx_size)]
            piece = lax.ppermute(piece, "ctx", pairs)
        origin = lax.rem(ctx_index + ctx_size - offset, ctx_size)
        seg_columns = lax.dynamic_update_slice_in_dim(seg_columns, piece, origin, 0)
    out_grad, full, input_b, seg_columns = lax.optimization_barrier(
        (out_grad, full, input_b, seg_columns)
    )
    grad_rows_b = lax.all_gather(out_grad, "tp", axis=1, tiled=True)
    side = 3 * head_width
    qkv_weight = full[:, :side]
    full_out = full[:, side : side + head_width]
    side = side + head_width
    full_router = full[:, side : side + experts]
    attn_gain_f = full[:, side + experts].astype(f32)
    moe_gain_f = full[:, side + experts + 1].astype(f32)
    width = input_b.shape[1]
    cosine, sine = rope_tables(position, head_dim)
    head_gains = jnp.stack([query_gain, key_gain])
    attn_gain_row = attn_gain_f[None, :]
    normed, inverse_one, heads_pre, query_rows, group_part = run_project(
        input_b,
        attn_gain_row,
        full,
        cosine,
        sine,
        head_gains,
        head_width,
    )
    group = gather_ctx(group_part, 1)
    after_group, group = lax.optimization_barrier((grad_rows_b, group))
    grad_packed = jnp.concatenate(
        [after_group, ranks, jnp.zeros((tok_count, EXTRA - experts), bf16)], axis=1
    )
    grad_all = lax.all_gather(grad_packed, ROWS, axis=0, tiled=True)
    chunks = grad_all.shape[0] // CHUNK
    first_expert = fc_index * local_experts
    local_ranks = lax.dynamic_slice_in_dim(
        grad_all[:, width:], first_expert, local_experts, 1
    ).astype(jnp.int32)
    ids = chunk_order(chunks)
    rank_columns = jnp.stack(
        [
            lax.dynamic_slice_in_dim(local_ranks, ids[at] * CHUNK, CHUNK, 0)
            for at in range(chunks)
        ]
    )
    rank_rows = jnp.transpose(rank_columns, (0, 2, 1))[:, :, None, :]

    seg_rows = segment.astype(f32).reshape(-1, 1, min(tok_count, QUERY_BLOCK))
    seg_columns = seg_columns.reshape(-1, 1)
    attn_b, log_total = run_attend(query_rows, group, seg_rows, seg_columns, heads, scale)
    attn_part = matmul_nt(attn_b, full_out).astype(bf16)
    attn_out = scatter_tp(attn_part, False, 2)
    resid = own_rows(input_b).astype(f32) + attn_out
    inverse_two = norm_scale(resid)
    moe_in = (resid * inverse_two * moe_gain_f).astype(bf16)
    logits = matmul(moe_in, full_router)
    own_named = own_rows(named)
    chosen = jnp.where(own_named, logits, -jnp.inf)
    gates = jax.nn.softmax(chosen, axis=-1)
    own_tokens = gather_tp(
        jnp.concatenate(
            [moe_in, *split_three(gates), jnp.zeros((share, EXTRA - 3 * experts), bf16)], axis=1
        ),
        False,
        3,
    )
    kept, grad_slots, back_sum, out_part = expert_steps(
        ids,
        own_tokens,
        grad_all,
        rank_rows,
        rank_columns,
        first_expert.reshape(1),
        (gate_weight, up_weight, down_weight),
    )
    token_slots, hidden_rows, gate_act_grad, up_act_grad, route_part = kept
    hit = jnp.arange(chunks, dtype=jnp.int32)[:, None] == ids[None, :]
    route_all = jnp.sum(
        jnp.where(hit[:, :, None, None], route_part[None, :, :, 0, :], 0.0), axis=1
    )
    route_all = jnp.transpose(route_all, (1, 0, 2)).reshape(
        local_experts, fc_size, tok_count
    )
    route_all = lax.all_to_all(
        jnp.transpose(route_all, (1, 0, 2)), ROWS, split_axis=0, concat_axis=0, tiled=True
    ).reshape(experts, tok_count)

    back_rows, gate_grad, grad_gate, grad_up, grad_down = run_grads_scatter(
        back_sum, route_all, token_slots, grad_slots, gate_act_grad, up_act_grad, hidden_rows
    )
    parts = own_tokens[:, width : width + 3 * experts].astype(f32)
    all_gates = parts[:, :experts] + parts[:, experts : 2 * experts] + parts[:, 2 * experts :]
    gate_grad = gate_grad.T
    logit_grad = all_gates * (
        gate_grad - jnp.sum(all_gates * gate_grad, axis=-1, keepdims=True)
    )
    grad_router = lax.dot_general(
        own_tokens[:, :width].astype(f32),
        logit_grad,
        (((0,), (0,)), ((), ())),
        precision=highest,
    )
    own_logit_grad = own_rows(logit_grad)
    router_back = lax.dot_general(
        own_logit_grad, full_router.astype(f32), (((1,), (1,)), ((), ())), precision=highest
    )
    moe_in_grad = (
        back_rows + router_back
    )
    resid_norm_grad, gain_terms = norm_back(moe_in_grad, resid, inverse_two, moe_gain_f)
    grad_moe_gain = jnp.sum(gain_terms, axis=0)
    resid_grad = own_rows(grad_rows_b).astype(f32) + resid_norm_grad
    resid_grad_b = gather_tp(resid_grad.astype(bf16), False, 5)

    out_sum = lax.psum_scatter(out_part, ROWS, scatter_dimension=0, tiled=True)

    grad_out = lax.dot_general(
        resid_grad_b, attn_b, (((0,), (0,)), ((), ())), preferred_element_type=f32
    )
    attn_grad = matmul(resid_grad_b, full_out).astype(bf16)
    query_rot_grad, key_part, value_part = run_attend_back(
        query_rows, group, seg_rows, seg_columns, attn_b, log_total, attn_grad, heads, scale
    )
    out_sum, key_part = lax.optimization_barrier((out_sum, key_part))
    out_sum = lax.psum_scatter(out_sum, "tp", scatter_dimension=0, tiled=True).astype(f32)
    group_grad = scatter_ctx(jnp.concatenate([key_part, value_part], axis=1), 6)
    qkv_grad, normed_part, along, attn_terms, head_terms = run_project_back(
        query_rot_grad,
        group_grad,
        heads_pre,
        cosine,
        sine,
        head_gains,
        full,
        input_b,
        inverse_one,
        attn_gain_row,
    )
    along = along[:, 0]
    gains = jnp.concatenate([attn_terms[0], grad_moe_gain, head_terms[0], head_terms[1]])
    normed_grad, gains, along = close_tp(normed_part, gains, along, 7)
    along = along[:, None] / width
    normed_grad, out_sum = lax.optimization_barrier((normed_grad, out_sum))
    grad_gate, grad_up, grad_down = then(normed_grad, grad_gate, grad_up, grad_down)
    grad_gate, grad_up, grad_down = [
        lax.clamp(jnp.float32(-jnp.inf), grad, jnp.float32(jnp.inf))
        for grad in (grad_gate, grad_up, grad_down)
    ]
    layer_sum = resid + out_sum
    layer_output = lax.all_to_all(
        layer_sum.astype(bf16), "tp", split_axis=1, concat_axis=0, tiled=True
    )
    input_quarter = layer_input.astype(f32)
    gain_quarter = lax.dynamic_slice_in_dim(attn_gain_f, tp_index * quarter, quarter, 0)
    grad_input = own_width(resid_grad_b).astype(f32) + inverse_one * (
        normed_grad * gain_quarter - input_quarter * inverse_one * inverse_one * along
    )
    grad_qkv = lax.dot_general(
        normed, qkv_grad, (((0,), (0,)), ((), ())), preferred_element_type=f32
    )
    owned_out = lax.psum_scatter(
        jnp.concatenate(
            [grad_out, grad_router, jnp.zeros((width, EXTRA - experts), f32)], axis=1
        ).astype(bf16),
        ROWS,
        scatter_dimension=0,
        tiled=True,
    )
    (owned_out,) = then(normed_grad, owned_out)
    owned_out = owned_out.astype(f32)
    owned_qkv = lax.psum_scatter(
        grad_qkv.astype(bf16), ROWS, scatter_dimension=0, tiled=True
    ).astype(f32)
    owned_gain = attn_gain.shape[0]
    own_gain = lambda at: lax.dynamic_slice_in_dim(
        gains, at * width + fc_index * owned_gain, owned_gain, 0
    )
    return (
        layer_output,
        grad_input,
        own_gain(0),
        owned_qkv[:, :head_width],
        owned_qkv[:, head_width : 2 * head_width],
        owned_qkv[:, 2 * head_width :],
        gains[2 * width : 2 * width + head_dim],
        gains[2 * width + head_dim :],
        owned_out[:, :head_width].T,
        own_gain(1),
        owned_out[:, head_width : head_width + experts],
        grad_gate,
        grad_up,
        grad_down,
    )


def solution(mesh):
    in_specs = (
        P(("fsdp", "ctx"), "tp"),
        P("fsdp", "ctx"),
        P("fsdp", None),
        P(("fsdp", "ctx"), None),
        P(("fsdp", "ctx")),
        P(("fsdp", "ctx"), "tp"),
        P(("fsdp", "ctx"), "tp"),
        P(("fsdp", "ctx"), "tp"),
        P(),
        P(),
        P("tp", ("fsdp", "ctx")),
        P(("fsdp", "ctx")),
        P(("fsdp", "ctx"), None),
        P(("fsdp", "ctx"), None, "tp"),
        P(("fsdp", "ctx"), None, "tp"),
        P(("fsdp", "ctx"), "tp", None),
        P(("fsdp", "ctx"), "tp"),
    )
    out_specs = (
        P(("fsdp", "ctx"), "tp"),
        P(("fsdp", "ctx"), "tp"),
        P(("fsdp", "ctx")),
        P(("fsdp", "ctx"), "tp"),
        P(("fsdp", "ctx"), "tp"),
        P(("fsdp", "ctx"), "tp"),
        P(),
        P(),
        P("tp", ("fsdp", "ctx")),
        P(("fsdp", "ctx")),
        P(("fsdp", "ctx"), None),
        P(("fsdp", "ctx"), None, "tp"),
        P(("fsdp", "ctx"), None, "tp"),
        P(("fsdp", "ctx"), "tp", None),
    )
    return jax.shard_map(
        on_device, mesh=mesh, in_specs=in_specs, out_specs=out_specs, check_vma=False
    )
```
